32 devices in a mesh: dp: 8 (over z, y), tensor: 4 (over x, core).
Axes of the slice: x: 2, y: 2, z: 4, core: 2. Of those that a mesh axis runs over, the one named last changes fastest.
Arguments:
- grad_up: bfloat16 [8, 512, 6144], P('dp', None, 'tensor'), may hold values from -400 to 400, as said below
- error_up: bfloat16 [8, 512, 6144], P('dp', None, 'tensor'), may hold values from -3 to 3
- grad_down: bfloat16 [8, 6144, 512], P('dp', 'tensor'), may hold values from -400 to 400, as said below
- error_down: bfloat16 [8, 6144, 512], P('dp', 'tensor'), may hold values from -3 to 3
- q_up: float32 [6144, 64], P('tensor'), may hold values from -6 to 6
- q_down: float32 [512, 64], replicated, may hold values from -6 to 6
Outputs:
- new_error_up: bfloat16 [8, 512, 6144], P('dp', None, 'tensor')
- update_up: bfloat16 [512, 6144], P(None, 'tensor')
- new_error_down: bfloat16 [8, 6144, 512], P('dp', 'tensor')
- update_down: bfloat16 [6144, 512], P('tensor')
The draws below stay inside these ranges and needn't reach their ends.
Inputs may be any that keep to these rules, and one draw needn't show every extreme that they name: `grad_up`: no structure beyond the range is promised. `grad_down`: no structure beyond the range is promised.
All inputs are finite; a program needn't handle non-finite values.
Results may differ from the reference program's by a relative error of at most 0.001.
Values sent between devices are 32-bit elements; how exact they have to be, the bound alone decides.
No kernel may reach another device: no remote copies, remote signals or barrier semaphores. Data moves between devices by JAX's collectives and lax.ppermute only.
A program may use at most 64 MiB of HBM per device.

```python
import math
import jax
import jax.numpy as jnp
from jax import lax

RANK = 64
ROWS = 512
FF = 6144
N_DP = 8


def scaled_draw(key, first, second, rise_first, shared, own, span):
    key_shared, key_own, key_first, key_second = jax.random.split(key, 4)
    common = jnp.clip(jax.random.normal(key_shared, (1, first, second), jnp.float32), -6.0, 6.0)
    alone = jnp.clip(jax.random.normal(key_own, (N_DP, first, second), jnp.float32), -6.0, 6.0)
    scale_first = jnp.exp(jax.random.uniform(key_first, (1, first, 1), jnp.float32) * math.log(span))
    scale_second = jnp.exp(jax.random.uniform(key_second, (1, 1, second), jnp.float32) * math.log(10.0))
    rising_first = jnp.exp(math.log(3.0) * rise_first * jnp.arange(first, dtype=jnp.float32) / first)
    rising_second = jnp.exp(math.log(3.0) * (1.0 - rise_first) * jnp.arange(second, dtype=jnp.float32) / second)
    values = (shared * common + own * alone) * scale_first * scale_second
    values = values * rising_first[None, :, None] * rising_second[None, None, :] * 0.05
    return values.astype(jnp.bfloat16)


def draw_grad_up(key, part):
    key = jax.random.fold_in(key, 11)
    return scaled_draw(key, ROWS, FF, 0.0, 0.7, 0.7, 10.0)


def draw_grad_down(key, part):
    key = jax.random.fold_in(key, 23)
    return scaled_draw(key, FF, ROWS, 1.0, 0.7, 0.7, 10.0)


def levels(key, extent, shards, low, largest):
    loudness = 1.0
    for dim, blocks in shards:
        heights = jax.random.uniform(jax.random.fold_in(jax.random.fold_in(key, 6), dim), (blocks,), jnp.float32, low / len(shards), largest / len(shards))
        loudness = loudness * jnp.repeat(jnp.exp(heights), extent[dim] // blocks).reshape((-1,) + (1,) * (len(extent) - 1 - dim))
    return loudness


def scatter_about(key, shape, spread, bound, shards=(), kind=jnp.bfloat16):
    level = levels(key, shape, shards, -0.22, 0.18) if shards else 1.0
    result = jax.random.normal(key, shape, jnp.float32) * spread * level
    return jnp.minimum(jnp.maximum(result, -bound), bound).astype(kind)


def setup_inputs(seed: int = 0) -> dict:
    seeds = jax.random.split(jax.random.key(seed), 7)
    grad_up = draw_grad_up(jax.random.fold_in(seeds[6], 71), 0)
    error_up = scatter_about(seeds[1], (N_DP, ROWS, FF), 0.5, 3.0, ((0, 8), (2, 4)))
    grad_down = draw_grad_down(jax.random.fold_in(seeds[6], 71), 0)
    error_down = scatter_about(seeds[3], (N_DP, FF, ROWS), 0.5, 3.0, ((0, 8), (1, 4)))
    q_up = scatter_about(seeds[4], (FF, RANK), 1.0, 6.0, ((0, 4),), jnp.float32)
    q_down = scatter_about(seeds[5], (ROWS, RANK), 1.0, 6.0, (), jnp.float32)
    return {"grad_up": grad_up, "error_up": error_up, "grad_down": grad_down, "error_down": error_down, "q_up": q_up, "q_down": q_down}


HIGHEST = lax.Precision.HIGHEST
CLIP_RMS = 0.1

def replica_mean(grad, error):

    def accumulate(position, running):
        return running + grad[position].astype(jnp.float32) + error[position].astype(jnp.float32)
    start = jnp.zeros(grad.shape[1:], jnp.float32)
    return lax.fori_loop(0, N_DP, accumulate, start) / N_DP

def orthonormal(left):
    gram_left = jnp.dot(left.T, left, precision=HIGHEST)
    factor = jnp.linalg.cholesky(gram_left)
    return lax.linalg.triangular_solve(factor, left, left_side=False, lower=True, transpose_a=True)

def compress(mean_merged, previous):
    left = jnp.dot(mean_merged, previous, precision=HIGHEST)
    basis = orthonormal(left)
    right = jnp.dot(mean_merged.T, basis, precision=HIGHEST)
    return jnp.dot(basis, right.T, precision=HIGHEST)

def reference(grad_up, error_up, grad_down, error_down, q_up, q_down):
    rebuilt_up = compress(replica_mean(grad_up, error_up), q_up)
    rebuilt_down = compress(replica_mean(grad_down, error_down), q_down)
    norm_sq = jnp.sum(rebuilt_up * rebuilt_up) + jnp.sum(rebuilt_down * rebuilt_down)
    limit = CLIP_RMS * jnp.sqrt(jnp.float32(2 * ROWS * FF))
    clip_factor = jnp.minimum(jnp.float32(1.0), limit / jnp.sqrt(norm_sq))

    def residual_up(pair):
        return (pair[0].astype(jnp.float32) + pair[1].astype(jnp.float32) - rebuilt_up).astype(jnp.bfloat16)

    def residual_down(pair):
        return (pair[0].astype(jnp.float32) + pair[1].astype(jnp.float32) - rebuilt_down).astype(jnp.bfloat16)
    new_error_up = lax.map(residual_up, (grad_up, error_up))
    new_error_down = lax.map(residual_down, (grad_down, error_down))
    update_up = (clip_factor * rebuilt_up).astype(jnp.bfloat16)
    update_down = (clip_factor * rebuilt_down).astype(jnp.bfloat16)
    return (new_error_up, update_up, new_error_down, update_down)
```

```python
import functools

import jax
import jax.numpy as jnp
from jax import lax
from jax.experimental import pallas as pl
from jax.experimental.pallas import tpu as pltpu
from jax.sharding import PartitionSpec as P

F32 = jnp.float32
BF16 = jnp.bfloat16
HIGHEST = lax.Precision.HIGHEST
CLIP_RMS = 0.1
STEPS = 4
VMEM_LIMIT = 48 * 1024 * 1024


def split3(x):
    first = x.astype(BF16)
    rest = x - first.astype(F32)
    second = rest.astype(BF16)
    return first, second, (rest - second.astype(F32)).astype(BF16)


def tree_sum(values):
    values = list(values)
    while len(values) > 1:
        values = [values[i] + values[i + 1] for i in range(0, len(values), 2)]
    return values[0]


def dot(a, b, dims=((1,), (0,)), precision=None):
    return lax.dot_general(a, b, (dims, ((), ())), precision=precision, preferred_element_type=F32)


def scatter_chunks(total, stage, keep, send):
    n_dp, per, _ = stage.shape
    me = lax.axis_index("dp")
    for c in range(n_dp):
        stage[c] = total[c * per : (c + 1) * per, :]
    for d in range(n_dp):
        (send if d % 2 else keep)[d // 2] = stage[lax.bitwise_xor(me, d)]


def gather_chunks(pieces, stage, total, start):
    n_dp, per, _ = stage.shape
    width = pieces[0].shape[1]
    me = lax.axis_index("dp")
    for d, piece in enumerate(pieces):
        stage[lax.bitwise_xor(me, d), :, :width] = piece[...]
    for c in range(n_dp):
        total[c * per : (c + 1) * per, start : start + width] = stage[c, :, :width]


def left_kernel(gu, eu, gd, ed, qu, qd, keep, send, qsu, qsd, total, stage):
    step = pl.program_id(0)
    rank = qu.shape[1]
    rows = total.shape[1] - qu.shape[0]

    @pl.when(step == 0)
    def _():
        for q, qs in ((qu, qsu), (qd, qsd)):
            first, second, third = split3(q[...])
            qs[:, :rank] = first
            qs[:, rank : 2 * rank] = second
            qs[:, 2 * rank : 3 * rank] = third
            qs[:, 3 * rank :] = jnp.zeros_like(third)

    def term(g, e, qs, start):
        block = g.shape[1]
        t = dot(g[0], qs[...]) + dot(e[0], qs[...])
        t = (t[:, : 2 * rank] + t[:, 2 * rank :]).T
        total[:, pl.ds(pl.multiple_of(start + step * block, 128), block)] = t[:rank] + t[rank:]

    term(gu, eu, qsu, 0)
    term(gd, ed, qsd, rows)

    @pl.when(step == STEPS - 1)
    def _():
        scatter_chunks(total, stage, keep, send)


def right_kernel(n_dp, gu, eu, gd, ed, *refs):
    step = pl.program_id(0)
    up, down = refs[:n_dp], refs[n_dp : 2 * n_dp]
    left, gram_up, gram_down, keep, send, pieces, total, stage = refs[2 * n_dp :]
    rank = left.shape[0]
    rows = gu.shape[1]
    ff = left.shape[1] - rows
    block = gu.shape[2]
    depth = gd.shape[1]

    @pl.when(step == 0)
    def _():
        gather_chunks(up, stage, left, 0)
        gather_chunks(down, stage, left, rows)
        for i, piece in enumerate(split3(left[...])):
            pieces[i * rank : (i + 1) * rank, :] = piece
        nt = ((1,), (1,))
        gram_up[...] = dot(left[:, :rows], left[:, :rows], nt, HIGHEST)
        gram_down[...] = dot(left[:, rows:], left[:, rows:], nt, HIGHEST)
        total[:, ff:] = jnp.zeros((rank, rows), F32)

    def fold(t):
        return t[:rank] + (t[rank : 2 * rank] + t[2 * rank :])

    lhs = pieces[:, :rows]
    total[:, pl.ds(pl.multiple_of(step * block, 128), block)] = fold(dot(lhs, gu[0]) + dot(lhs, eu[0]))
    lhs = pieces[:, pl.ds(pl.multiple_of(rows + step * depth, 128), depth)]
    total[:, ff:] += fold(dot(lhs, gd[0]) + dot(lhs, ed[0]))

    @pl.when(step == STEPS - 1)
    def _():
        scatter_chunks(total, stage, keep, send)


def half_kernel(keep, got, *outs):
    for i, out in enumerate(outs):
        out[...] = keep[i] + got[i]


def mean_kernel(n_dp, split, *refs):
    total = tree_sum(ref[...] for ref in refs[:-2]) / n_dp
    refs[-2][...] = total[:, :split]
    refs[-1][...] = total[:, split:]


def sum_kernel(*refs):
    refs[-1][...] = tree_sum(ref[...] for ref in refs[:-1])


def basis_kernel(left, gram_up, *refs):
    *grams, inv_up, inv_down, lhs_up, lhs_down = refs
    rank = left.shape[0]
    rows = lhs_up.shape[0]
    row_id = lax.broadcasted_iota(jnp.int32, (rank, 2 * rank), 0)
    lane_id = lax.broadcasted_iota(jnp.int32, (rank, 2 * rank), 1)
    eye = (lane_id == row_id + rank).astype(F32)

    def start(gram):
        return jnp.concatenate([gram, jnp.zeros_like(gram)], axis=1) + eye

    state = [start(gram_up[...]), start(tree_sum(g[...] for g in grams))]
    for k in range(rank):
        for s in range(2):
            a = state[s]
            pivot_row = a[k : k + 1, :]
            below = row_id[:, :1] > k
            factor = jnp.where(below, a[:, k : k + 1], 0.0) / a[k : k + 1, k : k + 1]
            state[s] = a - factor * pivot_row
    for a, inv, lhs, part in ((state[0], inv_up, lhs_up, slice(0, rows)), (state[1], inv_down, lhs_down, slice(rows, None))):
        diagonal = jnp.sum(jnp.where(lane_id == row_id, a, 0.0), axis=1, keepdims=True)
        inverse = (a / jnp.sqrt(diagonal))[:, rank:]
        inv[...] = inverse
        first, second, _ = split3(dot(inverse, left[:, part], precision=HIGHEST).T)
        lhs[:, :rank] = first
        lhs[:, rank : 2 * rank] = first
        lhs[:, 2 * rank : 3 * rank] = second
        lhs[:, 3 * rank :] = second


def factor_kernel(n_dp, inv_up, inv_down, *refs):
    up, down = refs[:n_dp], refs[n_dp : 2 * n_dp]
    rhs, sq_up, sq_down, total, stage = refs[2 * n_dp :]
    rank = total.shape[0]
    ff = up[0].shape[1]
    gather_chunks(up, stage, total, 0)
    gather_chunks(down, stage, total, ff)
    for inv, part, sq in ((inv_up, slice(0, ff), sq_up), (inv_down, slice(ff, None), sq_down)):
        right = dot(inv[...], total[:, part], precision=HIGHEST)
        sq[...] = jnp.full(sq.shape, jnp.sum(right * right), F32)
        first, second, _ = split3(right)
        rhs[:rank, part] = first
        rhs[rank : 2 * rank, part] = second
        rhs[2 * rank : 3 * rank, part] = first
        rhs[3 * rank :, part] = second


def error_kernel(gu, eu, gd, ed, lhs_up, lhs_down, rhs, out_up, out_down):
    ff = gu.shape[2]
    rebuilt = dot(lhs_up[...], rhs[:, :ff])
    out_up[0] = (gu[0].astype(F32) + eu[0].astype(F32) - rebuilt).astype(BF16)
    rebuilt = dot(lhs_down[...], rhs[:, ff:])
    out_down[0] = (gd[0].astype(F32) + ed[0].astype(F32) - rebuilt).astype(BF16)


def update_kernel(limit, lhs_up, lhs_down, rhs, *refs):
    *squares, sq_down, out_up, out_down = refs
    ff = out_up.shape[1]
    norm_sq = tree_sum(s[...] for s in squares) + sq_down[...]
    clip = jnp.minimum(jnp.float32(1.0), limit / jnp.sqrt(norm_sq))[:1, :1]
    out_up[...] = (clip * dot(lhs_up[...], rhs[:, :ff])).astype(BF16)
    out_down[...] = (clip * dot(lhs_down[...], rhs[:, ff:])).astype(BF16)


def shaped(*dims, dtype=F32):
    return jax.ShapeDtypeStruct(dims, dtype)


def whole(shape):
    return pl.BlockSpec(shape, lambda *_: (0,) * len(shape))


def params():
    return pltpu.CompilerParams(vmem_limit_bytes=VMEM_LIMIT)


def call(kernel, out_shape, *args, flops=0, name=None, **more):
    arrays = list(args) + jax.tree.leaves(out_shape)
    size = sum(a.size * a.dtype.itemsize for a in arrays)
    cost = pl.CostEstimate(flops=flops, bytes_accessed=size, transcendentals=0)
    return pl.pallas_call(kernel, out_shape=out_shape, compiler_params=params(), cost_estimate=cost, name=name, **more)(*args)


def swap(x, axis, distance):
    pairs = [(i, i ^ distance) for i in range(lax.axis_size(axis))]
    return lax.ppermute(x, axis, pairs)


def mean_over_replicas(keep, send, split):
    n_dp = lax.axis_size("dp")
    half, per, width = keep.shape
    got = swap(send, "dp", 1)
    parts = call(half_kernel, [shaped(per, width)] * half, keep, got, name="half_sum")
    got = [parts[0]] + [swap(parts[j], "dp", 2 * j) for j in range(1, half)]
    outs = [shaped(per, split), shaped(per, width - split)]
    return call(functools.partial(mean_kernel, n_dp, split), outs, *got, name="replica_mean")


def sum_over_shards(x):
    got = [x] + [swap(x, "tensor", j) for j in range(1, lax.axis_size("tensor"))]
    return call(sum_kernel, shaped(*x.shape), *got, name="shard_sum")


def gather(x):
    n_dp = lax.axis_size("dp")
    near = [x] + [swap(x, "dp", d) for d in range(2, n_dp, 2)]
    far = [swap(p, "dp", 1) for p in near]
    return [p for pair in zip(near, far) for p in pair]


def on_device(gu, eu, gd, ed, qu, qd):
    n_dp, n_shards = lax.axis_size("dp"), lax.axis_size("tensor")
    _, rows, ff = gu.shape
    rank = qu.shape[1]
    width = rows + ff
    half, per = n_dp // 2, rank // n_dp
    chunks = [shaped(half, per, width)] * 2
    chunk_specs = [whole((half, per, width))] * 2

    keep, send = call(
        left_kernel, chunks, gu, eu, gd, ed, qu, qd,
        name="left_terms", flops=8 * rows * ff * 4 * rank, grid=(STEPS,),
        in_specs=[pl.BlockSpec((1, rows // STEPS, ff), lambda i: (0, i, 0))] * 2
        + [pl.BlockSpec((1, ff // STEPS, rows), lambda i: (0, i, 0))] * 2
        + [whole(qu.shape), whole(qd.shape)],
        out_specs=chunk_specs,
        scratch_shapes=[pltpu.VMEM((ff, 4 * rank), BF16), pltpu.VMEM((rows, 4 * rank), BF16), pltpu.VMEM((rank, width), F32), pltpu.VMEM((n_dp, per, width), F32)],
    )
    chunk_up, chunk_down = mean_over_replicas(keep, send, rows)
    down = gather(chunk_down)
    up = gather(sum_over_shards(chunk_up))

    left, gram_up, gram_down, keep, send = call(
        functools.partial(right_kernel, n_dp),
        [shaped(rank, width), shaped(rank, rank), shaped(rank, rank)] + chunks, gu, eu, gd, ed, *up, *down,
        name="right_terms", flops=8 * rows * ff * 3 * rank, grid=(STEPS,),
        in_specs=[pl.BlockSpec((1, rows, ff // STEPS), lambda i: (0, 0, i))] * 2
        + [pl.BlockSpec((1, ff // STEPS, rows), lambda i: (0, i, 0))] * 2
        + [whole(p.shape) for p in up + down],
        out_specs=[whole((rank, width)), whole((rank, rank)), whole((rank, rank))] + chunk_specs,
        scratch_shapes=[pltpu.VMEM((3 * rank, width), BF16), pltpu.VMEM((rank, width), F32), pltpu.VMEM((n_dp, per, width), F32)],
    )
    grams = [gram_down] + [swap(gram_down, "tensor", j) for j in range(1, n_shards)]
    chunk_up, chunk_down = mean_over_replicas(keep, send, ff)
    inv_up, inv_down, lhs_up, lhs_down = call(
        basis_kernel,
        [shaped(rank, rank)] * 2 + [shaped(rows, 4 * rank, dtype=BF16), shaped(ff, 4 * rank, dtype=BF16)],
        left, gram_up, *grams, name="basis", flops=10**9,
    )
    up = gather(chunk_up)
    down = gather(sum_over_shards(chunk_down))

    rhs, sq_up, sq_down = call(
        functools.partial(factor_kernel, n_dp),
        [shaped(4 * rank, width, dtype=BF16), shaped(8, 128), shaped(8, 128)], inv_up, inv_down, *up, *down,
        name="right_factor", scratch_shapes=[pltpu.VMEM((rank, width), F32), pltpu.VMEM((n_dp, per, width), F32)],
    )
    squares = [sq_up] + [swap(sq_up, "tensor", j) for j in range(1, n_shards)]

    lhs_specs = [pl.BlockSpec((rows // STEPS, 4 * rank), lambda i: (i, 0)), pl.BlockSpec((ff // STEPS, 4 * rank), lambda i: (i, 0))]
    replica_specs = [pl.BlockSpec((1, rows // STEPS, ff), lambda i: (0, i, 0)), pl.BlockSpec((1, ff // STEPS, rows), lambda i: (0, i, 0))]
    new_error_up, new_error_down = call(
        error_kernel, [shaped(1, rows, ff, dtype=BF16), shaped(1, ff, rows, dtype=BF16)], gu, eu, gd, ed, lhs_up, lhs_down, rhs,
        name="new_error", flops=4 * rows * ff * 4 * rank, grid=(STEPS,),
        in_specs=[replica_specs[0]] * 2 + [replica_specs[1]] * 2 + lhs_specs + [whole(rhs.shape)],
        out_specs=replica_specs,
    )
    limit = CLIP_RMS * (2.0 * rows * ff * n_shards) ** 0.5
    update_up, update_down = call(
        functools.partial(update_kernel, limit), [shaped(rows, ff, dtype=BF16), shaped(ff, rows, dtype=BF16)],
        lhs_up, lhs_down, rhs, *squares, sq_down,
        name="update", flops=4 * rows * ff * 4 * rank, grid=(STEPS,),
        in_specs=lhs_specs + [whole(rhs.shape)] + [whole((8, 128))] * (n_shards + 1),
        out_specs=[pl.BlockSpec((rows // STEPS, ff), lambda i: (i, 0)), pl.BlockSpec((ff // STEPS, rows), lambda i: (i, 0))],
    )
    return new_error_up, update_up, new_error_down, update_down


def solution(mesh):
    placed = (
        P("dp", None, "tensor"),
        P("dp", None, "tensor"),
        P("dp", "tensor", None),
        P("dp", "tensor", None),
        P("tensor", None),
        P(),
    )
    return jax.shard_map(
        on_device,
        mesh=mesh,
        in_specs=placed,
        out_specs=(
            P("dp", None, "tensor"),
            P(None, "tensor"),
            P("dp", "tensor", None),
            P("tensor", None),
        ),
        check_vma=False,
    )
```

```python
import functools

import jax
import jax.numpy as jnp
from jax import lax
from jax.experimental import pallas as pl
from jax.experimental.pallas import tpu as pltpu
from jax.sharding import PartitionSpec as P

F32 = jnp.float32
BF16 = jnp.bfloat16
HIGHEST = lax.Precision.HIGHEST
CLIP_RMS = 0.1
STEPS = 4
VMEM_LIMIT = 48 * 1024 * 1024


def split3(x):
    first = x.astype(BF16)
    rest = x - first.astype(F32)
    second = rest.astype(BF16)
    return first, second, (rest - second.astype(F32)).astype(BF16)


def tree_sum(values):
    values = list(values)
    while len(values) > 1:
        values = [values[i] + values[i + 1] for i in range(0, len(values), 2)]
    return values[0]


def dot(a, b, dims=((1,), (0,)), precision=None):
    return lax.dot_general(a, b, (dims, ((), ())), precision=precision, preferred_element_type=F32)


def scatter_chunks(total, chunks):
    n_dp, per, _ = chunks.shape
    for c in range(n_dp):
        chunks[c] = total[c * per : (c + 1) * per, :]


def gather_chunks(chunks, total):
    n_dp, per, _ = chunks.shape
    for c in range(n_dp):
        total[c * per : (c + 1) * per, :] = chunks[c]


def left_kernel(gu, eu, gd, ed, qu, qd, chunks, qsu, qsd, total):
    step = pl.program_id(0)
    rank, ff = qu.shape
    rows = total.shape[1] - ff

    @pl.when(step == 0)
    def _():
        for q, qs in ((qu, qsu), (qd, qsd)):
            first, second, third = split3(q[...])
            qs[:rank, :] = first
            qs[rank : 2 * rank, :] = second
            qs[2 * rank : 3 * rank, :] = third
            qs[3 * rank :, :] = jnp.zeros_like(third)

    def term(g, e, qs, start):
        block = g.shape[1]
        t = dot(g[0], qs[...], ((1,), (1,))) + dot(e[0], qs[...], ((1,), (1,)))
        t = (t[:, : 2 * rank] + t[:, 2 * rank :]).T
        total[:, pl.ds(pl.multiple_of(start + step * block, 128), block)] = t[:rank] + t[rank:]

    term(gu, eu, qsu, 0)
    term(gd, ed, qsd, rows)

    @pl.when(step == STEPS - 1)
    def _():
        scatter_chunks(total, chunks)


def right_kernel(gu, eu, gd, ed, gathered, left, gram_up, gram_down, chunks, pieces, total):
    step = pl.program_id(0)
    rank = left.shape[0]
    rows = gu.shape[1]
    ff = left.shape[1] - rows
    block = gu.shape[2]
    depth = gd.shape[1]

    @pl.when(step == 0)
    def _():
        gather_chunks(gathered, left)
        for i, piece in enumerate(split3(left[...])):
            pieces[i * rank : (i + 1) * rank, :] = piece
        nt = ((1,), (1,))
        gram_up[...] = dot(left[:, :rows], left[:, :rows], nt, HIGHEST)
        gram_down[...] = dot(left[:, rows:], left[:, rows:], nt, HIGHEST)
        total[:, ff:] = jnp.zeros((rank, rows), F32)

    def fold(t):
        return t[:rank] + (t[rank : 2 * rank] + t[2 * rank :])

    lhs = pieces[:, :rows]
    total[:, pl.ds(pl.multiple_of(step * block, 128), block)] = fold(dot(lhs, gu[0]) + dot(lhs, eu[0]))
    lhs = pieces[:, pl.ds(pl.multiple_of(rows + step * depth, 128), depth)]
    total[:, ff:] += fold(dot(lhs, gd[0]) + dot(lhs, ed[0]))

    @pl.when(step == STEPS - 1)
    def _():
        scatter_chunks(total, chunks)


def mean_kernel(shared, got, own, parts):
    n_dp = got.shape[0]
    total = tree_sum(got[d] for d in range(n_dp)) / n_dp
    own[...] = total
    for t in range(parts.shape[0]):
        parts[t] = total[:, shared]


def copies_kernel(shared, own, parts, out):
    total = tree_sum(parts[t] for t in range(parts.shape[0]))
    for d in range(out.shape[0]):
        out[d] = own[...]
        out[d, :, shared] = total


def basis_kernel(left, gram_up, *refs):
    *grams, inv_up, inv_down, lhs_up, lhs_down = refs
    rank = left.shape[0]
    rows = lhs_up.shape[0]
    row_id = lax.broadcasted_iota(jnp.int32, (rank, 2 * rank), 0)
    lane_id = lax.broadcasted_iota(jnp.int32, (rank, 2 * rank), 1)
    eye = (lane_id == row_id + rank).astype(F32)

    def start(gram):
        return jnp.concatenate([gram, jnp.zeros_like(gram)], axis=1) + eye

    state = [start(gram_up[...]), start(tree_sum(g[...] for g in grams))]
    for k in range(rank):
        for s in range(2):
            a = state[s]
            pivot_row = a[k : k + 1, :]
            below = row_id[:, :1] > k
            factor = jnp.where(below, a[:, k : k + 1], 0.0) / a[k : k + 1, k : k + 1]
            state[s] = a - factor * pivot_row
    for a, inv, lhs, part in ((state[0], inv_up, lhs_up, slice(0, rows)), (state[1], inv_down, lhs_down, slice(rows, None))):
        diagonal = jnp.sum(jnp.where(lane_id == row_id, a, 0.0), axis=1, keepdims=True)
        inverse = (a / jnp.sqrt(diagonal))[:, rank:]
        inv[...] = inverse
        first, second, _ = split3(dot(inverse, left[:, part], precision=HIGHEST).T)
        lhs[:, :rank] = first
        lhs[:, rank : 2 * rank] = first
        lhs[:, 2 * rank : 3 * rank] = second
        lhs[:, 3 * rank :] = second


def factor_kernel(ff, inv_up, inv_down, gathered, rhs, sq_up, sq_down, total):
    rank = total.shape[0]
    gather_chunks(gathered, total)
    for inv, part, sq in ((inv_up, slice(0, ff), sq_up), (inv_down, slice(ff, None), sq_down)):
        right = dot(inv[...], total[:, part], precision=HIGHEST)
        sq[...] = jnp.full(sq.shape, jnp.sum(right * right), F32)
        first, second, _ = split3(right)
        rhs[:rank, part] = first
        rhs[rank : 2 * rank, part] = second
        rhs[2 * rank : 3 * rank, part] = first
        rhs[3 * rank :, part] = second


def error_kernel(gu, eu, gd, ed, lhs_up, lhs_down, rhs, out_up, out_down):
    ff = gu.shape[2]
    rebuilt = dot(lhs_up[...], rhs[:, :ff])
    out_up[0] = (gu[0].astype(F32) + eu[0].astype(F32) - rebuilt).astype(BF16)
    rebuilt = dot(lhs_down[...], rhs[:, ff:])
    out_down[0] = (gd[0].astype(F32) + ed[0].astype(F32) - rebuilt).astype(BF16)


def update_kernel(limit, lhs_up, lhs_down, rhs, *refs):
    *squares, sq_down, out_up, out_down = refs
    ff = out_up.shape[1]
    norm_sq = tree_sum(s[...] for s in squares) + sq_down[...]
    clip = jnp.minimum(jnp.float32(1.0), limit / jnp.sqrt(norm_sq))[:1, :1]
    out_up[...] = (clip * dot(lhs_up[...], rhs[:, :ff])).astype(BF16)
    out_down[...] = (clip * dot(lhs_down[...], rhs[:, ff:])).astype(BF16)


def shaped(*dims, dtype=F32):
    return jax.ShapeDtypeStruct(dims, dtype)


def whole(shape):
    return pl.BlockSpec(shape, lambda *_: (0,) * len(shape))


def params():
    return pltpu.CompilerParams(vmem_limit_bytes=VMEM_LIMIT)


def call(kernel, out_shape, *args, flops=0, name=None, **more):
    arrays = list(args) + jax.tree.leaves(out_shape)
    size = sum(a.size * a.dtype.itemsize for a in arrays)
    cost = pl.CostEstimate(flops=flops, bytes_accessed=size, transcendentals=0)
    return pl.pallas_call(kernel, out_shape=out_shape, compiler_params=params(), cost_estimate=cost, name=name, **more)(*args)


def swap(x, axis, distance):
    pairs = [(i, i ^ distance) for i in range(lax.axis_size(axis))]
    return lax.ppermute(x, axis, pairs)


def exchange(x, axis):
    return lax.all_to_all(x, axis, 0, 0)


def mean_over_replicas(chunks, shared):
    n_dp, n_shards = lax.axis_size("dp"), lax.axis_size("tensor")
    _, per, width = chunks.shape
    outs = [shaped(per, width), shaped(n_shards, per, shared.stop - shared.start)]
    own, parts = call(functools.partial(mean_kernel, shared), outs, exchange(chunks, "dp"), name="replica_mean")
    copies = call(functools.partial(copies_kernel, shared), shaped(n_dp, per, width), own, exchange(parts, "tensor"), name="shard_sum")
    return exchange(copies, "dp")


def on_device(gu, eu, gd, ed, qu, qd):
    qu, qd = qu.T, qd.T
    n_dp, n_shards = lax.axis_size("dp"), lax.axis_size("tensor")
    _, rows, ff = gu.shape
    rank = qu.shape[0]
    width = rows + ff
    chunks = shaped(n_dp, rank // n_dp, width)

    terms = call(
        left_kernel, chunks, gu, eu, gd, ed, qu, qd,
        name="left_terms", flops=8 * rows * ff * 4 * rank, grid=(STEPS,),
        in_specs=[pl.BlockSpec((1, rows // STEPS, ff), lambda i: (0, i, 0))] * 2
        + [pl.BlockSpec((1, ff // STEPS, rows), lambda i: (0, i, 0))] * 2
        + [whole(qu.shape), whole(qd.shape)],
        out_specs=whole(chunks.shape),
        scratch_shapes=[pltpu.VMEM((4 * rank, ff), BF16), pltpu.VMEM((4 * rank, rows), BF16), pltpu.VMEM((rank, width), F32)],
    )
    gathered = mean_over_replicas(terms, slice(0, rows))

    left, gram_up, gram_down, terms = call(
        right_kernel, [shaped(rank, width), shaped(rank, rank), shaped(rank, rank), chunks], gu, eu, gd, ed, gathered,
        name="right_terms", flops=8 * rows * ff * 3 * rank, grid=(STEPS,),
        in_specs=[pl.BlockSpec((1, rows, ff // STEPS), lambda i: (0, 0, i))] * 2
        + [pl.BlockSpec((1, ff // STEPS, rows), lambda i: (0, i, 0))] * 2
        + [whole(gathered.shape)],
        out_specs=[whole((rank, width)), whole((rank, rank)), whole((rank, rank)), whole(chunks.shape)],
        scratch_shapes=[pltpu.VMEM((3 * rank, width), BF16), pltpu.VMEM((rank, width), F32)],
    )
    grams = [gram_down] + [swap(gram_down, "tensor", j) for j in range(1, n_shards)]
    gathered = mean_over_replicas(terms, slice(ff, width))
    inv_up, inv_down, lhs_up, lhs_down = call(
        basis_kernel,
        [shaped(rank, rank)] * 2 + [shaped(rows, 4 * rank, dtype=BF16), shaped(ff, 4 * rank, dtype=BF16)],
        left, gram_up, *grams, name="basis", flops=10**9,
    )

    rhs, sq_up, sq_down = call(
        functools.partial(factor_kernel, ff),
        [shaped(4 * rank, width, dtype=BF16), shaped(8, 128), shaped(8, 128)], inv_up, inv_down, gathered,
        name="right_factor", scratch_shapes=[pltpu.VMEM((rank, width), F32)],
    )
    squares = [sq_up] + [swap(sq_up, "tensor", j) for j in range(1, n_shards)]

    lhs_specs = [pl.BlockSpec((rows // STEPS, 4 * rank), lambda i: (i, 0)), pl.BlockSpec((ff // STEPS, 4 * rank), lambda i: (i, 0))]
    replica_specs = [pl.BlockSpec((1, rows // STEPS, ff), lambda i: (0, i, 0)), pl.BlockSpec((1, ff // STEPS, rows), lambda i: (0, i, 0))]
    new_error_up, new_error_down = call(
        error_kernel, [shaped(1, rows, ff, dtype=BF16), shaped(1, ff, rows, dtype=BF16)], gu, eu, gd, ed, lhs_up, lhs_down, rhs,
        name="new_error", flops=4 * rows * ff * 4 * rank, grid=(STEPS,),
        in_specs=[replica_specs[0]] * 2 + [replica_specs[1]] * 2 + lhs_specs + [whole(rhs.shape)],
        out_specs=replica_specs,
    )
    limit = CLIP_RMS * (2.0 * rows * ff * n_shards) ** 0.5
    update_up, update_down = call(
        functools.partial(update_kernel, limit), [shaped(rows, ff, dtype=BF16), shaped(ff, rows, dtype=BF16)],
        lhs_up, lhs_down, rhs, *squares, sq_down,
        name="update", flops=4 * rows * ff * 4 * rank, grid=(STEPS,),
        in_specs=lhs_specs + [whole(rhs.shape)] + [whole((8, 128))] * (n_shards + 1),
        out_specs=[pl.BlockSpec((rows // STEPS, ff), lambda i: (i, 0)), pl.BlockSpec((ff // STEPS, rows), lambda i: (i, 0))],
    )
    return new_error_up, update_up, new_error_down, update_down


def solution(mesh):
    placed = (
        P("dp", None, "tensor"),
        P("dp", None, "tensor"),
        P("dp", "tensor", None),
        P("dp", "tensor", None),
        P("tensor", None),
        P(),
    )
    return jax.shard_map(
        on_device,
        mesh=mesh,
        in_specs=placed,
        out_specs=(
            P("dp", None, "tensor"),
            P(None, "tensor"),
            P("dp", "tensor", None),
            P("tensor", None),
        ),
        check_vma=False,
    )
```

```python
import functools

import jax
import jax.numpy as jnp
from jax import lax
from jax.experimental import pallas as pl
from jax.experimental.pallas import tpu as pltpu
from jax.sharding import PartitionSpec as P

F32 = jnp.float32
BF16 = jnp.bfloat16
HIGHEST = lax.Precision.HIGHEST
CLIP_RMS = 0.1
STEPS = 4
MIB = 1024 * 1024
NT = ((1,), (1,))


def split3(x):
    first = x.astype(BF16)
    rest = x - first.astype(F32)
    second = rest.astype(BF16)
    return first, second, (rest - second.astype(F32)).astype(BF16)


def tree_sum(values):
    values = list(values)
    while len(values) > 1:
        values = [values[i] + values[i + 1] for i in range(0, len(values), 2)]
    return values[0]


def dot(a, b, dims=((1,), (0,)), precision=None):
    return lax.dot_general(a, b, (dims, ((), ())), precision=precision, preferred_element_type=F32)


def fold(x, rows):
    return jnp.concatenate([x[i : i + rows] for i in range(0, x.shape[0], rows)], axis=1)


def unfold(x, rows):
    count = rows // x.shape[0]
    width = x.shape[1] // count
    return jnp.concatenate([x[:, i * width : (i + 1) * width] for i in range(count)], axis=0)


def place(axis):
    index = lax.axis_index(axis)
    return lax.bitwise_and(index, 1), lax.shift_right_logical(index, 1)


def split_cores(total, extra, keep, send):
    core, _ = place("tensor")
    rows, width = keep.shape[0], total.shape[1]
    keep[:, :width] = total[pl.ds(pl.multiple_of(core * rows, rows), rows), :]
    send[:, :width] = total[pl.ds(pl.multiple_of((1 - core) * rows, rows), rows), :]
    if extra is not None:
        keep[:, width:] = extra
        send[:, width:] = extra


def split_replicas(total, stage, keep, send):
    parity, _ = place("dp")
    half, per, _ = keep.shape
    for c in range(2 * half):
        stage[c] = total[c * per : (c + 1) * per, :]
    for c in range(half):
        keep[c] = stage[2 * c + parity]
        send[c] = stage[2 * c + 1 - parity]


def join_replicas(mine, other, stage, total):
    parity, _ = place("dp")
    half, per, _ = mine.shape
    width = total.shape[1]
    for c in range(half):
        stage[2 * c + parity] = mine[c, :, :width]
        stage[2 * c + 1 - parity] = other[c, :, :width]
    for c in range(2 * half):
        total[c * per : (c + 1) * per, :] = stage[c]


def join_cores(mine, other, total):
    core, _ = place("tensor")
    rows, width = mine.shape[0], total.shape[1]
    total[pl.ds(pl.multiple_of(core * rows, rows), rows), :] = mine[:, :width]
    total[pl.ds(pl.multiple_of((1 - core) * rows, rows), rows), :] = other[:, :width]


def left_product(g, e, q, pieces, total):
    step = pl.program_id(0)
    rank = q.shape[0]
    block = g.shape[1]

    @pl.when(step == 0)
    def _():
        for i, piece in enumerate(split3(q[...])):
            pieces[i * rank : (i + 1) * rank, :] = piece
        pieces[3 * rank :, :] = jnp.zeros((rank, q.shape[1]), BF16)

    t = dot(g[0], pieces[...], NT) + dot(e[0], pieces[...], NT)
    t = (t[:, : 2 * rank] + t[:, 2 * rank :]).T
    total[:, pl.ds(pl.multiple_of(step * block, 128), block)] = t[:rank] + t[rank:]


def left_up_kernel(g, e, q, keep, send, pieces, total):
    left_product(g, e, q, pieces, total)

    @pl.when(pl.program_id(0) == STEPS - 1)
    def _():
        split_cores(total, None, keep, send)


def left_down_kernel(g, e, q, keep, send, pieces, total, stage):
    left_product(g, e, q, pieces, total)

    @pl.when(pl.program_id(0) == STEPS - 1)
    def _():
        split_replicas(total, stage, keep, send)


def split_x_kernel(width, keep, got, *outs):
    _, x = place("tensor")
    total = outs[-1]
    outs = outs[:-1]
    rows = outs[0].shape[0]
    total[...] = keep[...] + got[...]
    for j, out in enumerate(outs):
        owner = lax.bitwise_xor(x, j)
        out[:, :width] = total[pl.ds(pl.multiple_of(owner * rows, rows), rows), :width]
        if total.shape[1] > width:
            out[:, width:] = fold(total[:, width:], rows)


def split_z_kernel(n_x, width, gram_shape, keep, got, *refs):
    shards, refs = refs[:n_x], refs[n_x:]
    gram = refs[0] if gram_shape else None
    outs, stage = refs[1 if gram_shape else 0 : -1], refs[-1]
    _, z = place("dp")
    half, per, ff = keep.shape
    summed = tree_sum(s[...] for s in shards)
    block = width // half
    for c in range(half):
        stage[c, :, :ff] = keep[c] + got[c]
        stage[c, :, ff:] = fold(summed[:, c * block : (c + 1) * block], per)
    for j, out in enumerate(outs):
        out[...] = stage[lax.bitwise_xor(z, j)]
    if gram_shape:
        whole_gram = unfold(summed[:, width:], gram_shape // 2)
        gram[...] = unfold(whole_gram, gram_shape)


def mean_kernel(n_dp, *refs):
    refs[-1][...] = tree_sum(ref[...] for ref in refs[:-1]) / n_dp


def stack_kernel(*refs):
    _, z = place("dp")
    for j, ref in enumerate(refs[:-1]):
        refs[-1][lax.bitwise_xor(z, j)] = ref[...]


def shard_rows(mine, other, ff, rows):
    half = mine.shape[0]
    return jnp.concatenate([unfold(mine[c, :, ff:] + other[c, :, ff:], rows) for c in range(half)], axis=1)


def shard_rows_kernel(ff, mine, other, out):
    out[...] = shard_rows(mine, other, ff, out.shape[0])


def stack_x_kernel(width, *refs):
    _, x = place("tensor")
    *pieces, out = refs
    rows = pieces[0].shape[0]
    for j, piece in enumerate(pieces):
        owner = lax.bitwise_xor(x, j)
        out[pl.ds(pl.multiple_of(owner * rows, rows), rows), :width] = piece[:, :width]
    if out.shape[1] > width:
        summed = tree_sum(piece[:, width:] for piece in pieces)
        for i in range(0, out.shape[0], rows):
            out[i : i + rows, width:] = summed


def split_rows(left, pieces):
    rank = left.shape[0]
    for i, piece in enumerate(split3(left[...])):
        pieces[i * rank : (i + 1) * rank, :] = piece


def add_pieces(t):
    rank = t.shape[0] // 3
    return t[:rank] + (t[rank : 2 * rank] + t[2 * rank :])


def right_down_kernel(mine, other, g, e, left, keep, send, pieces, total, stage):
    rank = left.shape[0]
    join_replicas(mine, other, stage, left)
    split_rows(left, pieces)
    total[...] = add_pieces(dot(pieces[...], g[0]) + dot(pieces[...], e[0]))
    gram = dot(left[...], left[...], NT, HIGHEST)
    split_cores(total, fold(gram, rank // 2), keep, send)


def right_up_kernel(mine, other, g, e, left, gram, keep, send, pieces, total, stage):
    join_cores(mine, other, left)
    split_rows(left, pieces)
    block = total.shape[1] // STEPS
    for i in range(STEPS):
        part = slice(i * block, (i + 1) * block)
        total[:, part] = add_pieces(dot(pieces[...], g[0, :, part]) + dot(pieces[...], e[0, :, part]))
    split_replicas(total, stage, keep, send)
    gram[...] = dot(left[...], left[...], NT, HIGHEST)


def inverse_factors(grams):
    rank = grams[0].shape[0]
    lane = lax.broadcasted_iota(jnp.int32, (8, 2 * rank), 1)
    row = lax.broadcasted_iota(jnp.int32, (8, 2 * rank), 0)
    states = []
    for gram in grams:
        wide = jnp.concatenate([gram, jnp.zeros_like(gram)], axis=1)
        states.append([wide[i : i + 8] + (lane == row + (rank + i)).astype(F32) for i in range(0, rank, 8)])
    for k in range(rank):
        at, inner = divmod(k, 8)
        for blocks in states:
            pivot_row = blocks[at][inner : inner + 1, :]
            scaled = pivot_row / pivot_row[:, k : k + 1]
            for i in range(at, rank // 8):
                column = blocks[i][:, k : k + 1]
                if i == at:
                    column = jnp.where(row[:, :1] > inner, column, 0.0)
                blocks[i] = blocks[i] - column * scaled
    results = []
    for blocks in states:
        rows = []
        for i, block in enumerate(blocks):
            diagonal = jnp.sum(jnp.where(lane == row + 8 * i, block, 0.0), axis=1, keepdims=True)
            rows.append((block / jnp.sqrt(diagonal))[:, rank:])
        results.append(jnp.concatenate(rows, axis=0))
    return results


def basis_kernel(left_up, left_down, gram_up, gram_down, inv_up, inv_down, lhs_up, lhs_down):
    inverses = inverse_factors([gram_up[...], gram_down[...]])
    rank = left_up.shape[0]
    for inverse, inv, left, lhs in zip(inverses, (inv_up, inv_down), (left_up, left_down), (lhs_up, lhs_down)):
        inv[...] = inverse
        first, second, _ = split3(dot(inverse, left[...], precision=HIGHEST).T)
        lhs[:, :rank] = first
        lhs[:, rank : 2 * rank] = first
        lhs[:, 2 * rank : 3 * rank] = second
        lhs[:, 3 * rank :] = second


def right_factor(inv, total, rhs):
    rank = inv.shape[0]
    right = dot(inv[...], total[...], precision=HIGHEST)
    first, second, _ = split3(right)
    rhs[:rank, :] = first
    rhs[rank : 2 * rank, :] = second
    rhs[2 * rank : 3 * rank, :] = first
    rhs[3 * rank :, :] = second
    return jnp.sum(right * right)


def factor_up_kernel(mine, other, inv, rhs, shard, total, stage):
    join_replicas(mine, other, stage, total)
    square = right_factor(inv, total, rhs)
    rows, ff = shard.shape[0], total.shape[1]
    width = shard.shape[1] - 128
    shard[:, :width] = shard_rows(mine, other, ff, rows)
    shard[:, width:] = jnp.full((rows, 128), square, F32)


def factor_down_kernel(limit, mine, other, inv, rhs, clip, total):
    join_cores(mine, other, total)
    square = right_factor(inv, total, rhs)
    width = total.shape[1]
    norm_sq = square + (mine[:8, width:] + other[:8, width:])
    clip[...] = jnp.minimum(jnp.float32(1.0), limit / jnp.sqrt(norm_sq))


def rows_of(block):
    return pl.ds(pl.multiple_of(pl.program_id(0) * block, block), block)


def error_up_kernel(g, e, lhs, rhs, error):
    part = rows_of(error.shape[1])
    rebuilt = dot(lhs[part, :], rhs[...])
    error[0] = (g[0, part, :].astype(F32) + e[0, part, :].astype(F32) - rebuilt).astype(BF16)


def last_kernel(g, e, lhs_up, rhs_up, lhs_down, rhs_down, clip, error, update_up, update_down):
    factor = clip[:1, :1]
    part = rows_of(update_down.shape[0])
    rebuilt = dot(lhs_down[part, :], rhs_down[...])
    update_down[...] = (factor * rebuilt).astype(BF16)
    error[0] = (g[0, part, :].astype(F32) + e[0, part, :].astype(F32) - rebuilt).astype(BF16)
    part = rows_of(update_up.shape[0])
    update_up[...] = (factor * dot(lhs_up[part, :], rhs_up[...])).astype(BF16)


def shaped(*dims, dtype=F32):
    return jax.ShapeDtypeStruct(dims, dtype)


def whole(shape):
    return pl.BlockSpec(shape, lambda *_: (0,) * len(shape))


def row_blocks(rows, columns):
    return pl.BlockSpec((rows // STEPS, columns), lambda i: (i, 0))


def replica_blocks(rows, columns):
    return pl.BlockSpec((1, rows // STEPS, columns), lambda i: (0, i, 0))


VMEM = pl.BlockSpec(memory_space=pltpu.VMEM)


def call(kernel, out_shape, *args, flops=0, limit=12, name=None, **more):
    arrays = list(args) + jax.tree.leaves(out_shape)
    size = sum(a.size * a.dtype.itemsize for a in arrays)
    cost = pl.CostEstimate(flops=flops, bytes_accessed=size, transcendentals=0)
    params = pltpu.CompilerParams(vmem_limit_bytes=limit * MIB)
    return pl.pallas_call(kernel, out_shape=out_shape, compiler_params=params, cost_estimate=cost, name=name, **more)(*args)


def swap(x, axis, distance):
    pairs = [(i, i ^ distance) for i in range(lax.axis_size(axis))]
    return lax.ppermute(x, axis, pairs)


def sum_shards(keep, send, width):
    n_x = lax.axis_size("tensor") // 2
    got = swap(send, "tensor", 1)
    rows, columns = keep.shape[0] // n_x, keep.shape[1]
    out = shaped(rows, width + (columns - width) * n_x)
    parts = call(
        functools.partial(split_x_kernel, width), [out] * n_x + [shaped(*keep.shape)], keep, got, name="split_x"
    )[:n_x]
    return [parts[0]] + [swap(parts[j], "tensor", 2 * j) for j in range(1, n_x)]


def mean_replicas(keep, got, shards, width, gram_rank=0):
    n_dp = lax.axis_size("dp")
    half, per, ff = keep.shape
    columns = ff + shards[0].shape[0] // per * (width // half)
    outs = [shaped(per, columns)] * half
    if gram_rank:
        outs = [shaped(gram_rank, gram_rank)] + outs
    parts = call(
        functools.partial(split_z_kernel, len(shards), width, gram_rank), outs, keep, got, *shards,
        name="split_z", scratch_shapes=[pltpu.VMEM((half, per, columns), F32)],
    )
    gram, parts = (parts[0], parts[1:]) if gram_rank else (None, parts)
    parts = [parts[0]] + [swap(parts[j], "dp", 2 * j) for j in range(1, half)]
    mean = call(functools.partial(mean_kernel, n_dp), shaped(per, columns), *parts, name="replica_mean")
    chunks = [mean] + [swap(mean, "dp", 2 * j) for j in range(1, half)]
    mine = call(stack_kernel, shaped(half, per, columns), *chunks, name="stack_z")
    return mine, swap(mine, "dp", 1), gram


def gather_shards(rows_here, width):
    n_x = lax.axis_size("tensor") // 2
    rows, columns = rows_here.shape
    pieces = [rows_here] + [swap(rows_here, "tensor", 2 * j) for j in range(1, n_x)]
    mine = call(functools.partial(stack_x_kernel, width), shaped(rows * n_x, columns), *pieces, name="stack_x")
    return mine, swap(mine, "tensor", 1)


def on_device(gu, eu, gd, ed, qu, qd):
    qu, qd = qu.T, qd.T
    n_dp, n_shards = lax.axis_size("dp"), lax.axis_size("tensor")
    _, rows, ff = gu.shape
    rank = qu.shape[0]
    half, per = n_dp // 2, rank // n_dp
    core_half = shaped(rank // 2, rows)
    replica_half = shaped(half, per, ff)
    stage = pltpu.VMEM((n_dp, per, ff), F32)
    wide = pltpu.VMEM((rank, ff), F32)
    narrow = pltpu.VMEM((rank, rows), F32)
    product = 4 * rows * ff * 4 * rank

    keep_up, send_up = call(
        left_up_kernel, [core_half] * 2, gu, eu, qu, name="left_up", flops=product, limit=60, grid=(STEPS,),
        in_specs=[replica_blocks(rows, ff)] * 2 + [whole(qu.shape)], out_specs=[whole(core_half.shape)] * 2,
        scratch_shapes=[pltpu.VMEM((4 * rank, ff), BF16), narrow],
    )
    shards = sum_shards(keep_up, send_up, rows)
    keep, send = call(
        left_down_kernel, [replica_half] * 2, gd, ed, qd, name="left_down", flops=product, limit=60, grid=(STEPS,),
        in_specs=[replica_blocks(ff, rows)] * 2 + [whole(qd.shape)], out_specs=[whole(replica_half.shape)] * 2,
        scratch_shapes=[pltpu.VMEM((4 * rank, rows), BF16), wide, stage],
    )
    mine, other, _ = mean_replicas(keep, swap(send, "dp", 1), shards, rows)

    shard = call(functools.partial(shard_rows_kernel, ff), shaped(rank // n_shards, rows), mine, other, name="shard_rows")
    left_half, left_other = gather_shards(shard, rows)
    core_half = shaped(rank // 2, rows + 2 * rank)
    left_down, keep_down, send_down = call(
        right_down_kernel, [shaped(rank, ff), core_half, core_half], mine, other, gd, ed, name="right_down", flops=product,
        in_specs=[VMEM] * 4, scratch_shapes=[pltpu.VMEM((3 * rank, ff), BF16), narrow, stage],
    )
    shards = sum_shards(keep_down, send_down, rows)
    left_up, gram_up, keep, send = call(
        right_up_kernel, [shaped(rank, rows), shaped(rank, rank), replica_half, replica_half], left_half, left_other, gu, eu,
        name="right_up", flops=product, in_specs=[VMEM] * 4, scratch_shapes=[pltpu.VMEM((3 * rank, rows), BF16), wide, stage],
    )
    mine, other, gram_down = mean_replicas(keep, swap(send, "dp", 1), shards, rows, rank)
    inv_up, inv_down, lhs_up, lhs_down = call(
        basis_kernel,
        [shaped(rank, rank)] * 2 + [shaped(rows, 4 * rank, dtype=BF16), shaped(ff, 4 * rank, dtype=BF16)],
        left_up, left_down, gram_up, gram_down, name="basis", flops=10**9,
    )
    rhs_up, shard = call(
        factor_up_kernel, [shaped(4 * rank, ff, dtype=BF16), shaped(rank // n_shards, rows + 128)], mine, other, inv_up,
        name="factor_up", scratch_shapes=[wide, stage],
    )
    right_half, right_other = gather_shards(shard, rows)
    new_error_up = call(
        error_up_kernel, shaped(1, rows, ff, dtype=BF16), gu, eu, lhs_up, rhs_up, name="error_up", flops=product // 2,
        grid=(STEPS,), in_specs=[VMEM] * 4, out_specs=replica_blocks(rows, ff),
    )
    limit = CLIP_RMS * (2.0 * rows * ff * n_shards) ** 0.5
    rhs_down, clip = call(
        functools.partial(factor_down_kernel, limit), [shaped(4 * rank, rows, dtype=BF16), shaped(8, 128)],
        right_half, right_other, inv_down, name="factor_down", scratch_shapes=[narrow],
    )
    new_error_down, update_up, update_down = call(
        last_kernel, [shaped(1, ff, rows, dtype=BF16), shaped(rows, ff, dtype=BF16), shaped(ff, rows, dtype=BF16)],
        gd, ed, lhs_up, rhs_up, lhs_down, rhs_down, clip, name="last", flops=product, grid=(STEPS,),
        in_specs=[VMEM] * 7, out_specs=[replica_blocks(ff, rows), row_blocks(rows, ff), row_blocks(ff, rows)],
    )
    return new_error_up, update_up, new_error_down, update_down


def solution(mesh):
    placed = (
        P("dp", None, "tensor"),
        P("dp", None, "tensor"),
        P("dp", "tensor", None),
        P("dp", "tensor", None),
        P("tensor", None),
        P(),
    )
    return jax.shard_map(
        on_device,
        mesh=mesh,
        in_specs=placed,
        out_specs=(
            P("dp", None, "tensor"),
            P(None, "tensor"),
            P("dp", "tensor", None),
            P("tensor", None),
        ),
        check_vma=False,
    )
```

```python
import functools

import jax
import jax.numpy as jnp
from jax import lax
from jax.experimental import pallas as pl
from jax.experimental.pallas import tpu as pltpu
from jax.sharding import PartitionSpec as P

F32 = jnp.float32
BF16 = jnp.bfloat16
HIGHEST = lax.Precision.HIGHEST
CLIP_RMS = 0.1
STEPS = 4
MIB = 1024 * 1024
NT = ((1,), (1,))


def split3(x):
    first = x.astype(BF16)
    rest = x - first.astype(F32)
    second = rest.astype(BF16)
    return first, second, (rest - second.astype(F32)).astype(BF16)


def tree_sum(values):
    values = list(values)
    while len(values) > 1:
        values = [values[i] + values[i + 1] for i in range(0, len(values), 2)]
    return values[0]


def dot(a, b, dims=((1,), (0,)), precision=None):
    return lax.dot_general(a, b, (dims, ((), ())), precision=precision, preferred_element_type=F32)


def fold(x, rows):
    return jnp.concatenate([x[i : i + rows] for i in range(0, x.shape[0], rows)], axis=1)


def unfold(x, rows):
    count = rows // x.shape[0]
    width = x.shape[1] // count
    return jnp.concatenate([x[:, i * width : (i + 1) * width] for i in range(count)], axis=0)


def place(axis):
    index = lax.axis_index(axis)
    return lax.bitwise_and(index, 1), lax.shift_right_logical(index, 1)


def split_cores(total, extra, keep, send):
    core, _ = place("tensor")
    rows, width = keep.shape[0], total.shape[1]
    keep[:, :width] = total[pl.ds(pl.multiple_of(core * rows, rows), rows), :]
    send[:, :width] = total[pl.ds(pl.multiple_of((1 - core) * rows, rows), rows), :]
    if extra is not None:
        keep[:, width:] = extra
        send[:, width:] = extra


def split_replicas(total, stage, keep, send):
    parity, _ = place("dp")
    half, per, _ = keep.shape
    for c in range(2 * half):
        stage[c] = total[c * per : (c + 1) * per, :]
    for c in range(half):
        keep[c] = stage[2 * c + parity]
        send[c] = stage[2 * c + 1 - parity]


def join_replicas(mine, other, stage, total):
    parity, _ = place("dp")
    half, per, _ = mine.shape
    width = total.shape[1]
    for c in range(half):
        stage[2 * c + parity] = mine[c, :, :width]
        stage[2 * c + 1 - parity] = other[c, :, :width]
    for c in range(2 * half):
        total[c * per : (c + 1) * per, :] = stage[c]


def join_cores(mine, other, total):
    core, _ = place("tensor")
    rows, width = mine.shape[0], total.shape[1]
    total[pl.ds(pl.multiple_of(core * rows, rows), rows), :] = mine[:, :width]
    total[pl.ds(pl.multiple_of((1 - core) * rows, rows), rows), :] = other[:, :width]


def left_product(g, e, q, total, g_in, e_in, q_in, pieces, sems):
    rank = q.shape[0]
    block = g.shape[1] // STEPS
    first = pltpu.make_async_copy(q, q_in, sems.at[2 * STEPS])
    first.start()
    copies = []
    for i in range(STEPS):
        rows = pl.ds(i * block, block)
        pair = [pltpu.make_async_copy(src.at[0, rows, :], dst.at[rows, :], sems.at[2 * i + j]) for j, (src, dst) in enumerate(((g, g_in), (e, e_in)))]
        for copy in pair:
            copy.start()
        copies.append(pair)
    first.wait()
    parts = split3(q_in[...])
    pieces[...] = jnp.concatenate(parts + (jnp.zeros_like(parts[0]),), axis=0).T
    for i, pair in enumerate(copies):
        for copy in pair:
            copy.wait()
        rows = slice(i * block, (i + 1) * block)
        t = dot(g_in[rows, :], pieces[...]) + dot(e_in[rows, :], pieces[...])
        t = (t[:, : 2 * rank] + t[:, 2 * rank :]).T
        total[:, rows] = t[:rank] + t[rank:]


def left_up_kernel(g, e, q, keep, send, total, *scratch):
    left_product(g, e, q, total, *scratch)
    split_cores(total, None, keep, send)


def left_down_kernel(g, e, q, keep, send, total, stage, *scratch):
    left_product(g, e, q, total, *scratch)
    split_replicas(total, stage, keep, send)


def split_x_kernel(width, keep, got, *outs):
    _, x = place("tensor")
    total = outs[-1]
    outs = outs[:-1]
    rows = outs[0].shape[0]
    total[...] = keep[...] + got[...]
    for j, out in enumerate(outs):
        owner = lax.bitwise_xor(x, j)
        out[:, :width] = total[pl.ds(pl.multiple_of(owner * rows, rows), rows), :width]
        if total.shape[1] > width:
            out[:, width:] = fold(total[:, width:], rows)


def split_z_kernel(n_x, width, gram_shape, keep, got, *refs):
    shards, refs = refs[:n_x], refs[n_x:]
    gram = refs[0] if gram_shape else None
    outs, stage = refs[1 if gram_shape else 0 : -1], refs[-1]
    _, z = place("dp")
    half, per, ff = keep.shape
    summed = tree_sum(s[...] for s in shards)
    block = width // half
    for c in range(half):
        stage[c, :, :ff] = keep[c] + got[c]
        stage[c, :, ff:] = fold(summed[:, c * block : (c + 1) * block], per)
    for j, out in enumerate(outs):
        out[...] = stage[lax.bitwise_xor(z, j)]
    if gram_shape:
        whole_gram = unfold(summed[:, width:], gram_shape // 2)
        gram[...] = unfold(whole_gram, gram_shape)


def mean_kernel(n_dp, *refs):
    refs[-1][...] = tree_sum(ref[...] for ref in refs[:-1]) / n_dp


def stack_kernel(*refs):
    _, z = place("dp")
    for j, ref in enumerate(refs[:-1]):
        refs[-1][lax.bitwise_xor(z, j)] = ref[...]


def shard_rows(mine, other, ff, rows):
    half = mine.shape[0]
    return jnp.concatenate([unfold(mine[c, :, ff:] + other[c, :, ff:], rows) for c in range(half)], axis=1)


def shard_rows_kernel(ff, mine, other, out):
    out[...] = shard_rows(mine, other, ff, out.shape[0])


def stack_x_kernel(width, _, *refs):
    _, x = place("tensor")
    *pieces, out = refs
    rows = pieces[0].shape[0]
    for j, piece in enumerate(pieces):
        owner = lax.bitwise_xor(x, j)
        out[pl.ds(pl.multiple_of(owner * rows, rows), rows), :width] = piece[:, :width]
    if out.shape[1] > width:
        summed = tree_sum(piece[:, width:] for piece in pieces)
        for i in range(0, out.shape[0], rows):
            out[i : i + rows, width:] = summed


def split_rows(left, pieces):
    rank = left.shape[0]
    for i, piece in enumerate(split3(left[...])):
        pieces[i * rank : (i + 1) * rank, :] = piece


def add_pieces(t):
    rank = t.shape[0] // 3
    return t[:rank] + (t[rank : 2 * rank] + t[2 * rank :])


def right_down_kernel(mine, other, g, e, left, keep, send, pieces, total, stage):
    rank = left.shape[0]
    join_replicas(mine, other, stage, left)
    split_rows(left, pieces)
    total[...] = add_pieces(dot(pieces[...], g[0]) + dot(pieces[...], e[0]))
    gram = dot(left[...], left[...], NT, HIGHEST)
    split_cores(total, fold(gram, rank // 2), keep, send)


def right_up_kernel(mine, other, g, e, left, gram, keep, send, pieces, total, stage):
    join_cores(mine, other, left)
    split_rows(left, pieces)
    block = total.shape[1] // STEPS
    for i in range(STEPS):
        part = slice(i * block, (i + 1) * block)
        total[:, part] = add_pieces(dot(pieces[...], g[0, :, part]) + dot(pieces[...], e[0, :, part]))
    split_replicas(total, stage, keep, send)
    gram[...] = dot(left[...], left[...], NT, HIGHEST)


def inverse_factors(grams):
    rank = grams[0].shape[0]
    count = rank // 8
    panel = 4
    lane = lax.broadcasted_iota(jnp.int32, (8, 2 * rank), 1)
    row = lax.broadcasted_iota(jnp.int32, (8, 2 * rank), 0)
    states, pivots = [], []
    for gram in grams:
        wide = jnp.concatenate([gram, jnp.zeros_like(gram)], axis=1)
        states.append([wide[i : i + 8] + (lane == row + (rank + i)).astype(F32) for i in range(0, rank, 8)])
        pivots.append([])
    for start in range(0, rank, panel):
        at = start // 8
        below = range(at, count)
        spread = [
            [{i: jnp.broadcast_to(blocks[i][:, start + j : start + j + 1], (8, 2 * rank)) for i in below} for j in range(panel)]
            for blocks in states
        ]
        for j in range(panel):
            inner = (start + j) % 8
            for blocks, columns, found in zip(states, spread, pivots):
                pivot = columns[j][at][inner : inner + 1, :]
                found.append(pivot)
                inverse = 1.0 / pivot
                factor = {i: jnp.where(row > inner, columns[j][i], 0.0) if i == at else columns[j][i] for i in below}
                for later in columns[j + 1 :]:
                    head = later[at][inner : inner + 1, :] * inverse
                    for i in below:
                        later[i] = later[i] - factor[i] * head
                scaled = blocks[at][inner : inner + 1, :] * inverse
                for i in below:
                    blocks[i] = blocks[i] - factor[i] * scaled
    results = []
    for blocks, found in zip(states, pivots):
        rows = [block / jnp.sqrt(jnp.concatenate(found[8 * i : 8 * i + 8], axis=0)) for i, block in enumerate(blocks)]
        results.append(jnp.concatenate(rows, axis=0)[:, rank:])
    return results


def basis_kernel(left_up, left_down, gram_up, gram_down, inv_up, inv_down, lhs_up, lhs_down):
    inverses = inverse_factors([gram_up[...], gram_down[...]])
    rank = left_up.shape[0]
    for inverse, inv, left, lhs in zip(inverses, (inv_up, inv_down), (left_up, left_down), (lhs_up, lhs_down)):
        inv[...] = inverse
        first, second, _ = split3(dot(inverse, left[...], precision=HIGHEST).T)
        lhs[:, :rank] = first
        lhs[:, rank : 2 * rank] = first
        lhs[:, 2 * rank : 3 * rank] = second
        lhs[:, 3 * rank :] = second


def right_factor(inv, total, rhs):
    rank = inv.shape[0]
    right = dot(inv[...], total[...], precision=HIGHEST)
    first, second, _ = split3(right)
    rhs[:rank, :] = first
    rhs[rank : 2 * rank, :] = second
    rhs[2 * rank : 3 * rank, :] = first
    rhs[3 * rank :, :] = second
    return jnp.sum(right * right)


def factor_up_kernel(mine, other, inv, rhs, shard, total, stage):
    join_replicas(mine, other, stage, total)
    square = right_factor(inv, total, rhs)
    rows, ff = shard.shape[0], total.shape[1]
    width = shard.shape[1] - 128
    shard[:, :width] = shard_rows(mine, other, ff, rows)
    shard[:, width:] = jnp.full((rows, 128), square, F32)


def factor_down_kernel(limit, mine, other, inv, rhs, clip, total):
    join_cores(mine, other, total)
    square = right_factor(inv, total, rhs)
    width = total.shape[1]
    norm_sq = square + (mine[:8, width:] + other[:8, width:])
    clip[...] = jnp.minimum(jnp.float32(1.0), limit / jnp.sqrt(norm_sq))


def rows_of(block):
    return pl.ds(pl.multiple_of(pl.program_id(0) * block, block), block)


def error_up_kernel(g, e, lhs, rhs, error):
    part = rows_of(error.shape[1])
    rebuilt = dot(lhs[part, :], rhs[...])
    error[0] = (g[0, part, :].astype(F32) + e[0, part, :].astype(F32) - rebuilt).astype(BF16)


def last_kernel(g, e, lhs_up, rhs_up, lhs_down, rhs_down, clip, error, update_up, update_down):
    factor = clip[:1, :1]
    part = rows_of(update_down.shape[0])
    rebuilt = dot(lhs_down[part, :], rhs_down[...])
    update_down[...] = (factor * rebuilt).astype(BF16)
    error[0] = (g[0, part, :].astype(F32) + e[0, part, :].astype(F32) - rebuilt).astype(BF16)
    part = rows_of(update_up.shape[0])
    update_up[...] = (factor * dot(lhs_up[part, :], rhs_up[...])).astype(BF16)


def shaped(*dims, dtype=F32):
    return jax.ShapeDtypeStruct(dims, dtype)


def whole(shape):
    return pl.BlockSpec(shape, lambda *_: (0,) * len(shape))


def row_blocks(rows, columns):
    return pl.BlockSpec((rows // STEPS, columns), lambda i: (i, 0))


def replica_blocks(rows, columns):
    return pl.BlockSpec((1, rows // STEPS, columns), lambda i: (0, i, 0))


VMEM = pl.BlockSpec(memory_space=pltpu.VMEM)


def call(kernel, out_shape, *args, flops=0, limit=12, name=None, **more):
    arrays = list(args) + jax.tree.leaves(out_shape)
    size = sum(a.size * a.dtype.itemsize for a in arrays)
    cost = pl.CostEstimate(flops=flops, bytes_accessed=size, transcendentals=0)
    params = pltpu.CompilerParams(vmem_limit_bytes=limit * MIB)
    return pl.pallas_call(kernel, out_shape=out_shape, compiler_params=params, cost_estimate=cost, name=name, **more)(*args)


def swap(x, axis, distance):
    pairs = [(i, i ^ distance) for i in range(lax.axis_size(axis))]
    return lax.ppermute(x, axis, pairs)


def sum_shards(keep, send, width):
    n_x = lax.axis_size("tensor") // 2
    got = swap(send, "tensor", 1)
    rows, columns = keep.shape[0] // n_x, keep.shape[1]
    out = shaped(rows, width + (columns - width) * n_x)
    parts = call(
        functools.partial(split_x_kernel, width), [out] * n_x, keep, got, name="split_x",
        scratch_shapes=[pltpu.VMEM(keep.shape, F32)],
    )
    return [parts[0]] + [swap(parts[j], "tensor", 2 * j) for j in range(1, n_x)]


def mean_replicas(keep, got, shards, width, gram_rank=0):
    n_dp = lax.axis_size("dp")
    half, per, ff = keep.shape
    columns = ff + shards[0].shape[0] // per * (width // half)
    outs = [shaped(per, columns)] * half
    if gram_rank:
        outs = [shaped(gram_rank, gram_rank)] + outs
    parts = call(
        functools.partial(split_z_kernel, len(shards), width, gram_rank), outs, keep, got, *shards,
        name="split_z", scratch_shapes=[pltpu.VMEM((half, per, columns), F32)],
    )
    gram, parts = (parts[0], parts[1:]) if gram_rank else (None, parts)
    parts = [parts[0]] + [swap(parts[j], "dp", 2 * j) for j in range(1, half)]
    mean = call(functools.partial(mean_kernel, n_dp), shaped(per, columns), *parts, name="replica_mean")
    chunks = [mean] + [swap(mean, "dp", 2 * j) for j in range(1, half)]
    mine = call(stack_kernel, shaped(half, per, columns), *chunks, name="stack_z")
    return mine, swap(mine, "dp", 1), gram


def gather_shards(rows_here, width, meanwhile):
    n_x = lax.axis_size("tensor") // 2
    rows, columns = rows_here.shape
    pieces = [rows_here] + [swap(rows_here, "tensor", 2 * j) for j in range(1, n_x)]
    mine = call(functools.partial(stack_x_kernel, width), shaped(rows * n_x, columns), meanwhile, *pieces, name="stack_x", in_specs=[pl.BlockSpec(memory_space=pl.ANY)] + [VMEM] * n_x)
    return mine, swap(mine, "tensor", 1)


def on_device(gu, eu, gd, ed, qu, qd):
    qu, qd = qu.T, qd.T
    n_dp, n_shards = lax.axis_size("dp"), lax.axis_size("tensor")
    _, rows, ff = gu.shape
    rank = qu.shape[0]
    half, per = n_dp // 2, rank // n_dp
    core_half = shaped(rank // 2, rows)
    replica_half = shaped(half, per, ff)
    stage = pltpu.VMEM((n_dp, per, ff), F32)
    wide = pltpu.VMEM((rank, ff), F32)
    narrow = pltpu.VMEM((rank, rows), F32)
    product = 4 * rows * ff * 4 * rank

    def left(kernel, outs, g, e, q, scratch, name):
        buffers = [pltpu.VMEM(g.shape[1:], BF16)] * 2 + [pltpu.VMEM(q.shape, F32), pltpu.VMEM((q.shape[1], 4 * rank), BF16)]
        return call(
            kernel, outs, g, e, q, name=name, flops=product, limit=61, in_specs=[pl.BlockSpec(memory_space=pltpu.HBM)] * 3,
            scratch_shapes=scratch + buffers + [pltpu.SemaphoreType.DMA((2 * STEPS + 1,))],
        )

    keep_up, send_up = left(left_up_kernel, [core_half] * 2, gu, eu, qu, [narrow], "left_up")
    shards = sum_shards(keep_up, send_up, rows)
    keep, send = left(left_down_kernel, [replica_half] * 2, gd, ed, qd, [wide, stage], "left_down")
    mine, other, _ = mean_replicas(keep, swap(send, "dp", 1), shards, rows)

    shard = call(functools.partial(shard_rows_kernel, ff), shaped(rank // n_shards, rows), mine, other, name="shard_rows")
    core_half = shaped(rank // 2, rows + 2 * rank)
    left_down, keep_down, send_down = call(
        right_down_kernel, [shaped(rank, ff), core_half, core_half], mine, other, gd, ed, name="right_down", flops=product,
        in_specs=[VMEM] * 4, scratch_shapes=[pltpu.VMEM((3 * rank, ff), BF16), narrow, stage],
    )
    left_half, left_other = gather_shards(shard, rows, left_down)
    shards = sum_shards(keep_down, send_down, rows)
    left_up, gram_up, keep, send = call(
        right_up_kernel, [shaped(rank, rows), shaped(rank, rank), replica_half, replica_half], left_half, left_other, gu, eu,
        name="right_up", flops=product, in_specs=[VMEM] * 4, scratch_shapes=[pltpu.VMEM((3 * rank, rows), BF16), wide, stage],
    )
    mine, other, gram_down = mean_replicas(keep, swap(send, "dp", 1), shards, rows, rank)
    inv_up, inv_down, lhs_up, lhs_down = call(
        basis_kernel,
        [shaped(rank, rank)] * 2 + [shaped(rows, 4 * rank, dtype=BF16), shaped(ff, 4 * rank, dtype=BF16)],
        left_up, left_down, gram_up, gram_down, name="basis", flops=10**9,
    )
    rhs_up, shard = call(
        factor_up_kernel, [shaped(4 * rank, ff, dtype=BF16), shaped(rank // n_shards, rows + 128)], mine, other, inv_up,
        name="factor_up", scratch_shapes=[wide, stage],
    )
    new_error_up = call(
        error_up_kernel, shaped(1, rows, ff, dtype=BF16), gu, eu, lhs_up, rhs_up, name="error_up", flops=product // 2,
        grid=(STEPS,), in_specs=[VMEM] * 4, out_specs=replica_blocks(rows, ff),
    )
    right_half, right_other = gather_shards(shard, rows, new_error_up)
    limit = CLIP_RMS * (2.0 * rows * ff * n_shards) ** 0.5
    rhs_down, clip = call(
        functools.partial(factor_down_kernel, limit), [shaped(4 * rank, rows, dtype=BF16), shaped(8, 128)],
        right_half, right_other, inv_down, name="factor_down", scratch_shapes=[narrow],
    )
    new_error_down, update_up, update_down = call(
        last_kernel, [shaped(1, ff, rows, dtype=BF16), shaped(rows, ff, dtype=BF16), shaped(ff, rows, dtype=BF16)],
        gd, ed, lhs_up, rhs_up, lhs_down, rhs_down, clip, name="last", flops=product, grid=(STEPS,),
        in_specs=[VMEM] * 7, out_specs=[replica_blocks(ff, rows), row_blocks(rows, ff), row_blocks(ff, rows)],
    )
    return new_error_up, update_up, new_error_down, update_down


def solution(mesh):
    placed = (
        P("dp", None, "tensor"),
        P("dp", None, "tensor"),
        P("dp", "tensor", None),
        P("dp", "tensor", None),
        P("tensor", None),
        P(),
    )
    return jax.shard_map(
        on_device,
        mesh=mesh,
        in_specs=placed,
        out_specs=(
            P("dp", None, "tensor"),
            P(None, "tensor"),
            P("dp", "tensor", None),
            P("tensor", None),
        ),
        check_vma=False,
    )
```

```python
import functools

import jax
import jax.numpy as jnp
from jax import lax
from jax.experimental import pallas as pl
from jax.experimental.pallas import tpu as pltpu
from jax.sharding import PartitionSpec as P

F32 = jnp.float32
BF16 = jnp.bfloat16
HIGHEST = lax.Precision.HIGHEST
CLIP_RMS = 0.1
STEPS = 4
AHEAD = 5
MIB = 1024 * 1024
NT = ((1,), (1,))


def split3(x):
    first = x.astype(BF16)
    rest = x - first.astype(F32)
    second = rest.astype(BF16)
    return first, second, (rest - second.astype(F32)).astype(BF16)


def tree_sum(values):
    values = list(values)
    while len(values) > 1:
        values = [values[i] + values[i + 1] for i in range(0, len(values), 2)]
    return values[0]


def dot(a, b, dims=((1,), (0,)), precision=None):
    return lax.dot_general(a, b, (dims, ((), ())), precision=precision, preferred_element_type=F32)


def fold(x, rows):
    return jnp.concatenate([x[i : i + rows] for i in range(0, x.shape[0], rows)], axis=1)


def unfold(x, rows):
    count = rows // x.shape[0]
    width = x.shape[1] // count
    return jnp.concatenate([x[:, i * width : (i + 1) * width] for i in range(count)], axis=0)


def place(axis):
    index = lax.axis_index(axis)
    return lax.bitwise_and(index, 1), lax.shift_right_logical(index, 1)


def split_cores(total, extra, keep, send):
    core, _ = place("tensor")
    rows, width = keep.shape[0], total.shape[1]
    keep[:, :width] = total[pl.ds(pl.multiple_of(core * rows, rows), rows), :]
    send[:, :width] = total[pl.ds(pl.multiple_of((1 - core) * rows, rows), rows), :]
    if extra is not None:
        keep[:, width:] = extra
        send[:, width:] = extra


def split_replicas(total, stage, keep, send):
    parity, _ = place("dp")
    half, per, _ = keep.shape
    for c in range(2 * half):
        stage[c] = total[c * per : (c + 1) * per, :]
    for c in range(half):
        keep[c] = stage[2 * c + parity]
        send[c] = stage[2 * c + 1 - parity]


def join_replicas(mine, other, stage, total):
    parity, _ = place("dp")
    half, per, _ = mine.shape
    width = total.shape[1]
    for c in range(half):
        stage[2 * c + parity] = mine[c, :, :width]
        stage[2 * c + 1 - parity] = other[c, :, :width]
    for c in range(2 * half):
        total[c * per : (c + 1) * per, :] = stage[c]


def join_cores(mine, other, total):
    core, _ = place("tensor")
    rows, width = mine.shape[0], total.shape[1]
    total[pl.ds(pl.multiple_of(core * rows, rows), rows), :] = mine[:, :width]
    total[pl.ds(pl.multiple_of((1 - core) * rows, rows), rows), :] = other[:, :width]


def left_kernel(gu, eu, qu, gd, ed, qd, keep_up, send_up, keep_down, send_down, *scratch):
    up, down, stage, q_sems, sems = scratch[:5], scratch[5:10], *scratch[10:]
    stages, waiting = [], []
    for i, (source, part) in enumerate(((qu, up), (qd, down))):
        waiting.append(pltpu.make_async_copy(source, part[2], q_sems.at[i]))
        waiting[i].start()
    for g, e, part in ((gu, eu, up), (gd, ed, down)):
        block = g.shape[1] // STEPS
        for i in range(STEPS):
            rows = pl.ds(i * block, block)
            n = 2 * len(stages)
            copies = [
                pltpu.make_async_copy(src.at[0, rows, :], dst.at[rows, :], sems.at[n + j])
                for j, (src, dst) in enumerate(((g, part[0]), (e, part[1])))
            ]
            stages.append((part, slice(i * block, (i + 1) * block), copies))

    def fetch(n):
        if n < len(stages):
            for copy in stages[n][2]:
                copy.start()

    for n in range(AHEAD):
        fetch(n)
    for copy, (_, _, q, pieces, _) in zip(waiting, (up, down)):
        copy.wait()
        parts = split3(q[...])
        pieces[...] = jnp.concatenate(parts + (jnp.zeros_like(parts[0]),), axis=0).T
    for n, ((g, e, q, pieces, total), rows, copies) in enumerate(stages):
        rank = q.shape[0]
        for copy in copies:
            copy.wait()
        fetch(n + AHEAD)
        t = dot(g[rows, :], pieces[...]) + dot(e[rows, :], pieces[...])
        t = (t[:, : 2 * rank] + t[:, 2 * rank :]).T
        total[:, rows] = t[:rank] + t[rank:]
    split_cores(up[4], None, keep_up, send_up)
    split_replicas(down[4], stage, keep_down, send_down)


def split_x_kernel(width, keep, got, *outs):
    _, x = place("tensor")
    total = outs[-1]
    outs = outs[:-1]
    rows = outs[0].shape[0]
    total[...] = keep[...] + got[...]
    for j, out in enumerate(outs):
        owner = lax.bitwise_xor(x, j)
        out[:, :width] = total[pl.ds(pl.multiple_of(owner * rows, rows), rows), :width]
        if total.shape[1] > width:
            out[:, width:] = fold(total[:, width:], rows)


def sum_kernel(scale, *refs):
    refs[-1][...] = tree_sum(ref[...] for ref in refs[:-1]) * scale


def sum_gram_kernel(*refs):
    *terms, out, gram = refs
    width = out.shape[1]
    total = tree_sum(term[...] for term in terms)
    out[...] = total[:, :width]
    gram[...] = unfold(unfold(total[:, width:], gram.shape[0] // 2), gram.shape[0])


def split_z_kernel(keep, got, *refs):
    *outs, stage = refs
    _, z = place("dp")
    stage[...] = keep[...] + got[...]
    for j, out in enumerate(outs):
        out[...] = stage[lax.bitwise_xor(z, j)]


def stack_z_kernel(*refs):
    _, z = place("dp")
    for j, ref in enumerate(refs[:-1]):
        refs[-1][lax.bitwise_xor(z, j)] = ref[...]


def stack_x_kernel(*refs):
    _, x = place("tensor")
    *pieces, out = refs
    rows = pieces[0].shape[0]
    for j, piece in enumerate(pieces):
        owner = lax.bitwise_xor(x, j)
        out[pl.ds(pl.multiple_of(owner * rows, rows), rows), :] = piece[...]


def split_rows(left, pieces):
    rank = left.shape[0]
    for i, piece in enumerate(split3(left[...])):
        pieces[i * rank : (i + 1) * rank, :] = piece


def add_pieces(t):
    rank = t.shape[0] // 3
    return t[:rank] + (t[rank : 2 * rank] + t[2 * rank :])


def right_down_kernel(mine, other, g, e, left, keep, send, pieces, total, stage):
    rank = left.shape[0]
    join_replicas(mine, other, stage, left)
    split_rows(left, pieces)
    total[...] = add_pieces(dot(pieces[...], g[0]) + dot(pieces[...], e[0]))
    gram = dot(left[...], left[...], NT, HIGHEST)
    split_cores(total, fold(gram, rank // 2), keep, send)


def right_up_kernel(mine, other, g, e, left, gram, keep, send, pieces, total, stage):
    join_cores(mine, other, left)
    split_rows(left, pieces)
    block = total.shape[1] // STEPS
    for i in range(STEPS):
        part = slice(i * block, (i + 1) * block)
        total[:, part] = add_pieces(dot(pieces[...], g[0, :, part]) + dot(pieces[...], e[0, :, part]))
    split_replicas(total, stage, keep, send)
    gram[...] = dot(left[...], left[...], NT, HIGHEST)


def inverse_factors(grams):
    rank = grams[0].shape[0]
    count = rank // 8
    panel = 4
    lane = lax.broadcasted_iota(jnp.int32, (8, 2 * rank), 1)
    row = lax.broadcasted_iota(jnp.int32, (8, 2 * rank), 0)
    states, pivots = [], []
    for gram in grams:
        wide = jnp.concatenate([gram, jnp.zeros_like(gram)], axis=1)
        states.append([wide[i : i + 8] + (lane == row + (rank + i)).astype(F32) for i in range(0, rank, 8)])
        pivots.append([])
    for start in range(0, rank, panel):
        at = start // 8
        below = range(at, count)
        spread = [
            [{i: jnp.broadcast_to(blocks[i][:, start + j : start + j + 1], (8, 2 * rank)) for i in below} for j in range(panel)]
            for blocks in states
        ]
        for j in range(panel):
            inner = (start + j) % 8
            for blocks, columns, found in zip(states, spread, pivots):
                pivot = columns[j][at][inner : inner + 1, :]
                found.append(pivot)
                inverse = 1.0 / pivot
                factor = {i: jnp.where(row > inner, columns[j][i], 0.0) if i == at else columns[j][i] for i in below}
                for later in columns[j + 1 :]:
                    head = later[at][inner : inner + 1, :] * inverse
                    for i in below:
                        later[i] = later[i] - factor[i] * head
                scaled = blocks[at][inner : inner + 1, :] * inverse
                for i in below:
                    blocks[i] = blocks[i] - factor[i] * scaled
    results = []
    for blocks, found in zip(states, pivots):
        rows = [block / jnp.sqrt(jnp.concatenate(found[8 * i : 8 * i + 8], axis=0)) for i, block in enumerate(blocks)]
        results.append(jnp.concatenate(rows, axis=0)[:, rank:])
    return results


def basis_kernel(left_up, left_down, gram_up, gram_down, inv_up, inv_down, lhs_up, lhs_down):
    inverses = inverse_factors([gram_up[...], gram_down[...]])
    rank = left_up.shape[0]
    for inverse, inv, left, lhs in zip(inverses, (inv_up, inv_down), (left_up, left_down), (lhs_up, lhs_down)):
        inv[...] = inverse
        first, second, _ = split3(dot(inverse, left[...], precision=HIGHEST).T)
        lhs[:, :rank] = first
        lhs[:, rank : 2 * rank] = first
        lhs[:, 2 * rank : 3 * rank] = second
        lhs[:, 3 * rank :] = second


def right_factor(inv, total, rhs):
    rank = inv.shape[0]
    right = dot(inv[...], total[...], precision=HIGHEST)
    first, second, _ = split3(right)
    rhs[:rank, :] = first
    rhs[rank : 2 * rank, :] = second
    rhs[2 * rank : 3 * rank, :] = first
    rhs[3 * rank :, :] = second
    return jnp.sum(right * right)


def factor_up_kernel(mine, other, inv, rhs, square, total, stage):
    join_replicas(mine, other, stage, total)
    square[...] = jnp.full(square.shape, right_factor(inv, total, rhs), F32)


def factor_down_kernel(mine, other, inv, rhs, square, total):
    join_cores(mine, other, total)
    square[...] = jnp.full(square.shape, right_factor(inv, total, rhs), F32)


def rows_of(block):
    return pl.ds(pl.multiple_of(pl.program_id(0) * block, block), block)


def error_kernel(g, e, lhs, rhs, error, made):
    made[...] = jnp.zeros_like(made)
    part = rows_of(error.shape[1])
    rebuilt = dot(lhs[part, :], rhs[...])
    error[0] = (g[0, part, :].astype(F32) + e[0, part, :].astype(F32) - rebuilt).astype(BF16)


def update_kernel(limit, lhs_up, rhs_up, lhs_down, rhs_down, square_down, *refs):
    *squares_up, update_up, update_down = refs
    norm_sq = tree_sum(square[...] for square in squares_up) + square_down[...]
    factor = jnp.minimum(jnp.float32(1.0), limit / jnp.sqrt(norm_sq))[:1, :1]
    for lhs, rhs, update in ((lhs_up, rhs_up, update_up), (lhs_down, rhs_down, update_down)):
        update[...] = (factor * dot(lhs[rows_of(update.shape[0]), :], rhs[...])).astype(BF16)


def shaped(*dims, dtype=F32):
    return jax.ShapeDtypeStruct(dims, dtype)


def whole(shape):
    return pl.BlockSpec(shape, lambda *_: (0,) * len(shape))


def row_blocks(rows, columns):
    return pl.BlockSpec((rows // STEPS, columns), lambda i: (i, 0))


def replica_blocks(rows, columns):
    return pl.BlockSpec((1, rows // STEPS, columns), lambda i: (0, i, 0))


VMEM = pl.BlockSpec(memory_space=pltpu.VMEM)


ANY = pl.BlockSpec(memory_space=pl.ANY)


def call(kernel, out_shape, *args, after=(), in_specs=None, limit=12, name=None, **more):
    skip = len(after)
    return pl.pallas_call(
        lambda *refs: kernel(*refs[skip:]), out_shape=out_shape, in_specs=[ANY] * skip + (in_specs or [VMEM] * len(args)),
        compiler_params=pltpu.CompilerParams(vmem_limit_bytes=limit * MIB),
        cost_estimate=pl.CostEstimate(flops=0, bytes_accessed=0, transcendentals=0), name=name, **more,
    )(*after, *args)


def swap(x, axis, distance):
    pairs = [(i, i ^ distance) for i in range(lax.axis_size(axis))]
    return lax.ppermute(x, axis, pairs)


def others(parts, axis):
    return [swap(part, axis, 2 * j) for j, part in enumerate(parts) if j]


def total_of(name, terms, scale=1.0, after=()):
    return call(functools.partial(sum_kernel, scale), shaped(*terms[0].shape), *terms, after=after, name=name)


def on_device(gu, eu, gd, ed, qu, qd):
    qu, qd = qu.T, qd.T
    n_dp, n_shards = lax.axis_size("dp"), lax.axis_size("tensor")
    _, rows, ff = gu.shape
    rank = qu.shape[0]
    half, per, n_x = n_dp // 2, rank // n_dp, n_shards // 2
    core_half = shaped(rank // 2, rows)
    shard = shaped(rank // n_shards, rows)
    replica_half = shaped(half, per, ff)
    chunk = shaped(per, ff)
    stage = pltpu.VMEM((n_dp, per, ff), F32)
    wide = pltpu.VMEM((rank, ff), F32)
    narrow = pltpu.VMEM((rank, rows), F32)

    def split_x(keep, got, out):
        return call(
            functools.partial(split_x_kernel, rows), [out] * n_x, keep, got, name="split_x",
            scratch_shapes=[pltpu.VMEM(keep.shape, F32)],
        )

    def split_z(keep, got, after):
        return call(
            split_z_kernel, [chunk] * half, keep, got, after=after, name="split_z",
            scratch_shapes=[pltpu.VMEM(replica_half.shape, F32)],
        )

    def stack_z(parts, after):
        return call(stack_z_kernel, replica_half, *parts, after=after, name="stack_z")

    def stack_x(parts, after):
        return call(stack_x_kernel, core_half, *parts, after=after, name="stack_x")

    buffers = [
        [pltpu.VMEM(g.shape[1:], BF16)] * 2 + [pltpu.VMEM(q.shape, F32), pltpu.VMEM((q.shape[1], 4 * rank), BF16), total]
        for g, q, total in ((gu, qu, narrow), (gd, qd, wide))
    ]
    keep_up, send_up, keep_down, send_down = call(
        left_kernel, [core_half] * 2 + [replica_half] * 2, gu, eu, qu, gd, ed, qd, name="left", limit=61,
        in_specs=[pl.BlockSpec(memory_space=pltpu.HBM)] * 6,
        scratch_shapes=buffers[0] + buffers[1] + [stage, pltpu.SemaphoreType.DMA((2,)), pltpu.SemaphoreType.DMA((4 * STEPS,))],
    )

    down_y = swap(send_down, "dp", 1)
    parts = split_x(keep_up, swap(send_up, "tensor", 1), shard)
    up = total_of("sum_x", [parts[0]] + others(parts, "tensor"))
    up = total_of("sum_y", [up, swap(up, "dp", 1)])
    up_z = others([up] * half, "dp")
    parts = split_z(keep_down, down_y, (up,))
    down_z = others(parts, "dp")
    up = total_of("sum_z", [up] + up_z, 1.0 / n_dp, after=(parts[0],))
    up_x = others([up] * n_x, "tensor")
    down = total_of("replica_mean", [parts[0]] + down_z, 1.0 / n_dp, after=(up,))
    down_z = others([down] * half, "dp")
    mine = stack_x([up] + up_x, (down,))
    left_up, gram_up, keep, send = call(
        right_up_kernel, [shaped(rank, rows), shaped(rank, rank), replica_half, replica_half],
        mine, swap(mine, "tensor", 1), gu, eu, name="right_up",
        scratch_shapes=[pltpu.VMEM((3 * rank, rows), BF16), wide, stage],
    )
    up_y = swap(send, "dp", 1)
    mine = stack_z([down] + down_z, (keep,))
    down_y = swap(mine, "dp", 1)

    up_parts = split_z(keep, up_y, (mine,))
    up_z = others(up_parts, "dp")
    core_wide = shaped(rank // 2, rows + 2 * rank)
    left_down, keep, send = call(
        right_down_kernel, [shaped(rank, ff), core_wide, core_wide], mine, down_y, gd, ed, after=(up_parts[0],),
        name="right_down", scratch_shapes=[pltpu.VMEM((3 * rank, ff), BF16), narrow, stage],
    )
    parts = split_x(keep, swap(send, "tensor", 1), shaped(rank // n_shards, rows + 2 * rank * n_x))
    down_x = others(parts, "tensor")
    up = total_of("replica_mean", [up_parts[0]] + up_z, 1.0 / n_dp, after=(parts[0],))
    up_z = others([up] * half, "dp")
    down, gram_down = call(sum_gram_kernel, [shard, shaped(rank, rank)], parts[0], *down_x, after=(up,), name="sum_x")
    down_y = swap(down, "dp", 1)
    inv_up, inv_down, lhs_up, lhs_down = call(
        basis_kernel,
        [shaped(rank, rank)] * 2 + [shaped(rows, 4 * rank, dtype=BF16), shaped(ff, 4 * rank, dtype=BF16)],
        left_up, left_down, gram_up, gram_down, name="basis",
    )
    down = total_of("sum_y", [down, down_y], after=(inv_up,))
    down_z = others([down] * half, "dp")
    mine = stack_z([up] + up_z, (down,))
    up_y = swap(mine, "dp", 1)
    down = total_of("sum_z", [down] + down_z, 1.0 / n_dp, after=(mine,))
    down_x = others([down] * n_x, "tensor")
    mine_down = stack_x([down] + down_x, ())
    rhs_down, square_down = call(
        factor_down_kernel, [shaped(4 * rank, rows, dtype=BF16), shaped(8, 128)],
        mine_down, swap(mine_down, "tensor", 1), inv_down, name="factor_down", scratch_shapes=[narrow],
    )

    def new_error(g, e, lhs, rhs, name):
        spec = replica_blocks(*g.shape[1:])
        outs = [shaped(*g.shape, dtype=BF16), shaped(8, 128)]
        return call(error_kernel, outs, g, e, lhs, rhs, name=name, grid=(STEPS,), out_specs=[spec, whole((8, 128))])

    new_error_down, made_down = new_error(gd, ed, lhs_down, rhs_down, "error_down")
    rhs_up, square_up = call(
        factor_up_kernel, [shaped(4 * rank, ff, dtype=BF16), shaped(8, 128)], mine, up_y, inv_up, after=(made_down,),
        name="factor_up", scratch_shapes=[wide, stage],
    )
    squares_up = [square_up] + [swap(square_up, "tensor", j) for j in range(1, n_shards)]
    new_error_up, made_up = new_error(gu, eu, lhs_up, rhs_up, "error_up")
    limit = CLIP_RMS * (2.0 * rows * ff * n_shards) ** 0.5
    update_up, update_down = call(
        functools.partial(update_kernel, limit), [shaped(rows, ff, dtype=BF16), shaped(ff, rows, dtype=BF16)],
        lhs_up, rhs_up, lhs_down, rhs_down, square_down, *squares_up, after=(made_up,),
        name="update", grid=(STEPS,), out_specs=[row_blocks(rows, ff), row_blocks(ff, rows)],
    )
    return new_error_up, update_up, new_error_down, update_down


def solution(mesh):
    placed = (
        P("dp", None, "tensor"),
        P("dp", None, "tensor"),
        P("dp", "tensor", None),
        P("dp", "tensor", None),
        P("tensor", None),
        P(),
    )
    return jax.shard_map(
        on_device,
        mesh=mesh,
        in_specs=placed,
        out_specs=(
            P("dp", None, "tensor"),
            P(None, "tensor"),
            P("dp", "tensor", None),
            P("tensor", None),
        ),
        check_vma=False,
    )
```

```python
import functools

import jax
import jax.numpy as jnp
from jax import lax
from jax.experimental import pallas as pl
from jax.experimental.pallas import tpu as pltpu
from jax.sharding import PartitionSpec as P

F32 = jnp.float32
BF16 = jnp.bfloat16
HIGHEST = lax.Precision.HIGHEST
CLIP_RMS = 0.1
STEPS = 4
MIB = 1024 * 1024
NT = ((1,), (1,))


def split3(x):
    first = x.astype(BF16)
    rest = x - first.astype(F32)
    second = rest.astype(BF16)
    return first, second, (rest - second.astype(F32)).astype(BF16)


def tree_sum(values):
    values = list(values)
    while len(values) > 1:
        values = [values[i] + values[i + 1] for i in range(0, len(values), 2)]
    return values[0]


def dot(a, b, dims=((1,), (0,)), precision=None):
    return lax.dot_general(a, b, (dims, ((), ())), precision=precision, preferred_element_type=F32)


def fold(x, rows):
    return jnp.concatenate([x[i : i + rows] for i in range(0, x.shape[0], rows)], axis=1)


def unfold(x, rows):
    count = rows // x.shape[0]
    width = x.shape[1] // count
    return jnp.concatenate([x[:, i * width : (i + 1) * width] for i in range(count)], axis=0)


def place(axis):
    index = lax.axis_index(axis)
    return lax.bitwise_and(index, 1), lax.shift_right_logical(index, 1)


def split_cores(total, extra, keep, send):
    core, _ = place("tensor")
    rows, width = keep.shape[0], total.shape[1]
    keep[:, :width] = total[pl.ds(pl.multiple_of(core * rows, rows), rows), :]
    send[:, :width] = total[pl.ds(pl.multiple_of((1 - core) * rows, rows), rows), :]
    if extra is not None:
        keep[:, width:] = extra
        send[:, width:] = extra


def split_replicas(total, stage, keep, send):
    parity, _ = place("dp")
    half, per, _ = keep.shape
    for c in range(2 * half):
        stage[c] = total[c * per : (c + 1) * per, :]
    for c in range(half):
        keep[c] = stage[2 * c + parity]
        send[c] = stage[2 * c + 1 - parity]


def join_replicas(mine, other, stage, total):
    parity, _ = place("dp")
    half, per, _ = mine.shape
    width = total.shape[1]
    for c in range(half):
        stage[2 * c + parity] = mine[c, :, :width]
        stage[2 * c + 1 - parity] = other[c, :, :width]
    for c in range(2 * half):
        total[c * per : (c + 1) * per, :] = stage[c]


def join_cores(mine, other, total):
    core, _ = place("tensor")
    rows, width = mine.shape[0], total.shape[1]
    total[pl.ds(pl.multiple_of(core * rows, rows), rows), :] = mine[:, :width]
    total[pl.ds(pl.multiple_of((1 - core) * rows, rows), rows), :] = other[:, :width]


def left_kernel(gu, eu, qu, gd, ed, qd, keep_up, send_up, keep_down, send_down, *scratch):
    up, down, stage, q_sems, sems = scratch[:5], scratch[5:10], *scratch[10:]
    stages, waiting = [], []
    for i, (source, part) in enumerate(((qu, up), (qd, down))):
        waiting.append(pltpu.make_async_copy(source, part[2], q_sems.at[i]))
        waiting[i].start()
    for g, e, part in ((gu, eu, up), (gd, ed, down)):
        block = g.shape[1] // STEPS
        for i in range(STEPS):
            rows = pl.ds(i * block, block)
            n = 2 * len(stages)
            copies = [
                pltpu.make_async_copy(src.at[0, rows, :], dst.at[rows, :], sems.at[n + j])
                for j, (src, dst) in enumerate(((g, part[0]), (e, part[1])))
            ]
            stages.append((part, slice(i * block, (i + 1) * block), copies))
    for _, _, copies in stages:
        for copy in copies:
            copy.start()
    for copy, (_, _, q, pieces, _) in zip(waiting, (up, down)):
        copy.wait()
        split_rows(q, pieces)
    for (g, e, q, pieces, total), rows, copies in stages:
        for copy in copies:
            copy.wait()
        total[:, rows] = add_pieces(dot(pieces[...], g[rows, :], NT) + dot(pieces[...], e[rows, :], NT))
    split_cores(up[4], None, keep_up, send_up)
    split_replicas(down[4], stage, keep_down, send_down)


def split_x_kernel(width, keep, got, *outs):
    _, x = place("tensor")
    total = outs[-1]
    outs = outs[:-1]
    rows = outs[0].shape[0]
    total[...] = keep[...] + got[...]
    for j, out in enumerate(outs):
        owner = lax.bitwise_xor(x, j)
        out[:, :width] = total[pl.ds(pl.multiple_of(owner * rows, rows), rows), :width]
        if total.shape[1] > width:
            out[:, width:] = fold(total[:, width:], rows)


def split_z_kernel(n_x, width, gram_shape, keep, got, *refs):
    shards, refs = refs[:n_x], refs[n_x:]
    gram = refs[0] if gram_shape else None
    outs, stage = refs[1 if gram_shape else 0 : -1], refs[-1]
    _, z = place("dp")
    half, per, ff = keep.shape
    summed = tree_sum(s[...] for s in shards)
    block = width // half
    for c in range(half):
        stage[c, :, :ff] = keep[c] + got[c]
        stage[c, :, ff:] = fold(summed[:, c * block : (c + 1) * block], per)
    for j, out in enumerate(outs):
        out[...] = stage[lax.bitwise_xor(z, j)]
    if gram_shape:
        whole_gram = unfold(summed[:, width:], gram_shape // 2)
        gram[...] = unfold(whole_gram, gram_shape)


def mean_kernel(n_dp, *refs):
    refs[-1][...] = tree_sum(ref[...] for ref in refs[:-1]) / n_dp


def stack_kernel(*refs):
    _, z = place("dp")
    for j, ref in enumerate(refs[:-1]):
        refs[-1][lax.bitwise_xor(z, j)] = ref[...]


def shard_rows(mine, other, ff, rows):
    half = mine.shape[0]
    return jnp.concatenate([unfold(mine[c, :, ff:] + other[c, :, ff:], rows) for c in range(half)], axis=1)


def shard_rows_kernel(ff, mine, other, out):
    out[...] = shard_rows(mine, other, ff, out.shape[0])


def stack_x_kernel(width, _, *refs):
    _, x = place("tensor")
    *pieces, out = refs
    rows = pieces[0].shape[0]
    for j, piece in enumerate(pieces):
        owner = lax.bitwise_xor(x, j)
        out[pl.ds(pl.multiple_of(owner * rows, rows), rows), :width] = piece[:, :width]
    if out.shape[1] > width:
        summed = tree_sum(piece[:, width:] for piece in pieces)
        for i in range(0, out.shape[0], rows):
            out[i : i + rows, width:] = summed


def split_rows(left, pieces):
    rank = left.shape[0]
    for i, piece in enumerate(split3(left[...])):
        pieces[i * rank : (i + 1) * rank, :] = piece


def add_pieces(t):
    rank = t.shape[0] // 3
    return t[:rank] + (t[rank : 2 * rank] + t[2 * rank :])


def right_down_kernel(mine, other, g, e, left, keep, send, pieces, total, stage):
    rank = left.shape[0]
    join_replicas(mine, other, stage, left)
    split_rows(left, pieces)
    total[...] = add_pieces(dot(pieces[...], g[0]) + dot(pieces[...], e[0]))
    gram = dot(left[...], left[...], NT, HIGHEST)
    split_cores(total, fold(gram, rank // 2), keep, send)


def right_up_kernel(mine, other, g, e, left, gram, keep, send, pieces, total, stage):
    join_cores(mine, other, left)
    split_rows(left, pieces)
    block = total.shape[1] // STEPS
    for i in range(STEPS):
        part = slice(i * block, (i + 1) * block)
        total[:, part] = add_pieces(dot(pieces[...], g[0, :, part]) + dot(pieces[...], e[0, :, part]))
    split_replicas(total, stage, keep, send)
    gram[...] = dot(left[...], left[...], NT, HIGHEST)


def inverse_factors(grams):
    rank = grams[0].shape[0]
    count = rank // 8
    panel = 4
    lane = lax.broadcasted_iota(jnp.int32, (8, 2 * rank), 1)
    row = lax.broadcasted_iota(jnp.int32, (8, 2 * rank), 0)
    states, pivots = [], []
    for gram in grams:
        wide = jnp.concatenate([gram, jnp.zeros_like(gram)], axis=1)
        states.append([wide[i : i + 8] + (lane == row + (rank + i)).astype(F32) for i in range(0, rank, 8)])
        pivots.append([])
    for start in range(0, rank, panel):
        at = start // 8
        below = range(at, count)
        spread = [
            [{i: jnp.broadcast_to(blocks[i][:, start + j : start + j + 1], (8, 2 * rank)) for i in below} for j in range(panel)]
            for blocks in states
        ]
        for j in range(panel):
            inner = (start + j) % 8
            for blocks, columns, found in zip(states, spread, pivots):
                pivot = columns[j][at][inner : inner + 1, :]
                found.append(pivot)
                inverse = 1.0 / pivot
                factor = {i: jnp.where(row > inner, columns[j][i], 0.0) if i == at else columns[j][i] for i in below}
                for later in columns[j + 1 :]:
                    head = later[at][inner : inner + 1, :] * inverse
                    for i in below:
                        later[i] = later[i] - factor[i] * head
                scaled = blocks[at][inner : inner + 1, :] * inverse
                for i in below:
                    blocks[i] = blocks[i] - factor[i] * scaled
    results = []
    for blocks, found in zip(states, pivots):
        rows = [block / jnp.sqrt(jnp.concatenate(found[8 * i : 8 * i + 8], axis=0)) for i, block in enumerate(blocks)]
        results.append(jnp.concatenate(rows, axis=0)[:, rank:])
    return results


def basis_kernel(left_up, left_down, gram_up, gram_down, *refs):
    inv_up, inv_down, lhs_up, lhs_down = refs[-4:]
    inverses = inverse_factors([gram_up[...], gram_down[...]])
    rank = left_up.shape[0]
    for inverse, inv, left, lhs in zip(inverses, (inv_up, inv_down), (left_up, left_down), (lhs_up, lhs_down)):
        inv[...] = inverse
        first, second, _ = split3(dot(inverse, left[...], precision=HIGHEST).T)
        lhs[:, :rank] = first
        lhs[:, rank : 2 * rank] = first
        lhs[:, 2 * rank : 3 * rank] = second
        lhs[:, 3 * rank :] = second


def right_factor(inv, total, rhs):
    rank = inv.shape[0]
    right = dot(inv[...], total[...], precision=HIGHEST)
    first, second, _ = split3(right)
    rhs[:rank, :] = first
    rhs[rank : 2 * rank, :] = second
    rhs[2 * rank : 3 * rank, :] = first
    rhs[3 * rank :, :] = second
    return jnp.sum(right * right)


def factor_up_kernel(mine, other, inv, rhs, shard, total, stage):
    join_replicas(mine, other, stage, total)
    square = right_factor(inv, total, rhs)
    rows, ff = shard.shape[0], total.shape[1]
    width = shard.shape[1] - 128
    shard[:, :width] = shard_rows(mine, other, ff, rows)
    shard[:, width:] = jnp.full((rows, 128), square, F32)


def factor_down_kernel(limit, mine, other, inv, rhs, clip, total):
    join_cores(mine, other, total)
    square = right_factor(inv, total, rhs)
    width = total.shape[1]
    norm_sq = square + (mine[:8, width:] + other[:8, width:])
    clip[...] = jnp.minimum(jnp.float32(1.0), limit / jnp.sqrt(norm_sq))


def rows_of(block):
    return pl.ds(pl.multiple_of(pl.program_id(0) * block, block), block)


def error_up_kernel(g, e, lhs, rhs, error, made):
    made[...] = jnp.zeros_like(made)
    part = rows_of(error.shape[1])
    rebuilt = dot(lhs[part, :], rhs[...])
    error[0] = (g[0, part, :].astype(F32) + e[0, part, :].astype(F32) - rebuilt).astype(BF16)


def last_kernel(g, e, lhs_up, rhs_up, lhs_down, rhs_down, clip, error, update_up, update_down):
    factor = clip[:1, :1]
    part = rows_of(update_down.shape[0])
    rebuilt = dot(lhs_down[part, :], rhs_down[...])
    update_down[...] = (factor * rebuilt).astype(BF16)
    error[0] = (g[0, part, :].astype(F32) + e[0, part, :].astype(F32) - rebuilt).astype(BF16)
    part = rows_of(update_up.shape[0])
    update_up[...] = (factor * dot(lhs_up[part, :], rhs_up[...])).astype(BF16)


def shaped(*dims, dtype=F32):
    return jax.ShapeDtypeStruct(dims, dtype)


def whole(shape):
    return pl.BlockSpec(shape, lambda *_: (0,) * len(shape))


def row_blocks(rows, columns):
    return pl.BlockSpec((rows // STEPS, columns), lambda i: (i, 0))


def replica_blocks(rows, columns):
    return pl.BlockSpec((1, rows // STEPS, columns), lambda i: (0, i, 0))


VMEM = pl.BlockSpec(memory_space=pltpu.VMEM)


def call(kernel, out_shape, *args, flops=0, limit=12, name=None, **more):
    arrays = list(args) + jax.tree.leaves(out_shape)
    size = sum(a.size * a.dtype.itemsize for a in arrays)
    cost = pl.CostEstimate(flops=flops, bytes_accessed=size, transcendentals=0)
    params = pltpu.CompilerParams(vmem_limit_bytes=limit * MIB)
    return pl.pallas_call(kernel, out_shape=out_shape, compiler_params=params, cost_estimate=cost, name=name, **more)(*args)


def swap(x, axis, distance):
    pairs = [(i, i ^ distance) for i in range(lax.axis_size(axis))]
    return lax.ppermute(x, axis, pairs)


def sum_shards(keep, send, width):
    n_x = lax.axis_size("tensor") // 2
    got = swap(send, "tensor", 1)
    rows, columns = keep.shape[0] // n_x, keep.shape[1]
    out = shaped(rows, width + (columns - width) * n_x)
    parts = call(
        functools.partial(split_x_kernel, width), [out] * n_x, keep, got, name="split_x",
        scratch_shapes=[pltpu.VMEM(keep.shape, F32)],
    )
    return [parts[0]] + [swap(parts[j], "tensor", 2 * j) for j in range(1, n_x)]


def mean_replicas(keep, got, shards, width, gram_rank=0):
    n_dp = lax.axis_size("dp")
    half, per, ff = keep.shape
    columns = ff + shards[0].shape[0] // per * (width // half)
    outs = [shaped(per, columns)] * half
    if gram_rank:
        outs = [shaped(gram_rank, gram_rank)] + outs
    parts = call(
        functools.partial(split_z_kernel, len(shards), width, gram_rank), outs, keep, got, *shards,
        name="split_z", scratch_shapes=[pltpu.VMEM((half, per, columns), F32)],
    )
    gram, parts = (parts[0], parts[1:]) if gram_rank else (None, parts)
    parts = [parts[0]] + [swap(parts[j], "dp", 2 * j) for j in range(1, half)]
    mean = call(functools.partial(mean_kernel, n_dp), shaped(per, columns), *parts, name="replica_mean")
    chunks = [mean] + [swap(mean, "dp", 2 * j) for j in range(1, half)]
    mine = call(stack_kernel, shaped(half, per, columns), *chunks, name="stack_z")
    return mine, swap(mine, "dp", 1), gram


def gather_shards(rows_here, width, meanwhile):
    n_x = lax.axis_size("tensor") // 2
    rows, columns = rows_here.shape
    pieces = [rows_here] + [swap(rows_here, "tensor", 2 * j) for j in range(1, n_x)]
    mine = call(functools.partial(stack_x_kernel, width), shaped(rows * n_x, columns), meanwhile, *pieces, name="stack_x", in_specs=[pl.BlockSpec(memory_space=pl.ANY)] + [VMEM] * n_x)
    return mine, swap(mine, "tensor", 1)


def on_device(gu, eu, gd, ed, qu, qd):
    qu, qd = qu.T, qd.T
    n_dp, n_shards = lax.axis_size("dp"), lax.axis_size("tensor")
    _, rows, ff = gu.shape
    rank = qu.shape[0]
    half, per = n_dp // 2, rank // n_dp
    core_half = shaped(rank // 2, rows)
    replica_half = shaped(half, per, ff)
    stage = pltpu.VMEM((n_dp, per, ff), F32)
    wide = pltpu.VMEM((rank, ff), F32)
    narrow = pltpu.VMEM((rank, rows), F32)
    product = 4 * rows * ff * 4 * rank

    buffers = [
        [pltpu.VMEM(g.shape[1:], BF16)] * 2 + [pltpu.VMEM(q.shape, F32), pltpu.VMEM((3 * rank, q.shape[1]), BF16), total]
        for g, q, total in ((gu, qu, narrow), (gd, qd, wide))
    ]
    keep_up, send_up, keep, send = call(
        left_kernel, [core_half] * 2 + [replica_half] * 2, gu, eu, qu, gd, ed, qd, name="left", flops=2 * product, limit=61,
        in_specs=[pl.BlockSpec(memory_space=pltpu.HBM)] * 6,
        scratch_shapes=buffers[0] + buffers[1] + [stage, pltpu.SemaphoreType.DMA((2,)), pltpu.SemaphoreType.DMA((4 * STEPS,))],
    )
    shards = sum_shards(keep_up, send_up, rows)
    mine, other, _ = mean_replicas(keep, swap(send, "dp", 1), shards, rows)

    shard = call(functools.partial(shard_rows_kernel, ff), shaped(rank // n_shards, rows), mine, other, name="shard_rows")
    core_half = shaped(rank // 2, rows + 2 * rank)
    left_down, keep_down, send_down = call(
        right_down_kernel, [shaped(rank, ff), core_half, core_half], mine, other, gd, ed, name="right_down", flops=product,
        in_specs=[VMEM] * 4, scratch_shapes=[pltpu.VMEM((3 * rank, ff), BF16), narrow, stage],
    )
    left_half, left_other = gather_shards(shard, rows, left_down)
    shards = sum_shards(keep_down, send_down, rows)
    left_up, gram_up, keep, send = call(
        right_up_kernel, [shaped(rank, rows), shaped(rank, rank), replica_half, replica_half], left_half, left_other, gu, eu,
        name="right_up", flops=product, in_specs=[VMEM] * 4, scratch_shapes=[pltpu.VMEM((3 * rank, rows), BF16), wide, stage],
    )
    mine, other, gram_down = mean_replicas(keep, swap(send, "dp", 1), shards, rows, rank)
    inv_up, inv_down, lhs_up, lhs_down = call(
        basis_kernel,
        [shaped(rank, rank)] * 2 + [shaped(rows, 4 * rank, dtype=BF16), shaped(ff, 4 * rank, dtype=BF16)],
        left_up, left_down, gram_up, gram_down, gu, eu, gd, ed, name="basis", in_specs=[VMEM] * 8,
    )
    rhs_up, shard = call(
        factor_up_kernel, [shaped(4 * rank, ff, dtype=BF16), shaped(rank // n_shards, rows + 128)], mine, other, inv_up,
        name="factor_up", scratch_shapes=[wide, stage],
    )
    new_error_up, made = call(
        error_up_kernel, [shaped(1, rows, ff, dtype=BF16), shaped(8, 128)], gu, eu, lhs_up, rhs_up, name="error_up", flops=product // 2,
        grid=(STEPS,), in_specs=[VMEM] * 4, out_specs=[replica_blocks(rows, ff), whole((8, 128))],
    )
    right_half, right_other = gather_shards(shard, rows, made)
    limit = CLIP_RMS * (2.0 * rows * ff * n_shards) ** 0.5
    rhs_down, clip = call(
        functools.partial(factor_down_kernel, limit), [shaped(4 * rank, rows, dtype=BF16), shaped(8, 128)],
        right_half, right_other, inv_down, name="factor_down", scratch_shapes=[narrow],
    )
    new_error_down, update_up, update_down = call(
        last_kernel, [shaped(1, ff, rows, dtype=BF16), shaped(rows, ff, dtype=BF16), shaped(ff, rows, dtype=BF16)],
        gd, ed, lhs_up, rhs_up, lhs_down, rhs_down, clip, name="last", flops=product, grid=(STEPS,),
        in_specs=[VMEM] * 7, out_specs=[replica_blocks(ff, rows), row_blocks(rows, ff), row_blocks(ff, rows)],
    )
    return new_error_up, update_up, new_error_down, update_down


def solution(mesh):
    placed = (
        P("dp", None, "tensor"),
        P("dp", None, "tensor"),
        P("dp", "tensor", None),
        P("dp", "tensor", None),
        P("tensor", None),
        P(),
    )
    return jax.shard_map(
        on_device,
        mesh=mesh,
        in_specs=placed,
        out_specs=(
            P("dp", None, "tensor"),
            P(None, "tensor"),
            P("dp", "tensor", None),
            P("tensor", None),
        ),
        check_vma=False,
    )
```

```python
import functools

import jax
import jax.numpy as jnp
from jax import lax
from jax.experimental import pallas as pl
from jax.experimental.pallas import tpu as pltpu
from jax.sharding import PartitionSpec as P

F32 = jnp.float32
BF16 = jnp.bfloat16
HIGHEST = lax.Precision.HIGHEST
CLIP_RMS = 0.1
STEPS = 4
MIB = 1024 * 1024
NT = ((1,), (1,))


def split3(x):
    first = x.astype(BF16)
    rest = x - first.astype(F32)
    second = rest.astype(BF16)
    return first, second, (rest - second.astype(F32)).astype(BF16)


def tree_sum(values):
    values = list(values)
    while len(values) > 1:
        values = [values[i] + values[i + 1] for i in range(0, len(values), 2)]
    return values[0]


def dot(a, b, dims=((1,), (0,)), precision=None):
    return lax.dot_general(a, b, (dims, ((), ())), precision=precision, preferred_element_type=F32)


def fold(x, rows):
    return jnp.concatenate([x[i : i + rows] for i in range(0, x.shape[0], rows)], axis=1)


def unfold(x, rows):
    count = rows // x.shape[0]
    width = x.shape[1] // count
    return jnp.concatenate([x[:, i * width : (i + 1) * width] for i in range(count)], axis=0)


def mine_and_other(j, bit, position):
    mine = lax.bitwise_and(lax.shift_right_logical(lax.axis_index("dp"), bit), 1)
    base = ((j >> position) << (position + 1)) | (j & ((1 << position) - 1))
    return base + mine * (1 << position), base + (1 - mine) * (1 << position)


def split_bit(chunks, bit, position, keep, send):
    for j in range(keep.shape[0]):
        mine, other = mine_and_other(j, bit, position)
        keep[j] = chunks[mine]
        send[j] = chunks[other]


def split_replicas(total, stage, halves):
    n_dp, per, _ = stage.shape
    for c in range(n_dp):
        stage[c] = total[c * per : (c + 1) * per, :]
    start = 0
    for (bit, position), keep, send in halves:
        width = keep.shape[2]
        split_bit(stage.at[:, :, start : start + width], bit, position, keep, send)
        start += width


def join_replicas(halves, stage, total):
    n_dp, per, ff = stage.shape
    start = 0
    for (bit, position), mine, other in halves:
        width = ff // 2
        for j in range(n_dp // 2):
            here, there = mine_and_other(j, bit, position)
            stage[here, :, start : start + width] = mine[j, :, :width]
            stage[there, :, start : start + width] = other[j, :, :width]
        start += width
    for c in range(n_dp):
        total[c * per : (c + 1) * per, :] = stage[c]


def split_shards(total, extra, outs):
    me = lax.axis_index("tensor")
    rows, width = outs[0].shape[0], total.shape[1]
    for j, out in enumerate(outs):
        owner = lax.bitwise_xor(me, j)
        out[:, :width] = total[pl.ds(pl.multiple_of(owner * rows, rows), rows), :]
        if extra is not None:
            out[:, width:] = fold(extra, rows)


def join_shards(pieces, total):
    me = lax.axis_index("tensor")
    rows, width = pieces[0].shape[0], total.shape[1]
    for j, piece in enumerate(pieces):
        owner = lax.bitwise_xor(me, j)
        total[pl.ds(pl.multiple_of(owner * rows, rows), rows), :] = piece[:, :width]


def left_kernel(firsts, gu, eu, qu, gd, ed, qd, *refs):
    *outs, gu_in, eu_in, qu_in, pieces_up, total_up, gd_in, ed_in, qd_in, pieces_down, total_down, stage, q_sems, sems = refs
    step = pl.program_id(0)
    arrays = ((gu, gu_in), (eu, eu_in), (gd, gd_in), (ed, ed_in))

    def copy(i, n):
        src, dst = arrays[n]
        block = dst.shape[0] // STEPS
        rows = pl.ds(pl.multiple_of(i * block, block), block)
        return pltpu.make_async_copy(src.at[0, rows, :], dst.at[rows, :], sems.at[i, n])

    @pl.when(step == 0)
    def _():
        firsts_in = [pltpu.make_async_copy(src, dst, q_sems.at[i]) for i, (src, dst) in enumerate(((qu, qu_in), (qd, qd_in)))]
        for first in firsts_in:
            first.start()
        for i in range(STEPS):
            for n in range(4):
                copy(i, n).start()
        for first in firsts_in:
            first.wait()
        split_rows(qu_in, pieces_up)
        split_rows(qd_in, pieces_down)

    for n in range(4):
        copy(step, n).wait()
    for g, e, pieces, total in ((gu_in, eu_in, pieces_up, total_up), (gd_in, ed_in, pieces_down, total_down)):
        block = g.shape[0] // STEPS
        rows = pl.ds(pl.multiple_of(step * block, 128), block)
        total[:, rows] = add_pieces(dot(pieces[...], g[rows, :], NT) + dot(pieces[...], e[rows, :], NT))

    @pl.when(step == STEPS - 1)
    def _():
        split_shards(total_up, None, outs[:-4])
        split_replicas(total_down, stage, [(firsts[0], *outs[-4:-2]), (firsts[1], *outs[-2:])])


def halve_kernel(bit, position, keep, got, keep_out, send_out, chunks):
    chunks[...] = keep[...] + got[...]
    split_bit(chunks, bit, position, keep_out, send_out)


def halve_with_shards_kernel(bit, position, width, keep, got, *refs):
    *terms, gram, keep_out, send_out, chunks = refs
    half, per, columns = keep.shape
    summed = tree_sum(term[...] for term in terms)
    block = width // half
    for c in range(half):
        chunks[c, :, :columns] = keep[c] + got[c]
        chunks[c, :, columns:] = fold(summed[:, c * block : (c + 1) * block], per)
    split_bit(chunks, bit, position, keep_out, send_out)
    if summed.shape[1] > width:
        gram[...] = unfold(summed[:, width:], gram.shape[0])
    else:
        gram[...] = jnp.zeros_like(gram)


def mean_kernel(n_dp, keep, got, out):
    out[...] = (keep[...] + got[...]) / n_dp


def double_kernel(bit, position, mine, other, out):
    for j in range(mine.shape[0]):
        here, there = mine_and_other(j, bit, position)
        out[here] = mine[j]
        out[there] = other[j]


def shard_rows(mine, other, ff, rows):
    half = mine.shape[0]
    return jnp.concatenate([unfold(mine[c, :, ff:] + other[c, :, ff:], rows) for c in range(half)], axis=1)


def shard_rows_kernel(ff, mine, other, out):
    out[...] = shard_rows(mine, other, ff, out.shape[0])


def split_rows(left, pieces):
    rank = left.shape[0]
    for i, piece in enumerate(split3(left[...])):
        pieces[i * rank : (i + 1) * rank, :] = piece


def add_pieces(t):
    rank = t.shape[0] // 3
    return t[:rank] + (t[rank : 2 * rank] + t[2 * rank :])


def right_down_kernel(lasts, mine_a, other_a, mine_b, other_b, g, e, left, *refs):
    *outs, pieces, total, stage = refs
    join_replicas([(lasts[0], mine_a, other_a), (lasts[1], mine_b, other_b)], stage, left)
    split_rows(left, pieces)
    total[...] = add_pieces(dot(pieces[...], g[0]) + dot(pieces[...], e[0]))
    split_shards(total, dot(left[...], left[...], NT, HIGHEST), outs)


def right_up_kernel(firsts, n_shards, *refs):
    shards, refs = refs[:n_shards], refs[n_shards:]
    g, e, _, left, gram, keep_a, send_a, keep_b, send_b, pieces, total, stage = refs
    join_shards(shards, left)
    split_rows(left, pieces)
    block = total.shape[1] // STEPS
    for i in range(STEPS):
        part = slice(i * block, (i + 1) * block)
        total[:, part] = add_pieces(dot(pieces[...], g[0, :, part]) + dot(pieces[...], e[0, :, part]))
    split_replicas(total, stage, [(firsts[0], keep_a, send_a), (firsts[1], keep_b, send_b)])
    gram[...] = dot(left[...], left[...], NT, HIGHEST)


def inverse_factors(grams):
    rank = grams[0].shape[0]
    count = rank // 8
    panel = 4
    lane = lax.broadcasted_iota(jnp.int32, (8, 2 * rank), 1)
    row = lax.broadcasted_iota(jnp.int32, (8, 2 * rank), 0)
    states, pivots = [], []
    for gram in grams:
        wide = jnp.concatenate([gram, jnp.zeros_like(gram)], axis=1)
        states.append([wide[i : i + 8] + (lane == row + (rank + i)).astype(F32) for i in range(0, rank, 8)])
        pivots.append([])
    for start in range(0, rank, panel):
        at = start // 8
        below = range(at, count)
        spread = [
            [{i: jnp.broadcast_to(blocks[i][:, start + j : start + j + 1], (8, 2 * rank)) for i in below} for j in range(panel)]
            for blocks in states
        ]
        for j in range(panel):
            inner = (start + j) % 8
            for blocks, columns, found in zip(states, spread, pivots):
                pivot = columns[j][at][inner : inner + 1, :]
                found.append(pivot)
                inverse = 1.0 / pivot
                factor = {i: jnp.where(row > inner, columns[j][i], 0.0) if i == at else columns[j][i] for i in below}
                for later in columns[j + 1 :]:
                    head = later[at][inner : inner + 1, :] * inverse
                    for i in below:
                        later[i] = later[i] - factor[i] * head
                scaled = blocks[at][inner : inner + 1, :] * inverse
                for i in below:
                    blocks[i] = blocks[i] - factor[i] * scaled
    results = []
    for blocks, found in zip(states, pivots):
        rows = [block / jnp.sqrt(jnp.concatenate(found[8 * i : 8 * i + 8], axis=0)) for i, block in enumerate(blocks)]
        results.append(jnp.concatenate(rows, axis=0)[:, rank:])
    return results


def basis_kernel(left_up, left_down, gram_up, gram_down, *refs):
    inv_up, inv_down, lhs_up, lhs_down = refs[-4:]
    inverses = inverse_factors([gram_up[...], gram_down[...]])
    rank = left_up.shape[0]
    for inverse, inv, left, lhs in zip(inverses, (inv_up, inv_down), (left_up, left_down), (lhs_up, lhs_down)):
        inv[...] = inverse
        first, second, _ = split3(dot(inverse, left[...], precision=HIGHEST).T)
        lhs[:, :rank] = first
        lhs[:, rank : 2 * rank] = first
        lhs[:, 2 * rank : 3 * rank] = second
        lhs[:, 3 * rank :] = second


def right_factor(inv, total, rhs):
    rank = inv.shape[0]
    right = dot(inv[...], total[...], precision=HIGHEST)
    first, second, _ = split3(right)
    rhs[:rank, :] = first
    rhs[rank : 2 * rank, :] = second
    rhs[2 * rank : 3 * rank, :] = first
    rhs[3 * rank :, :] = second
    return jnp.sum(right * right)


def factor_up_kernel(lasts, mine_a, other_a, mine_b, other_b, inv, rhs, shard, total, stage):
    join_replicas([(lasts[0], mine_a, other_a), (lasts[1], mine_b, other_b)], stage, total)
    square = right_factor(inv, total, rhs)
    rows, ff = shard.shape[0], total.shape[1]
    width = shard.shape[1] - 128
    shard[:, :width] = shard_rows(mine_a, other_a, ff // 2, rows)
    shard[:, width:] = jnp.full((rows, 128), square, F32)


def factor_down_kernel(limit, n_shards, *refs):
    shards, refs = refs[:n_shards], refs[n_shards:]
    inv, _, rhs, clip, total = refs
    join_shards(shards, total)
    square = right_factor(inv, total, rhs)
    width = total.shape[1]
    norm_sq = square + tree_sum(shard[:8, width:] for shard in shards)
    clip[...] = jnp.minimum(jnp.float32(1.0), limit / jnp.sqrt(norm_sq))


def rows_of(block):
    return pl.ds(pl.multiple_of(pl.program_id(0) * block, block), block)


def error_up_kernel(g, e, lhs, rhs, error, made):
    made[...] = jnp.zeros_like(made)
    part = rows_of(error.shape[1])
    rebuilt = dot(lhs[part, :], rhs[...])
    error[0] = (g[0, part, :].astype(F32) + e[0, part, :].astype(F32) - rebuilt).astype(BF16)


def last_kernel(g, e, lhs_up, rhs_up, lhs_down, rhs_down, clip, error, update_up, update_down):
    factor = clip[:1, :1]
    part = rows_of(update_down.shape[0])
    rebuilt = dot(lhs_down[part, :], rhs_down[...])
    update_down[...] = (factor * rebuilt).astype(BF16)
    error[0] = (g[0, part, :].astype(F32) + e[0, part, :].astype(F32) - rebuilt).astype(BF16)
    part = rows_of(update_up.shape[0])
    update_up[...] = (factor * dot(lhs_up[part, :], rhs_up[...])).astype(BF16)


def shaped(*dims, dtype=F32):
    return jax.ShapeDtypeStruct(dims, dtype)


def whole(shape):
    return pl.BlockSpec(shape, lambda *_: (0,) * len(shape))


def row_blocks(rows, columns):
    return pl.BlockSpec((rows // STEPS, columns), lambda i: (i, 0))


def replica_blocks(rows, columns):
    return pl.BlockSpec((1, rows // STEPS, columns), lambda i: (0, i, 0))


VMEM = pl.BlockSpec(memory_space=pltpu.VMEM)
ANY = pl.BlockSpec(memory_space=pl.ANY)


def call(kernel, out_shape, *args, flops=0, limit=12, name=None, **more):
    arrays = list(args) + jax.tree.leaves(out_shape)
    size = sum(a.size * a.dtype.itemsize for a in arrays)
    cost = pl.CostEstimate(flops=flops, bytes_accessed=size, transcendentals=0)
    params = pltpu.CompilerParams(vmem_limit_bytes=limit * MIB)
    return pl.pallas_call(kernel, out_shape=out_shape, compiler_params=params, cost_estimate=cost, name=name, **more)(*args)


def swap(x, axis, distance):
    pairs = [(i, i ^ distance) for i in range(lax.axis_size(axis))]
    return lax.ppermute(x, axis, pairs)


def exchange_orders(n_dp):
    bits = n_dp.bit_length() - 1
    return [(b, 0) for b in range(bits)], [(b, 1) for b in range(1, bits)] + [(0, 0)]


def scatter_mean(order, keep, send, shards=(), width=0, rank=0):
    n_dp = lax.axis_size("dp")
    gram = None
    for i, (bit, _) in enumerate(order):
        got = swap(send, "dp", 1 << bit)
        if i == len(order) - 1:
            return call(functools.partial(mean_kernel, n_dp), shaped(*keep.shape), keep, got, name="replica_mean"), gram
        count, per, columns = keep.shape
        if shards and i == 0:
            columns += shards[0].shape[0] // per * (width // count)
            out = shaped(count // 2, per, columns)
            gram, keep, send = call(
                functools.partial(halve_with_shards_kernel, *order[i + 1], width), [shaped(rank, rank), out, out], keep, got, *shards,
                name="halve_with_shards", scratch_shapes=[pltpu.VMEM((count, per, columns), F32)],
            )
        else:
            out = shaped(count // 2, per, columns)
            keep, send = call(
                functools.partial(halve_kernel, *order[i + 1]), [out, out], keep, got, name="halve",
                scratch_shapes=[pltpu.VMEM(keep.shape, F32)],
            )


def gather_chunks(order, mine):
    for bit, position in order[:0:-1]:
        other = swap(mine, "dp", 1 << bit)
        out = shaped(2 * mine.shape[0], *mine.shape[1:])
        mine = call(functools.partial(double_kernel, bit, position), out, mine, other, name="double")
    return mine, swap(mine, "dp", 1 << order[0][0])


def from_shards(parts):
    n_shards = lax.axis_size("tensor")
    parts = parts if isinstance(parts, (list, tuple)) else [parts] * n_shards
    return [parts[0]] + [swap(parts[j], "tensor", j) for j in range(1, n_shards)]


def on_device(gu, eu, gd, ed, qu, qd):
    qu, qd = qu.T, qd.T
    n_dp, n_shards = lax.axis_size("dp"), lax.axis_size("tensor")
    _, rows, ff = gu.shape
    rank = qu.shape[0]
    half, per, rows_here = n_dp // 2, rank // n_dp, rank // n_shards
    order_a, order_b = exchange_orders(n_dp)
    firsts = order_a[0], order_b[0]
    halves = [shaped(half, per, ff // 2)] * 4
    stage = pltpu.VMEM((n_dp, per, ff), F32)
    wide = pltpu.VMEM((rank, ff), F32)
    narrow = pltpu.VMEM((rank, rows), F32)
    product = 4 * rows * ff * 4 * rank

    buffers = [
        [pltpu.VMEM(g.shape[1:], BF16)] * 2 + [pltpu.VMEM(q.shape, F32), pltpu.VMEM((3 * rank, q.shape[1]), BF16), total]
        for g, q, total in ((gu, qu, narrow), (gd, qd, wide))
    ]
    outs = [shaped(rows_here, rows)] * n_shards + halves
    *parts, keep_a, send_a, keep_b, send_b = call(
        functools.partial(left_kernel, firsts), outs, gu, eu, qu, gd, ed, qd, name="left", flops=2 * product, limit=61,
        grid=(STEPS,), in_specs=[pl.BlockSpec(memory_space=pltpu.HBM)] * 6, out_specs=[whole(out.shape) for out in outs],
        scratch_shapes=buffers[0] + buffers[1] + [stage, pltpu.SemaphoreType.DMA((2,)), pltpu.SemaphoreType.DMA((STEPS, 4))],
    )
    mean_a, _ = scatter_mean(order_a, keep_a, send_a, from_shards(parts), rows, rank)
    mean_b, _ = scatter_mean(order_b, keep_b, send_b)
    mine_a, other_a = gather_chunks(order_a, mean_a)
    mine_b, other_b = gather_chunks(order_b, mean_b)

    shard = call(functools.partial(shard_rows_kernel, ff // 2), shaped(rows_here, rows), mine_a, other_a, name="shard_rows")
    left_rows = from_shards(shard)
    out = shaped(rows_here, rows + rank * n_shards)
    left_down, *parts = call(
        functools.partial(right_down_kernel, firsts), [shaped(rank, ff)] + [out] * n_shards, mine_a, other_a, mine_b, other_b, gd, ed,
        name="right_down", flops=product, scratch_shapes=[pltpu.VMEM((3 * rank, ff), BF16), narrow, stage],
    )
    left_up, gram_up, keep_a, send_a, keep_b, send_b = call(
        functools.partial(right_up_kernel, firsts, n_shards), [shaped(rank, rows), shaped(rank, rank)] + halves,
        *left_rows, gu, eu, left_down, name="right_up", flops=product, in_specs=[VMEM] * (n_shards + 2) + [ANY],
        scratch_shapes=[pltpu.VMEM((3 * rank, rows), BF16), wide, stage],
    )
    mean_a, gram_down = scatter_mean(order_a, keep_a, send_a, from_shards(parts), rows, rank)
    mean_b, _ = scatter_mean(order_b, keep_b, send_b)
    mine_a, other_a = gather_chunks(order_a, mean_a)
    mine_b, other_b = gather_chunks(order_b, mean_b)
    inv_up, inv_down, lhs_up, lhs_down = call(
        basis_kernel,
        [shaped(rank, rank)] * 2 + [shaped(rows, 4 * rank, dtype=BF16), shaped(ff, 4 * rank, dtype=BF16)],
        left_up, left_down, gram_up, gram_down, gu, eu, gd, ed, mine_a, name="basis", in_specs=[VMEM] * 8 + [ANY],
    )
    rhs_up, shard = call(
        functools.partial(factor_up_kernel, firsts), [shaped(4 * rank, ff, dtype=BF16), shaped(rows_here, rows + 128)],
        mine_a, other_a, mine_b, other_b, inv_up, name="factor_up", scratch_shapes=[wide, stage],
    )
    right_rows = from_shards(shard)
    new_error_up, made = call(
        error_up_kernel, [shaped(1, rows, ff, dtype=BF16), shaped(8, 128)], gu, eu, lhs_up, rhs_up, name="error_up", flops=product // 2,
        grid=(STEPS,), in_specs=[VMEM] * 4, out_specs=[replica_blocks(rows, ff), whole((8, 128))],
    )
    limit = CLIP_RMS * (2.0 * rows * ff * n_shards) ** 0.5
    rhs_down, clip = call(
        functools.partial(factor_down_kernel, limit, n_shards), [shaped(4 * rank, rows, dtype=BF16), shaped(8, 128)],
        *right_rows, inv_down, made, name="factor_down", in_specs=[VMEM] * (n_shards + 1) + [ANY], scratch_shapes=[narrow],
    )
    new_error_down, update_up, update_down = call(
        last_kernel, [shaped(1, ff, rows, dtype=BF16), shaped(rows, ff, dtype=BF16), shaped(ff, rows, dtype=BF16)],
        gd, ed, lhs_up, rhs_up, lhs_down, rhs_down, clip, name="last", flops=product, grid=(STEPS,),
        in_specs=[VMEM] * 7, out_specs=[replica_blocks(ff, rows), row_blocks(rows, ff), row_blocks(ff, rows)],
    )
    return new_error_up, update_up, new_error_down, update_down


def solution(mesh):
    placed = (
        P("dp", None, "tensor"),
        P("dp", None, "tensor"),
        P("dp", "tensor", None),
        P("dp", "tensor", None),
        P("tensor", None),
        P(),
    )
    return jax.shard_map(
        on_device,
        mesh=mesh,
        in_specs=placed,
        out_specs=(
            P("dp", None, "tensor"),
            P(None, "tensor"),
            P("dp", "tensor", None),
            P("tensor", None),
        ),
        check_vma=False,
    )
```

```python
import functools

import jax
import jax.numpy as jnp
from jax import lax
from jax.experimental import pallas as pl
from jax.experimental.pallas import tpu as pltpu
from jax.sharding import PartitionSpec as P

F32 = jnp.float32
BF16 = jnp.bfloat16
HIGHEST = lax.Precision.HIGHEST
CLIP_RMS = 0.1
STEPS = 4
LEFT_STEPS = 2
MIB = 1024 * 1024
NT = ((1,), (1,))


def split3(x):
    first = x.astype(BF16)
    rest = x - first.astype(F32)
    second = rest.astype(BF16)
    return first, second, (rest - second.astype(F32)).astype(BF16)


def tree_sum(values):
    values = list(values)
    while len(values) > 1:
        values = [values[i] + values[i + 1] for i in range(0, len(values), 2)]
    return values[0]


def dot(a, b, dims=((1,), (0,)), precision=None):
    return lax.dot_general(a, b, (dims, ((), ())), precision=precision, preferred_element_type=F32)


def fold(x, rows):
    return jnp.concatenate([x[i : i + rows] for i in range(0, x.shape[0], rows)], axis=1)


def unfold(x, rows):
    count = rows // x.shape[0]
    width = x.shape[1] // count
    return jnp.concatenate([x[:, i * width : (i + 1) * width] for i in range(count)], axis=0)


def split_z(total, stage, outs):
    half, rows, _ = stage.shape
    z = lax.shift_right_logical(lax.axis_index("dp"), 1)
    for c in range(half):
        stage[c] = total[c * rows : (c + 1) * rows, :]
    for j, out in enumerate(outs):
        out[...] = stage[lax.bitwise_xor(z, j)]


def join_z(pieces, stage, total):
    half, rows, _ = stage.shape
    z = lax.shift_right_logical(lax.axis_index("dp"), 1)
    for j, piece in enumerate(pieces):
        stage[lax.bitwise_xor(z, j)] = piece[...]
    for c in range(half):
        total[c * rows : (c + 1) * rows, :] = stage[c]


def split_shards(total, extra, outs):
    me = lax.axis_index("tensor")
    rows, width = outs[0].shape[0], total.shape[1]
    for j, out in enumerate(outs):
        owner = lax.bitwise_xor(me, j)
        out[:, :width] = total[pl.ds(pl.multiple_of(owner * rows, rows), rows), :]
        if extra is not None:
            out[:, width:] = fold(extra, rows)


def join_shards(pieces, total):
    me = lax.axis_index("tensor")
    rows = pieces[0].shape[0]
    for j, piece in enumerate(pieces):
        owner = lax.bitwise_xor(me, j)
        total[pl.ds(pl.multiple_of(owner * rows, rows), rows), :] = piece[...]


def left_kernel(n_shards, gu, eu, qu, gd, ed, qd, *refs):
    *outs, gu_in, eu_in, qu_in, pieces_up, total_up, gd_in, ed_in, qd_in, pieces_down, total_down, stage, q_sems, sems = refs
    up, down = (qu_in, pieces_up, total_up), (qd_in, pieces_down, total_down)
    firsts = [pltpu.make_async_copy(src, dst, q_sems.at[i]) for i, (src, dst) in enumerate(((qu, qu_in), (qd, qd_in)))]
    for first in firsts:
        first.start()
    stages = []
    for g, e, g_in, e_in, part in ((gu, eu, gu_in, eu_in, up), (gd, ed, gd_in, ed_in, down)):
        block = g_in.shape[0] // LEFT_STEPS
        for i in range(LEFT_STEPS):
            rows = pl.ds(i * block, block)
            n = len(stages)
            copies = [pltpu.make_async_copy(src.at[0, rows, :], dst.at[rows, :], sems.at[n, k]) for k, (src, dst) in enumerate(((g, g_in), (e, e_in)))]
            for copy in copies:
                copy.start()
            stages.append((copies, g_in, e_in, slice(i * block, (i + 1) * block), part))
    for first, (q, pieces, _) in zip(firsts, (up, down)):
        first.wait()
        split_rows(q, pieces)
    for copies, g, e, rows, (_, pieces, total) in stages:
        for copy in copies:
            copy.wait()
        total[:, rows] = add_pieces(dot(pieces[...], g[rows, :], NT) + dot(pieces[...], e[rows, :], NT))
    split_shards(total_up, None, outs[:n_shards])
    split_z(total_down, stage, outs[n_shards:])


def sum_shards_kernel(*refs):
    *terms, out, gram = refs
    width = out.shape[1]
    total = tree_sum(term[...] for term in terms)
    out[...] = total[:, :width]
    if total.shape[1] > width:
        gram[...] = unfold(total[:, width:], gram.shape[0])
    else:
        gram[...] = jnp.zeros_like(gram)


def sum_z_kernel(half, *refs):
    chunks, shards, out = refs[:half], refs[half:-1], refs[-1]
    rows, width = chunks[0].shape
    out[:, :width] = tree_sum(chunk[...] for chunk in chunks)
    out[:, width:] = fold(tree_sum(shard[...] for shard in shards), rows)


def mean_kernel(n_dp, mine, other, chunk, shard):
    width = chunk.shape[1]
    total = (mine[...] + other[...]) / n_dp
    chunk[...] = total[:, :width]
    shard[...] = unfold(total[:, width:], shard.shape[0])


def split_rows(left, pieces):
    rank = left.shape[0]
    for i, piece in enumerate(split3(left[...])):
        pieces[i * rank : (i + 1) * rank, :] = piece


def add_pieces(t):
    rank = t.shape[0] // 3
    return t[:rank] + (t[rank : 2 * rank] + t[2 * rank :])


def right_down_kernel(half, *refs):
    chunks, refs = refs[:half], refs[half:]
    g, e, left, *outs, pieces, total, stage = refs
    join_z(chunks, stage, left)
    split_rows(left, pieces)
    total[...] = add_pieces(dot(pieces[...], g[0]) + dot(pieces[...], e[0]))
    split_shards(total, dot(left[...], left[...], NT, HIGHEST), outs)


def right_up_kernel(n_shards, *refs):
    shards, refs = refs[:n_shards], refs[n_shards:]
    g, e, left, gram, *outs, pieces, total, stage = refs
    join_shards(shards, left)
    split_rows(left, pieces)
    block = total.shape[1] // STEPS
    for i in range(STEPS):
        part = slice(i * block, (i + 1) * block)
        total[:, part] = add_pieces(dot(pieces[...], g[0, :, part]) + dot(pieces[...], e[0, :, part]))
    split_z(total, stage, outs)
    gram[...] = dot(left[...], left[...], NT, HIGHEST)


def inverse_factors(grams):
    rank = grams[0].shape[0]
    count = rank // 8
    panel = 4
    lane = lax.broadcasted_iota(jnp.int32, (8, 2 * rank), 1)
    row = lax.broadcasted_iota(jnp.int32, (8, 2 * rank), 0)
    states, pivots = [], []
    for gram in grams:
        wide = jnp.concatenate([gram, jnp.zeros_like(gram)], axis=1)
        states.append([wide[i : i + 8] + (lane == row + (rank + i)).astype(F32) for i in range(0, rank, 8)])
        pivots.append([])
    for start in range(0, rank, panel):
        at = start // 8
        below = range(at, count)
        spread = [
            [{i: jnp.broadcast_to(blocks[i][:, start + j : start + j + 1], (8, 2 * rank)) for i in below} for j in range(panel)]
            for blocks in states
        ]
        for j in range(panel):
            inner = (start + j) % 8
            for blocks, columns, found in zip(states, spread, pivots):
                pivot = columns[j][at][inner : inner + 1, :]
                found.append(pivot)
                inverse = 1.0 / pivot
                factor = {i: jnp.where(row > inner, columns[j][i], 0.0) if i == at else columns[j][i] for i in below}
                for later in columns[j + 1 :]:
                    head = later[at][inner : inner + 1, :] * inverse
                    for i in below:
                        later[i] = later[i] - factor[i] * head
                scaled = blocks[at][inner : inner + 1, :] * inverse
                for i in below:
                    blocks[i] = blocks[i] - factor[i] * scaled
    results = []
    for blocks, found in zip(states, pivots):
        rows = [block / jnp.sqrt(jnp.concatenate(found[8 * i : 8 * i + 8], axis=0)) for i, block in enumerate(blocks)]
        results.append(jnp.concatenate(rows, axis=0)[:, rank:])
    return results


def basis_kernel(left_up, left_down, gram_up, gram_down, *refs):
    inv_up, inv_down, lhs_up, lhs_down = refs[-4:]
    inverses = inverse_factors([gram_up[...], gram_down[...]])
    rank = left_up.shape[0]
    for inverse, inv, left, lhs in zip(inverses, (inv_up, inv_down), (left_up, left_down), (lhs_up, lhs_down)):
        inv[...] = inverse
        first, second, _ = split3(dot(inverse, left[...], precision=HIGHEST).T)
        lhs[:, :rank] = first
        lhs[:, rank : 2 * rank] = first
        lhs[:, 2 * rank : 3 * rank] = second
        lhs[:, 3 * rank :] = second


def right_factor(inv, total, rhs):
    rank = inv.shape[0]
    right = dot(inv[...], total[...], precision=HIGHEST)
    first, second, _ = split3(right)
    rhs[:rank, :] = first
    rhs[rank : 2 * rank, :] = second
    rhs[2 * rank : 3 * rank, :] = first
    rhs[3 * rank :, :] = second
    return jnp.sum(right * right)


def factor_up_kernel(half, *refs):
    chunks, (inv, rhs, square, total, stage) = refs[:half], refs[half:]
    join_z(chunks, stage, total)
    square[...] = jnp.full(square.shape, right_factor(inv, total, rhs), F32)


def factor_down_kernel(n_shards, *refs):
    shards, (inv, rhs, square, total) = refs[:n_shards], refs[n_shards:]
    join_shards(shards, total)
    square[...] = jnp.full(square.shape, right_factor(inv, total, rhs), F32)


def rows_of(block):
    return pl.ds(pl.multiple_of(pl.program_id(0) * block, block), block)


def error_kernel(g, e, lhs, rhs, error, made):
    made[...] = jnp.zeros_like(made)
    part = rows_of(error.shape[1])
    rebuilt = dot(lhs[part, :], rhs[...])
    error[0] = (g[0, part, :].astype(F32) + e[0, part, :].astype(F32) - rebuilt).astype(BF16)


def update_kernel(limit, lhs_up, rhs_up, lhs_down, rhs_down, square_down, *refs):
    *squares_up, update_up, update_down = refs
    norm_sq = tree_sum(square[...] for square in squares_up) + square_down[...]
    factor = jnp.minimum(jnp.float32(1.0), limit / jnp.sqrt(norm_sq))[:1, :1]
    for lhs, rhs, update in ((lhs_up, rhs_up, update_up), (lhs_down, rhs_down, update_down)):
        update[...] = (factor * dot(lhs[rows_of(update.shape[0]), :], rhs[...])).astype(BF16)


def shaped(*dims, dtype=F32):
    return jax.ShapeDtypeStruct(dims, dtype)


def whole(shape):
    return pl.BlockSpec(shape, lambda *_: (0,) * len(shape))


def row_blocks(rows, columns):
    return pl.BlockSpec((rows // STEPS, columns), lambda i: (i, 0))


def replica_blocks(rows, columns):
    return pl.BlockSpec((1, rows // STEPS, columns), lambda i: (0, i, 0))


VMEM = pl.BlockSpec(memory_space=pltpu.VMEM)
ANY = pl.BlockSpec(memory_space=pl.ANY)


def call(kernel, out_shape, *args, after=(), in_specs=None, flops=0, limit=12, name=None, **more):
    arrays = list(args) + jax.tree.leaves(out_shape)
    size = sum(a.size * a.dtype.itemsize for a in arrays)
    skip = len(after)
    return pl.pallas_call(
        lambda *refs: kernel(*refs[skip:]), out_shape=out_shape, in_specs=[ANY] * skip + (in_specs or [VMEM] * len(args)),
        compiler_params=pltpu.CompilerParams(vmem_limit_bytes=limit * MIB),
        cost_estimate=pl.CostEstimate(flops=flops, bytes_accessed=size, transcendentals=0), name=name, **more,
    )(*after, *args)


def swap(x, axis, distance):
    pairs = [(i, i ^ distance) for i in range(lax.axis_size(axis))]
    return lax.ppermute(x, axis, pairs)


def from_z(parts):
    return [parts[0]] + [swap(part, "dp", 2 * j) for j, part in enumerate(parts) if j]


def from_shards(parts):
    return [parts[0]] + [swap(part, "tensor", j) for j, part in enumerate(parts) if j]


def reduce_both(chunks, shards, rows, rank, after):
    n_dp, half = lax.axis_size("dp"), len(chunks)
    chunks = from_z(chunks)
    rows_here = shards[0].shape[0]
    shard, gram = call(sum_shards_kernel, [shaped(rows_here, rows), shaped(rank, rank)], *from_shards(shards), after=after, name="shard_sum")
    per, width = chunks[0].shape
    buffer = shaped(per, width + rows_here * rows // per)
    mine = call(functools.partial(sum_z_kernel, half), buffer, *chunks, *from_z([shard] * half), name="z_sum")
    chunk, shard = call(
        functools.partial(mean_kernel, n_dp), [shaped(per, width), shaped(rows_here, rows)], mine, swap(mine, "dp", 1), name="mean"
    )
    return chunk, shard, gram


def on_device(gu, eu, gd, ed, qu, qd):
    qu, qd = qu.T, qd.T
    n_dp, n_shards = lax.axis_size("dp"), lax.axis_size("tensor")
    _, rows, ff = gu.shape
    rank = qu.shape[0]
    half, rows_here = n_dp // 2, rank // n_shards
    chunks = [shaped(rank // half, ff)] * half
    stage = pltpu.VMEM((half, rank // half, ff), F32)
    wide = pltpu.VMEM((rank, ff), F32)
    narrow = pltpu.VMEM((rank, rows), F32)
    product = 4 * rows * ff * 4 * rank

    buffers = [
        [pltpu.VMEM(g.shape[1:], BF16)] * 2 + [pltpu.VMEM(q.shape, F32), pltpu.VMEM((3 * rank, q.shape[1]), BF16), total]
        for g, q, total in ((gu, qu, narrow), (gd, qd, wide))
    ]
    outs = call(
        functools.partial(left_kernel, n_shards), [shaped(rows_here, rows)] * n_shards + chunks, gu, eu, qu, gd, ed, qd, name="left",
        flops=2 * product, limit=61, in_specs=[pl.BlockSpec(memory_space=pltpu.HBM)] * 6,
        scratch_shapes=buffers[0] + buffers[1] + [stage, pltpu.SemaphoreType.DMA((2,)), pltpu.SemaphoreType.DMA((2 * LEFT_STEPS, 2))],
    )
    chunk, shard, _ = reduce_both(outs[n_shards:], outs[:n_shards], rows, rank, ())
    left_chunks, left_rows = from_z([chunk] * half), from_shards([shard] * n_shards)
    left_up, gram_up, *terms = call(
        functools.partial(right_up_kernel, n_shards), [shaped(rank, rows), shaped(rank, rank)] + chunks, *left_rows, gu, eu,
        name="right_up", flops=product, scratch_shapes=[pltpu.VMEM((3 * rank, rows), BF16), wide, stage],
    )
    left_down, *shards = call(
        functools.partial(right_down_kernel, half), [shaped(rank, ff)] + [shaped(rows_here, rows + rank * n_shards)] * n_shards,
        *left_chunks, gd, ed, after=(left_up,), name="right_down", flops=product,
        scratch_shapes=[pltpu.VMEM((3 * rank, ff), BF16), narrow, stage],
    )
    chunk, shard, gram_down = reduce_both(terms, shards, rows, rank, ())
    right_chunks, right_rows = from_z([chunk] * half), from_shards([shard] * n_shards)
    inv_up, inv_down, lhs_up, lhs_down = call(
        basis_kernel,
        [shaped(rank, rank)] * 2 + [shaped(rows, 4 * rank, dtype=BF16), shaped(ff, 4 * rank, dtype=BF16)],
        left_up, left_down, gram_up, gram_down, gu, eu, gd, ed, after=(chunk,), name="basis",
    )
    rhs_down, square_down = call(
        functools.partial(factor_down_kernel, n_shards), [shaped(4 * rank, rows, dtype=BF16), shaped(8, 128)],
        *right_rows, inv_down, name="factor_down", scratch_shapes=[narrow],
    )

    def new_error(g, e, lhs, rhs, name):
        outs = [shaped(*g.shape, dtype=BF16), shaped(8, 128)]
        specs = [replica_blocks(*g.shape[1:]), whole((8, 128))]
        return call(error_kernel, outs, g, e, lhs, rhs, name=name, flops=product // 2, grid=(STEPS,), out_specs=specs)

    new_error_down, made_down = new_error(gd, ed, lhs_down, rhs_down, "error_down")
    rhs_up, square_up = call(
        functools.partial(factor_up_kernel, half), [shaped(4 * rank, ff, dtype=BF16), shaped(8, 128)], *right_chunks, inv_up,
        after=(made_down,), name="factor_up", scratch_shapes=[wide, stage],
    )
    squares_up = from_shards([square_up] * n_shards)
    new_error_up, made_up = new_error(gu, eu, lhs_up, rhs_up, "error_up")
    limit = CLIP_RMS * (2.0 * rows * ff * n_shards) ** 0.5
    update_up, update_down = call(
        functools.partial(update_kernel, limit), [shaped(rows, ff, dtype=BF16), shaped(ff, rows, dtype=BF16)],
        lhs_up, rhs_up, lhs_down, rhs_down, square_down, *squares_up, after=(made_up,),
        name="update", flops=product, grid=(STEPS,), out_specs=[row_blocks(rows, ff), row_blocks(ff, rows)],
    )
    return new_error_up, update_up, new_error_down, update_down


def solution(mesh):
    placed = (
        P("dp", None, "tensor"),
        P("dp", None, "tensor"),
        P("dp", "tensor", None),
        P("dp", "tensor", None),
        P("tensor", None),
        P(),
    )
    return jax.shard_map(
        on_device,
        mesh=mesh,
        in_specs=placed,
        out_specs=(
            P("dp", None, "tensor"),
            P(None, "tensor"),
            P("dp", "tensor", None),
            P("tensor", None),
        ),
        check_vma=False,
    )
```

```python
import functools

import jax
import jax.numpy as jnp
from jax import lax
from jax.experimental import pallas as pl
from jax.experimental.pallas import tpu as pltpu
from jax.sharding import PartitionSpec as P

F32 = jnp.float32
BF16 = jnp.bfloat16
HIGHEST = lax.Precision.HIGHEST
CLIP_RMS = 0.1
STEPS = 4
LEFT_STEPS = 2
MIB = 1024 * 1024
NT = ((1,), (1,))


def split3(x):
    first = x.astype(BF16)
    rest = x - first.astype(F32)
    second = rest.astype(BF16)
    return first, second, (rest - second.astype(F32)).astype(BF16)


def tree_sum(values):
    values = list(values)
    while len(values) > 1:
        values = [values[i] + values[i + 1] for i in range(0, len(values), 2)]
    return values[0]


def dot(a, b, dims=((1,), (0,)), precision=None):
    return lax.dot_general(a, b, (dims, ((), ())), precision=precision, preferred_element_type=F32)


def fold(x, rows):
    return jnp.concatenate([x[i : i + rows] for i in range(0, x.shape[0], rows)], axis=1)


def unfold(x, rows):
    count = rows // x.shape[0]
    width = x.shape[1] // count
    return jnp.concatenate([x[:, i * width : (i + 1) * width] for i in range(count)], axis=0)


def place(axis):
    index = lax.axis_index(axis)
    return lax.bitwise_and(index, 1), lax.shift_right_logical(index, 1)


def split_replicas(total, stage, keep, send):
    parity, _ = place("dp")
    half, per, _ = keep.shape
    for c in range(2 * half):
        stage[c] = total[c * per : (c + 1) * per, :]
    for c in range(half):
        keep[c] = stage[2 * c + parity]
        send[c] = stage[2 * c + 1 - parity]


def join_replicas(mine, other, stage, total):
    parity, _ = place("dp")
    half, per, _ = mine.shape
    width = total.shape[1]
    for c in range(half):
        stage[2 * c + parity] = mine[c, :, :width]
        stage[2 * c + 1 - parity] = other[c, :, :width]
    for c in range(2 * half):
        total[c * per : (c + 1) * per, :] = stage[c]


def split_shards(total, extra, outs):
    me = lax.axis_index("tensor")
    rows, width = outs[0].shape[0], total.shape[1]
    for j, out in enumerate(outs):
        owner = lax.bitwise_xor(me, j)
        out[:, :width] = total[pl.ds(pl.multiple_of(owner * rows, rows), rows), :]
        if extra is not None:
            out[:, width:] = fold(extra, rows)


def join_shards(pieces, total):
    me = lax.axis_index("tensor")
    rows, width = pieces[0].shape[0], total.shape[1]
    for j, piece in enumerate(pieces):
        owner = lax.bitwise_xor(me, j)
        total[pl.ds(pl.multiple_of(owner * rows, rows), rows), :] = piece[:, :width]


def left_kernel(n_shards, gu, eu, qu, gd, ed, qd, *refs):
    *outs, gu_in, eu_in, qu_in, pieces_up, total_up, gd_in, ed_in, qd_in, pieces_down, total_down, stage, q_sems, sems = refs
    up, down = (qu_in, pieces_up, total_up), (qd_in, pieces_down, total_down)
    firsts = [pltpu.make_async_copy(src, dst, q_sems.at[i]) for i, (src, dst) in enumerate(((qu, qu_in), (qd, qd_in)))]
    for first in firsts:
        first.start()
    stages = []
    for g, e, g_in, e_in, part in ((gu, eu, gu_in, eu_in, up), (gd, ed, gd_in, ed_in, down)):
        block = g_in.shape[0] // LEFT_STEPS
        for i in range(LEFT_STEPS):
            rows = pl.ds(i * block, block)
            n = len(stages)
            copies = [pltpu.make_async_copy(src.at[0, rows, :], dst.at[rows, :], sems.at[n, k]) for k, (src, dst) in enumerate(((g, g_in), (e, e_in)))]
            for copy in copies:
                copy.start()
            stages.append((copies, g_in, e_in, slice(i * block, (i + 1) * block), part))
    for first, (q, pieces, _) in zip(firsts, (up, down)):
        first.wait()
        rank = q.shape[0]
        for i, piece in enumerate(split3(q[...].T)):
            pieces[:, i * rank : (i + 1) * rank] = piece
        pieces[:, 3 * rank :] = jnp.zeros((q.shape[1], rank), BF16)
    for copies, g, e, rows, (q, pieces, total) in stages:
        rank = q.shape[0]
        for copy in copies:
            copy.wait()
        t = dot(g[rows, :], pieces[...]) + dot(e[rows, :], pieces[...])
        t = (t[:, : 2 * rank] + t[:, 2 * rank :]).T
        total[:, rows] = t[:rank] + t[rank:]
    split_shards(total_up, None, outs[:n_shards])
    split_replicas(total_down, stage, *outs[n_shards:])


def sum_shards_kernel(n_shards, *refs):
    terms, (out, gram) = refs[:n_shards], refs[n_shards:]
    total = tree_sum(term[...] for term in terms)
    out[...] = total[:, : out.shape[1]]
    gram[...] = unfold(total[:, out.shape[1] :], gram.shape[0])


def first_shards_kernel(n_shards, own, kept, *refs):
    *others, out, copy, own_in, sems = refs
    copies = [pltpu.make_async_copy(own, own_in, sems.at[0]), pltpu.make_async_copy(kept, copy, sems.at[1])]
    for each in copies:
        each.start()
    for each in copies:
        each.wait()
    out[...] = tree_sum([own_in[...]] + [term[...] for term in others])


def split_z_kernel(keep, got, shard, *refs):
    *outs, stage = refs
    _, z = place("dp")
    half, per, ff = keep.shape
    block = shard.shape[1] // half
    for c in range(half):
        stage[c, :, :ff] = keep[c] + got[c]
        stage[c, :, ff:] = fold(shard[:, c * block : (c + 1) * block], per)
    for j, out in zip([0, *range(half - 1, 0, -1)], outs):
        out[...] = stage[lax.bitwise_xor(z, j)]


def mean_kernel(n_dp, *refs):
    refs[-1][...] = tree_sum(ref[...] for ref in refs[:-1]) / n_dp


def stack_kernel(*refs):
    _, z = place("dp")
    for j, ref in enumerate(refs[:-1]):
        refs[-1][lax.bitwise_xor(z, j)] = ref[...]


def shard_rows(mine, other, ff, rows):
    half = mine.shape[0]
    return jnp.concatenate([unfold(mine[c, :, ff:] + other[c, :, ff:], rows) for c in range(half)], axis=1)


def shard_rows_kernel(ff, mine, other, out):
    out[...] = shard_rows(mine, other, ff, out.shape[0])


def split_rows(left, pieces):
    rank = left.shape[0]
    for i, piece in enumerate(split3(left[...])):
        pieces[i * rank : (i + 1) * rank, :] = piece


def add_pieces(t):
    rank = t.shape[0] // 3
    return t[:rank] + (t[rank : 2 * rank] + t[2 * rank :])


def right_down_kernel(mine, other, g, e, left, *refs):
    *outs, pieces, total, stage = refs
    join_replicas(mine, other, stage, left)
    split_rows(left, pieces)
    total[...] = add_pieces(dot(pieces[...], g[0]) + dot(pieces[...], e[0]))
    split_shards(total, dot(left[...], left[...], NT, HIGHEST), outs)


def right_up_kernel(n_shards, *refs):
    shards, refs = refs[:n_shards], refs[n_shards:]
    g, e, _, left, gram, keep, send, pieces, total, stage = refs
    join_shards(shards, left)
    split_rows(left, pieces)
    block = total.shape[1] // STEPS
    for i in range(STEPS):
        part = slice(i * block, (i + 1) * block)
        total[:, part] = add_pieces(dot(pieces[...], g[0, :, part]) + dot(pieces[...], e[0, :, part]))
    split_replicas(total, stage, keep, send)
    gram[...] = dot(left[...], left[...], NT, HIGHEST)


def inverse_factors(grams):
    rank = grams[0].shape[0]
    count = rank // 8
    panel = 4
    lane = lax.broadcasted_iota(jnp.int32, (8, 2 * rank), 1)
    row = lax.broadcasted_iota(jnp.int32, (8, 2 * rank), 0)
    states, pivots = [], []
    for gram in grams:
        wide = jnp.concatenate([gram, jnp.zeros_like(gram)], axis=1)
        states.append([wide[i : i + 8] + (lane == row + (rank + i)).astype(F32) for i in range(0, rank, 8)])
        pivots.append([])
    for start in range(0, rank, panel):
        at = start // 8
        below = range(at, count)
        spread = [
            [{i: jnp.broadcast_to(blocks[i][:, start + j : start + j + 1], (8, 2 * rank)) for i in below} for j in range(panel)]
            for blocks in states
        ]
        for j in range(panel):
            inner = (start + j) % 8
            for blocks, columns, found in zip(states, spread, pivots):
                pivot = columns[j][at][inner : inner + 1, :]
                found.append(pivot)
                inverse = 1.0 / pivot
                factor = {i: jnp.where(row > inner, columns[j][i], 0.0) if i == at else columns[j][i] for i in below}
                for later in columns[j + 1 :]:
                    head = later[at][inner : inner + 1, :] * inverse
                    for i in below:
                        later[i] = later[i] - factor[i] * head
                scaled = blocks[at][inner : inner + 1, :] * inverse
                for i in below:
                    blocks[i] = blocks[i] - factor[i] * scaled
    results = []
    for blocks, found in zip(states, pivots):
        rows = [block / jnp.sqrt(jnp.concatenate(found[8 * i : 8 * i + 8], axis=0)) for i, block in enumerate(blocks)]
        results.append(jnp.concatenate(rows, axis=0)[:, rank:])
    return results


def basis_kernel(left_up, left_down, gram_up, gram_down, *refs):
    inv_up, inv_down, lhs_up, lhs_down = refs[-4:]
    inverses = inverse_factors([gram_up[...], gram_down[...]])
    rank = left_up.shape[0]
    for inverse, inv, left, lhs in zip(inverses, (inv_up, inv_down), (left_up, left_down), (lhs_up, lhs_down)):
        inv[...] = inverse
        first, second, _ = split3(dot(inverse, left[...], precision=HIGHEST).T)
        lhs[:, :rank] = first
        lhs[:, rank : 2 * rank] = first
        lhs[:, 2 * rank : 3 * rank] = second
        lhs[:, 3 * rank :] = second


def right_factor(inv, total, rhs):
    rank = inv.shape[0]
    right = dot(inv[...], total[...], precision=HIGHEST)
    first, second, _ = split3(right)
    rhs[:rank, :] = first
    rhs[rank : 2 * rank, :] = second
    rhs[2 * rank : 3 * rank, :] = first
    rhs[3 * rank :, :] = second
    return jnp.sum(right * right)


def factor_up_kernel(mine, other, inv, rhs, shard, total, stage):
    join_replicas(mine, other, stage, total)
    square = right_factor(inv, total, rhs)
    rows, ff = shard.shape[0], total.shape[1]
    width = shard.shape[1] - 128
    shard[:, :width] = shard_rows(mine, other, ff, rows)
    shard[:, width:] = jnp.full((rows, 128), square, F32)


def factor_down_kernel(limit, n_shards, *refs):
    shards, refs = refs[:n_shards], refs[n_shards:]
    inv, _, rhs, clip, total = refs
    join_shards(shards, total)
    square = right_factor(inv, total, rhs)
    width = total.shape[1]
    norm_sq = square + tree_sum(shard[:8, width:] for shard in shards)
    clip[...] = jnp.minimum(jnp.float32(1.0), limit / jnp.sqrt(norm_sq))


def rows_of(block):
    return pl.ds(pl.multiple_of(pl.program_id(0) * block, block), block)


def error_up_kernel(g, e, lhs, rhs, error, made):
    made[...] = jnp.zeros_like(made)
    part = rows_of(error.shape[1])
    rebuilt = dot(lhs[part, :], rhs[...])
    error[0] = (g[0, part, :].astype(F32) + e[0, part, :].astype(F32) - rebuilt).astype(BF16)


def last_kernel(g, e, lhs_up, rhs_up, lhs_down, rhs_down, clip, error, update_up, update_down):
    factor = clip[:1, :1]
    part = rows_of(update_down.shape[0])
    rebuilt = dot(lhs_down[part, :], rhs_down[...])
    update_down[...] = (factor * rebuilt).astype(BF16)
    error[0] = (g[0, part, :].astype(F32) + e[0, part, :].astype(F32) - rebuilt).astype(BF16)
    part = rows_of(update_up.shape[0])
    update_up[...] = (factor * dot(lhs_up[part, :], rhs_up[...])).astype(BF16)


def shaped(*dims, dtype=F32):
    return jax.ShapeDtypeStruct(dims, dtype)


def whole(shape):
    return pl.BlockSpec(shape, lambda *_: (0,) * len(shape))


def row_blocks(rows, columns):
    return pl.BlockSpec((rows // STEPS, columns), lambda i: (i, 0))


def replica_blocks(rows, columns):
    return pl.BlockSpec((1, rows // STEPS, columns), lambda i: (0, i, 0))


VMEM = pl.BlockSpec(memory_space=pltpu.VMEM)
ANY = pl.BlockSpec(memory_space=pl.ANY)


def call(kernel, out_shape, *args, flops=0, limit=12, name=None, **more):
    arrays = list(args) + jax.tree.leaves(out_shape)
    size = sum(a.size * a.dtype.itemsize for a in arrays)
    cost = pl.CostEstimate(flops=flops, bytes_accessed=size, transcendentals=0)
    params = pltpu.CompilerParams(vmem_limit_bytes=limit * MIB)
    return pl.pallas_call(kernel, out_shape=out_shape, compiler_params=params, cost_estimate=cost, name=name, **more)(*args)


def swap(x, axis, distance):
    pairs = [(i, i ^ distance) for i in range(lax.axis_size(axis))]
    return lax.ppermute(x, axis, pairs)


def from_shards(parts):
    return [parts[0]] + [swap(parts[j], "tensor", j) for j in range(1, len(parts))]


def from_z(parts):
    got = {j: swap(parts[j], "dp", 2 * j) for j in range(len(parts) - 1, 0, -1)}
    return [parts[0]] + [got[j] for j in range(1, len(parts))]


def mean_replicas(keep, got, shard):
    n_dp = lax.axis_size("dp")
    half, per, ff = keep.shape
    piece = shaped(per, ff + shard.shape[0] * shard.shape[1] // (half * per))
    stack = shaped(half, *piece.shape)
    parts = call(split_z_kernel, [piece] * half, keep, got, shard, name="split_z", scratch_shapes=[pltpu.VMEM(stack.shape, F32)])
    parts = [parts[0], *parts[:0:-1]]
    mean = call(functools.partial(mean_kernel, n_dp), piece, *from_z(parts), name="replica_mean")
    mine = call(stack_kernel, stack, *from_z([mean] * half), name="stack_z")
    return mine, swap(mine, "dp", 1)


def on_device(gu, eu, gd, ed, qu, qd):
    qu, qd = qu.T, qd.T
    n_dp, n_shards = lax.axis_size("dp"), lax.axis_size("tensor")
    _, rows, ff = gu.shape
    rank = qu.shape[0]
    half, per, rows_here = n_dp // 2, rank // n_dp, rank // n_shards
    shard_rows_here = shaped(rows_here, rows)
    replica_half = shaped(half, per, ff)
    stage = pltpu.VMEM((n_dp, per, ff), F32)
    wide = pltpu.VMEM((rank, ff), F32)
    narrow = pltpu.VMEM((rank, rows), F32)
    product = 4 * rows * ff * 4 * rank

    buffers = [
        [pltpu.VMEM(g.shape[1:], BF16)] * 2 + [pltpu.VMEM(q.shape, F32), pltpu.VMEM((q.shape[1], 4 * rank), BF16), total]
        for g, q, total in ((gu, qu, narrow), (gd, qd, wide))
    ]
    *parts, keep, send = call(
        functools.partial(left_kernel, n_shards), [shard_rows_here] * n_shards + [replica_half] * 2, gu, eu, qu, gd, ed, qd,
        name="left", flops=2 * product, limit=61, in_specs=[pl.BlockSpec(memory_space=pltpu.HBM)] * 6,
        scratch_shapes=buffers[0] + buffers[1] + [stage, pltpu.SemaphoreType.DMA((2,)), pltpu.SemaphoreType.DMA((2 * LEFT_STEPS, 2))],
    )
    got = swap(send, "dp", 1)
    shard, keep = call(
        functools.partial(first_shards_kernel, n_shards), [shard_rows_here, replica_half], parts[0], keep, *from_shards(parts)[1:],
        name="shard_sum", in_specs=[pl.BlockSpec(memory_space=pltpu.HBM)] * 2 + [VMEM] * (n_shards - 1),
        scratch_shapes=[pltpu.VMEM((rows_here, rows), F32), pltpu.SemaphoreType.DMA((2,))],
    )
    mine, other = mean_replicas(keep, got, shard)

    shard = call(functools.partial(shard_rows_kernel, ff), shard_rows_here, mine, other, name="shard_rows")
    left_rows = from_shards([shard] * n_shards)
    left_down, *parts = call(
        right_down_kernel, [shaped(rank, ff)] + [shaped(rows_here, rows + rank * n_shards)] * n_shards, mine, other, gd, ed,
        name="right_down", flops=product, in_specs=[VMEM] * 4, scratch_shapes=[pltpu.VMEM((3 * rank, ff), BF16), narrow, stage],
    )
    left_up, gram_up, keep, send = call(
        functools.partial(right_up_kernel, n_shards), [shaped(rank, rows), shaped(rank, rank), replica_half, replica_half],
        *left_rows, gu, eu, left_down, name="right_up", flops=product, in_specs=[VMEM] * (n_shards + 2) + [ANY],
        scratch_shapes=[pltpu.VMEM((3 * rank, rows), BF16), wide, stage],
    )
    got = swap(send, "dp", 1)
    shard, gram_down = call(
        functools.partial(sum_shards_kernel, n_shards), [shard_rows_here, shaped(rank, rank)], *from_shards(parts), name="shard_sum"
    )
    mine, other = mean_replicas(keep, got, shard)
    inv_up, inv_down, lhs_up, lhs_down = call(
        basis_kernel,
        [shaped(rank, rank)] * 2 + [shaped(rows, 4 * rank, dtype=BF16), shaped(ff, 4 * rank, dtype=BF16)],
        left_up, left_down, gram_up, gram_down, gu, eu, gd, ed, mine, name="basis", in_specs=[VMEM] * 8 + [ANY],
    )
    rhs_up, shard = call(
        factor_up_kernel, [shaped(4 * rank, ff, dtype=BF16), shaped(rows_here, rows + 128)], mine, other, inv_up,
        name="factor_up", scratch_shapes=[wide, stage],
    )
    right_rows = from_shards([shard] * n_shards)
    new_error_up, made = call(
        error_up_kernel, [shaped(1, rows, ff, dtype=BF16), shaped(8, 128)], gu, eu, lhs_up, rhs_up, name="error_up", flops=product // 2,
        grid=(STEPS,), in_specs=[VMEM] * 4, out_specs=[replica_blocks(rows, ff), whole((8, 128))],
    )
    limit = CLIP_RMS * (2.0 * rows * ff * n_shards) ** 0.5
    rhs_down, clip = call(
        functools.partial(factor_down_kernel, limit, n_shards), [shaped(4 * rank, rows, dtype=BF16), shaped(8, 128)],
        *right_rows, inv_down, made, name="factor_down", in_specs=[VMEM] * (n_shards + 1) + [ANY], scratch_shapes=[narrow],
    )
    new_error_down, update_up, update_down = call(
        last_kernel, [shaped(1, ff, rows, dtype=BF16), shaped(rows, ff, dtype=BF16), shaped(ff, rows, dtype=BF16)],
        gd, ed, lhs_up, rhs_up, lhs_down, rhs_down, clip, name="last", flops=product, grid=(STEPS,),
        in_specs=[VMEM] * 7, out_specs=[replica_blocks(ff, rows), row_blocks(rows, ff), row_blocks(ff, rows)],
    )
    return new_error_up, update_up, new_error_down, update_down


def solution(mesh):
    placed = (
        P("dp", None, "tensor"),
        P("dp", None, "tensor"),
        P("dp", "tensor", None),
        P("dp", "tensor", None),
        P("tensor", None),
        P(),
    )
    return jax.shard_map(
        on_device,
        mesh=mesh,
        in_specs=placed,
        out_specs=(
            P("dp", None, "tensor"),
            P(None, "tensor"),
            P("dp", "tensor", None),
            P("tensor", None),
        ),
        check_vma=False,
    )
```

```python
import functools

import jax
import jax.numpy as jnp
from jax import lax
from jax.experimental import pallas as pl
from jax.experimental.pallas import tpu as pltpu
from jax.sharding import PartitionSpec as P

F32 = jnp.float32
BF16 = jnp.bfloat16
HIGHEST = lax.Precision.HIGHEST
CLIP_RMS = 0.1
STEPS = 4
MIB = 1024 * 1024
NT = ((1,), (1,))


def split3(x):
    first = x.astype(BF16)
    rest = x - first.astype(F32)
    second = rest.astype(BF16)
    return first, second, (rest - second.astype(F32)).astype(BF16)


def tree_sum(values):
    values = list(values)
    while len(values) > 1:
        values = [values[i] + values[i + 1] for i in range(0, len(values), 2)]
    return values[0]


def dot(a, b, dims=((1,), (0,)), precision=None):
    return lax.dot_general(a, b, (dims, ((), ())), precision=precision, preferred_element_type=F32)


def fold(x, rows):
    return jnp.concatenate([x[i : i + rows] for i in range(0, x.shape[0], rows)], axis=1)


def unfold(x, rows):
    count = rows // x.shape[0]
    width = x.shape[1] // count
    return jnp.concatenate([x[:, i * width : (i + 1) * width] for i in range(count)], axis=0)


def place(axis):
    index = lax.axis_index(axis)
    return lax.bitwise_and(index, 1), lax.shift_right_logical(index, 1)


def split_replicas(total, stage, keep, send):
    parity, _ = place("dp")
    half, per, _ = keep.shape
    for c in range(2 * half):
        stage[c] = total[c * per : (c + 1) * per, :]
    for c in range(half):
        keep[c] = stage[2 * c + parity]
        send[c] = stage[2 * c + 1 - parity]


def join_replicas(mine, other, stage, total):
    parity, _ = place("dp")
    half, per, _ = mine.shape
    width = total.shape[1]
    for c in range(half):
        stage[2 * c + parity] = mine[c, :, :width]
        stage[2 * c + 1 - parity] = other[c, :, :width]
    for c in range(2 * half):
        total[c * per : (c + 1) * per, :] = stage[c]


def split_shards(total, extra, outs):
    me = lax.axis_index("tensor")
    rows, width = outs[0].shape[0], total.shape[1]
    for j, out in enumerate(outs):
        owner = lax.bitwise_xor(me, j)
        out[:, :width] = total[pl.ds(pl.multiple_of(owner * rows, rows), rows), :]
        if extra is not None:
            out[:, width:] = fold(extra, rows)


def join_shards(pieces, total):
    me = lax.axis_index("tensor")
    rows, width = pieces[0].shape[0], total.shape[1]
    for j, piece in enumerate(pieces):
        owner = lax.bitwise_xor(me, j)
        total[pl.ds(pl.multiple_of(owner * rows, rows), rows), :] = piece[:, :width]


def left_kernel(n_shards, gu, eu, qu, gd, ed, qd, *refs):
    *outs, gu_in, eu_in, qu_in, pieces_up, total_up, gd_in, ed_in, qd_in, pieces_down, total_down, stage, q_sems, sems = refs
    up, down = (qu_in, pieces_up, total_up), (qd_in, pieces_down, total_down)
    firsts = [pltpu.make_async_copy(src, dst, q_sems.at[i]) for i, (src, dst) in enumerate(((qd, qd_in), (qu, qu_in)))]
    stages = []
    for g, e, g_in, e_in, part, count in ((gd, ed, gd_in, ed_in, down, 3), (gu, eu, gu_in, eu_in, up, 2)):
        block = g_in.shape[0] // count
        for i in range(count):
            rows = pl.ds(i * block, block)
            n = len(stages)
            copies = [pltpu.make_async_copy(src.at[0, rows, :], dst.at[rows, :], sems.at[n, k]) for k, (src, dst) in enumerate(((g, g_in), (e, e_in)))]
            stages.append((copies, g_in, e_in, slice(i * block, (i + 1) * block), part))

    def fetch(n):
        if n < len(stages):
            for copy in stages[n][0]:
                copy.start()

    firsts[0].start()
    fetch(0)
    firsts[1].start()
    for n, (first, (q, pieces, _)) in enumerate(zip(firsts, (down, up))):
        first.wait()
        fetch(n + 1)
        split_rows(q, pieces)
    for n, (copies, g, e, rows, (_, pieces, total)) in enumerate(stages):
        for copy in copies:
            copy.wait()
        fetch(n + 3)
        total[:, rows] = add_pieces(dot(pieces[...], g[rows, :], NT) + dot(pieces[...], e[rows, :], NT))
    split_shards(total_up, None, outs[:n_shards])
    split_replicas(total_down, stage, *outs[n_shards:])


def fetch_kernel(*refs):
    half = len(refs) // 2
    for source, out in zip(refs[:half], refs[half:]):
        out[...] = source[...]


def sum_shards_kernel(n_shards, *refs):
    terms, (out, gram) = refs[:n_shards], refs[n_shards:]
    total = tree_sum(term[...] for term in terms)
    out[...] = total[:, : out.shape[1]]
    gram[...] = unfold(total[:, out.shape[1] :], gram.shape[0])


def first_shards_kernel(*refs):
    refs[-1][...] = tree_sum(term[...] for term in refs[:-1])


def split_z_kernel(keep, got, shard, *refs):
    *outs, stage = refs
    _, z = place("dp")
    half, per, ff = keep.shape
    block = shard.shape[1] // half
    for c in range(half):
        stage[c, :, :ff] = keep[c] + got[c]
        stage[c, :, ff:] = fold(shard[:, c * block : (c + 1) * block], per)
    for j, out in zip([0, *range(half - 1, 0, -1)], outs):
        out[...] = stage[lax.bitwise_xor(z, j)]


def mean_kernel(n_dp, *refs):
    refs[-1][...] = tree_sum(ref[...] for ref in refs[:-1]) / n_dp


def stack_kernel(*refs):
    _, z = place("dp")
    for j, ref in enumerate(refs[:-1]):
        refs[-1][lax.bitwise_xor(z, j)] = ref[...]


def shard_rows(mine, other, ff, rows):
    half = mine.shape[0]
    return jnp.concatenate([unfold(mine[c, :, ff:] + other[c, :, ff:], rows) for c in range(half)], axis=1)


def shard_rows_kernel(ff, mine, other, out):
    out[...] = shard_rows(mine, other, ff, out.shape[0])


def split_rows(left, pieces):
    rank = left.shape[0]
    for i, piece in enumerate(split3(left[...])):
        pieces[i * rank : (i + 1) * rank, :] = piece


def add_pieces(t):
    rank = t.shape[0] // 3
    return t[:rank] + (t[rank : 2 * rank] + t[2 * rank :])


def right_down_kernel(mine, other, g, e, left, *refs):
    *outs, pieces, total, stage = refs
    join_replicas(mine, other, stage, left)
    split_rows(left, pieces)
    total[...] = add_pieces(dot(pieces[...], g[0]) + dot(pieces[...], e[0]))
    split_shards(total, dot(left[...], left[...], NT, HIGHEST), outs)


def right_up_kernel(n_shards, *refs):
    shards, refs = refs[:n_shards], refs[n_shards:]
    g, e, _, left, gram, keep, send, pieces, total, stage = refs
    join_shards(shards, left)
    split_rows(left, pieces)
    block = total.shape[1] // STEPS
    for i in range(STEPS):
        part = slice(i * block, (i + 1) * block)
        total[:, part] = add_pieces(dot(pieces[...], g[0, :, part]) + dot(pieces[...], e[0, :, part]))
    split_replicas(total, stage, keep, send)
    gram[...] = dot(left[...], left[...], NT, HIGHEST)


def inverse_factors(grams):
    rank = grams[0].shape[0]
    count = rank // 8
    panel = 4
    lane = lax.broadcasted_iota(jnp.int32, (8, 2 * rank), 1)
    row = lax.broadcasted_iota(jnp.int32, (8, 2 * rank), 0)
    states, pivots = [], []
    for gram in grams:
        wide = jnp.concatenate([gram, jnp.zeros_like(gram)], axis=1)
        states.append([wide[i : i + 8] + (lane == row + (rank + i)).astype(F32) for i in range(0, rank, 8)])
        pivots.append([])
    for start in range(0, rank, panel):
        at = start // 8
        below = range(at, count)
        spread = [
            [{i: jnp.broadcast_to(blocks[i][:, start + j : start + j + 1], (8, 2 * rank)) for i in below} for j in range(panel)]
            for blocks in states
        ]
        for j in range(panel):
            inner = (start + j) % 8
            for blocks, columns, found in zip(states, spread, pivots):
                pivot = columns[j][at][inner : inner + 1, :]
                found.append(pivot)
                inverse = 1.0 / pivot
                factor = {i: jnp.where(row > inner, columns[j][i], 0.0) if i == at else columns[j][i] for i in below}
                for later in columns[j + 1 :]:
                    head = later[at][inner : inner + 1, :] * inverse
                    for i in below:
                        later[i] = later[i] - factor[i] * head
                scaled = blocks[at][inner : inner + 1, :] * inverse
                for i in below:
                    blocks[i] = blocks[i] - factor[i] * scaled
    results = []
    for blocks, found in zip(states, pivots):
        rows = [block / jnp.sqrt(jnp.concatenate(found[8 * i : 8 * i + 8], axis=0)) for i, block in enumerate(blocks)]
        results.append(jnp.concatenate(rows, axis=0)[:, rank:])
    return results


def basis_kernel(left_up, left_down, gram_up, gram_down, *refs):
    inv_up, inv_down, lhs_up, lhs_down = refs[-4:]
    inverses = inverse_factors([gram_up[...], gram_down[...]])
    rank = left_up.shape[0]
    for inverse, inv, left, lhs in zip(inverses, (inv_up, inv_down), (left_up, left_down), (lhs_up, lhs_down)):
        inv[...] = inverse
        first, second, _ = split3(dot(inverse, left[...], precision=HIGHEST).T)
        lhs[:, :rank] = first
        lhs[:, rank : 2 * rank] = first
        lhs[:, 2 * rank : 3 * rank] = second
        lhs[:, 3 * rank :] = second


def right_factor(inv, total, rhs):
    rank = inv.shape[0]
    right = dot(inv[...], total[...], precision=HIGHEST)
    first, second, _ = split3(right)
    rhs[:rank, :] = first
    rhs[rank : 2 * rank, :] = second
    rhs[2 * rank : 3 * rank, :] = first
    rhs[3 * rank :, :] = second
    return jnp.sum(right * right)


def factor_up_kernel(mine, other, inv, rhs, shard, total, stage):
    join_replicas(mine, other, stage, total)
    square = right_factor(inv, total, rhs)
    rows, ff = shard.shape[0], total.shape[1]
    width = shard.shape[1] - 128
    shard[:, :width] = shard_rows(mine, other, ff, rows)
    shard[:, width:] = jnp.full((rows, 128), square, F32)


def factor_down_kernel(limit, n_shards, *refs):
    shards, refs = refs[:n_shards], refs[n_shards:]
    inv, _, rhs, clip, total = refs
    join_shards(shards, total)
    square = right_factor(inv, total, rhs)
    width = total.shape[1]
    norm_sq = square + tree_sum(shard[:8, width:] for shard in shards)
    clip[...] = jnp.minimum(jnp.float32(1.0), limit / jnp.sqrt(norm_sq))


def rows_of(block):
    return pl.ds(pl.multiple_of(pl.program_id(0) * block, block), block)


def error_up_kernel(g, e, lhs, rhs, error, made):
    made[...] = jnp.zeros_like(made)
    part = rows_of(error.shape[1])
    rebuilt = dot(lhs[part, :], rhs[...])
    error[0] = (g[0, part, :].astype(F32) + e[0, part, :].astype(F32) - rebuilt).astype(BF16)


def last_kernel(g, e, lhs_up, rhs_up, lhs_down, rhs_down, clip, error, update_up, update_down):
    factor = clip[:1, :1]
    part = rows_of(update_down.shape[0])
    rebuilt = dot(lhs_down[part, :], rhs_down[...])
    update_down[...] = (factor * rebuilt).astype(BF16)
    error[0] = (g[0, part, :].astype(F32) + e[0, part, :].astype(F32) - rebuilt).astype(BF16)
    part = rows_of(update_up.shape[0])
    update_up[...] = (factor * dot(lhs_up[part, :], rhs_up[...])).astype(BF16)


def shaped(*dims, dtype=F32):
    return jax.ShapeDtypeStruct(dims, dtype)


def whole(shape):
    return pl.BlockSpec(shape, lambda *_: (0,) * len(shape))


def row_blocks(rows, columns):
    return pl.BlockSpec((rows // STEPS, columns), lambda i: (i, 0))


def replica_blocks(rows, columns):
    return pl.BlockSpec((1, rows // STEPS, columns), lambda i: (0, i, 0))


VMEM = pl.BlockSpec(memory_space=pltpu.VMEM)
ANY = pl.BlockSpec(memory_space=pl.ANY)


def call(kernel, out_shape, *args, flops=0, limit=12, name=None, **more):
    arrays = list(args) + jax.tree.leaves(out_shape)
    size = sum(a.size * a.dtype.itemsize for a in arrays)
    cost = pl.CostEstimate(flops=flops, bytes_accessed=size, transcendentals=0)
    params = pltpu.CompilerParams(vmem_limit_bytes=limit * MIB)
    return pl.pallas_call(kernel, out_shape=out_shape, compiler_params=params, cost_estimate=cost, name=name, **more)(*args)


def swap(x, axis, distance):
    pairs = [(i, i ^ distance) for i in range(lax.axis_size(axis))]
    return lax.ppermute(x, axis, pairs)


def from_shards(parts):
    return [parts[0]] + [swap(parts[j], "tensor", j) for j in range(1, len(parts))]


def from_z(parts):
    got = {j: swap(parts[j], "dp", 2 * j) for j in range(len(parts) - 1, 0, -1)}
    return [parts[0]] + [got[j] for j in range(1, len(parts))]


def mean_replicas(keep, got, shard):
    n_dp = lax.axis_size("dp")
    half, per, ff = keep.shape
    piece = shaped(per, ff + shard.shape[0] * shard.shape[1] // (half * per))
    stack = shaped(half, *piece.shape)
    parts = call(split_z_kernel, [piece] * half, keep, got, shard, name="split_z", scratch_shapes=[pltpu.VMEM(stack.shape, F32)])
    parts = [parts[0], *parts[:0:-1]]
    mean = call(functools.partial(mean_kernel, n_dp), piece, *from_z(parts), name="replica_mean")
    mine = call(stack_kernel, stack, *from_z([mean] * half), name="stack_z")
    return mine, swap(mine, "dp", 1)


def on_device(gu, eu, gd, ed, qu, qd):
    qu, qd = qu.T, qd.T
    n_dp, n_shards = lax.axis_size("dp"), lax.axis_size("tensor")
    _, rows, ff = gu.shape
    rank = qu.shape[0]
    half, per, rows_here = n_dp // 2, rank // n_dp, rank // n_shards
    shard_rows_here = shaped(rows_here, rows)
    replica_half = shaped(half, per, ff)
    stage = pltpu.VMEM((n_dp, per, ff), F32)
    wide = pltpu.VMEM((rank, ff), F32)
    narrow = pltpu.VMEM((rank, rows), F32)
    product = 4 * rows * ff * 4 * rank

    buffers = [
        [pltpu.VMEM(g.shape[1:], BF16)] * 2 + [pltpu.VMEM(q.shape, F32), pltpu.VMEM((3 * rank, q.shape[1]), BF16), total]
        for g, q, total in ((gu, qu, narrow), (gd, qd, wide))
    ]
    *parts, keep, send = call(
        functools.partial(left_kernel, n_shards), [shard_rows_here] * n_shards + [replica_half] * 2, gu, eu, qu, gd, ed, qd,
        name="left", flops=2 * product, limit=61, in_specs=[pl.BlockSpec(memory_space=pltpu.HBM)] * 6,
        scratch_shapes=buffers[0] + buffers[1] + [stage, pltpu.SemaphoreType.DMA((2,)), pltpu.SemaphoreType.DMA((5, 2))],
    )
    got = swap(send, "dp", 1)
    parts = from_shards(parts)
    parts[0], keep = call(fetch_kernel, [shard_rows_here, replica_half], parts[0], keep, name="fetch", flops=product // 4)
    shard = call(first_shards_kernel, shard_rows_here, *parts, name="shard_sum")
    mine, other = mean_replicas(keep, got, shard)

    shard = call(functools.partial(shard_rows_kernel, ff), shard_rows_here, mine, other, name="shard_rows")
    left_rows = from_shards([shard] * n_shards)
    left_down, *parts = call(
        right_down_kernel, [shaped(rank, ff)] + [shaped(rows_here, rows + rank * n_shards)] * n_shards, mine, other, gd, ed,
        name="right_down", flops=product, in_specs=[VMEM] * 4, scratch_shapes=[pltpu.VMEM((3 * rank, ff), BF16), narrow, stage],
    )
    left_up, gram_up, keep, send = call(
        functools.partial(right_up_kernel, n_shards), [shaped(rank, rows), shaped(rank, rank), replica_half, replica_half],
        *left_rows, gu, eu, left_down, name="right_up", flops=product, in_specs=[VMEM] * (n_shards + 2) + [ANY],
        scratch_shapes=[pltpu.VMEM((3 * rank, rows), BF16), wide, stage],
    )
    got = swap(send, "dp", 1)
    shard, gram_down = call(
        functools.partial(sum_shards_kernel, n_shards), [shard_rows_here, shaped(rank, rank)], *from_shards(parts), name="shard_sum"
    )
    mine, other = mean_replicas(keep, got, shard)
    inv_up, inv_down, lhs_up, lhs_down = call(
        basis_kernel,
        [shaped(rank, rank)] * 2 + [shaped(rows, 4 * rank, dtype=BF16), shaped(ff, 4 * rank, dtype=BF16)],
        left_up, left_down, gram_up, gram_down, gu, eu, gd, ed, mine, name="basis", in_specs=[VMEM] * 8 + [ANY],
    )
    rhs_up, shard = call(
        factor_up_kernel, [shaped(4 * rank, ff, dtype=BF16), shaped(rows_here, rows + 128)], mine, other, inv_up,
        name="factor_up", scratch_shapes=[wide, stage],
    )
    right_rows = from_shards([shard] * n_shards)
    new_error_up, made = call(
        error_up_kernel, [shaped(1, rows, ff, dtype=BF16), shaped(8, 128)], gu, eu, lhs_up, rhs_up, name="error_up", flops=product // 2,
        grid=(STEPS,), in_specs=[VMEM] * 4, out_specs=[replica_blocks(rows, ff), whole((8, 128))],
    )
    limit = CLIP_RMS * (2.0 * rows * ff * n_shards) ** 0.5
    rhs_down, clip = call(
        functools.partial(factor_down_kernel, limit, n_shards), [shaped(4 * rank, rows, dtype=BF16), shaped(8, 128)],
        *right_rows, inv_down, made, name="factor_down", in_specs=[VMEM] * (n_shards + 1) + [ANY], scratch_shapes=[narrow],
    )
    new_error_down, update_up, update_down = call(
        last_kernel, [shaped(1, ff, rows, dtype=BF16), shaped(rows, ff, dtype=BF16), shaped(ff, rows, dtype=BF16)],
        gd, ed, lhs_up, rhs_up, lhs_down, rhs_down, clip, name="last", flops=product, grid=(STEPS,),
        in_specs=[VMEM] * 7, out_specs=[replica_blocks(ff, rows), row_blocks(rows, ff), row_blocks(ff, rows)],
    )
    return new_error_up, update_up, new_error_down, update_down


def solution(mesh):
    placed = (
        P("dp", None, "tensor"),
        P("dp", None, "tensor"),
        P("dp", "tensor", None),
        P("dp", "tensor", None),
        P("tensor", None),
        P(),
    )
    return jax.shard_map(
        on_device,
        mesh=mesh,
        in_specs=placed,
        out_specs=(
            P("dp", None, "tensor"),
            P(None, "tensor"),
            P("dp", "tensor", None),
            P("tensor", None),
        ),
        check_vma=False,
    )
```

```python
import functools

import jax
import jax.numpy as jnp
from jax import lax
from jax.experimental import pallas as pl
from jax.experimental.pallas import tpu as pltpu
from jax.sharding import PartitionSpec as P

F32 = jnp.float32
BF16 = jnp.bfloat16
HIGHEST = lax.Precision.HIGHEST
CLIP_RMS = 0.1
STEPS = 4
MIB = 1024 * 1024
NT = ((1,), (1,))


def split3(x):
    first = x.astype(BF16)
    rest = x - first.astype(F32)
    second = rest.astype(BF16)
    return first, second, (rest - second.astype(F32)).astype(BF16)


def tree_sum(values):
    values = list(values)
    while len(values) > 1:
        values = [values[i] + values[i + 1] for i in range(0, len(values), 2)]
    return values[0]


def dot(a, b, dims=((1,), (0,)), precision=None):
    return lax.dot_general(a, b, (dims, ((), ())), precision=precision, preferred_element_type=F32)


def fold(x, rows):
    return jnp.concatenate([x[i : i + rows] for i in range(0, x.shape[0], rows)], axis=1)


def unfold(x, rows):
    count = rows // x.shape[0]
    width = x.shape[1] // count
    return jnp.concatenate([x[:, i * width : (i + 1) * width] for i in range(count)], axis=0)


def place(axis):
    index = lax.axis_index(axis)
    return lax.bitwise_and(index, 1), lax.shift_right_logical(index, 1)


def split_replicas(total, stage, keep, send):
    parity, _ = place("dp")
    half, per, _ = keep.shape
    for c in range(2 * half):
        stage[c] = total[c * per : (c + 1) * per, :]
    for c in range(half):
        keep[c] = stage[2 * c + parity]
        send[c] = stage[2 * c + 1 - parity]


def join_replicas(mine, other, stage, total):
    parity, _ = place("dp")
    half, per, _ = mine.shape
    width = total.shape[1]
    for c in range(half):
        stage[2 * c + parity] = mine[c, :, :width]
        stage[2 * c + 1 - parity] = other[c, :, :width]
    for c in range(2 * half):
        total[c * per : (c + 1) * per, :] = stage[c]


def split_shards(total, extra, outs):
    me = lax.axis_index("tensor")
    rows, width = outs[0].shape[0], total.shape[1]
    for j, out in enumerate(outs):
        owner = lax.bitwise_xor(me, j)
        out[:, :width] = total[pl.ds(pl.multiple_of(owner * rows, rows), rows), :]
        if extra is not None:
            out[:, width:] = fold(extra, rows)


def join_shards(pieces, total):
    me = lax.axis_index("tensor")
    rows, width = pieces[0].shape[0], total.shape[1]
    for j, piece in enumerate(pieces):
        owner = lax.bitwise_xor(me, j)
        total[pl.ds(pl.multiple_of(owner * rows, rows), rows), :] = piece[:, :width]


def left_kernel(n_shards, gu, eu, qu, gd, ed, qd, *refs):
    *outs, gu_in, eu_in, qu_in, pieces_up, total_up, gd_in, ed_in, qd_in, pieces_down, total_down, stage, q_sems, sems = refs
    up, down = (qu_in, pieces_up, total_up), (qd_in, pieces_down, total_down)
    firsts = [pltpu.make_async_copy(src, dst, q_sems.at[i]) for i, (src, dst) in enumerate(((qd, qd_in), (qu, qu_in)))]
    stages = []
    for g, e, g_in, e_in, part, count in ((gd, ed, gd_in, ed_in, down, 3), (gu, eu, gu_in, eu_in, up, 2)):
        block = g_in.shape[0] // count
        for i in range(count):
            rows = pl.ds(i * block, block)
            n = len(stages)
            copies = [pltpu.make_async_copy(src.at[0, rows, :], dst.at[rows, :], sems.at[n, k]) for k, (src, dst) in enumerate(((g, g_in), (e, e_in)))]
            stages.append((copies, g_in, e_in, slice(i * block, (i + 1) * block), part))

    def fetch(n):
        if n < len(stages):
            for copy in stages[n][0]:
                copy.start()

    firsts[0].start()
    fetch(0)
    firsts[1].start()
    for n, (first, (q, pieces, _)) in enumerate(zip(firsts, (down, up))):
        first.wait()
        fetch(n + 1)
        split_rows(q, pieces)
    for n, (copies, g, e, rows, (_, pieces, total)) in enumerate(stages):
        for copy in copies:
            copy.wait()
        fetch(n + 3)
        total[:, rows] = add_pieces(dot(pieces[...], g[rows, :], NT) + dot(pieces[...], e[rows, :], NT))
    split_shards(total_up, None, outs[:n_shards])
    split_replicas(total_down, stage, *outs[n_shards:])


def fetch_kernel(*refs):
    half = len(refs) // 2
    for source, out in zip(refs[:half], refs[half:]):
        out[...] = source[...]


def sum_shards_kernel(n_shards, *refs):
    terms, (out, gram) = refs[:n_shards], refs[n_shards:]
    total = tree_sum(term[...] for term in terms)
    out[...] = total[:, : out.shape[1]]
    gram[...] = unfold(total[:, out.shape[1] :], gram.shape[0])


def first_shards_kernel(*refs):
    refs[-1][...] = tree_sum(term[...] for term in refs[:-1])


def split_z_kernel(keep, got, shard, *refs):
    *outs, stage = refs
    _, z = place("dp")
    half, per, ff = keep.shape
    block = shard.shape[1] // half
    for c in range(half):
        stage[c, :, :ff] = keep[c] + got[c]
        stage[c, :, ff:] = fold(shard[:, c * block : (c + 1) * block], per)
    for j, out in zip([0, *range(half - 1, 0, -1)], outs):
        out[...] = stage[lax.bitwise_xor(z, j)]


def mean_kernel(n_dp, *refs):
    refs[-1][...] = tree_sum(ref[...] for ref in refs[:-1]) / n_dp


def stack_kernel(*refs):
    _, z = place("dp")
    for j, ref in enumerate(refs[:-1]):
        refs[-1][lax.bitwise_xor(z, j)] = ref[...]


def stack_apart_kernel(*refs):
    *pieces, out, shard, stack = refs
    stack_kernel(*pieces, stack)
    half, _, ff = out.shape
    out[...] = stack[:, :, :ff]
    shard[...] = jnp.concatenate([unfold(stack[c, :, ff:], shard.shape[0]) for c in range(half)], axis=1)


def shard_rows(mine, other, ff, rows):
    half = mine.shape[0]
    return jnp.concatenate([unfold(mine[c, :, ff:] + other[c, :, ff:], rows) for c in range(half)], axis=1)


def split_rows(left, pieces):
    rank = left.shape[0]
    for i, piece in enumerate(split3(left[...])):
        pieces[i * rank : (i + 1) * rank, :] = piece


def add_pieces(t):
    rank = t.shape[0] // 3
    return t[:rank] + (t[rank : 2 * rank] + t[2 * rank :])


def right_down_kernel(_, mine, other, g, e, left, *refs):
    *outs, pieces, total, stage = refs
    join_replicas(mine, other, stage, left)
    split_rows(left, pieces)
    total[...] = add_pieces(dot(pieces[...], g[0]) + dot(pieces[...], e[0]))
    split_shards(total, dot(left[...], left[...], NT, HIGHEST), outs)


def right_up_kernel(n_shards, *refs):
    shards, refs = refs[:n_shards], refs[n_shards:]
    g, e, left, gram, keep, send, pieces, total, stage = refs
    join_shards(shards, left)
    split_rows(left, pieces)
    block = total.shape[1] // STEPS
    for i in range(STEPS):
        part = slice(i * block, (i + 1) * block)
        total[:, part] = add_pieces(dot(pieces[...], g[0, :, part]) + dot(pieces[...], e[0, :, part]))
    split_replicas(total, stage, keep, send)
    gram[...] = dot(left[...], left[...], NT, HIGHEST)


def inverse_factors(grams):
    rank = grams[0].shape[0]
    count = rank // 8
    panel = 4
    lane = lax.broadcasted_iota(jnp.int32, (8, 2 * rank), 1)
    row = lax.broadcasted_iota(jnp.int32, (8, 2 * rank), 0)
    states, pivots = [], []
    for gram in grams:
        wide = jnp.concatenate([gram, jnp.zeros_like(gram)], axis=1)
        states.append([wide[i : i + 8] + (lane == row + (rank + i)).astype(F32) for i in range(0, rank, 8)])
        pivots.append([])
    for start in range(0, rank, panel):
        at = start // 8
        below = range(at, count)
        spread = [
            [{i: jnp.broadcast_to(blocks[i][:, start + j : start + j + 1], (8, 2 * rank)) for i in below} for j in range(panel)]
            for blocks in states
        ]
        for j in range(panel):
            inner = (start + j) % 8
            for blocks, columns, found in zip(states, spread, pivots):
                pivot = columns[j][at][inner : inner + 1, :]
                found.append(pivot)
                inverse = 1.0 / pivot
                factor = {i: jnp.where(row > inner, columns[j][i], 0.0) if i == at else columns[j][i] for i in below}
                for later in columns[j + 1 :]:
                    head = later[at][inner : inner + 1, :] * inverse
                    for i in below:
                        later[i] = later[i] - factor[i] * head
                scaled = blocks[at][inner : inner + 1, :] * inverse
                for i in below:
                    blocks[i] = blocks[i] - factor[i] * scaled
    results = []
    for blocks, found in zip(states, pivots):
        rows = [block / jnp.sqrt(jnp.concatenate(found[8 * i : 8 * i + 8], axis=0)) for i, block in enumerate(blocks)]
        results.append(jnp.concatenate(rows, axis=0)[:, rank:])
    return results


def basis_kernel(left_up, left_down, gram_up, gram_down, *refs):
    inv_up, inv_down, lhs_up, lhs_down = refs[-4:]
    inverses = inverse_factors([gram_up[...], gram_down[...]])
    rank = left_up.shape[0]
    for inverse, inv, left, lhs in zip(inverses, (inv_up, inv_down), (left_up, left_down), (lhs_up, lhs_down)):
        inv[...] = inverse
        first, second, _ = split3(dot(inverse, left[...], precision=HIGHEST).T)
        lhs[:, :rank] = first
        lhs[:, rank : 2 * rank] = first
        lhs[:, 2 * rank : 3 * rank] = second
        lhs[:, 3 * rank :] = second


def right_factor(inv, total, rhs):
    rank = inv.shape[0]
    right = dot(inv[...], total[...], precision=HIGHEST)
    first, second, _ = split3(right)
    rhs[:rank, :] = first
    rhs[rank : 2 * rank, :] = second
    rhs[2 * rank : 3 * rank, :] = first
    rhs[3 * rank :, :] = second
    return jnp.sum(right * right)


def factor_up_kernel(mine, other, inv, rhs, shard, total, stage):
    join_replicas(mine, other, stage, total)
    square = right_factor(inv, total, rhs)
    rows, ff = shard.shape[0], total.shape[1]
    width = shard.shape[1] - 128
    shard[:, :width] = shard_rows(mine, other, ff, rows)
    shard[:, width:] = jnp.full((rows, 128), square, F32)


def factor_down_kernel(limit, n_shards, *refs):
    shards, refs = refs[:n_shards], refs[n_shards:]
    inv, _, rhs, clip, total = refs
    join_shards(shards, total)
    square = right_factor(inv, total, rhs)
    width = total.shape[1]
    norm_sq = square + tree_sum(shard[:8, width:] for shard in shards)
    clip[...] = jnp.minimum(jnp.float32(1.0), limit / jnp.sqrt(norm_sq))


def rows_of(block):
    return pl.ds(pl.multiple_of(pl.program_id(0) * block, block), block)


def error_up_kernel(g, e, lhs, rhs, error, made):
    made[...] = jnp.zeros_like(made)
    part = rows_of(error.shape[1])
    rebuilt = dot(lhs[part, :], rhs[...])
    error[0] = (g[0, part, :].astype(F32) + e[0, part, :].astype(F32) - rebuilt).astype(BF16)


def last_kernel(g, e, lhs_up, rhs_up, lhs_down, rhs_down, clip, error, update_up, update_down):
    factor = clip[:1, :1]
    part = rows_of(update_down.shape[0])
    rebuilt = dot(lhs_down[part, :], rhs_down[...])
    update_down[...] = (factor * rebuilt).astype(BF16)
    error[0] = (g[0, part, :].astype(F32) + e[0, part, :].astype(F32) - rebuilt).astype(BF16)
    part = rows_of(update_up.shape[0])
    update_up[...] = (factor * dot(lhs_up[part, :], rhs_up[...])).astype(BF16)


def shaped(*dims, dtype=F32):
    return jax.ShapeDtypeStruct(dims, dtype)


def whole(shape):
    return pl.BlockSpec(shape, lambda *_: (0,) * len(shape))


def row_blocks(rows, columns):
    return pl.BlockSpec((rows // STEPS, columns), lambda i: (i, 0))


def replica_blocks(rows, columns):
    return pl.BlockSpec((1, rows // STEPS, columns), lambda i: (0, i, 0))


VMEM = pl.BlockSpec(memory_space=pltpu.VMEM)
ANY = pl.BlockSpec(memory_space=pl.ANY)


def call(kernel, out_shape, *args, flops=0, limit=12, name=None, **more):
    arrays = list(args) + jax.tree.leaves(out_shape)
    size = sum(a.size * a.dtype.itemsize for a in arrays)
    cost = pl.CostEstimate(flops=flops, bytes_accessed=size, transcendentals=0)
    params = pltpu.CompilerParams(vmem_limit_bytes=limit * MIB)
    return pl.pallas_call(kernel, out_shape=out_shape, compiler_params=params, cost_estimate=cost, name=name, **more)(*args)


def swap(x, axis, distance):
    pairs = [(i, i ^ distance) for i in range(lax.axis_size(axis))]
    return lax.ppermute(x, axis, pairs)


def from_shards(parts):
    return [parts[0]] + [swap(parts[j], "tensor", j) for j in range(1, len(parts))]


def from_z(parts):
    got = {j: swap(parts[j], "dp", 2 * j) for j in range(len(parts) - 1, 0, -1)}
    return [parts[0]] + [got[j] for j in range(1, len(parts))]


def mean_replicas(keep, got, shard):
    n_dp = lax.axis_size("dp")
    half, per, ff = keep.shape
    piece = shaped(per, ff + shard.shape[0] * shard.shape[1] // (half * per))
    stage = pltpu.VMEM((half, *piece.shape), F32)
    parts = call(split_z_kernel, [piece] * half, keep, got, shard, name="split_z", scratch_shapes=[stage])
    parts = [parts[0], *parts[:0:-1]]
    mean = call(functools.partial(mean_kernel, n_dp), piece, *from_z(parts), name="replica_mean")
    return from_z([mean] * half)


def on_device(gu, eu, gd, ed, qu, qd):
    qu, qd = qu.T, qd.T
    n_dp, n_shards = lax.axis_size("dp"), lax.axis_size("tensor")
    _, rows, ff = gu.shape
    rank = qu.shape[0]
    half, per, rows_here = n_dp // 2, rank // n_dp, rank // n_shards
    shard_rows_here = shaped(rows_here, rows)
    replica_half = shaped(half, per, ff)
    stage = pltpu.VMEM((n_dp, per, ff), F32)
    wide = pltpu.VMEM((rank, ff), F32)
    narrow = pltpu.VMEM((rank, rows), F32)
    product = 4 * rows * ff * 4 * rank

    buffers = [
        [pltpu.VMEM(g.shape[1:], BF16)] * 2 + [pltpu.VMEM(q.shape, F32), pltpu.VMEM((3 * rank, q.shape[1]), BF16), total]
        for g, q, total in ((gu, qu, narrow), (gd, qd, wide))
    ]
    *parts, keep, send = call(
        functools.partial(left_kernel, n_shards), [shard_rows_here] * n_shards + [replica_half] * 2, gu, eu, qu, gd, ed, qd,
        name="left", flops=2 * product, limit=61, in_specs=[pl.BlockSpec(memory_space=pltpu.HBM)] * 6,
        scratch_shapes=buffers[0] + buffers[1] + [stage, pltpu.SemaphoreType.DMA((2,)), pltpu.SemaphoreType.DMA((5, 2))],
    )
    got = swap(send, "dp", 1)
    parts = from_shards(parts)
    parts[0], keep = call(fetch_kernel, [shard_rows_here, replica_half], parts[0], keep, name="fetch", flops=product // 4)
    shard = call(first_shards_kernel, shard_rows_here, *parts, name="shard_sum")
    pieces = mean_replicas(keep, got, shard)
    mine, shard = call(
        stack_apart_kernel, [replica_half, shard_rows_here], *pieces, name="stack_z",
        scratch_shapes=[pltpu.VMEM((half, *pieces[0].shape), F32)],
    )
    shard = call(first_shards_kernel, shard_rows_here, shard, swap(shard, "dp", 1), name="replica_sum")
    other = swap(mine, "dp", 1)
    left_rows = from_shards([shard] * n_shards)
    left_up, gram_up, keep, send = call(
        functools.partial(right_up_kernel, n_shards), [shaped(rank, rows), shaped(rank, rank), replica_half, replica_half],
        *left_rows, gu, eu, name="right_up", flops=product,
        scratch_shapes=[pltpu.VMEM((3 * rank, rows), BF16), wide, stage],
    )
    left_down, *parts = call(
        right_down_kernel, [shaped(rank, ff)] + [shaped(rows_here, rows + rank * n_shards)] * n_shards, left_up, mine, other, gd, ed,
        name="right_down", flops=product, in_specs=[ANY] + [VMEM] * 4, scratch_shapes=[pltpu.VMEM((3 * rank, ff), BF16), narrow, stage],
    )
    got = swap(send, "dp", 1)
    shard, gram_down = call(
        functools.partial(sum_shards_kernel, n_shards), [shard_rows_here, shaped(rank, rank)], *from_shards(parts), name="shard_sum"
    )
    pieces = mean_replicas(keep, got, shard)
    mine = call(stack_kernel, shaped(half, *pieces[0].shape), *pieces, name="stack_z")
    other = swap(mine, "dp", 1)
    inv_up, inv_down, lhs_up, lhs_down = call(
        basis_kernel,
        [shaped(rank, rank)] * 2 + [shaped(rows, 4 * rank, dtype=BF16), shaped(ff, 4 * rank, dtype=BF16)],
        left_up, left_down, gram_up, gram_down, gu, eu, gd, ed, mine, name="basis", in_specs=[VMEM] * 8 + [ANY],
    )
    rhs_up, shard = call(
        factor_up_kernel, [shaped(4 * rank, ff, dtype=BF16), shaped(rows_here, rows + 128)], mine, other, inv_up,
        name="factor_up", scratch_shapes=[wide, stage],
    )
    right_rows = from_shards([shard] * n_shards)
    new_error_up, made = call(
        error_up_kernel, [shaped(1, rows, ff, dtype=BF16), shaped(8, 128)], gu, eu, lhs_up, rhs_up, name="error_up", flops=product // 2,
        grid=(STEPS,), in_specs=[VMEM] * 4, out_specs=[replica_blocks(rows, ff), whole((8, 128))],
    )
    limit = CLIP_RMS * (2.0 * rows * ff * n_shards) ** 0.5
    rhs_down, clip = call(
        functools.partial(factor_down_kernel, limit, n_shards), [shaped(4 * rank, rows, dtype=BF16), shaped(8, 128)],
        *right_rows, inv_down, made, name="factor_down", in_specs=[VMEM] * (n_shards + 1) + [ANY], scratch_shapes=[narrow],
    )
    new_error_down, update_up, update_down = call(
        last_kernel, [shaped(1, ff, rows, dtype=BF16), shaped(rows, ff, dtype=BF16), shaped(ff, rows, dtype=BF16)],
        gd, ed, lhs_up, rhs_up, lhs_down, rhs_down, clip, name="last", flops=product, grid=(STEPS,),
        in_specs=[VMEM] * 7, out_specs=[replica_blocks(ff, rows), row_blocks(rows, ff), row_blocks(ff, rows)],
    )
    return new_error_up, update_up, new_error_down, update_down


def solution(mesh):
    placed = (
        P("dp", None, "tensor"),
        P("dp", None, "tensor"),
        P("dp", "tensor", None),
        P("dp", "tensor", None),
        P("tensor", None),
        P(),
    )
    return jax.shard_map(
        on_device,
        mesh=mesh,
        in_specs=placed,
        out_specs=(
            P("dp", None, "tensor"),
            P(None, "tensor"),
            P("dp", "tensor", None),
            P("tensor", None),
        ),
        check_vma=False,
    )
```

```python
import functools

import jax
import jax.numpy as jnp
from jax import lax
from jax.experimental import pallas as pl
from jax.experimental.pallas import tpu as pltpu
from jax.sharding import PartitionSpec as P

F32 = jnp.float32
BF16 = jnp.bfloat16
HIGHEST = lax.Precision.HIGHEST
CLIP_RMS = 0.1
STEPS = 4
MIB = 1024 * 1024
NT = ((1,), (1,))


def split3(x):
    first = x.astype(BF16)
    rest = x - first.astype(F32)
    second = rest.astype(BF16)
    return first, second, (rest - second.astype(F32)).astype(BF16)


def tree_sum(values):
    values = list(values)
    while len(values) > 1:
        values = [values[i] + values[i + 1] for i in range(0, len(values), 2)]
    return values[0]


def dot(a, b, dims=((1,), (0,)), precision=None):
    return lax.dot_general(a, b, (dims, ((), ())), precision=precision, preferred_element_type=F32)


def fold(x, rows):
    return jnp.concatenate([x[i : i + rows] for i in range(0, x.shape[0], rows)], axis=1)


def unfold(x, rows):
    count = rows // x.shape[0]
    width = x.shape[1] // count
    return jnp.concatenate([x[:, i * width : (i + 1) * width] for i in range(count)], axis=0)


def place(axis):
    index = lax.axis_index(axis)
    return lax.bitwise_and(index, 1), lax.shift_right_logical(index, 1)


def split_replicas(total, stage, keep, send):
    parity, _ = place("dp")
    half, per, _ = keep.shape
    for c in range(2 * half):
        stage[c] = total[c * per : (c + 1) * per, :]
    for c in range(half):
        keep[c] = stage[2 * c + parity]
        send[c] = stage[2 * c + 1 - parity]


def join_replicas(mine, other, stage, total):
    parity, _ = place("dp")
    half, per, _ = mine.shape
    width = total.shape[1]
    for c in range(half):
        stage[2 * c + parity] = mine[c, :, :width]
        stage[2 * c + 1 - parity] = other[c, :, :width]
    for c in range(2 * half):
        total[c * per : (c + 1) * per, :] = stage[c]


def split_shards(total, extra, outs):
    me = lax.axis_index("tensor")
    rows, width = outs[0].shape[0], total.shape[1]
    for j, out in enumerate(outs):
        owner = lax.bitwise_xor(me, j)
        out[:, :width] = total[pl.ds(pl.multiple_of(owner * rows, rows), rows), :]
        if extra is not None:
            out[:, width:] = fold(extra, rows)


def join_shards(pieces, total):
    me = lax.axis_index("tensor")
    rows, width = pieces[0].shape[0], total.shape[1]
    for j, piece in enumerate(pieces):
        owner = lax.bitwise_xor(me, j)
        total[pl.ds(pl.multiple_of(owner * rows, rows), rows), :] = piece[:, :width]


def left_kernel(n_shards, gu, eu, qu, gd, ed, qd, *refs):
    *outs, gu_in, eu_in, qu_in, pieces_up, total_up, gd_in, ed_in, qd_in, pieces_down, total_down, stage, q_sems, sems = refs
    up, down = (qu_in, pieces_up, total_up), (qd_in, pieces_down, total_down)
    firsts = [pltpu.make_async_copy(src, dst, q_sems.at[i]) for i, (src, dst) in enumerate(((qd, qd_in), (qu, qu_in)))]
    stages = []
    for g, e, g_in, e_in, part, count in ((gd, ed, gd_in, ed_in, down, 3), (gu, eu, gu_in, eu_in, up, 2)):
        block = g_in.shape[0] // count
        for i in range(count):
            rows = pl.ds(i * block, block)
            n = len(stages)
            copies = [pltpu.make_async_copy(src.at[0, rows, :], dst.at[rows, :], sems.at[n, k]) for k, (src, dst) in enumerate(((g, g_in), (e, e_in)))]
            stages.append((copies, g_in, e_in, slice(i * block, (i + 1) * block), part))

    def fetch(n):
        if n < len(stages):
            for copy in stages[n][0]:
                copy.start()

    firsts[0].start()
    fetch(0)
    firsts[1].start()
    for n, (first, (q, pieces, _)) in enumerate(zip(firsts, (down, up))):
        first.wait()
        fetch(n + 1)
        split_rows(q, pieces)
    for n, (copies, g, e, rows, (_, pieces, total)) in enumerate(stages):
        for copy in copies:
            copy.wait()
        fetch(n + 3)
        total[:, rows] = add_pieces(dot(pieces[...], g[rows, :], NT) + dot(pieces[...], e[rows, :], NT))
    split_shards(total_up, None, outs[:n_shards])
    split_replicas(total_down, stage, *outs[n_shards:])


def fetch_kernel(*refs):
    half = len(refs) // 2
    for source, out in zip(refs[:half], refs[half:]):
        out[...] = source[...]


def sum_shards_kernel(n_shards, *refs):
    terms, (out, gram) = refs[:n_shards], refs[n_shards:]
    total = tree_sum(term[...] for term in terms)
    out[...] = total[:, : out.shape[1]]
    gram[...] = unfold(total[:, out.shape[1] :], gram.shape[0])


def first_shards_kernel(*refs):
    refs[-1][...] = tree_sum(term[...] for term in refs[:-1])


def own_and_other(j, bit):
    mine = lax.bitwise_and(lax.shift_right_logical(lax.axis_index("dp"), bit), 1)
    return 2 * j + mine, 2 * j + 1 - mine


def split_chunks(bit, chunks, keep, send):
    for j in range(keep.shape[0]):
        mine, other = own_and_other(j, bit)
        keep[j] = chunks[mine]
        send[j] = chunks[other]


def halve_with_shard_kernel(bit, keep, got, shard, keep_out, send_out, chunks):
    half, per, ff = keep.shape
    block = shard.shape[1] // half
    for c in range(half):
        chunks[c, :, :ff] = keep[c] + got[c]
        chunks[c, :, ff:] = fold(shard[:, c * block : (c + 1) * block], per)
    split_chunks(bit, chunks, keep_out, send_out)


def halve_kernel(bit, keep, got, keep_out, send_out, chunks):
    chunks[...] = keep[...] + got[...]
    split_chunks(bit, chunks, keep_out, send_out)


def sum_kernel(scale, mine, other, out):
    out[...] = (mine[...] + other[...]) * scale


def double_kernel(bit, mine, other, out):
    for j in range(mine.shape[0]):
        here, there = own_and_other(j, bit)
        out[here] = mine[j]
        out[there] = other[j]


def apart_kernel(stack, out, shard):
    half, _, ff = out.shape
    out[...] = stack[:, :, :ff]
    shard[...] = jnp.concatenate([unfold(stack[c, :, ff:], shard.shape[0]) for c in range(half)], axis=1)


def shard_rows(mine, other, ff, rows):
    half = mine.shape[0]
    return jnp.concatenate([unfold(mine[c, :, ff:] + other[c, :, ff:], rows) for c in range(half)], axis=1)


def split_rows(left, pieces):
    rank = left.shape[0]
    for i, piece in enumerate(split3(left[...])):
        pieces[i * rank : (i + 1) * rank, :] = piece


def add_pieces(t):
    rank = t.shape[0] // 3
    return t[:rank] + (t[rank : 2 * rank] + t[2 * rank :])


def right_down_kernel(_, mine, other, g, e, left, *refs):
    *outs, pieces, total, stage = refs
    join_replicas(mine, other, stage, left)
    split_rows(left, pieces)
    total[...] = add_pieces(dot(pieces[...], g[0]) + dot(pieces[...], e[0]))
    split_shards(total, dot(left[...], left[...], NT, HIGHEST), outs)


def right_up_kernel(n_shards, *refs):
    shards, refs = refs[:n_shards], refs[n_shards:]
    g, e, left, gram, keep, send, pieces, total, stage = refs
    join_shards(shards, left)
    split_rows(left, pieces)
    block = total.shape[1] // STEPS
    for i in range(STEPS):
        part = slice(i * block, (i + 1) * block)
        total[:, part] = add_pieces(dot(pieces[...], g[0, :, part]) + dot(pieces[...], e[0, :, part]))
    split_replicas(total, stage, keep, send)
    gram[...] = dot(left[...], left[...], NT, HIGHEST)


def inverse_factors(grams):
    rank = grams[0].shape[0]
    count = rank // 8
    panel = 4
    lane = lax.broadcasted_iota(jnp.int32, (8, 2 * rank), 1)
    row = lax.broadcasted_iota(jnp.int32, (8, 2 * rank), 0)
    states, pivots = [], []
    for gram in grams:
        wide = jnp.concatenate([gram, jnp.zeros_like(gram)], axis=1)
        states.append([wide[i : i + 8] + (lane == row + (rank + i)).astype(F32) for i in range(0, rank, 8)])
        pivots.append([])
    for start in range(0, rank, panel):
        at = start // 8
        below = range(at, count)
        spread = [
            [{i: jnp.broadcast_to(blocks[i][:, start + j : start + j + 1], (8, 2 * rank)) for i in below} for j in range(panel)]
            for blocks in states
        ]
        for j in range(panel):
            inner = (start + j) % 8
            for blocks, columns, found in zip(states, spread, pivots):
                pivot = columns[j][at][inner : inner + 1, :]
                found.append(pivot)
                inverse = 1.0 / pivot
                factor = {i: jnp.where(row > inner, columns[j][i], 0.0) if i == at else columns[j][i] for i in below}
                for later in columns[j + 1 :]:
                    head = later[at][inner : inner + 1, :] * inverse
                    for i in below:
                        later[i] = later[i] - factor[i] * head
                scaled = blocks[at][inner : inner + 1, :] * inverse
                for i in below:
                    blocks[i] = blocks[i] - factor[i] * scaled
    results = []
    for blocks, found in zip(states, pivots):
        rows = [block / jnp.sqrt(jnp.concatenate(found[8 * i : 8 * i + 8], axis=0)) for i, block in enumerate(blocks)]
        results.append(jnp.concatenate(rows, axis=0)[:, rank:])
    return results


def basis_kernel(left_up, left_down, gram_up, gram_down, *refs):
    inv_up, inv_down, lhs_up, lhs_down = refs[-4:]
    inverses = inverse_factors([gram_up[...], gram_down[...]])
    rank = left_up.shape[0]
    for inverse, inv, left, lhs in zip(inverses, (inv_up, inv_down), (left_up, left_down), (lhs_up, lhs_down)):
        inv[...] = inverse
        first, second, _ = split3(dot(inverse, left[...], precision=HIGHEST).T)
        lhs[:, :rank] = first
        lhs[:, rank : 2 * rank] = first
        lhs[:, 2 * rank : 3 * rank] = second
        lhs[:, 3 * rank :] = second


def right_factor(inv, total, rhs):
    rank = inv.shape[0]
    right = dot(inv[...], total[...], precision=HIGHEST)
    first, second, _ = split3(right)
    rhs[:rank, :] = first
    rhs[rank : 2 * rank, :] = second
    rhs[2 * rank : 3 * rank, :] = first
    rhs[3 * rank :, :] = second
    return jnp.sum(right * right)


def factor_up_kernel(mine, other, inv, rhs, shard, total, stage):
    join_replicas(mine, other, stage, total)
    square = right_factor(inv, total, rhs)
    rows, ff = shard.shape[0], total.shape[1]
    width = shard.shape[1] - 128
    shard[:, :width] = shard_rows(mine, other, ff, rows)
    shard[:, width:] = jnp.full((rows, 128), square, F32)


def factor_down_kernel(limit, n_shards, *refs):
    shards, refs = refs[:n_shards], refs[n_shards:]
    inv, _, rhs, clip, total = refs
    join_shards(shards, total)
    square = right_factor(inv, total, rhs)
    width = total.shape[1]
    norm_sq = square + tree_sum(shard[:8, width:] for shard in shards)
    clip[...] = jnp.minimum(jnp.float32(1.0), limit / jnp.sqrt(norm_sq))


def rows_of(block):
    return pl.ds(pl.multiple_of(pl.program_id(0) * block, block), block)


def error_up_kernel(g, e, lhs, rhs, error, made):
    made[...] = jnp.zeros_like(made)
    part = rows_of(error.shape[1])
    rebuilt = dot(lhs[part, :], rhs[...])
    error[0] = (g[0, part, :].astype(F32) + e[0, part, :].astype(F32) - rebuilt).astype(BF16)


def last_kernel(g, e, lhs_up, rhs_up, lhs_down, rhs_down, clip, error, update_up, update_down):
    factor = clip[:1, :1]
    part = rows_of(update_down.shape[0])
    rebuilt = dot(lhs_down[part, :], rhs_down[...])
    update_down[...] = (factor * rebuilt).astype(BF16)
    error[0] = (g[0, part, :].astype(F32) + e[0, part, :].astype(F32) - rebuilt).astype(BF16)
    part = rows_of(update_up.shape[0])
    update_up[...] = (factor * dot(lhs_up[part, :], rhs_up[...])).astype(BF16)


def shaped(*dims, dtype=F32):
    return jax.ShapeDtypeStruct(dims, dtype)


def whole(shape):
    return pl.BlockSpec(shape, lambda *_: (0,) * len(shape))


def row_blocks(rows, columns):
    return pl.BlockSpec((rows // STEPS, columns), lambda i: (i, 0))


def replica_blocks(rows, columns):
    return pl.BlockSpec((1, rows // STEPS, columns), lambda i: (0, i, 0))


VMEM = pl.BlockSpec(memory_space=pltpu.VMEM)
ANY = pl.BlockSpec(memory_space=pl.ANY)


def call(kernel, out_shape, *args, flops=0, limit=12, name=None, **more):
    arrays = list(args) + jax.tree.leaves(out_shape)
    size = sum(a.size * a.dtype.itemsize for a in arrays)
    cost = pl.CostEstimate(flops=flops, bytes_accessed=size, transcendentals=0)
    params = pltpu.CompilerParams(vmem_limit_bytes=limit * MIB)
    return pl.pallas_call(kernel, out_shape=out_shape, compiler_params=params, cost_estimate=cost, name=name, **more)(*args)


def swap(x, axis, distance):
    pairs = [(i, i ^ distance) for i in range(lax.axis_size(axis))]
    return lax.ppermute(x, axis, pairs)


def from_shards(parts):
    return [parts[0]] + [swap(parts[j], "tensor", j) for j in range(1, len(parts))]


def mean_replicas(keep, got, shard):
    n_dp = lax.axis_size("dp")
    last = n_dp.bit_length() - 2
    count, per, ff = keep.shape
    columns = ff + shard.shape[0] * shard.shape[1] // (count * per)
    for bit in range(1, last):
        out = shaped(count // 2, per, columns)
        kernel, more = (halve_with_shard_kernel, (shard,)) if bit == 1 else (halve_kernel, ())
        keep, send = call(
            functools.partial(kernel, bit), [out, out], keep, got, *more, name="halve",
            scratch_shapes=[pltpu.VMEM((count, per, columns), F32)],
        )
        got = swap(send, "dp", 1 << bit)
        count //= 2
    total = call(functools.partial(sum_kernel, 1.0), out, keep, got, name="half_sum")
    mine = call(functools.partial(sum_kernel, 1.0 / n_dp), out, total, swap(total, "dp", 1 << last), name="mean")
    for bit in range(last - 1, 0, -1):
        count *= 2
        out = shaped(count, per, columns)
        mine = call(functools.partial(double_kernel, bit), out, mine, swap(mine, "dp", 1 << bit), name="double")
    return mine


def on_device(gu, eu, gd, ed, qu, qd):
    qu, qd = qu.T, qd.T
    n_dp, n_shards = lax.axis_size("dp"), lax.axis_size("tensor")
    _, rows, ff = gu.shape
    rank = qu.shape[0]
    half, per, rows_here = n_dp // 2, rank // n_dp, rank // n_shards
    shard_rows_here = shaped(rows_here, rows)
    replica_half = shaped(half, per, ff)
    stage = pltpu.VMEM((n_dp, per, ff), F32)
    wide = pltpu.VMEM((rank, ff), F32)
    narrow = pltpu.VMEM((rank, rows), F32)
    product = 4 * rows * ff * 4 * rank

    buffers = [
        [pltpu.VMEM(g.shape[1:], BF16)] * 2 + [pltpu.VMEM(q.shape, F32), pltpu.VMEM((3 * rank, q.shape[1]), BF16), total]
        for g, q, total in ((gu, qu, narrow), (gd, qd, wide))
    ]
    *parts, keep, send = call(
        functools.partial(left_kernel, n_shards), [shard_rows_here] * n_shards + [replica_half] * 2, gu, eu, qu, gd, ed, qd,
        name="left", flops=2 * product, limit=61, in_specs=[pl.BlockSpec(memory_space=pltpu.HBM)] * 6,
        scratch_shapes=buffers[0] + buffers[1] + [stage, pltpu.SemaphoreType.DMA((2,)), pltpu.SemaphoreType.DMA((5, 2))],
    )
    got = swap(send, "dp", 1)
    parts = from_shards(parts)
    parts[0], keep = call(fetch_kernel, [shard_rows_here, replica_half], parts[0], keep, name="fetch", flops=product // 4)
    shard = call(first_shards_kernel, shard_rows_here, *parts, name="shard_sum")
    mine, shard = call(apart_kernel, [replica_half, shard_rows_here], mean_replicas(keep, got, shard), name="apart")
    shard = call(first_shards_kernel, shard_rows_here, shard, swap(shard, "dp", 1), name="replica_sum")
    other = swap(mine, "dp", 1)
    left_rows = from_shards([shard] * n_shards)
    left_up, gram_up, keep, send = call(
        functools.partial(right_up_kernel, n_shards), [shaped(rank, rows), shaped(rank, rank), replica_half, replica_half],
        *left_rows, gu, eu, name="right_up", flops=product,
        scratch_shapes=[pltpu.VMEM((3 * rank, rows), BF16), wide, stage],
    )
    left_down, *parts = call(
        right_down_kernel, [shaped(rank, ff)] + [shaped(rows_here, rows + rank * n_shards)] * n_shards, left_up, mine, other, gd, ed,
        name="right_down", flops=product, in_specs=[ANY] + [VMEM] * 4, scratch_shapes=[pltpu.VMEM((3 * rank, ff), BF16), narrow, stage],
    )
    got = swap(send, "dp", 1)
    shard, gram_down = call(
        functools.partial(sum_shards_kernel, n_shards), [shard_rows_here, shaped(rank, rank)], *from_shards(parts), name="shard_sum"
    )
    mine = mean_replicas(keep, got, shard)
    other = swap(mine, "dp", 1)
    inv_up, inv_down, lhs_up, lhs_down = call(
        basis_kernel,
        [shaped(rank, rank)] * 2 + [shaped(rows, 4 * rank, dtype=BF16), shaped(ff, 4 * rank, dtype=BF16)],
        left_up, left_down, gram_up, gram_down, gu, eu, gd, ed, mine, name="basis", in_specs=[VMEM] * 8 + [ANY],
    )
    rhs_up, shard = call(
        factor_up_kernel, [shaped(4 * rank, ff, dtype=BF16), shaped(rows_here, rows + 128)], mine, other, inv_up,
        name="factor_up", scratch_shapes=[wide, stage],
    )
    right_rows = from_shards([shard] * n_shards)
    new_error_up, made = call(
        error_up_kernel, [shaped(1, rows, ff, dtype=BF16), shaped(8, 128)], gu, eu, lhs_up, rhs_up, name="error_up", flops=product // 2,
        grid=(STEPS,), in_specs=[VMEM] * 4, out_specs=[replica_blocks(rows, ff), whole((8, 128))],
    )
    limit = CLIP_RMS * (2.0 * rows * ff * n_shards) ** 0.5
    rhs_down, clip = call(
        functools.partial(factor_down_kernel, limit, n_shards), [shaped(4 * rank, rows, dtype=BF16), shaped(8, 128)],
        *right_rows, inv_down, made, name="factor_down", in_specs=[VMEM] * (n_shards + 1) + [ANY], scratch_shapes=[narrow],
    )
    new_error_down, update_up, update_down = call(
        last_kernel, [shaped(1, ff, rows, dtype=BF16), shaped(rows, ff, dtype=BF16), shaped(ff, rows, dtype=BF16)],
        gd, ed, lhs_up, rhs_up, lhs_down, rhs_down, clip, name="last", flops=product, grid=(STEPS,),
        in_specs=[VMEM] * 7, out_specs=[replica_blocks(ff, rows), row_blocks(rows, ff), row_blocks(ff, rows)],
    )
    return new_error_up, update_up, new_error_down, update_down


def solution(mesh):
    placed = (
        P("dp", None, "tensor"),
        P("dp", None, "tensor"),
        P("dp", "tensor", None),
        P("dp", "tensor", None),
        P("tensor", None),
        P(),
    )
    return jax.shard_map(
        on_device,
        mesh=mesh,
        in_specs=placed,
        out_specs=(
            P("dp", None, "tensor"),
            P(None, "tensor"),
            P("dp", "tensor", None),
            P("tensor", None),
        ),
        check_vma=False,
    )
```

```python
import functools

import jax
import jax.numpy as jnp
from jax import lax
from jax.experimental import pallas as pl
from jax.experimental.pallas import tpu as pltpu
from jax.sharding import PartitionSpec as P

F32 = jnp.float32
BF16 = jnp.bfloat16
HIGHEST = lax.Precision.HIGHEST
CLIP_RMS = 0.1
STEPS = 4
MIB = 1024 * 1024
NT = ((1,), (1,))


def split3(x):
    first = x.astype(BF16)
    rest = x - first.astype(F32)
    second = rest.astype(BF16)
    return first, second, (rest - second.astype(F32)).astype(BF16)


def tree_sum(values):
    values = list(values)
    while len(values) > 1:
        values = [values[i] + values[i + 1] for i in range(0, len(values), 2)]
    return values[0]


def dot(a, b, dims=((1,), (0,)), precision=None):
    return lax.dot_general(a, b, (dims, ((), ())), precision=precision, preferred_element_type=F32)


def fold(x, rows):
    return jnp.concatenate([x[i : i + rows] for i in range(0, x.shape[0], rows)], axis=1)


def unfold(x, rows):
    count = rows // x.shape[0]
    width = x.shape[1] // count
    return jnp.concatenate([x[:, i * width : (i + 1) * width] for i in range(count)], axis=0)


def place(axis):
    index = lax.axis_index(axis)
    return lax.bitwise_and(index, 1), lax.shift_right_logical(index, 1)


def split_replicas(total, stage, keep, send):
    parity, _ = place("dp")
    half, per, _ = keep.shape
    for c in range(2 * half):
        stage[c] = total[c * per : (c + 1) * per, :]
    for c in range(half):
        keep[c] = stage[2 * c + parity]
        send[c] = stage[2 * c + 1 - parity]


def join_replicas(mine, other, stage, total):
    parity, _ = place("dp")
    half, per, _ = mine.shape
    width = total.shape[1]
    for c in range(half):
        stage[2 * c + parity] = mine[c, :, :width]
        stage[2 * c + 1 - parity] = other[c, :, :width]
    for c in range(2 * half):
        total[c * per : (c + 1) * per, :] = stage[c]


def split_shards(total, extra, outs):
    me = lax.axis_index("tensor")
    rows, width = outs[0].shape[0], total.shape[1]
    for j, out in enumerate(outs):
        owner = lax.bitwise_xor(me, j)
        out[:, :width] = total[pl.ds(pl.multiple_of(owner * rows, rows), rows), :]
        if extra is not None:
            out[:, width:] = fold(extra, rows)


def join_shards(pieces, total):
    me = lax.axis_index("tensor")
    rows, width = pieces[0].shape[0], total.shape[1]
    for j, piece in enumerate(pieces):
        owner = lax.bitwise_xor(me, j)
        total[pl.ds(pl.multiple_of(owner * rows, rows), rows), :] = piece[:, :width]


def left_product(g, e, q, g_in, e_in, q_in, pieces, total, sems):
    count = sems.shape[0] - 1
    block = g_in.shape[0] // count
    first = pltpu.make_async_copy(q, q_in, sems.at[count, 0])
    stages = []
    for i in range(count):
        rows = pl.ds(i * block, block)
        stages.append([pltpu.make_async_copy(src.at[0, rows, :], dst.at[rows, :], sems.at[i, k]) for k, (src, dst) in enumerate(((g, g_in), (e, e_in)))])

    def fetch(n):
        if n < count:
            for copy in stages[n]:
                copy.start()

    first.start()
    fetch(0)
    first.wait()
    fetch(1)
    split_rows(q_in, pieces)
    for i, copies in enumerate(stages):
        for copy in copies:
            copy.wait()
        fetch(i + 2)
        rows = slice(i * block, (i + 1) * block)
        total[:, rows] = add_pieces(dot(pieces[...], g_in[rows, :], NT) + dot(pieces[...], e_in[rows, :], NT))


def left_up_kernel(g, e, q, *refs):
    *outs, g_in, e_in, q_in, pieces, total, sems = refs
    left_product(g, e, q, g_in, e_in, q_in, pieces, total, sems)
    split_shards(total, None, outs)


def left_down_kernel(g, e, q, keep, send, g_in, e_in, q_in, pieces, total, sems, stage):
    left_product(g, e, q, g_in, e_in, q_in, pieces, total, sems)
    split_replicas(total, stage, keep, send)


def fetch_kernel(source, out):
    out[...] = source[...]


def sum_shards_kernel(n_shards, *refs):
    terms, (out, gram) = refs[:n_shards], refs[n_shards:]
    total = tree_sum(term[...] for term in terms)
    out[...] = total[:, : out.shape[1]]
    gram[...] = unfold(total[:, out.shape[1] :], gram.shape[0])


def first_shards_kernel(*refs):
    refs[-1][...] = tree_sum(term[...] for term in refs[:-1])


def own_and_other(j, bit):
    mine = lax.bitwise_and(lax.shift_right_logical(lax.axis_index("dp"), bit), 1)
    return 2 * j + mine, 2 * j + 1 - mine


def split_chunks(bit, chunks, keep, send):
    for j in range(keep.shape[0]):
        mine, other = own_and_other(j, bit)
        keep[j] = chunks[mine]
        send[j] = chunks[other]


def halve_kernel(bit, keep, got, keep_out, send_out, chunks):
    chunks[...] = keep[...] + got[...]
    split_chunks(bit, chunks, keep_out, send_out)


def sum_kernel(scale, mine, other, out):
    out[...] = (mine[...] + other[...]) * scale


def double_kernel(bit, mine, other, out):
    for j in range(mine.shape[0]):
        here, there = own_and_other(j, bit)
        out[here] = mine[j]
        out[there] = other[j]


def half_sum_kernel(keep, got, shard, out):
    count, per, ff = keep.shape
    block = shard.shape[1] // count
    for c in range(count):
        out[c, :, :ff] = keep[c] + got[c]
        out[c, :, ff:] = fold(shard[:, c * block : (c + 1) * block], per)


def join_shard(chunks, ff, rows):
    return jnp.concatenate([unfold(chunks[c, :, ff:], rows) for c in range(chunks.shape[0])], axis=1)


def double_apart_kernel(bit, mine, other, out, shard):
    ff = out.shape[2]
    for j in range(mine.shape[0]):
        here, there = own_and_other(j, bit)
        out[here] = mine[j, :, :ff]
        out[there] = other[j, :, :ff]
    shard[...] = join_shard(mine, ff, shard.shape[0]) + join_shard(other, ff, shard.shape[0])


def add_columns_kernel(chunks, shard, out):
    count, per, ff = chunks.shape
    block = shard.shape[1] // count
    for c in range(count):
        out[c, :, :ff] = chunks[c]
        out[c, :, ff:] = fold(shard[:, c * block : (c + 1) * block], per)


def shard_rows(mine, other, ff, rows):
    half = mine.shape[0]
    return jnp.concatenate([unfold(mine[c, :, ff:] + other[c, :, ff:], rows) for c in range(half)], axis=1)


def split_rows(left, pieces):
    rank = left.shape[0]
    for i, piece in enumerate(split3(left[...])):
        pieces[i * rank : (i + 1) * rank, :] = piece


def add_pieces(t):
    rank = t.shape[0] // 3
    return t[:rank] + (t[rank : 2 * rank] + t[2 * rank :])


def right_down_kernel(mine, other, g, e, left, *refs):
    *outs, pieces, total, stage = refs
    join_replicas(mine, other, stage, left)
    split_rows(left, pieces)
    total[...] = add_pieces(dot(pieces[...], g[0]) + dot(pieces[...], e[0]))
    split_shards(total, dot(left[...], left[...], NT, HIGHEST), outs)


def right_up_kernel(n_shards, *refs):
    shards, refs = refs[:n_shards], refs[n_shards:]
    g, e, left, gram, keep, send, pieces, total, stage = refs
    join_shards(shards, left)
    split_rows(left, pieces)
    block = total.shape[1] // STEPS
    for i in range(STEPS):
        part = slice(i * block, (i + 1) * block)
        total[:, part] = add_pieces(dot(pieces[...], g[0, :, part]) + dot(pieces[...], e[0, :, part]))
    split_replicas(total, stage, keep, send)
    gram[...] = dot(left[...], left[...], NT, HIGHEST)


def inverse_factors(grams):
    rank = grams[0].shape[0]
    count = rank // 8
    panel = 4
    lane = lax.broadcasted_iota(jnp.int32, (8, 2 * rank), 1)
    row = lax.broadcasted_iota(jnp.int32, (8, 2 * rank), 0)
    states, pivots = [], []
    for gram in grams:
        wide = jnp.concatenate([gram, jnp.zeros_like(gram)], axis=1)
        states.append([wide[i : i + 8] + (lane == row + (rank + i)).astype(F32) for i in range(0, rank, 8)])
        pivots.append([])
    for start in range(0, rank, panel):
        at = start // 8
        below = range(at, count)
        spread = [
            [{i: jnp.broadcast_to(blocks[i][:, start + j : start + j + 1], (8, 2 * rank)) for i in below} for j in range(panel)]
            for blocks in states
        ]
        for j in range(panel):
            inner = (start + j) % 8
            for blocks, columns, found in zip(states, spread, pivots):
                pivot = columns[j][at][inner : inner + 1, :]
                found.append(pivot)
                inverse = 1.0 / pivot
                factor = {i: jnp.where(row > inner, columns[j][i], 0.0) if i == at else columns[j][i] for i in below}
                for later in columns[j + 1 :]:
                    head = later[at][inner : inner + 1, :] * inverse
                    for i in below:
                        later[i] = later[i] - factor[i] * head
                scaled = blocks[at][inner : inner + 1, :] * inverse
                for i in below:
                    blocks[i] = blocks[i] - factor[i] * scaled
    results = []
    for blocks, found in zip(states, pivots):
        rows = [block / jnp.sqrt(jnp.concatenate(found[8 * i : 8 * i + 8], axis=0)) for i, block in enumerate(blocks)]
        results.append(jnp.concatenate(rows, axis=0)[:, rank:])
    return results


def basis_kernel(left_up, left_down, gram_up, gram_down, *refs):
    inv_up, inv_down, lhs_up, lhs_down = refs[-4:]
    inverses = inverse_factors([gram_up[...], gram_down[...]])
    rank = left_up.shape[0]
    for inverse, inv, left, lhs in zip(inverses, (inv_up, inv_down), (left_up, left_down), (lhs_up, lhs_down)):
        inv[...] = inverse
        first, second, _ = split3(dot(inverse, left[...], precision=HIGHEST).T)
        lhs[:, :rank] = first
        lhs[:, rank : 2 * rank] = first
        lhs[:, 2 * rank : 3 * rank] = second
        lhs[:, 3 * rank :] = second


def right_factor(inv, total, rhs):
    rank = inv.shape[0]
    right = dot(inv[...], total[...], precision=HIGHEST)
    first, second, _ = split3(right)
    rhs[:rank, :] = first
    rhs[rank : 2 * rank, :] = second
    rhs[2 * rank : 3 * rank, :] = first
    rhs[3 * rank :, :] = second
    return jnp.sum(right * right)


def factor_up_kernel(mine, other, inv, rhs, shard, total, stage):
    join_replicas(mine, other, stage, total)
    square = right_factor(inv, total, rhs)
    rows, ff = shard.shape[0], total.shape[1]
    width = shard.shape[1] - 128
    shard[:, :width] = shard_rows(mine, other, ff, rows)
    shard[:, width:] = jnp.full((rows, 128), square, F32)


def factor_down_kernel(limit, n_shards, *refs):
    shards, refs = refs[:n_shards], refs[n_shards:]
    inv, _, rhs, clip, total = refs
    join_shards(shards, total)
    square = right_factor(inv, total, rhs)
    width = total.shape[1]
    norm_sq = square + tree_sum(shard[:8, width:] for shard in shards)
    clip[...] = jnp.minimum(jnp.float32(1.0), limit / jnp.sqrt(norm_sq))


def rows_of(block):
    return pl.ds(pl.multiple_of(pl.program_id(0) * block, block), block)


def error_up_kernel(g, e, lhs, rhs, error, made):
    made[...] = jnp.zeros_like(made)
    part = rows_of(error.shape[1])
    rebuilt = dot(lhs[part, :], rhs[...])
    error[0] = (g[0, part, :].astype(F32) + e[0, part, :].astype(F32) - rebuilt).astype(BF16)


def last_kernel(g, e, lhs_up, rhs_up, lhs_down, rhs_down, clip, error, update_up, update_down):
    factor = clip[:1, :1]
    part = rows_of(update_down.shape[0])
    rebuilt = dot(lhs_down[part, :], rhs_down[...])
    update_down[...] = (factor * rebuilt).astype(BF16)
    error[0] = (g[0, part, :].astype(F32) + e[0, part, :].astype(F32) - rebuilt).astype(BF16)
    part = rows_of(update_up.shape[0])
    update_up[...] = (factor * dot(lhs_up[part, :], rhs_up[...])).astype(BF16)


def shaped(*dims, dtype=F32):
    return jax.ShapeDtypeStruct(dims, dtype)


def whole(shape):
    return pl.BlockSpec(shape, lambda *_: (0,) * len(shape))


def row_blocks(rows, columns):
    return pl.BlockSpec((rows // STEPS, columns), lambda i: (i, 0))


def replica_blocks(rows, columns):
    return pl.BlockSpec((1, rows // STEPS, columns), lambda i: (0, i, 0))


VMEM = pl.BlockSpec(memory_space=pltpu.VMEM)
ANY = pl.BlockSpec(memory_space=pl.ANY)


def call(kernel, out_shape, *args, after=(), in_specs=None, flops=0, limit=12, name=None, **more):
    arrays = list(args) + jax.tree.leaves(out_shape)
    size = sum(a.size * a.dtype.itemsize for a in arrays)
    skip = len(after)
    return pl.pallas_call(
        lambda *refs: kernel(*refs[skip:]), out_shape=out_shape, in_specs=[ANY] * skip + (in_specs or [VMEM] * len(args)),
        compiler_params=pltpu.CompilerParams(vmem_limit_bytes=limit * MIB),
        cost_estimate=pl.CostEstimate(flops=flops, bytes_accessed=size, transcendentals=0), name=name, **more,
    )(*after, *args)


def swap(x, axis, distance):
    pairs = [(i, i ^ distance) for i in range(lax.axis_size(axis))]
    return lax.ppermute(x, axis, pairs)


def from_shards(parts):
    return [parts[0]] + [swap(parts[j], "tensor", j) for j in range(1, len(parts))]


def scatter_replicas(keep, send, got, after):
    n_dp = lax.axis_size("dp")
    for bit in range(n_dp.bit_length() - 2):
        got = swap(send, "dp", 1 << bit) if bit else got
        if bit == n_dp.bit_length() - 3:
            return keep, got
        count, per, ff = keep.shape
        out = shaped(count // 2, per, ff)
        keep, send = call(
            functools.partial(halve_kernel, bit + 1), [out, out], keep, got, after=after if bit == 0 else (), name="halve",
            scratch_shapes=[pltpu.VMEM(keep.shape, F32)],
        )


def gather_replicas(keep, got, shard):
    n_dp = lax.axis_size("dp")
    last = n_dp.bit_length() - 2
    count, per, ff = keep.shape
    columns = ff + shard.shape[0] * shard.shape[1] // (count * per)
    both = shaped(count, per, columns)
    total = call(half_sum_kernel, both, keep, got, shard, name="half_sum")
    mine = call(functools.partial(sum_kernel, 1.0 / n_dp), both, total, swap(total, "dp", 1 << last), name="mean")
    for bit in range(last - 1, 0, -1):
        other = swap(mine, "dp", 1 << bit)
        count *= 2
        mine, shard = call(functools.partial(double_apart_kernel, bit), [shaped(count, per, ff), shaped(*shard.shape)], mine, other, name="double")
        if bit > 1:
            mine = add_columns(mine, shard)
    return mine, shard


def add_columns(mine, shard):
    count, per, ff = mine.shape
    columns = ff + shard.shape[0] * shard.shape[1] // (count * per)
    return call(add_columns_kernel, shaped(count, per, columns), mine, shard, name="add_columns")


def on_device(gu, eu, gd, ed, qu, qd):
    qu, qd = qu.T, qd.T
    n_dp, n_shards = lax.axis_size("dp"), lax.axis_size("tensor")
    _, rows, ff = gu.shape
    rank = qu.shape[0]
    half, per, rows_here = n_dp // 2, rank // n_dp, rank // n_shards
    shard_rows_here = shaped(rows_here, rows)
    replica_half = shaped(half, per, ff)
    stage = pltpu.VMEM((n_dp, per, ff), F32)
    wide = pltpu.VMEM((rank, ff), F32)
    narrow = pltpu.VMEM((rank, rows), F32)
    product = 4 * rows * ff * 4 * rank

    def left(kernel, outs, g, e, q, total, count, scratch, name):
        buffers = [pltpu.VMEM(g.shape[1:], BF16)] * 2 + [pltpu.VMEM(q.shape, F32), pltpu.VMEM((3 * rank, q.shape[1]), BF16), total]
        return call(
            kernel, outs, g, e, q, name=name, flops=product, limit=61, in_specs=[pl.BlockSpec(memory_space=pltpu.HBM)] * 3,
            scratch_shapes=buffers + [pltpu.SemaphoreType.DMA((count + 1, 2))] + scratch,
        )

    keep, send = left(left_down_kernel, [replica_half] * 2, gd, ed, qd, wide, 3, [stage], "left_down")
    parts = left(left_up_kernel, [shard_rows_here] * n_shards, gu, eu, qu, narrow, 2, [], "left_up")
    keep = call(fetch_kernel, replica_half, keep, after=(parts[0],), name="fetch", flops=product // 4)
    got = swap(send, "dp", 1)
    shard = call(first_shards_kernel, shard_rows_here, *from_shards(parts), name="shard_sum")
    keep, got = scatter_replicas(keep, send, got, (shard,))
    shard = call(first_shards_kernel, shard_rows_here, shard, swap(shard, "dp", 1), name="replica_sum")
    mine, shard = gather_replicas(keep, got, shard)
    other = swap(mine, "dp", 1)
    left_rows = from_shards([shard] * n_shards)
    left_up, gram_up, keep, send = call(
        functools.partial(right_up_kernel, n_shards), [shaped(rank, rows), shaped(rank, rank), replica_half, replica_half],
        *left_rows, gu, eu, after=(other,), name="right_up", flops=product,
        scratch_shapes=[pltpu.VMEM((3 * rank, rows), BF16), wide, stage],
    )
    left_down, *parts = call(
        right_down_kernel, [shaped(rank, ff)] + [shaped(rows_here, rows + rank * n_shards)] * n_shards, mine, other, gd, ed, after=(left_up,),
        name="right_down", flops=product, scratch_shapes=[pltpu.VMEM((3 * rank, ff), BF16), narrow, stage],
    )
    keep, got = scatter_replicas(keep, send, swap(send, "dp", 1), (left_down,))
    shard, gram_down = call(
        functools.partial(sum_shards_kernel, n_shards), [shard_rows_here, shaped(rank, rank)], *from_shards(parts), name="shard_sum"
    )
    mine = add_columns(*gather_replicas(keep, got, shard))
    other = swap(mine, "dp", 1)
    inv_up, inv_down, lhs_up, lhs_down = call(
        basis_kernel,
        [shaped(rank, rank)] * 2 + [shaped(rows, 4 * rank, dtype=BF16), shaped(ff, 4 * rank, dtype=BF16)],
        left_up, left_down, gram_up, gram_down, gu, eu, gd, ed, mine, name="basis", in_specs=[VMEM] * 8 + [ANY],
    )
    rhs_up, shard = call(
        factor_up_kernel, [shaped(4 * rank, ff, dtype=BF16), shaped(rows_here, rows + 128)], mine, other, inv_up,
        name="factor_up", scratch_shapes=[wide, stage],
    )
    right_rows = from_shards([shard] * n_shards)
    new_error_up, made = call(
        error_up_kernel, [shaped(1, rows, ff, dtype=BF16), shaped(8, 128)], gu, eu, lhs_up, rhs_up, name="error_up", flops=product // 2,
        grid=(STEPS,), in_specs=[VMEM] * 4, out_specs=[replica_blocks(rows, ff), whole((8, 128))],
    )
    limit = CLIP_RMS * (2.0 * rows * ff * n_shards) ** 0.5
    rhs_down, clip = call(
        functools.partial(factor_down_kernel, limit, n_shards), [shaped(4 * rank, rows, dtype=BF16), shaped(8, 128)],
        *right_rows, inv_down, made, name="factor_down", in_specs=[VMEM] * (n_shards + 1) + [ANY], scratch_shapes=[narrow],
    )
    new_error_down, update_up, update_down = call(
        last_kernel, [shaped(1, ff, rows, dtype=BF16), shaped(rows, ff, dtype=BF16), shaped(ff, rows, dtype=BF16)],
        gd, ed, lhs_up, rhs_up, lhs_down, rhs_down, clip, name="last", flops=product, grid=(STEPS,),
        in_specs=[VMEM] * 7, out_specs=[replica_blocks(ff, rows), row_blocks(rows, ff), row_blocks(ff, rows)],
    )
    return new_error_up, update_up, new_error_down, update_down


def solution(mesh):
    placed = (
        P("dp", None, "tensor"),
        P("dp", None, "tensor"),
        P("dp", "tensor", None),
        P("dp", "tensor", None),
        P("tensor", None),
        P(),
    )
    return jax.shard_map(
        on_device,
        mesh=mesh,
        in_specs=placed,
        out_specs=(
            P("dp", None, "tensor"),
            P(None, "tensor"),
            P("dp", "tensor", None),
            P("tensor", None),
        ),
        check_vma=False,
    )
```

```python
import functools

import jax
import jax.numpy as jnp
from jax import lax
from jax.experimental import pallas as pl
from jax.experimental.pallas import tpu as pltpu
from jax.sharding import PartitionSpec as P

F32 = jnp.float32
BF16 = jnp.bfloat16
HIGHEST = lax.Precision.HIGHEST
CLIP_RMS = 0.1
STEPS = 4
MIB = 1024 * 1024
NT = ((1,), (1,))


def split3(x):
    first = x.astype(BF16)
    rest = x - first.astype(F32)
    second = rest.astype(BF16)
    return first, second, (rest - second.astype(F32)).astype(BF16)


def tree_sum(values):
    values = list(values)
    while len(values) > 1:
        values = [values[i] + values[i + 1] for i in range(0, len(values), 2)]
    return values[0]


def dot(a, b, dims=((1,), (0,)), precision=None):
    return lax.dot_general(a, b, (dims, ((), ())), precision=precision, preferred_element_type=F32)


def fold(x, rows):
    return jnp.concatenate([x[i : i + rows] for i in range(0, x.shape[0], rows)], axis=1)


def unfold(x, rows):
    count = rows // x.shape[0]
    width = x.shape[1] // count
    return jnp.concatenate([x[:, i * width : (i + 1) * width] for i in range(count)], axis=0)


def place(axis):
    index = lax.axis_index(axis)
    return lax.bitwise_and(index, 1), lax.shift_right_logical(index, 1)


def split_replicas(total, stage, keep, send):
    parity, _ = place("dp")
    half, per, _ = keep.shape
    for c in range(2 * half):
        stage[c] = total[c * per : (c + 1) * per, :]
    for c in range(half):
        keep[c] = stage[2 * c + parity]
        send[c] = stage[2 * c + 1 - parity]


def join_replicas(mine, other, stage, total):
    parity, _ = place("dp")
    half, per, _ = mine.shape
    width = total.shape[1]
    for c in range(half):
        stage[2 * c + parity] = mine[c, :, :width]
        stage[2 * c + 1 - parity] = other[c, :, :width]
    for c in range(2 * half):
        total[c * per : (c + 1) * per, :] = stage[c]


def split_shards(total, extra, outs):
    me = lax.axis_index("tensor")
    rows, width = outs[0].shape[0], total.shape[1]
    for j, out in enumerate(outs):
        owner = lax.bitwise_xor(me, j)
        out[:, :width] = total[pl.ds(pl.multiple_of(owner * rows, rows), rows), :]
        if extra is not None:
            out[:, width:] = fold(extra, rows)


def join_shards(pieces, total):
    me = lax.axis_index("tensor")
    rows, width = pieces[0].shape[0], total.shape[1]
    for j, piece in enumerate(pieces):
        owner = lax.bitwise_xor(me, j)
        total[pl.ds(pl.multiple_of(owner * rows, rows), rows), :] = piece[:, :width]


def left_kernel(n_shards, gu, eu, qu, gd, ed, qd, *refs):
    *outs, gu_in, eu_in, qu_in, pieces_up, total_up, gd_in, ed_in, qd_in, pieces_down, total_down, stage, q_sems, sems = refs
    up, down = (qu_in, pieces_up, total_up), (qd_in, pieces_down, total_down)
    firsts = [pltpu.make_async_copy(src, dst, q_sems.at[i]) for i, (src, dst) in enumerate(((qd, qd_in), (qu, qu_in)))]
    stages = []
    for g, e, g_in, e_in, part, count in ((gd, ed, gd_in, ed_in, down, 3), (gu, eu, gu_in, eu_in, up, 2)):
        block = g_in.shape[0] // count
        for i in range(count):
            rows = pl.ds(i * block, block)
            n = len(stages)
            copies = [pltpu.make_async_copy(src.at[0, rows, :], dst.at[rows, :], sems.at[n, k]) for k, (src, dst) in enumerate(((g, g_in), (e, e_in)))]
            stages.append((copies, g_in, e_in, slice(i * block, (i + 1) * block), part))

    def fetch(n):
        if n < len(stages):
            for copy in stages[n][0]:
                copy.start()

    firsts[0].start()
    fetch(0)
    firsts[1].start()
    for n, (first, (q, pieces, _)) in enumerate(zip(firsts, (down, up))):
        first.wait()
        fetch(n + 1)
        split_rows(q, pieces)
    for n, (copies, g, e, rows, (_, pieces, total)) in enumerate(stages):
        for copy in copies:
            copy.wait()
        fetch(n + 3)
        total[:, rows] = add_pieces(dot(pieces[...], g[rows, :], NT) + dot(pieces[...], e[rows, :], NT))
    split_shards(total_up, None, outs[:n_shards])
    split_replicas(total_down, stage, *outs[n_shards:])


def fetch_kernel(*refs):
    half = len(refs) // 2
    for source, out in zip(refs[:half], refs[half:]):
        out[...] = source[...]


def sum_shards_kernel(n_shards, *refs):
    terms, (out, gram) = refs[:n_shards], refs[n_shards:]
    total = tree_sum(term[...] for term in terms)
    out[...] = total[:, : out.shape[1]]
    gram[...] = unfold(total[:, out.shape[1] :], gram.shape[0])


def first_shards_kernel(*refs):
    refs[-1][...] = tree_sum(term[...] for term in refs[:-1])


def own_and_other(j, bit):
    mine = lax.bitwise_and(lax.shift_right_logical(lax.axis_index("dp"), bit), 1)
    return 2 * j + mine, 2 * j + 1 - mine


def split_chunks(bit, chunks, keep, send):
    for j in range(keep.shape[0]):
        mine, other = own_and_other(j, bit)
        keep[j] = chunks[mine]
        send[j] = chunks[other]


def halve_kernel(bit, keep, got, keep_out, send_out, chunks):
    chunks[...] = keep[...] + got[...]
    split_chunks(bit, chunks, keep_out, send_out)


def sum_kernel(scale, mine, other, out):
    out[...] = (mine[...] + other[...]) * scale


def double_kernel(bit, mine, other, out):
    for j in range(mine.shape[0]):
        here, there = own_and_other(j, bit)
        out[here] = mine[j]
        out[there] = other[j]


def half_sum_kernel(keep, got, shard, out):
    count, per, ff = keep.shape
    block = shard.shape[1] // count
    for c in range(count):
        out[c, :, :ff] = keep[c] + got[c]
        out[c, :, ff:] = fold(shard[:, c * block : (c + 1) * block], per)


def join_shard(chunks, ff, rows):
    return jnp.concatenate([unfold(chunks[c, :, ff:], rows) for c in range(chunks.shape[0])], axis=1)


def double_apart_kernel(bit, mine, other, out, shard):
    ff = out.shape[2]
    for j in range(mine.shape[0]):
        here, there = own_and_other(j, bit)
        out[here] = mine[j, :, :ff]
        out[there] = other[j, :, :ff]
    shard[...] = join_shard(mine, ff, shard.shape[0]) + join_shard(other, ff, shard.shape[0])


def add_columns_kernel(chunks, shard, out):
    count, per, ff = chunks.shape
    block = shard.shape[1] // count
    for c in range(count):
        out[c, :, :ff] = chunks[c]
        out[c, :, ff:] = fold(shard[:, c * block : (c + 1) * block], per)


def split_z_kernel(keep, got, shard, *refs):
    *outs, stage = refs
    _, z = place("dp")
    half, per, ff = keep.shape
    block = shard.shape[1] // half
    for c in range(half):
        stage[c, :, :ff] = keep[c] + got[c]
        stage[c, :, ff:] = fold(shard[:, c * block : (c + 1) * block], per)
    for j, out in zip([0, *range(half - 1, 0, -1)], outs):
        out[...] = stage[lax.bitwise_xor(z, j)]


def mean_kernel(n_dp, *refs):
    refs[-1][...] = tree_sum(ref[...] for ref in refs[:-1]) / n_dp


def stack_kernel(*refs):
    _, z = place("dp")
    for j, ref in enumerate(refs[:-1]):
        refs[-1][lax.bitwise_xor(z, j)] = ref[...]


def shard_rows(mine, other, ff, rows):
    half = mine.shape[0]
    return jnp.concatenate([unfold(mine[c, :, ff:] + other[c, :, ff:], rows) for c in range(half)], axis=1)


def split_rows(left, pieces):
    rank = left.shape[0]
    for i, piece in enumerate(split3(left[...])):
        pieces[i * rank : (i + 1) * rank, :] = piece


def add_pieces(t):
    rank = t.shape[0] // 3
    return t[:rank] + (t[rank : 2 * rank] + t[2 * rank :])


def right_down_kernel(mine, other, g, e, left, *refs):
    *outs, pieces, total, stage = refs
    join_replicas(mine, other, stage, left)
    split_rows(left, pieces)
    total[...] = add_pieces(dot(pieces[...], g[0]) + dot(pieces[...], e[0]))
    split_shards(total, dot(left[...], left[...], NT, HIGHEST), outs)


def right_up_kernel(n_shards, *refs):
    shards, refs = refs[:n_shards], refs[n_shards:]
    g, e, left, gram, keep, send, pieces, total, stage = refs
    join_shards(shards, left)
    split_rows(left, pieces)
    block = total.shape[1] // STEPS
    for i in range(STEPS):
        part = slice(i * block, (i + 1) * block)
        total[:, part] = add_pieces(dot(pieces[...], g[0, :, part]) + dot(pieces[...], e[0, :, part]))
    split_replicas(total, stage, keep, send)
    gram[...] = dot(left[...], left[...], NT, HIGHEST)


def inverse_factors(grams):
    rank = grams[0].shape[0]
    count = rank // 8
    panel = 4
    lane = lax.broadcasted_iota(jnp.int32, (8, 2 * rank), 1)
    row = lax.broadcasted_iota(jnp.int32, (8, 2 * rank), 0)
    states, pivots = [], []
    for gram in grams:
        wide = jnp.concatenate([gram, jnp.zeros_like(gram)], axis=1)
        states.append([wide[i : i + 8] + (lane == row + (rank + i)).astype(F32) for i in range(0, rank, 8)])
        pivots.append([])
    for start in range(0, rank, panel):
        at = start // 8
        below = range(at, count)
        spread = [
            [{i: jnp.broadcast_to(blocks[i][:, start + j : start + j + 1], (8, 2 * rank)) for i in below} for j in range(panel)]
            for blocks in states
        ]
        for j in range(panel):
            inner = (start + j) % 8
            for blocks, columns, found in zip(states, spread, pivots):
                pivot = columns[j][at][inner : inner + 1, :]
                found.append(pivot)
                inverse = 1.0 / pivot
                factor = {i: jnp.where(row > inner, columns[j][i], 0.0) if i == at else columns[j][i] for i in below}
                for later in columns[j + 1 :]:
                    head = later[at][inner : inner + 1, :] * inverse
                    for i in below:
                        later[i] = later[i] - factor[i] * head
                scaled = blocks[at][inner : inner + 1, :] * inverse
                for i in below:
                    blocks[i] = blocks[i] - factor[i] * scaled
    results = []
    for blocks, found in zip(states, pivots):
        rows = [block / jnp.sqrt(jnp.concatenate(found[8 * i : 8 * i + 8], axis=0)) for i, block in enumerate(blocks)]
        results.append(jnp.concatenate(rows, axis=0)[:, rank:])
    return results


def basis_kernel(left_up, left_down, gram_up, gram_down, *refs):
    inv_up, inv_down, lhs_up, lhs_down = refs[-4:]
    inverses = inverse_factors([gram_up[...], gram_down[...]])
    rank = left_up.shape[0]
    for inverse, inv, left, lhs in zip(inverses, (inv_up, inv_down), (left_up, left_down), (lhs_up, lhs_down)):
        inv[...] = inverse
        first, second, _ = split3(dot(inverse, left[...], precision=HIGHEST).T)
        lhs[:, :rank] = first
        lhs[:, rank : 2 * rank] = first
        lhs[:, 2 * rank : 3 * rank] = second
        lhs[:, 3 * rank :] = second


def right_factor(inv, total, rhs):
    rank = inv.shape[0]
    right = dot(inv[...], total[...], precision=HIGHEST)
    first, second, _ = split3(right)
    rhs[:rank, :] = first
    rhs[rank : 2 * rank, :] = second
    rhs[2 * rank : 3 * rank, :] = first
    rhs[3 * rank :, :] = second
    return jnp.sum(right * right)


def factor_up_kernel(mine, other, inv, rhs, shard, total, stage):
    join_replicas(mine, other, stage, total)
    square = right_factor(inv, total, rhs)
    rows, ff = shard.shape[0], total.shape[1]
    width = shard.shape[1] - 128
    shard[:, :width] = shard_rows(mine, other, ff, rows)
    shard[:, width:] = jnp.full((rows, 128), square, F32)


def factor_down_kernel(limit, n_shards, *refs):
    shards, refs = refs[:n_shards], refs[n_shards:]
    inv, _, rhs, clip, total = refs
    join_shards(shards, total)
    square = right_factor(inv, total, rhs)
    width = total.shape[1]
    norm_sq = square + tree_sum(shard[:8, width:] for shard in shards)
    clip[...] = jnp.minimum(jnp.float32(1.0), limit / jnp.sqrt(norm_sq))


def rows_of(block):
    return pl.ds(pl.multiple_of(pl.program_id(0) * block, block), block)


def error_up_kernel(g, e, lhs, rhs, error, kept):
    part = rows_of(error.shape[1])
    rebuilt = dot(lhs[part, :], rhs[...])
    kept[part, :] = rebuilt
    error[0] = (g[0, part, :].astype(F32) + e[0, part, :].astype(F32) - rebuilt).astype(BF16)


def last_kernel(g, e, rebuilt_up, lhs_down, rhs_down, clip, error, update_up, update_down):
    factor = clip[:1, :1]
    part = rows_of(update_down.shape[0])
    rebuilt = dot(lhs_down[part, :], rhs_down[...])
    update_down[...] = (factor * rebuilt).astype(BF16)
    error[0] = (g[0, part, :].astype(F32) + e[0, part, :].astype(F32) - rebuilt).astype(BF16)
    part = rows_of(update_up.shape[0])
    update_up[...] = (factor * rebuilt_up[part, :]).astype(BF16)


def shaped(*dims, dtype=F32):
    return jax.ShapeDtypeStruct(dims, dtype)


def whole(shape):
    return pl.BlockSpec(shape, lambda *_: (0,) * len(shape))


def row_blocks(rows, columns):
    return pl.BlockSpec((rows // STEPS, columns), lambda i: (i, 0))


def replica_blocks(rows, columns):
    return pl.BlockSpec((1, rows // STEPS, columns), lambda i: (0, i, 0))


VMEM = pl.BlockSpec(memory_space=pltpu.VMEM)
ANY = pl.BlockSpec(memory_space=pl.ANY)


def call(kernel, out_shape, *args, after=(), in_specs=None, flops=0, limit=12, name=None, **more):
    arrays = list(args) + jax.tree.leaves(out_shape)
    size = sum(a.size * a.dtype.itemsize for a in arrays)
    skip = len(after)
    return pl.pallas_call(
        lambda *refs: kernel(*refs[skip:]), out_shape=out_shape, in_specs=[ANY] * skip + (in_specs or [VMEM] * len(args)),
        compiler_params=pltpu.CompilerParams(vmem_limit_bytes=limit * MIB),
        cost_estimate=pl.CostEstimate(flops=flops, bytes_accessed=size, transcendentals=0), name=name, **more,
    )(*after, *args)


def swap(x, axis, distance):
    pairs = [(i, i ^ distance) for i in range(lax.axis_size(axis))]
    return lax.ppermute(x, axis, pairs)


def from_shards(parts):
    return [parts[0]] + [swap(parts[j], "tensor", j) for j in range(1, len(parts))]


def scatter_replicas(keep, send, got, after):
    n_dp = lax.axis_size("dp")
    for bit in range(n_dp.bit_length() - 2):
        got = swap(send, "dp", 1 << bit) if bit else got
        if bit == n_dp.bit_length() - 3:
            return keep, got
        count, per, ff = keep.shape
        out = shaped(count // 2, per, ff)
        keep, send = call(
            functools.partial(halve_kernel, bit + 1), [out, out], keep, got, after=after if bit == 0 else (), name="halve",
            scratch_shapes=[pltpu.VMEM(keep.shape, F32)],
        )


def gather_replicas(keep, got, shard):
    n_dp = lax.axis_size("dp")
    last = n_dp.bit_length() - 2
    count, per, ff = keep.shape
    columns = ff + shard.shape[0] * shard.shape[1] // (count * per)
    both = shaped(count, per, columns)
    total = call(half_sum_kernel, both, keep, got, shard, name="half_sum")
    mine = call(functools.partial(sum_kernel, 1.0 / n_dp), both, total, swap(total, "dp", 1 << last), name="mean")
    for bit in range(last - 1, 0, -1):
        other = swap(mine, "dp", 1 << bit)
        count *= 2
        mine, shard = call(functools.partial(double_apart_kernel, bit), [shaped(count, per, ff), shaped(*shard.shape)], mine, other, name="double")
        if bit > 1:
            mine = call(add_columns_kernel, shaped(count, per, ff + (columns - ff) // (count // keep.shape[0])), mine, shard, name="add_columns")
    return mine, shard


def from_z(parts):
    got = {j: swap(parts[j], "dp", 2 * j) for j in range(len(parts) - 1, 0, -1)}
    return [parts[0]] + [got[j] for j in range(1, len(parts))]


def mean_replicas(keep, got, shard):
    n_dp = lax.axis_size("dp")
    half, per, ff = keep.shape
    piece = shaped(per, ff + shard.shape[0] * shard.shape[1] // (half * per))
    stage = pltpu.VMEM((half, *piece.shape), F32)
    parts = call(split_z_kernel, [piece] * half, keep, got, shard, name="split_z", scratch_shapes=[stage])
    parts = [parts[0], *parts[:0:-1]]
    mean = call(functools.partial(mean_kernel, n_dp), piece, *from_z(parts), name="replica_mean")
    return from_z([mean] * half)


def on_device(gu, eu, gd, ed, qu, qd):
    qu, qd = qu.T, qd.T
    n_dp, n_shards = lax.axis_size("dp"), lax.axis_size("tensor")
    _, rows, ff = gu.shape
    rank = qu.shape[0]
    half, per, rows_here = n_dp // 2, rank // n_dp, rank // n_shards
    shard_rows_here = shaped(rows_here, rows)
    replica_half = shaped(half, per, ff)
    stage = pltpu.VMEM((n_dp, per, ff), F32)
    wide = pltpu.VMEM((rank, ff), F32)
    narrow = pltpu.VMEM((rank, rows), F32)
    product = 4 * rows * ff * 4 * rank

    buffers = [
        [pltpu.VMEM(g.shape[1:], BF16)] * 2 + [pltpu.VMEM(q.shape, F32), pltpu.VMEM((3 * rank, q.shape[1]), BF16), total]
        for g, q, total in ((gu, qu, narrow), (gd, qd, wide))
    ]
    *parts, keep, send = call(
        functools.partial(left_kernel, n_shards), [shard_rows_here] * n_shards + [replica_half] * 2, gu, eu, qu, gd, ed, qd,
        name="left", flops=2 * product, limit=61, in_specs=[pl.BlockSpec(memory_space=pltpu.HBM)] * 6,
        scratch_shapes=buffers[0] + buffers[1] + [stage, pltpu.SemaphoreType.DMA((2,)), pltpu.SemaphoreType.DMA((5, 2))],
    )
    got = swap(send, "dp", 1)
    parts = from_shards(parts)
    parts[0], keep = call(fetch_kernel, [shard_rows_here, replica_half], parts[0], keep, name="fetch", flops=product // 4)
    shard = call(first_shards_kernel, shard_rows_here, *parts, name="shard_sum")
    keep, got = scatter_replicas(keep, send, got, (shard,))
    shard = call(first_shards_kernel, shard_rows_here, shard, swap(shard, "dp", 1), name="replica_sum")
    mine, shard = gather_replicas(keep, got, shard)
    other = swap(mine, "dp", 1)
    left_rows = from_shards([shard] * n_shards)
    left_up, gram_up, keep, send = call(
        functools.partial(right_up_kernel, n_shards), [shaped(rank, rows), shaped(rank, rank), replica_half, replica_half],
        *left_rows, gu, eu, after=(other,), name="right_up", flops=product,
        scratch_shapes=[pltpu.VMEM((3 * rank, rows), BF16), wide, stage],
    )
    left_down, *parts = call(
        right_down_kernel, [shaped(rank, ff)] + [shaped(rows_here, rows + rank * n_shards)] * n_shards, mine, other, gd, ed, after=(left_up,),
        name="right_down", flops=product, scratch_shapes=[pltpu.VMEM((3 * rank, ff), BF16), narrow, stage],
    )
    got = swap(send, "dp", 1)
    shard, gram_down = call(
        functools.partial(sum_shards_kernel, n_shards), [shard_rows_here, shaped(rank, rank)], *from_shards(parts), name="shard_sum"
    )
    pieces = mean_replicas(keep, got, shard)
    mine = call(stack_kernel, shaped(half, *pieces[0].shape), *pieces, name="stack_z")
    other = swap(mine, "dp", 1)
    inv_up, inv_down, lhs_up, lhs_down = call(
        basis_kernel,
        [shaped(rank, rank)] * 2 + [shaped(rows, 4 * rank, dtype=BF16), shaped(ff, 4 * rank, dtype=BF16)],
        left_up, left_down, gram_up, gram_down, gu, eu, gd, ed, mine, name="basis", in_specs=[VMEM] * 8 + [ANY],
    )
    rhs_up, shard = call(
        factor_up_kernel, [shaped(4 * rank, ff, dtype=BF16), shaped(rows_here, rows + 128)], mine, other, inv_up,
        name="factor_up", scratch_shapes=[wide, stage],
    )
    right_rows = from_shards([shard] * n_shards)
    new_error_up, rebuilt_up = call(
        error_up_kernel, [shaped(1, rows, ff, dtype=BF16), shaped(rows, ff)], gu, eu, lhs_up, rhs_up, name="error_up", flops=product // 2,
        grid=(STEPS,), in_specs=[VMEM] * 4, out_specs=[replica_blocks(rows, ff), VMEM],
    )
    limit = CLIP_RMS * (2.0 * rows * ff * n_shards) ** 0.5
    rhs_down, clip = call(
        functools.partial(factor_down_kernel, limit, n_shards), [shaped(4 * rank, rows, dtype=BF16), shaped(8, 128)],
        *right_rows, inv_down, rebuilt_up, name="factor_down", in_specs=[VMEM] * (n_shards + 1) + [ANY], scratch_shapes=[narrow],
    )
    new_error_down, update_up, update_down = call(
        last_kernel, [shaped(1, ff, rows, dtype=BF16), shaped(rows, ff, dtype=BF16), shaped(ff, rows, dtype=BF16)],
        gd, ed, rebuilt_up, lhs_down, rhs_down, clip, name="last", flops=product, grid=(STEPS,),
        in_specs=[VMEM] * 6, out_specs=[replica_blocks(ff, rows), row_blocks(rows, ff), row_blocks(ff, rows)],
    )
    return new_error_up, update_up, new_error_down, update_down


def solution(mesh):
    placed = (
        P("dp", None, "tensor"),
        P("dp", None, "tensor"),
        P("dp", "tensor", None),
        P("dp", "tensor", None),
        P("tensor", None),
        P(),
    )
    return jax.shard_map(
        on_device,
        mesh=mesh,
        in_specs=placed,
        out_specs=(
            P("dp", None, "tensor"),
            P(None, "tensor"),
            P("dp", "tensor", None),
            P("tensor", None),
        ),
        check_vma=False,
    )
```

```python
import functools

import jax
import jax.numpy as jnp
from jax import lax
from jax.experimental import pallas as pl
from jax.experimental.pallas import tpu as pltpu
from jax.sharding import PartitionSpec as P

F32 = jnp.float32
BF16 = jnp.bfloat16
HIGHEST = lax.Precision.HIGHEST
CLIP_RMS = 0.1
STEPS = 4
MIB = 1024 * 1024
NT = ((1,), (1,))


def split3(x):
    first = x.astype(BF16)
    rest = x - first.astype(F32)
    second = rest.astype(BF16)
    return first, second, (rest - second.astype(F32)).astype(BF16)


def tree_sum(values):
    values = list(values)
    while len(values) > 1:
        values = [values[i] + values[i + 1] for i in range(0, len(values), 2)]
    return values[0]


def dot(a, b, dims=((1,), (0,)), precision=None):
    return lax.dot_general(a, b, (dims, ((), ())), precision=precision, preferred_element_type=F32)


def fold(x, rows):
    return jnp.concatenate([x[i : i + rows] for i in range(0, x.shape[0], rows)], axis=1)


def unfold(x, rows):
    count = rows // x.shape[0]
    width = x.shape[1] // count
    return jnp.concatenate([x[:, i * width : (i + 1) * width] for i in range(count)], axis=0)


def place(axis):
    index = lax.axis_index(axis)
    return lax.bitwise_and(index, 1), lax.shift_right_logical(index, 1)


def split_replicas(total, stage, keep, send):
    parity, _ = place("dp")
    half, per, _ = keep.shape
    for c in range(2 * half):
        stage[c] = total[c * per : (c + 1) * per, :]
    for c in range(half):
        keep[c] = stage[2 * c + parity]
        send[c] = stage[2 * c + 1 - parity]


def join_replicas(mine, other, stage, total):
    parity, _ = place("dp")
    half, per, _ = mine.shape
    width = total.shape[1]
    for c in range(half):
        stage[2 * c + parity] = mine[c, :, :width]
        stage[2 * c + 1 - parity] = other[c, :, :width]
    for c in range(2 * half):
        total[c * per : (c + 1) * per, :] = stage[c]


def split_shards(total, extra, outs):
    me = lax.axis_index("tensor")
    rows, width = outs[0].shape[0], total.shape[1]
    for j, out in enumerate(outs):
        owner = lax.bitwise_xor(me, j)
        out[:, :width] = total[pl.ds(pl.multiple_of(owner * rows, rows), rows), :]
        if extra is not None:
            out[:, width:] = fold(extra, rows)


def join_shards(pieces, total):
    me = lax.axis_index("tensor")
    rows, width = pieces[0].shape[0], total.shape[1]
    for j, piece in enumerate(pieces):
        owner = lax.bitwise_xor(me, j)
        total[pl.ds(pl.multiple_of(owner * rows, rows), rows), :] = piece[:, :width]


def left_kernel(n_shards, gu, eu, qu, gd, ed, qd, *refs):
    *outs, gu_in, eu_in, qu_in, pieces_up, total_up, gd_in, ed_in, qd_in, pieces_down, total_down, stage, q_sems, sems = refs
    up, down = (qu_in, pieces_up, total_up), (qd_in, pieces_down, total_down)
    firsts = [pltpu.make_async_copy(src, dst, q_sems.at[i]) for i, (src, dst) in enumerate(((qd, qd_in), (qu, qu_in)))]
    stages = []
    for g, e, g_in, e_in, part, count in ((gd, ed, gd_in, ed_in, down, 3), (gu, eu, gu_in, eu_in, up, 2)):
        block = g_in.shape[0] // count
        for i in range(count):
            rows = pl.ds(i * block, block)
            n = len(stages)
            copies = [pltpu.make_async_copy(src.at[0, rows, :], dst.at[rows, :], sems.at[n, k]) for k, (src, dst) in enumerate(((g, g_in), (e, e_in)))]
            stages.append((copies, g_in, e_in, slice(i * block, (i + 1) * block), part))

    def fetch(n):
        if n < len(stages):
            for copy in stages[n][0]:
                copy.start()

    firsts[0].start()
    fetch(0)
    firsts[1].start()
    for n, (first, (q, pieces, _)) in enumerate(zip(firsts, (down, up))):
        first.wait()
        fetch(n + 1)
        split_rows(q, pieces)
    for n, (copies, g, e, rows, (_, pieces, total)) in enumerate(stages):
        for copy in copies:
            copy.wait()
        fetch(n + 3)
        total[:, rows] = add_pieces(dot(pieces[...], g[rows, :], NT) + dot(pieces[...], e[rows, :], NT))
    split_shards(total_up, None, outs[:n_shards])
    split_replicas(total_down, stage, *outs[n_shards:])


def fetch_kernel(*refs):
    half = len(refs) // 2
    for source, out in zip(refs[:half], refs[half:]):
        out[...] = source[...]


def sum_shards_kernel(n_shards, *refs):
    terms, (out, gram) = refs[:n_shards], refs[n_shards:]
    total = tree_sum(term[...] for term in terms)
    out[...] = total[:, : out.shape[1]]
    gram[...] = unfold(total[:, out.shape[1] :], gram.shape[0])


def first_shards_kernel(*refs):
    refs[-1][...] = tree_sum(term[...] for term in refs[:-1])


def own_and_other(j, bit):
    mine = lax.bitwise_and(lax.shift_right_logical(lax.axis_index("dp"), bit), 1)
    return 2 * j + mine, 2 * j + 1 - mine


def split_chunks(bit, chunks, keep, send):
    for j in range(keep.shape[0]):
        mine, other = own_and_other(j, bit)
        keep[j] = chunks[mine]
        send[j] = chunks[other]


def halve_kernel(bit, keep, got, keep_out, send_out, chunks):
    chunks[...] = keep[...] + got[...]
    split_chunks(bit, chunks, keep_out, send_out)


def sum_kernel(scale, mine, other, out):
    out[...] = (mine[...] + other[...]) * scale


def double_kernel(bit, mine, other, out):
    for j in range(mine.shape[0]):
        here, there = own_and_other(j, bit)
        out[here] = mine[j]
        out[there] = other[j]


def half_sum_kernel(keep, got, shard, out):
    count, per, ff = keep.shape
    block = shard.shape[1] // count
    for c in range(count):
        out[c, :, :ff] = keep[c] + got[c]
        out[c, :, ff:] = fold(shard[:, c * block : (c + 1) * block], per)


def join_shard(chunks, ff, rows):
    return jnp.concatenate([unfold(chunks[c, :, ff:], rows) for c in range(chunks.shape[0])], axis=1)


def double_apart_kernel(bit, mine, other, out, rest, shard):
    ff = out.shape[2]
    for j in range(mine.shape[0]):
        here, there = own_and_other(j, bit)
        out[here] = mine[j, :, :ff]
        out[there] = other[j, :, :ff]
        rest[j] = other[j, :, :ff]
    shard[...] = join_shard(mine, ff, shard.shape[0]) + join_shard(other, ff, shard.shape[0])


def strip_kernel(both, out):
    out[...] = both[:, :, : out.shape[2]]


def stack_rest_kernel(own, *refs):
    *pieces, out, rest = refs
    stack_kernel(own, *pieces, out)
    for j, piece in enumerate(pieces):
        rest[j] = piece[...]


def place_other_kernel(own, rest, out):
    stack_kernel(own, *[rest.at[j] for j in range(rest.shape[0])], out)


def add_columns_kernel(chunks, shard, out):
    count, per, ff = chunks.shape
    block = shard.shape[1] // count
    for c in range(count):
        out[c, :, :ff] = chunks[c]
        out[c, :, ff:] = fold(shard[:, c * block : (c + 1) * block], per)


def split_z_kernel(keep, got, shard, *refs):
    *outs, stage = refs
    _, z = place("dp")
    half, per, ff = keep.shape
    block = shard.shape[1] // half
    for c in range(half):
        stage[c, :, :ff] = keep[c] + got[c]
        stage[c, :, ff:] = fold(shard[:, c * block : (c + 1) * block], per)
    for j, out in zip([0, *range(half - 1, 0, -1)], outs):
        out[...] = stage[lax.bitwise_xor(z, j)]


def mean_kernel(n_dp, *refs):
    refs[-1][...] = tree_sum(ref[...] for ref in refs[:-1]) / n_dp


def stack_kernel(*refs):
    _, z = place("dp")
    for j, ref in enumerate(refs[:-1]):
        refs[-1][lax.bitwise_xor(z, j)] = ref[...]


def shard_rows(mine, other, ff, rows):
    half = mine.shape[0]
    return jnp.concatenate([unfold(mine[c, :, ff:] + other[c, :, ff:], rows) for c in range(half)], axis=1)


def split_rows(left, pieces):
    rank = left.shape[0]
    for i, piece in enumerate(split3(left[...])):
        pieces[i * rank : (i + 1) * rank, :] = piece


def add_pieces(t):
    rank = t.shape[0] // 3
    return t[:rank] + (t[rank : 2 * rank] + t[2 * rank :])


def right_down_kernel(mine, other, g, e, left, *refs):
    *outs, pieces, total, stage = refs
    join_replicas(mine, other, stage, left)
    split_rows(left, pieces)
    total[...] = add_pieces(dot(pieces[...], g[0]) + dot(pieces[...], e[0]))
    split_shards(total, dot(left[...], left[...], NT, HIGHEST), outs)


def right_up_kernel(n_shards, *refs):
    shards, refs = refs[:n_shards], refs[n_shards:]
    g, e, left, gram, keep, send, pieces, total, stage = refs
    join_shards(shards, left)
    split_rows(left, pieces)
    block = total.shape[1] // STEPS
    for i in range(STEPS):
        part = slice(i * block, (i + 1) * block)
        total[:, part] = add_pieces(dot(pieces[...], g[0, :, part]) + dot(pieces[...], e[0, :, part]))
    split_replicas(total, stage, keep, send)
    gram[...] = dot(left[...], left[...], NT, HIGHEST)


def inverse_factors(grams):
    rank = grams[0].shape[0]
    count = rank // 8
    panel = 4
    lane = lax.broadcasted_iota(jnp.int32, (8, 2 * rank), 1)
    row = lax.broadcasted_iota(jnp.int32, (8, 2 * rank), 0)
    states, pivots = [], []
    for gram in grams:
        wide = jnp.concatenate([gram, jnp.zeros_like(gram)], axis=1)
        states.append([wide[i : i + 8] + (lane == row + (rank + i)).astype(F32) for i in range(0, rank, 8)])
        pivots.append([])
    for start in range(0, rank, panel):
        at = start // 8
        below = range(at, count)
        spread = [
            [{i: jnp.broadcast_to(blocks[i][:, start + j : start + j + 1], (8, 2 * rank)) for i in below} for j in range(panel)]
            for blocks in states
        ]
        for j in range(panel):
            inner = (start + j) % 8
            for blocks, columns, found in zip(states, spread, pivots):
                pivot = columns[j][at][inner : inner + 1, :]
                found.append(pivot)
                inverse = 1.0 / pivot
                factor = {i: jnp.where(row > inner, columns[j][i], 0.0) if i == at else columns[j][i] for i in below}
                for later in columns[j + 1 :]:
                    head = later[at][inner : inner + 1, :] * inverse
                    for i in below:
                        later[i] = later[i] - factor[i] * head
                scaled = blocks[at][inner : inner + 1, :] * inverse
                for i in below:
                    blocks[i] = blocks[i] - factor[i] * scaled
    results = []
    for blocks, found in zip(states, pivots):
        rows = [block / jnp.sqrt(jnp.concatenate(found[8 * i : 8 * i + 8], axis=0)) for i, block in enumerate(blocks)]
        results.append(jnp.concatenate(rows, axis=0)[:, rank:])
    return results


def basis_kernel(left_up, left_down, gram_up, gram_down, *refs):
    inv_up, inv_down, lhs_up, lhs_down = refs[-4:]
    inverses = inverse_factors([gram_up[...], gram_down[...]])
    rank = left_up.shape[0]
    for inverse, inv, left, lhs in zip(inverses, (inv_up, inv_down), (left_up, left_down), (lhs_up, lhs_down)):
        inv[...] = inverse
        first, second, _ = split3(dot(inverse, left[...], precision=HIGHEST).T)
        lhs[:, :rank] = first
        lhs[:, rank : 2 * rank] = first
        lhs[:, 2 * rank : 3 * rank] = second
        lhs[:, 3 * rank :] = second


def right_factor(inv, total, rhs):
    rank = inv.shape[0]
    right = dot(inv[...], total[...], precision=HIGHEST)
    first, second, _ = split3(right)
    rhs[:rank, :] = first
    rhs[rank : 2 * rank, :] = second
    rhs[2 * rank : 3 * rank, :] = first
    rhs[3 * rank :, :] = second
    return jnp.sum(right * right)


def factor_up_kernel(mine, other, inv, rhs, shard, total, stage):
    join_replicas(mine, other, stage, total)
    square = right_factor(inv, total, rhs)
    rows, ff = shard.shape[0], total.shape[1]
    width = shard.shape[1] - 128
    shard[:, :width] = shard_rows(mine, other, ff, rows)
    shard[:, width:] = jnp.full((rows, 128), square, F32)


def factor_down_kernel(limit, n_shards, *refs):
    shards, refs = refs[:n_shards], refs[n_shards:]
    inv, _, rhs, clip, total = refs
    join_shards(shards, total)
    square = right_factor(inv, total, rhs)
    width = total.shape[1]
    norm_sq = square + tree_sum(shard[:8, width:] for shard in shards)
    clip[...] = jnp.minimum(jnp.float32(1.0), limit / jnp.sqrt(norm_sq))


def rows_of(block):
    return pl.ds(pl.multiple_of(pl.program_id(0) * block, block), block)


def error_up_kernel(g, e, lhs, rhs, error, kept):
    part = rows_of(error.shape[1])
    rebuilt = dot(lhs[part, :], rhs[...])
    kept[part, :] = rebuilt
    error[0] = (g[0, part, :].astype(F32) + e[0, part, :].astype(F32) - rebuilt).astype(BF16)


def last_kernel(g, e, rebuilt_up, lhs_down, rhs_down, clip, error, update_up, update_down):
    factor = clip[:1, :1]
    part = rows_of(update_down.shape[0])
    rebuilt = dot(lhs_down[part, :], rhs_down[...])
    update_down[...] = (factor * rebuilt).astype(BF16)
    error[0] = (g[0, part, :].astype(F32) + e[0, part, :].astype(F32) - rebuilt).astype(BF16)
    part = rows_of(update_up.shape[0])
    update_up[...] = (factor * rebuilt_up[part, :]).astype(BF16)


def shaped(*dims, dtype=F32):
    return jax.ShapeDtypeStruct(dims, dtype)


def whole(shape):
    return pl.BlockSpec(shape, lambda *_: (0,) * len(shape))


def row_blocks(rows, columns):
    return pl.BlockSpec((rows // STEPS, columns), lambda i: (i, 0))


def replica_blocks(rows, columns):
    return pl.BlockSpec((1, rows // STEPS, columns), lambda i: (0, i, 0))


VMEM = pl.BlockSpec(memory_space=pltpu.VMEM)
ANY = pl.BlockSpec(memory_space=pl.ANY)


def call(kernel, out_shape, *args, after=(), in_specs=None, flops=0, limit=12, name=None, **more):
    arrays = list(args) + jax.tree.leaves(out_shape)
    size = sum(a.size * a.dtype.itemsize for a in arrays)
    skip = len(after)
    return pl.pallas_call(
        lambda *refs: kernel(*refs[skip:]), out_shape=out_shape, in_specs=[ANY] * skip + (in_specs or [VMEM] * len(args)),
        compiler_params=pltpu.CompilerParams(vmem_limit_bytes=limit * MIB),
        cost_estimate=pl.CostEstimate(flops=flops, bytes_accessed=size, transcendentals=0), name=name, **more,
    )(*after, *args)


def swap(x, axis, distance):
    pairs = [(i, i ^ distance) for i in range(lax.axis_size(axis))]
    return lax.ppermute(x, axis, pairs)


def from_shards(parts):
    return [parts[0]] + [swap(parts[j], "tensor", j) for j in range(1, len(parts))]


def scatter_replicas(keep, send, got, after):
    n_dp = lax.axis_size("dp")
    for bit in range(n_dp.bit_length() - 2):
        got = swap(send, "dp", 1 << bit) if bit else got
        if bit == n_dp.bit_length() - 3:
            return keep, got
        count, per, ff = keep.shape
        out = shaped(count // 2, per, ff)
        keep, send = call(
            functools.partial(halve_kernel, bit + 1), [out, out], keep, got, after=after if bit == 0 else (), name="halve",
            scratch_shapes=[pltpu.VMEM(keep.shape, F32)],
        )


def gather_replicas(keep, got, shard):
    n_dp = lax.axis_size("dp")
    last = n_dp.bit_length() - 2
    count, per, ff = keep.shape
    columns = ff + shard.shape[0] * shard.shape[1] // (count * per)
    both = shaped(count, per, columns)
    total = call(half_sum_kernel, both, keep, got, shard, name="half_sum")
    mine = call(functools.partial(sum_kernel, 1.0 / n_dp), both, total, swap(total, "dp", 1 << last), name="mean")
    for bit in range(last - 1, 0, -1):
        other = swap(mine, "dp", 1 << bit)
        half = shaped(count, per, ff)
        early = swap(call(strip_kernel, half, mine, name="strip"), "dp", 1) if bit == 1 else None
        count *= 2
        mine, rest, shard = call(
            functools.partial(double_apart_kernel, bit), [shaped(count, per, ff), half, shaped(*shard.shape)], mine, other,
            after=(early,) if bit == 1 else (), name="double",
        )
        if bit > 1:
            mine = call(add_columns_kernel, shaped(count, per, ff + (columns - ff) // (count // keep.shape[0])), mine, shard, name="add_columns")
    return mine, early, swap(rest, "dp", 1), shard


def from_z(parts):
    got = {j: swap(parts[j], "dp", 2 * j) for j in range(len(parts) - 1, 0, -1)}
    return [parts[0]] + [got[j] for j in range(1, len(parts))]


def mean_replicas(keep, got, shard):
    n_dp = lax.axis_size("dp")
    half, per, ff = keep.shape
    piece = shaped(per, ff + shard.shape[0] * shard.shape[1] // (half * per))
    stage = pltpu.VMEM((half, *piece.shape), F32)
    parts = call(split_z_kernel, [piece] * half, keep, got, shard, name="split_z", scratch_shapes=[stage])
    parts = [parts[0], *parts[:0:-1]]
    mean = call(functools.partial(mean_kernel, n_dp), piece, *from_z(parts), name="replica_mean")
    return from_z([mean] * half)


def on_device(gu, eu, gd, ed, qu, qd):
    qu, qd = qu.T, qd.T
    n_dp, n_shards = lax.axis_size("dp"), lax.axis_size("tensor")
    _, rows, ff = gu.shape
    rank = qu.shape[0]
    half, per, rows_here = n_dp // 2, rank // n_dp, rank // n_shards
    shard_rows_here = shaped(rows_here, rows)
    replica_half = shaped(half, per, ff)
    stage = pltpu.VMEM((n_dp, per, ff), F32)
    wide = pltpu.VMEM((rank, ff), F32)
    narrow = pltpu.VMEM((rank, rows), F32)
    product = 4 * rows * ff * 4 * rank

    buffers = [
        [pltpu.VMEM(g.shape[1:], BF16)] * 2 + [pltpu.VMEM(q.shape, F32), pltpu.VMEM((3 * rank, q.shape[1]), BF16), total]
        for g, q, total in ((gu, qu, narrow), (gd, qd, wide))
    ]
    *parts, keep, send = call(
        functools.partial(left_kernel, n_shards), [shard_rows_here] * n_shards + [replica_half] * 2, gu, eu, qu, gd, ed, qd,
        name="left", flops=2 * product, limit=61, in_specs=[pl.BlockSpec(memory_space=pltpu.HBM)] * 6,
        scratch_shapes=buffers[0] + buffers[1] + [stage, pltpu.SemaphoreType.DMA((2,)), pltpu.SemaphoreType.DMA((5, 2))],
    )
    got = swap(send, "dp", 1)
    parts = from_shards(parts)
    parts[0], keep = call(fetch_kernel, [shard_rows_here, replica_half], parts[0], keep, name="fetch", flops=product // 4)
    shard = call(first_shards_kernel, shard_rows_here, *parts, name="shard_sum")
    keep, got = scatter_replicas(keep, send, got, (shard,))
    shard = call(first_shards_kernel, shard_rows_here, shard, swap(shard, "dp", 1), name="replica_sum")
    mine, early, late, shard = gather_replicas(keep, got, shard)
    other = call(functools.partial(double_kernel, 1), replica_half, early, late, name="other")
    left_rows = from_shards([shard] * n_shards)
    left_up, gram_up, keep, send = call(
        functools.partial(right_up_kernel, n_shards), [shaped(rank, rows), shaped(rank, rank), replica_half, replica_half],
        *left_rows, gu, eu, after=(late,), name="right_up", flops=product,
        scratch_shapes=[pltpu.VMEM((3 * rank, rows), BF16), wide, stage],
    )
    left_down, *parts = call(
        right_down_kernel, [shaped(rank, ff)] + [shaped(rows_here, rows + rank * n_shards)] * n_shards, mine, other, gd, ed, after=(left_up,),
        name="right_down", flops=product, scratch_shapes=[pltpu.VMEM((3 * rank, ff), BF16), narrow, stage],
    )
    got = swap(send, "dp", 1)
    shard, gram_down = call(
        functools.partial(sum_shards_kernel, n_shards), [shard_rows_here, shaped(rank, rank)], *from_shards(parts), name="shard_sum"
    )
    pieces = mean_replicas(keep, got, shard)
    early = swap(pieces[0], "dp", 1)
    piece = pieces[0].shape
    mine, rest = call(stack_rest_kernel, [shaped(half, *piece), shaped(half - 1, *piece)], *pieces, after=(early,), name="stack_z")
    other = call(place_other_kernel, shaped(half, *piece), early, swap(rest, "dp", 1), name="other")
    inv_up, inv_down, lhs_up, lhs_down = call(
        basis_kernel,
        [shaped(rank, rank)] * 2 + [shaped(rows, 4 * rank, dtype=BF16), shaped(ff, 4 * rank, dtype=BF16)],
        left_up, left_down, gram_up, gram_down, gu, eu, gd, ed, mine, name="basis", in_specs=[VMEM] * 8 + [ANY],
    )
    rhs_up, shard = call(
        factor_up_kernel, [shaped(4 * rank, ff, dtype=BF16), shaped(rows_here, rows + 128)], mine, other, inv_up,
        name="factor_up", scratch_shapes=[wide, stage],
    )
    right_rows = from_shards([shard] * n_shards)
    new_error_up, rebuilt_up = call(
        error_up_kernel, [shaped(1, rows, ff, dtype=BF16), shaped(rows, ff)], gu, eu, lhs_up, rhs_up, name="error_up", flops=product // 2,
        grid=(STEPS,), in_specs=[VMEM] * 4, out_specs=[replica_blocks(rows, ff), VMEM],
    )
    limit = CLIP_RMS * (2.0 * rows * ff * n_shards) ** 0.5
    rhs_down, clip = call(
        functools.partial(factor_down_kernel, limit, n_shards), [shaped(4 * rank, rows, dtype=BF16), shaped(8, 128)],
        *right_rows, inv_down, rebuilt_up, name="factor_down", in_specs=[VMEM] * (n_shards + 1) + [ANY], scratch_shapes=[narrow],
    )
    new_error_down, update_up, update_down = call(
        last_kernel, [shaped(1, ff, rows, dtype=BF16), shaped(rows, ff, dtype=BF16), shaped(ff, rows, dtype=BF16)],
        gd, ed, rebuilt_up, lhs_down, rhs_down, clip, name="last", flops=product, grid=(STEPS,),
        in_specs=[VMEM] * 6, out_specs=[replica_blocks(ff, rows), row_blocks(rows, ff), row_blocks(ff, rows)],
    )
    return new_error_up, update_up, new_error_down, update_down


def solution(mesh):
    placed = (
        P("dp", None, "tensor"),
        P("dp", None, "tensor"),
        P("dp", "tensor", None),
        P("dp", "tensor", None),
        P("tensor", None),
        P(),
    )
    return jax.shard_map(
        on_device,
        mesh=mesh,
        in_specs=placed,
        out_specs=(
            P("dp", None, "tensor"),
            P(None, "tensor"),
            P("dp", "tensor", None),
            P("tensor", None),
        ),
        check_vma=False,
    )
```

```python
import functools

import jax
import jax.numpy as jnp
from jax import lax
from jax.experimental import pallas as pl
from jax.experimental.pallas import tpu as pltpu
from jax.sharding import PartitionSpec as P

F32 = jnp.float32
BF16 = jnp.bfloat16
HIGHEST = lax.Precision.HIGHEST
CLIP_RMS = 0.1
STEPS = 4
MIB = 1024 * 1024
NT = ((1,), (1,))


def split3(x):
    first = x.astype(BF16)
    rest = x - first.astype(F32)
    second = rest.astype(BF16)
    return first, second, (rest - second.astype(F32)).astype(BF16)


def tree_sum(values):
    values = list(values)
    while len(values) > 1:
        values = [values[i] + values[i + 1] for i in range(0, len(values), 2)]
    return values[0]


def dot(a, b, dims=((1,), (0,)), precision=None):
    return lax.dot_general(a, b, (dims, ((), ())), precision=precision, preferred_element_type=F32)


def fold(x, rows):
    return jnp.concatenate([x[i : i + rows] for i in range(0, x.shape[0], rows)], axis=1)


def unfold(x, rows):
    count = rows // x.shape[0]
    width = x.shape[1] // count
    return jnp.concatenate([x[:, i * width : (i + 1) * width] for i in range(count)], axis=0)


def place(axis):
    index = lax.axis_index(axis)
    return lax.bitwise_and(index, 1), lax.shift_right_logical(index, 1)


def split_replicas(total, stage, keep, send):
    parity, _ = place("dp")
    half, per, _ = keep.shape
    for c in range(2 * half):
        stage[c] = total[c * per : (c + 1) * per, :]
    for c in range(half):
        keep[c] = stage[2 * c + parity]
        send[c] = stage[2 * c + 1 - parity]


def join_replicas(mine, other, stage, total):
    parity, _ = place("dp")
    half, per, _ = mine.shape
    width = total.shape[1]
    for c in range(half):
        stage[2 * c + parity] = mine[c, :, :width]
        stage[2 * c + 1 - parity] = other[c, :, :width]
    for c in range(2 * half):
        total[c * per : (c + 1) * per, :] = stage[c]


def split_shards(total, extra, outs):
    me = lax.axis_index("tensor")
    rows, width = outs[0].shape[0], total.shape[1]
    for j, out in enumerate(outs):
        owner = lax.bitwise_xor(me, j)
        out[:, :width] = total[pl.ds(pl.multiple_of(owner * rows, rows), rows), :]
        if extra is not None:
            out[:, width:] = fold(extra, rows)


def join_shards(pieces, total):
    me = lax.axis_index("tensor")
    rows, width = pieces[0].shape[0], total.shape[1]
    for j, piece in enumerate(pieces):
        owner = lax.bitwise_xor(me, j)
        total[pl.ds(pl.multiple_of(owner * rows, rows), rows), :] = piece[:, :width]


def left_kernel(n_shards, gu, eu, qu, gd, ed, qd, *refs):
    *outs, gu_in, eu_in, qu_in, pieces_up, total_up, gd_in, ed_in, qd_in, pieces_down, total_down, stage, q_sems, sems = refs
    up, down = (qu_in, pieces_up, total_up), (qd_in, pieces_down, total_down)
    firsts = [pltpu.make_async_copy(src, dst, q_sems.at[i]) for i, (src, dst) in enumerate(((qd, qd_in), (qu, qu_in)))]
    stages = []
    for g, e, g_in, e_in, part, count in ((gd, ed, gd_in, ed_in, down, 6), (gu, eu, gu_in, eu_in, up, 2)):
        block = g_in.shape[0] // count
        at = 0
        for size in (1, 1, 2, 2) if count == 6 else (1, 1):
            rows = slice(at * block, (at + size) * block)
            window = pl.ds(at * block, size * block)
            n = len(stages)
            copies = [pltpu.make_async_copy(src.at[0, window, :], dst.at[window, :], sems.at[n, k]) for k, (src, dst) in enumerate(((g, g_in), (e, e_in)))]
            stages.append((copies, g_in, e_in, rows, part))
            at += size

    def fetch(n):
        if n < len(stages):
            for copy in stages[n][0]:
                copy.start()

    firsts[0].start()
    fetch(0)
    fetch(1)
    firsts[1].start()
    for n, (first, (q, pieces, _)) in enumerate(zip(firsts, (down, up))):
        first.wait()
        fetch(n + 2)
        split_rows(q, pieces)
    for n, (copies, g, e, rows, (_, pieces, total)) in enumerate(stages):
        for copy in copies:
            copy.wait()
        fetch(n + 4)
        total[:, rows] = add_pieces(dot(pieces[...], g[rows, :], NT) + dot(pieces[...], e[rows, :], NT))
    split_shards(total_up, None, outs[:n_shards])
    split_replicas(total_down, stage, *outs[n_shards:])


def fetch_kernel(*refs):
    half = len(refs) // 2
    for source, out in zip(refs[:half], refs[half:]):
        out[...] = source[...]


def sum_shards_kernel(n_shards, *refs):
    terms, (out, gram) = refs[:n_shards], refs[n_shards:]
    total = tree_sum(term[...] for term in terms)
    out[...] = total[:, : out.shape[1]]
    gram[...] = unfold(total[:, out.shape[1] :], gram.shape[0])


def first_shards_kernel(*refs):
    refs[-1][...] = tree_sum(term[...] for term in refs[:-1])


def own_and_other(j, bit):
    mine = lax.bitwise_and(lax.shift_right_logical(lax.axis_index("dp"), bit), 1)
    return 2 * j + mine, 2 * j + 1 - mine


def split_chunks(bit, chunks, keep, send):
    for j in range(keep.shape[0]):
        mine, other = own_and_other(j, bit)
        keep[j] = chunks[mine]
        send[j] = chunks[other]


def halve_kernel(bit, keep, got, keep_out, send_out, chunks):
    chunks[...] = keep[...] + got[...]
    split_chunks(bit, chunks, keep_out, send_out)


def sum_kernel(scale, mine, other, out):
    out[...] = (mine[...] + other[...]) * scale


def double_kernel(bit, mine, other, out):
    for j in range(mine.shape[0]):
        here, there = own_and_other(j, bit)
        out[here] = mine[j]
        out[there] = other[j]


def half_sum_kernel(keep, got, shard, out):
    count, per, ff = keep.shape
    block = shard.shape[1] // count
    for c in range(count):
        out[c, :, :ff] = keep[c] + got[c]
        out[c, :, ff:] = fold(shard[:, c * block : (c + 1) * block], per)


def join_shard(chunks, ff, rows):
    return jnp.concatenate([unfold(chunks[c, :, ff:], rows) for c in range(chunks.shape[0])], axis=1)


def double_apart_kernel(bit, mine, other, out, rest, shard):
    ff = out.shape[2]
    for j in range(mine.shape[0]):
        here, there = own_and_other(j, bit)
        out[here] = mine[j, :, :ff]
        out[there] = other[j, :, :ff]
        rest[j] = other[j, :, :ff]
    shard[...] = join_shard(mine, ff, shard.shape[0]) + join_shard(other, ff, shard.shape[0])


def strip_kernel(both, out):
    out[...] = both[:, :, : out.shape[2]]


def add_columns_kernel(chunks, shard, out):
    count, per, ff = chunks.shape
    block = shard.shape[1] // count
    for c in range(count):
        out[c, :, :ff] = chunks[c]
        out[c, :, ff:] = fold(shard[:, c * block : (c + 1) * block], per)


def split_z_kernel(keep, got, shard, *refs):
    *outs, stage = refs
    _, z = place("dp")
    half, per, ff = keep.shape
    block = shard.shape[1] // half
    for c in range(half):
        stage[c, :, :ff] = keep[c] + got[c]
        stage[c, :, ff:] = fold(shard[:, c * block : (c + 1) * block], per)
    for j, out in zip([0, *range(half - 1, 0, -1)], outs):
        out[...] = stage[lax.bitwise_xor(z, j)]


def mean_kernel(n_dp, *refs):
    refs[-1][...] = tree_sum(ref[...] for ref in refs[:-1]) / n_dp


def stack_kernel(*refs):
    _, z = place("dp")
    for j, ref in enumerate(refs[:-1]):
        refs[-1][lax.bitwise_xor(z, j)] = ref[...]


def shard_rows(mine, other, ff, rows):
    half = mine.shape[0]
    return jnp.concatenate([unfold(mine[c, :, ff:] + other[c, :, ff:], rows) for c in range(half)], axis=1)


def split_rows(left, pieces):
    rank = left.shape[0]
    for i, piece in enumerate(split3(left[...])):
        pieces[i * rank : (i + 1) * rank, :] = piece


def add_pieces(t):
    rank = t.shape[0] // 3
    return t[:rank] + (t[rank : 2 * rank] + t[2 * rank :])


def right_down_kernel(mine, other, g, e, left, *refs):
    *outs, pieces, total, stage = refs
    join_replicas(mine, other, stage, left)
    split_rows(left, pieces)
    total[...] = add_pieces(dot(pieces[...], g[0]) + dot(pieces[...], e[0]))
    split_shards(total, dot(left[...], left[...], NT, HIGHEST), outs)


def right_up_kernel(n_shards, *refs):
    shards, refs = refs[:n_shards], refs[n_shards:]
    g, e, left, gram, keep, send, pieces, total, stage = refs
    join_shards(shards, left)
    split_rows(left, pieces)
    block = total.shape[1] // STEPS
    for i in range(STEPS):
        part = slice(i * block, (i + 1) * block)
        total[:, part] = add_pieces(dot(pieces[...], g[0, :, part]) + dot(pieces[...], e[0, :, part]))
    split_replicas(total, stage, keep, send)
    gram[...] = dot(left[...], left[...], NT, HIGHEST)


def inverse_factors(grams):
    rank = grams[0].shape[0]
    count = rank // 8
    panel = 4
    lane = lax.broadcasted_iota(jnp.int32, (8, 2 * rank), 1)
    row = lax.broadcasted_iota(jnp.int32, (8, 2 * rank), 0)
    states, pivots = [], []
    for gram in grams:
        wide = jnp.concatenate([gram, jnp.zeros_like(gram)], axis=1)
        states.append([wide[i : i + 8] + (lane == row + (rank + i)).astype(F32) for i in range(0, rank, 8)])
        pivots.append([])
    for start in range(0, rank, panel):
        at = start // 8
        below = range(at, count)
        spread = [
            [{i: jnp.broadcast_to(blocks[i][:, start + j : start + j + 1], (8, 2 * rank)) for i in below} for j in range(panel)]
            for blocks in states
        ]
        for j in range(panel):
            inner = (start + j) % 8
            for blocks, columns, found in zip(states, spread, pivots):
                pivot = columns[j][at][inner : inner + 1, :]
                found.append(pivot)
                inverse = 1.0 / pivot
                factor = {i: jnp.where(row > inner, columns[j][i], 0.0) if i == at else columns[j][i] for i in below}
                for later in columns[j + 1 :]:
                    head = later[at][inner : inner + 1, :] * inverse
                    for i in below:
                        later[i] = later[i] - factor[i] * head
                scaled = blocks[at][inner : inner + 1, :] * inverse
                for i in below:
                    blocks[i] = blocks[i] - factor[i] * scaled
    results = []
    for blocks, found in zip(states, pivots):
        rows = [block / jnp.sqrt(jnp.concatenate(found[8 * i : 8 * i + 8], axis=0)) for i, block in enumerate(blocks)]
        results.append(jnp.concatenate(rows, axis=0)[:, rank:])
    return results


def basis_kernel(left_up, left_down, gram_up, gram_down, *refs):
    inv_up, inv_down, lhs_up, lhs_down = refs[-4:]
    inverses = inverse_factors([gram_up[...], gram_down[...]])
    rank = left_up.shape[0]
    for inverse, inv, left, lhs in zip(inverses, (inv_up, inv_down), (left_up, left_down), (lhs_up, lhs_down)):
        inv[...] = inverse
        first, second, _ = split3(dot(inverse, left[...], precision=HIGHEST).T)
        lhs[:, :rank] = first
        lhs[:, rank : 2 * rank] = first
        lhs[:, 2 * rank : 3 * rank] = second
        lhs[:, 3 * rank :] = second


def right_factor(inv, total, rhs):
    rank = inv.shape[0]
    right = dot(inv[...], total[...], precision=HIGHEST)
    first, second, _ = split3(right)
    rhs[:rank, :] = first
    rhs[rank : 2 * rank, :] = second
    rhs[2 * rank : 3 * rank, :] = first
    rhs[3 * rank :, :] = second
    return jnp.sum(right * right)


def factor_up_kernel(mine, other, inv, rhs, shard, total, stage):
    join_replicas(mine, other, stage, total)
    square = right_factor(inv, total, rhs)
    rows, ff = shard.shape[0], total.shape[1]
    width = shard.shape[1] - 128
    shard[:, :width] = shard_rows(mine, other, ff, rows)
    shard[:, width:] = jnp.full((rows, 128), square, F32)


def factor_down_kernel(limit, n_shards, *refs):
    shards, refs = refs[:n_shards], refs[n_shards:]
    inv, _, rhs, clip, total = refs
    join_shards(shards, total)
    square = right_factor(inv, total, rhs)
    width = total.shape[1]
    norm_sq = square + tree_sum(shard[:8, width:] for shard in shards)
    clip[...] = jnp.minimum(jnp.float32(1.0), limit / jnp.sqrt(norm_sq))


def rows_of(block):
    return pl.ds(pl.multiple_of(pl.program_id(0) * block, block), block)


def error_up_kernel(g, e, lhs, rhs, error, kept):
    part = rows_of(error.shape[1])
    rebuilt = dot(lhs[part, :], rhs[...])
    kept[part, :] = rebuilt
    error[0] = (g[0, part, :].astype(F32) + e[0, part, :].astype(F32) - rebuilt).astype(BF16)


def last_kernel(g, e, rebuilt_up, lhs_down, rhs_down, clip, error, update_up, update_down):
    factor = clip[:1, :1]
    part = rows_of(update_down.shape[0])
    rebuilt = dot(lhs_down[part, :], rhs_down[...])
    update_down[...] = (factor * rebuilt).astype(BF16)
    error[0] = (g[0, part, :].astype(F32) + e[0, part, :].astype(F32) - rebuilt).astype(BF16)
    part = rows_of(update_up.shape[0])
    update_up[...] = (factor * rebuilt_up[part, :]).astype(BF16)


def shaped(*dims, dtype=F32):
    return jax.ShapeDtypeStruct(dims, dtype)


def whole(shape):
    return pl.BlockSpec(shape, lambda *_: (0,) * len(shape))


def row_blocks(rows, columns):
    return pl.BlockSpec((rows // STEPS, columns), lambda i: (i, 0))


def replica_blocks(rows, columns):
    return pl.BlockSpec((1, rows // STEPS, columns), lambda i: (0, i, 0))


VMEM = pl.BlockSpec(memory_space=pltpu.VMEM)
ANY = pl.BlockSpec(memory_space=pl.ANY)


def call(kernel, out_shape, *args, after=(), in_specs=None, flops=0, limit=12, name=None, **more):
    arrays = list(args) + jax.tree.leaves(out_shape)
    size = sum(a.size * a.dtype.itemsize for a in arrays)
    skip = len(after)
    return pl.pallas_call(
        lambda *refs: kernel(*refs[skip:]), out_shape=out_shape, in_specs=[ANY] * skip + (in_specs or [VMEM] * len(args)),
        compiler_params=pltpu.CompilerParams(vmem_limit_bytes=limit * MIB),
        cost_estimate=pl.CostEstimate(flops=flops, bytes_accessed=size, transcendentals=0), name=name, **more,
    )(*after, *args)


def swap(x, axis, distance):
    pairs = [(i, i ^ distance) for i in range(lax.axis_size(axis))]
    return lax.ppermute(x, axis, pairs)


def from_shards(parts):
    return [parts[0]] + [swap(parts[j], "tensor", j) for j in range(1, len(parts))]


def scatter_replicas(keep, send, got, after):
    n_dp = lax.axis_size("dp")
    for bit in range(n_dp.bit_length() - 2):
        got = swap(send, "dp", 1 << bit) if bit else got
        if bit == n_dp.bit_length() - 3:
            return keep, got
        count, per, ff = keep.shape
        out = shaped(count // 2, per, ff)
        keep, send = call(
            functools.partial(halve_kernel, bit + 1), [out, out], keep, got, after=after if bit == 0 else (), name="halve",
            scratch_shapes=[pltpu.VMEM(keep.shape, F32)],
        )


def gather_replicas(keep, got, shard):
    n_dp = lax.axis_size("dp")
    last = n_dp.bit_length() - 2
    count, per, ff = keep.shape
    columns = ff + shard.shape[0] * shard.shape[1] // (count * per)
    both = shaped(count, per, columns)
    total = call(half_sum_kernel, both, keep, got, shard, name="half_sum")
    mine = call(functools.partial(sum_kernel, 1.0 / n_dp), both, total, swap(total, "dp", 1 << last), name="mean")
    for bit in range(last - 1, 0, -1):
        other = swap(mine, "dp", 1 << bit)
        half = shaped(count, per, ff)
        early = swap(call(strip_kernel, half, mine, name="strip"), "dp", 1) if bit == 1 else None
        count *= 2
        mine, rest, shard = call(
            functools.partial(double_apart_kernel, bit), [shaped(count, per, ff), half, shaped(*shard.shape)], mine, other,
            after=(early,) if bit == 1 else (), name="double",
        )
        if bit > 1:
            mine = call(add_columns_kernel, shaped(count, per, ff + (columns - ff) // (count // keep.shape[0])), mine, shard, name="add_columns")
    return mine, early, swap(rest, "dp", 1), shard


def from_z(parts):
    got = {j: swap(parts[j], "dp", 2 * j) for j in range(len(parts) - 1, 0, -1)}
    return [parts[0]] + [got[j] for j in range(1, len(parts))]


def mean_replicas(keep, got, shard):
    n_dp = lax.axis_size("dp")
    half, per, ff = keep.shape
    piece = shaped(per, ff + shard.shape[0] * shard.shape[1] // (half * per))
    stage = pltpu.VMEM((half, *piece.shape), F32)
    parts = call(split_z_kernel, [piece] * half, keep, got, shard, name="split_z", scratch_shapes=[stage])
    parts = [parts[0], *parts[:0:-1]]
    mean = call(functools.partial(mean_kernel, n_dp), piece, *from_z(parts), name="replica_mean")
    return from_z([mean] * half)


def on_device(gu, eu, gd, ed, qu, qd):
    qu, qd = qu.T, qd.T
    n_dp, n_shards = lax.axis_size("dp"), lax.axis_size("tensor")
    _, rows, ff = gu.shape
    rank = qu.shape[0]
    half, per, rows_here = n_dp // 2, rank // n_dp, rank // n_shards
    shard_rows_here = shaped(rows_here, rows)
    replica_half = shaped(half, per, ff)
    stage = pltpu.VMEM((n_dp, per, ff), F32)
    wide = pltpu.VMEM((rank, ff), F32)
    narrow = pltpu.VMEM((rank, rows), F32)
    product = 4 * rows * ff * 4 * rank

    buffers = [
        [pltpu.VMEM(g.shape[1:], BF16)] * 2 + [pltpu.VMEM(q.shape, F32), pltpu.VMEM((3 * rank, q.shape[1]), BF16), total]
        for g, q, total in ((gu, qu, narrow), (gd, qd, wide))
    ]
    *parts, keep, send = call(
        functools.partial(left_kernel, n_shards), [shard_rows_here] * n_shards + [replica_half] * 2, gu, eu, qu, gd, ed, qd,
        name="left", flops=2 * product, limit=61, in_specs=[pl.BlockSpec(memory_space=pltpu.HBM)] * 6,
        scratch_shapes=buffers[0] + buffers[1] + [stage, pltpu.SemaphoreType.DMA((2,)), pltpu.SemaphoreType.DMA((6, 2))],
    )
    got = swap(send, "dp", 1)
    parts = from_shards(parts)
    parts[0], keep = call(fetch_kernel, [shard_rows_here, replica_half], parts[0], keep, name="fetch", flops=product // 4)
    shard = call(first_shards_kernel, shard_rows_here, *parts, name="shard_sum")
    keep, got = scatter_replicas(keep, send, got, (shard,))
    shard = call(first_shards_kernel, shard_rows_here, shard, swap(shard, "dp", 1), name="replica_sum")
    mine, early, late, shard = gather_replicas(keep, got, shard)
    other = call(functools.partial(double_kernel, 1), replica_half, early, late, name="other")
    left_rows = from_shards([shard] * n_shards)
    left_up, gram_up, keep, send = call(
        functools.partial(right_up_kernel, n_shards), [shaped(rank, rows), shaped(rank, rank), replica_half, replica_half],
        *left_rows, gu, eu, after=(late,), name="right_up", flops=product,
        scratch_shapes=[pltpu.VMEM((3 * rank, rows), BF16), wide, stage],
    )
    left_down, *parts = call(
        right_down_kernel, [shaped(rank, ff)] + [shaped(rows_here, rows + rank * n_shards)] * n_shards, mine, other, gd, ed, after=(left_up,),
        name="right_down", flops=product, scratch_shapes=[pltpu.VMEM((3 * rank, ff), BF16), narrow, stage],
    )
    got = swap(send, "dp", 1)
    shard, gram_down = call(
        functools.partial(sum_shards_kernel, n_shards), [shard_rows_here, shaped(rank, rank)], *from_shards(parts), name="shard_sum"
    )
    pieces = mean_replicas(keep, got, shard)
    mine = call(stack_kernel, shaped(half, *pieces[0].shape), *pieces, name="stack_z")
    other = swap(mine, "dp", 1)
    inv_up, inv_down, lhs_up, lhs_down = call(
        basis_kernel,
        [shaped(rank, rank)] * 2 + [shaped(rows, 4 * rank, dtype=BF16), shaped(ff, 4 * rank, dtype=BF16)],
        left_up, left_down, gram_up, gram_down, gu, eu, gd, ed, mine, name="basis", in_specs=[VMEM] * 8 + [ANY],
    )
    rhs_up, shard = call(
        factor_up_kernel, [shaped(4 * rank, ff, dtype=BF16), shaped(rows_here, rows + 128)], mine, other, inv_up,
        name="factor_up", scratch_shapes=[wide, stage],
    )
    right_rows = from_shards([shard] * n_shards)
    new_error_up, rebuilt_up = call(
        error_up_kernel, [shaped(1, rows, ff, dtype=BF16), shaped(rows, ff)], gu, eu, lhs_up, rhs_up, name="error_up", flops=product // 2,
        grid=(STEPS,), in_specs=[VMEM] * 4, out_specs=[replica_blocks(rows, ff), VMEM],
    )
    limit = CLIP_RMS * (2.0 * rows * ff * n_shards) ** 0.5
    rhs_down, clip = call(
        functools.partial(factor_down_kernel, limit, n_shards), [shaped(4 * rank, rows, dtype=BF16), shaped(8, 128)],
        *right_rows, inv_down, rebuilt_up, name="factor_down", in_specs=[VMEM] * (n_shards + 1) + [ANY], scratch_shapes=[narrow],
    )
    new_error_down, update_up, update_down = call(
        last_kernel, [shaped(1, ff, rows, dtype=BF16), shaped(rows, ff, dtype=BF16), shaped(ff, rows, dtype=BF16)],
        gd, ed, rebuilt_up, lhs_down, rhs_down, clip, name="last", flops=product, grid=(STEPS,),
        in_specs=[VMEM] * 6, out_specs=[replica_blocks(ff, rows), row_blocks(rows, ff), row_blocks(ff, rows)],
    )
    return new_error_up, update_up, new_error_down, update_down


def solution(mesh):
    placed = (
        P("dp", None, "tensor"),
        P("dp", None, "tensor"),
        P("dp", "tensor", None),
        P("dp", "tensor", None),
        P("tensor", None),
        P(),
    )
    return jax.shard_map(
        on_device,
        mesh=mesh,
        in_specs=placed,
        out_specs=(
            P("dp", None, "tensor"),
            P(None, "tensor"),
            P("dp", "tensor", None),
            P("tensor", None),
        ),
        check_vma=False,
    )
```

```python
import functools

import jax
import jax.numpy as jnp
from jax import lax
from jax.experimental import pallas as pl
from jax.experimental.pallas import tpu as pltpu
from jax.sharding import PartitionSpec as P

F32 = jnp.float32
BF16 = jnp.bfloat16
HIGHEST = lax.Precision.HIGHEST
CLIP_RMS = 0.1
STEPS = 4
MIB = 1024 * 1024
NT = ((1,), (1,))


def split3(x):
    first = x.astype(BF16)
    rest = x - first.astype(F32)
    second = rest.astype(BF16)
    return first, second, (rest - second.astype(F32)).astype(BF16)


def tree_sum(values):
    values = list(values)
    while len(values) > 1:
        values = [values[i] + values[i + 1] for i in range(0, len(values), 2)]
    return values[0]


def dot(a, b, dims=((1,), (0,)), precision=None):
    return lax.dot_general(a, b, (dims, ((), ())), precision=precision, preferred_element_type=F32)


def fold(x, rows):
    return jnp.concatenate([x[i : i + rows] for i in range(0, x.shape[0], rows)], axis=1)


def unfold(x, rows):
    count = rows // x.shape[0]
    width = x.shape[1] // count
    return jnp.concatenate([x[:, i * width : (i + 1) * width] for i in range(count)], axis=0)


def place(axis):
    index = lax.axis_index(axis)
    return lax.bitwise_and(index, 1), lax.shift_right_logical(index, 1)


def split_replicas(total, stage, keep, send):
    parity, _ = place("dp")
    half, per, _ = keep.shape
    for c in range(2 * half):
        stage[c] = total[c * per : (c + 1) * per, :]
    for c in range(half):
        keep[c] = stage[2 * c + parity]
        send[c] = stage[2 * c + 1 - parity]


def join_replicas(mine, other, stage, total):
    parity, _ = place("dp")
    half, per, _ = mine.shape
    width = total.shape[1]
    for c in range(half):
        stage[2 * c + parity] = mine[c, :, :width]
        stage[2 * c + 1 - parity] = other[c, :, :width]
    for c in range(2 * half):
        total[c * per : (c + 1) * per, :] = stage[c]


def split_shards(total, extra, outs):
    me = lax.axis_index("tensor")
    rows, width = outs[0].shape[0], total.shape[1]
    for j, out in enumerate(outs):
        owner = lax.bitwise_xor(me, j)
        out[:, :width] = total[pl.ds(pl.multiple_of(owner * rows, rows), rows), :]
        if extra is not None:
            out[:, width:] = fold(extra, rows)


def join_shards(pieces, total):
    me = lax.axis_index("tensor")
    rows, width = pieces[0].shape[0], total.shape[1]
    for j, piece in enumerate(pieces):
        owner = lax.bitwise_xor(me, j)
        total[pl.ds(pl.multiple_of(owner * rows, rows), rows), :] = piece[:, :width]


def left_kernel(n_shards, gu, eu, qu, gd, ed, qd, *refs):
    *outs, gu_in, eu_in, qu_in, pieces_up, total_up, gd_in, ed_in, qd_in, pieces_down, total_down, stage, kept, sent, q_sems, sems, out_sems = refs
    halves = [pltpu.make_async_copy(src, dst, out_sems.at[i]) for i, (src, dst) in enumerate(((sent, outs[-1]), (kept, outs[-2])))]
    up, down = (qu_in, pieces_up, total_up), (qd_in, pieces_down, total_down)
    firsts = [pltpu.make_async_copy(src, dst, q_sems.at[i]) for i, (src, dst) in enumerate(((qd, qd_in), (qu, qu_in)))]
    stages = []
    for g, e, g_in, e_in, part, count in ((gd, ed, gd_in, ed_in, down, 3), (gu, eu, gu_in, eu_in, up, 2)):
        block = g_in.shape[0] // count
        for i in range(count):
            rows = pl.ds(i * block, block)
            n = len(stages)
            copies = [pltpu.make_async_copy(src.at[0, rows, :], dst.at[rows, :], sems.at[n, k]) for k, (src, dst) in enumerate(((g, g_in), (e, e_in)))]
            stages.append((copies, g_in, e_in, slice(i * block, (i + 1) * block), part))

    def fetch(n):
        if n < len(stages):
            for copy in stages[n][0]:
                copy.start()

    firsts[0].start()
    fetch(0)
    firsts[1].start()
    for n, (first, (q, pieces, _)) in enumerate(zip(firsts, (down, up))):
        first.wait()
        fetch(n + 1)
        split_rows(q, pieces)
    for n, (copies, g, e, rows, (_, pieces, total)) in enumerate(stages):
        for copy in copies:
            copy.wait()
        fetch(n + 3)
        total[:, rows] = add_pieces(dot(pieces[...], g[rows, :], NT) + dot(pieces[...], e[rows, :], NT))
        if n == 2:
            split_replicas(total_down, stage, kept, sent)
            for half in halves:
                half.start()
    split_shards(total_up, None, outs[:n_shards])
    for half in halves:
        half.wait()


def fetch_kernel(*refs):
    half = len(refs) // 2
    for source, out in zip(refs[:half], refs[half:]):
        out[...] = source[...]


def sum_shards_kernel(n_shards, *refs):
    terms, (out, gram) = refs[:n_shards], refs[n_shards:]
    total = tree_sum(term[...] for term in terms)
    out[...] = total[:, : out.shape[1]]
    gram[...] = unfold(total[:, out.shape[1] :], gram.shape[0])


def first_shards_kernel(*refs):
    refs[-1][...] = tree_sum(term[...] for term in refs[:-1])


def own_and_other(j, bit):
    mine = lax.bitwise_and(lax.shift_right_logical(lax.axis_index("dp"), bit), 1)
    return 2 * j + mine, 2 * j + 1 - mine


def split_chunks(bit, chunks, keep, send):
    for j in range(keep.shape[0]):
        mine, other = own_and_other(j, bit)
        keep[j] = chunks[mine]
        send[j] = chunks[other]


def halve_kernel(bit, keep, got, keep_out, send_out, chunks):
    chunks[...] = keep[...] + got[...]
    split_chunks(bit, chunks, keep_out, send_out)


def sum_kernel(scale, mine, other, out):
    out[...] = (mine[...] + other[...]) * scale


def double_kernel(bit, mine, other, out):
    for j in range(mine.shape[0]):
        here, there = own_and_other(j, bit)
        out[here] = mine[j]
        out[there] = other[j]


def half_sum_kernel(keep, got, shard, out):
    count, per, ff = keep.shape
    block = shard.shape[1] // count
    for c in range(count):
        out[c, :, :ff] = keep[c] + got[c]
        out[c, :, ff:] = fold(shard[:, c * block : (c + 1) * block], per)


def join_shard(chunks, ff, rows):
    return jnp.concatenate([unfold(chunks[c, :, ff:], rows) for c in range(chunks.shape[0])], axis=1)


def double_apart_kernel(bit, mine, other, out, shard):
    ff = out.shape[2]
    for j in range(mine.shape[0]):
        here, there = own_and_other(j, bit)
        out[here] = mine[j, :, :ff]
        out[there] = other[j, :, :ff]
    shard[...] = join_shard(mine, ff, shard.shape[0]) + join_shard(other, ff, shard.shape[0])


def add_columns_kernel(chunks, shard, out):
    count, per, ff = chunks.shape
    block = shard.shape[1] // count
    for c in range(count):
        out[c, :, :ff] = chunks[c]
        out[c, :, ff:] = fold(shard[:, c * block : (c + 1) * block], per)


def split_z_kernel(keep, got, shard, *refs):
    *outs, stage = refs
    _, z = place("dp")
    half, per, ff = keep.shape
    block = shard.shape[1] // half
    for c in range(half):
        stage[c, :, :ff] = keep[c] + got[c]
        stage[c, :, ff:] = fold(shard[:, c * block : (c + 1) * block], per)
    for j, out in zip([0, *range(half - 1, 0, -1)], outs):
        out[...] = stage[lax.bitwise_xor(z, j)]


def mean_kernel(n_dp, *refs):
    refs[-1][...] = tree_sum(ref[...] for ref in refs[:-1]) / n_dp


def stack_kernel(*refs):
    _, z = place("dp")
    for j, ref in enumerate(refs[:-1]):
        refs[-1][lax.bitwise_xor(z, j)] = ref[...]


def shard_rows(mine, other, ff, rows):
    half = mine.shape[0]
    return jnp.concatenate([unfold(mine[c, :, ff:] + other[c, :, ff:], rows) for c in range(half)], axis=1)


def split_rows(left, pieces):
    rank = left.shape[0]
    for i, piece in enumerate(split3(left[...])):
        pieces[i * rank : (i + 1) * rank, :] = piece


def add_pieces(t):
    rank = t.shape[0] // 3
    return t[:rank] + (t[rank : 2 * rank] + t[2 * rank :])


def right_down_kernel(mine, other, g, e, left, *refs):
    *outs, pieces, total, stage = refs
    join_replicas(mine, other, stage, left)
    split_rows(left, pieces)
    total[...] = add_pieces(dot(pieces[...], g[0]) + dot(pieces[...], e[0]))
    split_shards(total, dot(left[...], left[...], NT, HIGHEST), outs)


def right_up_kernel(n_shards, *refs):
    shards, refs = refs[:n_shards], refs[n_shards:]
    g, e, left, gram, keep, send, pieces, total, stage = refs
    join_shards(shards, left)
    split_rows(left, pieces)
    block = total.shape[1] // STEPS
    for i in range(STEPS):
        part = slice(i * block, (i + 1) * block)
        total[:, part] = add_pieces(dot(pieces[...], g[0, :, part]) + dot(pieces[...], e[0, :, part]))
    split_replicas(total, stage, keep, send)
    gram[...] = dot(left[...], left[...], NT, HIGHEST)


def inverse_factors(grams):
    rank = grams[0].shape[0]
    count = rank // 8
    panel = 4
    lane = lax.broadcasted_iota(jnp.int32, (8, 2 * rank), 1)
    row = lax.broadcasted_iota(jnp.int32, (8, 2 * rank), 0)
    states, pivots = [], []
    for gram in grams:
        wide = jnp.concatenate([gram, jnp.zeros_like(gram)], axis=1)
        states.append([wide[i : i + 8] + (lane == row + (rank + i)).astype(F32) for i in range(0, rank, 8)])
        pivots.append([])
    for start in range(0, rank, panel):
        at = start // 8
        below = range(at, count)
        spread = [
            [{i: jnp.broadcast_to(blocks[i][:, start + j : start + j + 1], (8, 2 * rank)) for i in below} for j in range(panel)]
            for blocks in states
        ]
        for j in range(panel):
            inner = (start + j) % 8
            for blocks, columns, found in zip(states, spread, pivots):
                pivot = columns[j][at][inner : inner + 1, :]
                found.append(pivot)
                inverse = 1.0 / pivot
                factor = {i: jnp.where(row > inner, columns[j][i], 0.0) if i == at else columns[j][i] for i in below}
                for later in columns[j + 1 :]:
                    head = later[at][inner : inner + 1, :] * inverse
                    for i in below:
                        later[i] = later[i] - factor[i] * head
                scaled = blocks[at][inner : inner + 1, :] * inverse
                for i in below:
                    blocks[i] = blocks[i] - factor[i] * scaled
    results = []
    for blocks, found in zip(states, pivots):
        rows = [block / jnp.sqrt(jnp.concatenate(found[8 * i : 8 * i + 8], axis=0)) for i, block in enumerate(blocks)]
        results.append(jnp.concatenate(rows, axis=0)[:, rank:])
    return results


def basis_kernel(left_up, left_down, gram_up, gram_down, *refs):
    inv_up, inv_down, lhs_up, lhs_down = refs[-4:]
    inverses = inverse_factors([gram_up[...], gram_down[...]])
    rank = left_up.shape[0]
    for inverse, inv, left, lhs in zip(inverses, (inv_up, inv_down), (left_up, left_down), (lhs_up, lhs_down)):
        inv[...] = inverse
        first, second, _ = split3(dot(inverse, left[...], precision=HIGHEST).T)
        lhs[:, :rank] = first
        lhs[:, rank : 2 * rank] = first
        lhs[:, 2 * rank : 3 * rank] = second
        lhs[:, 3 * rank :] = second


def right_factor(inv, total, rhs):
    rank = inv.shape[0]
    right = dot(inv[...], total[...], precision=HIGHEST)
    first, second, _ = split3(right)
    rhs[:rank, :] = first
    rhs[rank : 2 * rank, :] = second
    rhs[2 * rank : 3 * rank, :] = first
    rhs[3 * rank :, :] = second
    return jnp.sum(right * right)


def factor_up_kernel(mine, other, inv, rhs, shard, total, stage):
    join_replicas(mine, other, stage, total)
    square = right_factor(inv, total, rhs)
    rows, ff = shard.shape[0], total.shape[1]
    width = shard.shape[1] - 128
    shard[:, :width] = shard_rows(mine, other, ff, rows)
    shard[:, width:] = jnp.full((rows, 128), square, F32)


def factor_down_kernel(limit, n_shards, *refs):
    shards, refs = refs[:n_shards], refs[n_shards:]
    inv, _, rhs, clip, total = refs
    join_shards(shards, total)
    square = right_factor(inv, total, rhs)
    width = total.shape[1]
    norm_sq = square + tree_sum(shard[:8, width:] for shard in shards)
    clip[...] = jnp.minimum(jnp.float32(1.0), limit / jnp.sqrt(norm_sq))


def rows_of(block):
    return pl.ds(pl.multiple_of(pl.program_id(0) * block, block), block)


def error_up_kernel(g, e, lhs, rhs, error, kept):
    part = rows_of(error.shape[1])
    rebuilt = dot(lhs[part, :], rhs[...])
    kept[part, :] = rebuilt
    error[0] = (g[0, part, :].astype(F32) + e[0, part, :].astype(F32) - rebuilt).astype(BF16)


def last_kernel(g, e, rebuilt_up, lhs_down, rhs_down, clip, error, update_up, update_down):
    factor = clip[:1, :1]
    part = rows_of(update_down.shape[0])
    rebuilt = dot(lhs_down[part, :], rhs_down[...])
    update_down[...] = (factor * rebuilt).astype(BF16)
    error[0] = (g[0, part, :].astype(F32) + e[0, part, :].astype(F32) - rebuilt).astype(BF16)
    part = rows_of(update_up.shape[0])
    update_up[...] = (factor * rebuilt_up[part, :]).astype(BF16)


def shaped(*dims, dtype=F32):
    return jax.ShapeDtypeStruct(dims, dtype)


def whole(shape):
    return pl.BlockSpec(shape, lambda *_: (0,) * len(shape))


def row_blocks(rows, columns):
    return pl.BlockSpec((rows // STEPS, columns), lambda i: (i, 0))


def replica_blocks(rows, columns):
    return pl.BlockSpec((1, rows // STEPS, columns), lambda i: (0, i, 0))


VMEM = pl.BlockSpec(memory_space=pltpu.VMEM)
ANY = pl.BlockSpec(memory_space=pl.ANY)
HBM = pl.BlockSpec(memory_space=pltpu.HBM)


def call(kernel, out_shape, *args, after=(), in_specs=None, flops=0, limit=12, name=None, **more):
    arrays = list(args) + jax.tree.leaves(out_shape)
    size = sum(a.size * a.dtype.itemsize for a in arrays)
    skip = len(after)
    return pl.pallas_call(
        lambda *refs: kernel(*refs[skip:]), out_shape=out_shape, in_specs=[ANY] * skip + (in_specs or [VMEM] * len(args)),
        compiler_params=pltpu.CompilerParams(vmem_limit_bytes=int(limit * MIB)),
        cost_estimate=pl.CostEstimate(flops=flops, bytes_accessed=size, transcendentals=0), name=name, **more,
    )(*after, *args)


def swap(x, axis, distance):
    pairs = [(i, i ^ distance) for i in range(lax.axis_size(axis))]
    return lax.ppermute(x, axis, pairs)


def from_shards(parts):
    return [parts[0]] + [swap(parts[j], "tensor", j) for j in range(1, len(parts))]


def scatter_replicas(keep, send, got, after):
    n_dp = lax.axis_size("dp")
    for bit in range(n_dp.bit_length() - 2):
        got = swap(send, "dp", 1 << bit) if bit else got
        if bit == n_dp.bit_length() - 3:
            return keep, got
        count, per, ff = keep.shape
        out = shaped(count // 2, per, ff)
        keep, send = call(
            functools.partial(halve_kernel, bit + 1), [out, out], keep, got, after=after if bit == 0 else (), name="halve",
            scratch_shapes=[pltpu.VMEM(keep.shape, F32)],
        )


def gather_replicas(keep, got, shard):
    n_dp = lax.axis_size("dp")
    last = n_dp.bit_length() - 2
    count, per, ff = keep.shape
    columns = ff + shard.shape[0] * shard.shape[1] // (count * per)
    both = shaped(count, per, columns)
    total = call(half_sum_kernel, both, keep, got, shard, name="half_sum")
    mine = call(functools.partial(sum_kernel, 1.0 / n_dp), both, total, swap(total, "dp", 1 << last), name="mean")
    for bit in range(last - 1, 0, -1):
        other = swap(mine, "dp", 1 << bit)
        count *= 2
        mine, shard = call(functools.partial(double_apart_kernel, bit), [shaped(count, per, ff), shaped(*shard.shape)], mine, other, name="double")
        if bit > 1:
            mine = call(add_columns_kernel, shaped(count, per, ff + (columns - ff) // (count // keep.shape[0])), mine, shard, name="add_columns")
    return mine, shard


def from_z(parts):
    got = {j: swap(parts[j], "dp", 2 * j) for j in range(len(parts) - 1, 0, -1)}
    return [parts[0]] + [got[j] for j in range(1, len(parts))]


def mean_replicas(keep, got, shard):
    n_dp = lax.axis_size("dp")
    half, per, ff = keep.shape
    piece = shaped(per, ff + shard.shape[0] * shard.shape[1] // (half * per))
    stage = pltpu.VMEM((half, *piece.shape), F32)
    parts = call(split_z_kernel, [piece] * half, keep, got, shard, name="split_z", scratch_shapes=[stage])
    parts = [parts[0], *parts[:0:-1]]
    mean = call(functools.partial(mean_kernel, n_dp), piece, *from_z(parts), name="replica_mean")
    return from_z([mean] * half)


def on_device(gu, eu, gd, ed, qu, qd):
    qu, qd = qu.T, qd.T
    n_dp, n_shards = lax.axis_size("dp"), lax.axis_size("tensor")
    _, rows, ff = gu.shape
    rank = qu.shape[0]
    half, per, rows_here = n_dp // 2, rank // n_dp, rank // n_shards
    shard_rows_here = shaped(rows_here, rows)
    replica_half = shaped(half, per, ff)
    stage = pltpu.VMEM((n_dp, per, ff), F32)
    wide = pltpu.VMEM((rank, ff), F32)
    narrow = pltpu.VMEM((rank, rows), F32)
    product = 4 * rows * ff * 4 * rank

    buffers = [
        [pltpu.VMEM(g.shape[1:], BF16)] * 2 + [pltpu.VMEM(q.shape, F32), pltpu.VMEM((3 * rank, q.shape[1]), BF16), total]
        for g, q, total in ((gu, qu, narrow), (gd, qd, wide))
    ]
    *parts, keep, send = call(
        functools.partial(left_kernel, n_shards), [shard_rows_here] * n_shards + [replica_half] * 2, gu, eu, qu, gd, ed, qd,
        name="left", flops=2 * product, limit=53.75, in_specs=[HBM] * 6, out_specs=[VMEM] * n_shards + [HBM] * 2,
        scratch_shapes=buffers[0] + buffers[1] + [stage] + [pltpu.VMEM(replica_half.shape, F32)] * 2
        + [pltpu.SemaphoreType.DMA((2,)), pltpu.SemaphoreType.DMA((5, 2)), pltpu.SemaphoreType.DMA((2,))],
    )
    got = swap(send, "dp", 1)
    parts = from_shards(parts)
    parts[0], keep = call(fetch_kernel, [shard_rows_here, replica_half], parts[0], keep, name="fetch", flops=product // 4)
    shard = call(first_shards_kernel, shard_rows_here, *parts, name="shard_sum")
    keep, got = scatter_replicas(keep, send, got, (shard,))
    shard = call(first_shards_kernel, shard_rows_here, shard, swap(shard, "dp", 1), name="replica_sum")
    mine, shard = gather_replicas(keep, got, shard)
    other = swap(mine, "dp", 1)
    left_rows = from_shards([shard] * n_shards)
    left_up, gram_up, keep, send = call(
        functools.partial(right_up_kernel, n_shards), [shaped(rank, rows), shaped(rank, rank), replica_half, replica_half],
        *left_rows, gu, eu, after=(other,), name="right_up", flops=product,
        scratch_shapes=[pltpu.VMEM((3 * rank, rows), BF16), wide, stage],
    )
    left_down, *parts = call(
        right_down_kernel, [shaped(rank, ff)] + [shaped(rows_here, rows + rank * n_shards)] * n_shards, mine, other, gd, ed, after=(left_up,),
        name="right_down", flops=product, scratch_shapes=[pltpu.VMEM((3 * rank, ff), BF16), narrow, stage],
    )
    got = swap(send, "dp", 1)
    shard, gram_down = call(
        functools.partial(sum_shards_kernel, n_shards), [shard_rows_here, shaped(rank, rank)], *from_shards(parts), name="shard_sum"
    )
    pieces = mean_replicas(keep, got, shard)
    mine = call(stack_kernel, shaped(half, *pieces[0].shape), *pieces, name="stack_z")
    other = swap(mine, "dp", 1)
    inv_up, inv_down, lhs_up, lhs_down = call(
        basis_kernel,
        [shaped(rank, rank)] * 2 + [shaped(rows, 4 * rank, dtype=BF16), shaped(ff, 4 * rank, dtype=BF16)],
        left_up, left_down, gram_up, gram_down, gu, eu, gd, ed, mine, name="basis", in_specs=[VMEM] * 8 + [ANY],
    )
    rhs_up, shard = call(
        factor_up_kernel, [shaped(4 * rank, ff, dtype=BF16), shaped(rows_here, rows + 128)], mine, other, inv_up,
        name="factor_up", scratch_shapes=[wide, stage],
    )
    right_rows = from_shards([shard] * n_shards)
    new_error_up, rebuilt_up = call(
        error_up_kernel, [shaped(1, rows, ff, dtype=BF16), shaped(rows, ff)], gu, eu, lhs_up, rhs_up, name="error_up", flops=product // 2,
        grid=(STEPS,), in_specs=[VMEM] * 4, out_specs=[replica_blocks(rows, ff), VMEM],
    )
    limit = CLIP_RMS * (2.0 * rows * ff * n_shards) ** 0.5
    rhs_down, clip = call(
        functools.partial(factor_down_kernel, limit, n_shards), [shaped(4 * rank, rows, dtype=BF16), shaped(8, 128)],
        *right_rows, inv_down, rebuilt_up, name="factor_down", in_specs=[VMEM] * (n_shards + 1) + [ANY], scratch_shapes=[narrow],
    )
    new_error_down, update_up, update_down = call(
        last_kernel, [shaped(1, ff, rows, dtype=BF16), shaped(rows, ff, dtype=BF16), shaped(ff, rows, dtype=BF16)],
        gd, ed, rebuilt_up, lhs_down, rhs_down, clip, name="last", flops=product, grid=(STEPS,),
        in_specs=[VMEM] * 6, out_specs=[replica_blocks(ff, rows), row_blocks(rows, ff), row_blocks(ff, rows)],
    )
    return new_error_up, update_up, new_error_down, update_down


def solution(mesh):
    placed = (
        P("dp", None, "tensor"),
        P("dp", None, "tensor"),
        P("dp", "tensor", None),
        P("dp", "tensor", None),
        P("tensor", None),
        P(),
    )
    return jax.shard_map(
        on_device,
        mesh=mesh,
        in_specs=placed,
        out_specs=(
            P("dp", None, "tensor"),
            P(None, "tensor"),
            P("dp", "tensor", None),
            P("tensor", None),
        ),
        check_vma=False,
    )
```

```python
import functools

import jax
import jax.numpy as jnp
from jax import lax
from jax.experimental import pallas as pl
from jax.experimental.pallas import tpu as pltpu
from jax.sharding import PartitionSpec as P

F32 = jnp.float32
BF16 = jnp.bfloat16
HIGHEST = lax.Precision.HIGHEST
CLIP_RMS = 0.1
STEPS = 4
MIB = 1024 * 1024
NT = ((1,), (1,))


def split3(x):
    first = x.astype(BF16)
    rest = x - first.astype(F32)
    second = rest.astype(BF16)
    return first, second, (rest - second.astype(F32)).astype(BF16)


def tree_sum(values):
    values = list(values)
    while len(values) > 1:
        values = [values[i] + values[i + 1] for i in range(0, len(values), 2)]
    return values[0]


def dot(a, b, dims=((1,), (0,)), precision=None):
    return lax.dot_general(a, b, (dims, ((), ())), precision=precision, preferred_element_type=F32)


def fold(x, rows):
    return jnp.concatenate([x[i : i + rows] for i in range(0, x.shape[0], rows)], axis=1)


def unfold(x, rows):
    count = rows // x.shape[0]
    width = x.shape[1] // count
    return jnp.concatenate([x[:, i * width : (i + 1) * width] for i in range(count)], axis=0)


def place(axis):
    index = lax.axis_index(axis)
    return lax.bitwise_and(index, 1), lax.shift_right_logical(index, 1)


def split_replicas(total, stage, keep, send):
    parity, _ = place("dp")
    half, per, _ = keep.shape
    for c in range(2 * half):
        stage[c] = total[c * per : (c + 1) * per, :]
    for c in range(half):
        keep[c] = stage[2 * c + parity]
        send[c] = stage[2 * c + 1 - parity]


def join_replicas(mine, other, stage, total):
    parity, _ = place("dp")
    half, per, _ = mine.shape
    width = total.shape[1]
    for c in range(half):
        stage[2 * c + parity] = mine[c, :, :width]
        stage[2 * c + 1 - parity] = other[c, :, :width]
    for c in range(2 * half):
        total[c * per : (c + 1) * per, :] = stage[c]


def split_shards(total, extra, outs):
    me = lax.axis_index("tensor")
    rows, width = outs[0].shape[0], total.shape[1]
    for j, out in enumerate(outs):
        owner = lax.bitwise_xor(me, j)
        out[:, :width] = total[pl.ds(pl.multiple_of(owner * rows, rows), rows), :]
        if extra is not None:
            out[:, width:] = fold(extra, rows)


def join_shards(pieces, total):
    me = lax.axis_index("tensor")
    rows, width = pieces[0].shape[0], total.shape[1]
    for j, piece in enumerate(pieces):
        owner = lax.bitwise_xor(me, j)
        total[pl.ds(pl.multiple_of(owner * rows, rows), rows), :] = piece[:, :width]


def left_kernel(n_shards, gu, eu, qu, gd, ed, qd, *refs):
    *outs, gu_in, eu_in, qu_in, pieces_up, total_up, gd_in, ed_in, qd_in, pieces_down, total_down, stage, kept, sent, q_sems, sems, out_sems = refs
    halves = [pltpu.make_async_copy(src, dst, out_sems.at[i]) for i, (src, dst) in enumerate(((sent, outs[-1]), (kept, outs[-2])))]
    up, down = (qu_in, pieces_up, total_up), (qd_in, pieces_down, total_down)
    firsts = [pltpu.make_async_copy(src, dst, q_sems.at[i]) for i, (src, dst) in enumerate(((qd, qd_in), (qu, qu_in)))]
    stages = []
    for g, e, g_in, e_in, part, count in ((gd, ed, gd_in, ed_in, down, 3), (gu, eu, gu_in, eu_in, up, 2)):
        block = g_in.shape[0] // count
        for i in range(count):
            rows = pl.ds(i * block, block)
            n = len(stages)
            copies = [pltpu.make_async_copy(src.at[0, rows, :], dst.at[rows, :], sems.at[n, k]) for k, (src, dst) in enumerate(((g, g_in), (e, e_in)))]
            stages.append((copies, g_in, e_in, slice(i * block, (i + 1) * block), part))

    def fetch(n):
        if n < len(stages):
            for copy in stages[n][0]:
                copy.start()

    firsts[0].start()
    fetch(0)
    firsts[1].start()
    for n, (first, (q, pieces, _)) in enumerate(zip(firsts, (down, up))):
        first.wait()
        fetch(n + 1)
        split_rows(q, pieces)
    for n, (copies, g, e, rows, (_, pieces, total)) in enumerate(stages):
        for copy in copies:
            copy.wait()
        fetch(n + 3)
        total[:, rows] = add_pieces(dot(pieces[...], g[rows, :], NT) + dot(pieces[...], e[rows, :], NT))
        if n == 2:
            split_replicas(total_down, stage, kept, sent)
            for half in halves:
                half.start()
    split_shards(total_up, None, outs[:n_shards])
    for half in halves:
        half.wait()


def fetch_kernel(*refs):
    half = len(refs) // 2
    for source, out in zip(refs[:half], refs[half:]):
        out[...] = source[...]


def sum_shards_kernel(n_shards, *refs):
    terms, (out, gram) = refs[:n_shards], refs[n_shards:]
    total = tree_sum(term[...] for term in terms)
    out[...] = total[:, : out.shape[1]]
    gram[...] = unfold(total[:, out.shape[1] :], gram.shape[0])


def first_shards_kernel(*refs):
    refs[-1][...] = tree_sum(term[...] for term in refs[:-1])


def own_and_other(j, bit):
    mine = lax.bitwise_and(lax.shift_right_logical(lax.axis_index("dp"), bit), 1)
    return 2 * j + mine, 2 * j + 1 - mine


def split_chunks(bit, chunks, keep, send):
    for j in range(keep.shape[0]):
        mine, other = own_and_other(j, bit)
        keep[j] = chunks[mine]
        send[j] = chunks[other]


def halve_kernel(bit, keep, got, keep_out, send_out, chunks):
    chunks[...] = keep[...] + got[...]
    split_chunks(bit, chunks, keep_out, send_out)


def sum_kernel(scale, mine, other, out):
    out[...] = (mine[...] + other[...]) * scale


def double_kernel(bit, mine, other, out):
    for j in range(mine.shape[0]):
        here, there = own_and_other(j, bit)
        out[here] = mine[j]
        out[there] = other[j]


def half_sum_kernel(keep, got, shard, out):
    count, per, ff = keep.shape
    block = shard.shape[1] // count
    for c in range(count):
        out[c, :, :ff] = keep[c] + got[c]
        out[c, :, ff:] = fold(shard[:, c * block : (c + 1) * block], per)


def join_shard(chunks, ff, rows):
    return jnp.concatenate([unfold(chunks[c, :, ff:], rows) for c in range(chunks.shape[0])], axis=1)


def double_apart_kernel(bit, mine, other, out, shard):
    ff = out.shape[2]
    for j in range(mine.shape[0]):
        here, there = own_and_other(j, bit)
        out[here] = mine[j, :, :ff]
        out[there] = other[j, :, :ff]
    shard[...] = join_shard(mine, ff, shard.shape[0]) + join_shard(other, ff, shard.shape[0])


def add_columns_kernel(chunks, shard, out):
    count, per, ff = chunks.shape
    block = shard.shape[1] // count
    for c in range(count):
        out[c, :, :ff] = chunks[c]
        out[c, :, ff:] = fold(shard[:, c * block : (c + 1) * block], per)


def split_z_kernel(keep, got, shard, *refs):
    *outs, stage = refs
    _, z = place("dp")
    half, per, ff = keep.shape
    block = shard.shape[1] // half
    for c in range(half):
        stage[c, :, :ff] = keep[c] + got[c]
        stage[c, :, ff:] = fold(shard[:, c * block : (c + 1) * block], per)
    for j, out in zip([0, *range(half - 1, 0, -1)], outs):
        out[...] = stage[lax.bitwise_xor(z, j)]


def mean_kernel(n_dp, *refs):
    refs[-1][...] = tree_sum(ref[...] for ref in refs[:-1]) / n_dp


def stack_kernel(*refs):
    _, z = place("dp")
    for j, ref in enumerate(refs[:-1]):
        refs[-1][lax.bitwise_xor(z, j)] = ref[...]


def shard_rows(mine, other, ff, rows):
    half = mine.shape[0]
    return jnp.concatenate([unfold(mine[c, :, ff:] + other[c, :, ff:], rows) for c in range(half)], axis=1)


def split_rows(left, pieces):
    rank = left.shape[0]
    for i, piece in enumerate(split3(left[...])):
        pieces[i * rank : (i + 1) * rank, :] = piece


def add_pieces(t):
    rank = t.shape[0] // 3
    return t[:rank] + (t[rank : 2 * rank] + t[2 * rank :])


def right_down_kernel(mine, other, g, e, left, *refs):
    *outs, pieces, total, stage = refs
    join_replicas(mine, other, stage, left)
    split_rows(left, pieces)
    total[...] = add_pieces(dot(pieces[...], g[0]) + dot(pieces[...], e[0]))
    split_shards(total, dot(left[...], left[...], NT, HIGHEST), outs)


def right_up_kernel(n_shards, *refs):
    shards, refs = refs[:n_shards], refs[n_shards:]
    g, e, left, gram, keep, send, pieces, total, stage = refs
    join_shards(shards, left)
    split_rows(left, pieces)
    block = total.shape[1] // STEPS
    for i in range(STEPS):
        part = slice(i * block, (i + 1) * block)
        total[:, part] = add_pieces(dot(pieces[...], g[0, :, part]) + dot(pieces[...], e[0, :, part]))
    split_replicas(total, stage, keep, send)
    gram[...] = dot(left[...], left[...], NT, HIGHEST)


def inverse_factors(grams):
    rank = grams[0].shape[0]
    count = rank // 8
    panel = 4
    lane = lax.broadcasted_iota(jnp.int32, (8, 2 * rank), 1)
    row = lax.broadcasted_iota(jnp.int32, (8, 2 * rank), 0)
    states, pivots = [], []
    for gram in grams:
        wide = jnp.concatenate([gram, jnp.zeros_like(gram)], axis=1)
        states.append([wide[i : i + 8] + (lane == row + (rank + i)).astype(F32) for i in range(0, rank, 8)])
        pivots.append([])
    for start in range(0, rank, panel):
        at = start // 8
        below = range(at, count)
        spread = [
            [{i: jnp.broadcast_to(blocks[i][:, start + j : start + j + 1], (8, 2 * rank)) for i in below} for j in range(panel)]
            for blocks in states
        ]
        for j in range(panel):
            inner = (start + j) % 8
            for blocks, columns, found in zip(states, spread, pivots):
                pivot = columns[j][at][inner : inner + 1, :]
                found.append(pivot)
                inverse = 1.0 / pivot
                factor = {i: jnp.where(row > inner, columns[j][i], 0.0) if i == at else columns[j][i] for i in below}
                for later in columns[j + 1 :]:
                    head = later[at][inner : inner + 1, :] * inverse
                    for i in below:
                        later[i] = later[i] - factor[i] * head
                scaled = blocks[at][inner : inner + 1, :] * inverse
                for i in below:
                    blocks[i] = blocks[i] - factor[i] * scaled
    results = []
    for blocks, found in zip(states, pivots):
        rows = [block / jnp.sqrt(jnp.concatenate(found[8 * i : 8 * i + 8], axis=0)) for i, block in enumerate(blocks)]
        results.append(jnp.concatenate(rows, axis=0)[:, rank:])
    return results


def basis_kernel(left_up, left_down, gram_up, gram_down, *refs):
    inv_up, inv_down, lhs_up, lhs_down = refs[-4:]
    inverses = inverse_factors([gram_up[...], gram_down[...]])
    rank = left_up.shape[0]
    for inverse, inv, left, lhs in zip(inverses, (inv_up, inv_down), (left_up, left_down), (lhs_up, lhs_down)):
        inv[...] = inverse
        first, second, _ = split3(dot(inverse, left[...], precision=HIGHEST).T)
        lhs[:, :rank] = first
        lhs[:, rank : 2 * rank] = first
        lhs[:, 2 * rank : 3 * rank] = second
        lhs[:, 3 * rank :] = second


def right_factor(inv, total, rhs):
    rank = inv.shape[0]
    right = dot(inv[...], total[...], precision=HIGHEST)
    first, second, _ = split3(right)
    rhs[:rank, :] = first
    rhs[rank : 2 * rank, :] = second
    rhs[2 * rank : 3 * rank, :] = first
    rhs[3 * rank :, :] = second
    return jnp.sum(right * right)


def factor_up_kernel(mine, other, inv, rhs, shard, total, stage):
    join_replicas(mine, other, stage, total)
    square = right_factor(inv, total, rhs)
    rows, ff = shard.shape[0], total.shape[1]
    width = shard.shape[1] - 128
    shard[:, :width] = shard_rows(mine, other, ff, rows)
    shard[:, width:] = jnp.full((rows, 128), square, F32)


def blocks_of(rows):
    block = rows // STEPS
    return [slice(i * block, (i + 1) * block) for i in range(STEPS)]


def error_up_kernel(g, e, lhs, rhs, error, kept):
    for part in blocks_of(error.shape[1]):
        rebuilt = dot(lhs[part, :], rhs[...])
        kept[part, :] = rebuilt
        error[0, part, :] = (g[0, part, :].astype(F32) + e[0, part, :].astype(F32) - rebuilt).astype(BF16)


def last_kernel(limit, n_shards, error_up, *refs):
    shards, refs = refs[:n_shards], refs[n_shards:]
    inv, g, e, rebuilt_up, lhs, out_error_up, out_error, out_up, out_down, total, rhs, error, up, down, sems = refs
    copies = []

    def write(src, dst):
        copies.append(pltpu.make_async_copy(src, dst, sems.at[len(copies)]))
        copies[-1].start()

    write(error_up, out_error_up)
    join_shards(shards, total)
    square = right_factor(inv, total, rhs)
    width = total.shape[1]
    norm_sq = square + tree_sum(shard[:8, width:] for shard in shards)
    factor = jnp.minimum(jnp.float32(1.0), limit / jnp.sqrt(norm_sq))[:1, :1]
    for part, part_up in zip(blocks_of(down.shape[0]), blocks_of(up.shape[0])):
        rebuilt = dot(lhs[part, :], rhs[...])
        down[part, :] = (factor * rebuilt).astype(BF16)
        error[part, :] = (g[0, part, :].astype(F32) + e[0, part, :].astype(F32) - rebuilt).astype(BF16)
        up[part_up, :] = (factor * rebuilt_up[part_up, :]).astype(BF16)
        window = pl.ds(part.start, part.stop - part.start)
        write(down.at[window, :], out_down.at[window, :])
        write(error.at[window, :], out_error.at[0, window, :])
        window = pl.ds(part_up.start, part_up.stop - part_up.start)
        write(up.at[window, :], out_up.at[window, :])
    for copy in copies:
        copy.wait()


def shaped(*dims, dtype=F32):
    return jax.ShapeDtypeStruct(dims, dtype)


def whole(shape):
    return pl.BlockSpec(shape, lambda *_: (0,) * len(shape))


def row_blocks(rows, columns):
    return pl.BlockSpec((rows // STEPS, columns), lambda i: (i, 0))


def replica_blocks(rows, columns):
    return pl.BlockSpec((1, rows // STEPS, columns), lambda i: (0, i, 0))


VMEM = pl.BlockSpec(memory_space=pltpu.VMEM)
ANY = pl.BlockSpec(memory_space=pl.ANY)
HBM = pl.BlockSpec(memory_space=pltpu.HBM)


def call(kernel, out_shape, *args, after=(), in_specs=None, flops=0, limit=12, name=None, **more):
    arrays = list(args) + jax.tree.leaves(out_shape)
    size = sum(a.size * a.dtype.itemsize for a in arrays)
    skip = len(after)
    return pl.pallas_call(
        lambda *refs: kernel(*refs[skip:]), out_shape=out_shape, in_specs=[ANY] * skip + (in_specs or [VMEM] * len(args)),
        compiler_params=pltpu.CompilerParams(vmem_limit_bytes=int(limit * MIB)),
        cost_estimate=pl.CostEstimate(flops=flops, bytes_accessed=size, transcendentals=0), name=name, **more,
    )(*after, *args)


def swap(x, axis, distance):
    pairs = [(i, i ^ distance) for i in range(lax.axis_size(axis))]
    return lax.ppermute(x, axis, pairs)


def from_shards(parts):
    return [parts[0]] + [swap(parts[j], "tensor", j) for j in range(1, len(parts))]


def scatter_replicas(keep, send, got, after):
    n_dp = lax.axis_size("dp")
    for bit in range(n_dp.bit_length() - 2):
        got = swap(send, "dp", 1 << bit) if bit else got
        if bit == n_dp.bit_length() - 3:
            return keep, got
        count, per, ff = keep.shape
        out = shaped(count // 2, per, ff)
        keep, send = call(
            functools.partial(halve_kernel, bit + 1), [out, out], keep, got, after=after if bit == 0 else (), name="halve",
            scratch_shapes=[pltpu.VMEM(keep.shape, F32)],
        )


def gather_replicas(keep, got, shard):
    n_dp = lax.axis_size("dp")
    last = n_dp.bit_length() - 2
    count, per, ff = keep.shape
    columns = ff + shard.shape[0] * shard.shape[1] // (count * per)
    both = shaped(count, per, columns)
    total = call(half_sum_kernel, both, keep, got, shard, name="half_sum")
    mine = call(functools.partial(sum_kernel, 1.0 / n_dp), both, total, swap(total, "dp", 1 << last), name="mean")
    for bit in range(last - 1, 0, -1):
        other = swap(mine, "dp", 1 << bit)
        count *= 2
        mine, shard = call(functools.partial(double_apart_kernel, bit), [shaped(count, per, ff), shaped(*shard.shape)], mine, other, name="double")
        if bit > 1:
            mine = call(add_columns_kernel, shaped(count, per, ff + (columns - ff) // (count // keep.shape[0])), mine, shard, name="add_columns")
    return mine, shard


def from_z(parts):
    got = {j: swap(parts[j], "dp", 2 * j) for j in range(len(parts) - 1, 0, -1)}
    return [parts[0]] + [got[j] for j in range(1, len(parts))]


def mean_replicas(keep, got, shard):
    n_dp = lax.axis_size("dp")
    half, per, ff = keep.shape
    piece = shaped(per, ff + shard.shape[0] * shard.shape[1] // (half * per))
    stage = pltpu.VMEM((half, *piece.shape), F32)
    parts = call(split_z_kernel, [piece] * half, keep, got, shard, name="split_z", scratch_shapes=[stage])
    parts = [parts[0], *parts[:0:-1]]
    mean = call(functools.partial(mean_kernel, n_dp), piece, *from_z(parts), name="replica_mean")
    return from_z([mean] * half)


def on_device(gu, eu, gd, ed, qu, qd):
    qu, qd = qu.T, qd.T
    n_dp, n_shards = lax.axis_size("dp"), lax.axis_size("tensor")
    _, rows, ff = gu.shape
    rank = qu.shape[0]
    half, per, rows_here = n_dp // 2, rank // n_dp, rank // n_shards
    shard_rows_here = shaped(rows_here, rows)
    replica_half = shaped(half, per, ff)
    stage = pltpu.VMEM((n_dp, per, ff), F32)
    wide = pltpu.VMEM((rank, ff), F32)
    narrow = pltpu.VMEM((rank, rows), F32)
    product = 4 * rows * ff * 4 * rank

    buffers = [
        [pltpu.VMEM(g.shape[1:], BF16)] * 2 + [pltpu.VMEM(q.shape, F32), pltpu.VMEM((3 * rank, q.shape[1]), BF16), total]
        for g, q, total in ((gu, qu, narrow), (gd, qd, wide))
    ]
    *parts, keep, send = call(
        functools.partial(left_kernel, n_shards), [shard_rows_here] * n_shards + [replica_half] * 2, gu, eu, qu, gd, ed, qd,
        name="left", flops=2 * product, limit=53.75, in_specs=[HBM] * 6, out_specs=[VMEM] * n_shards + [HBM] * 2,
        scratch_shapes=buffers[0] + buffers[1] + [stage] + [pltpu.VMEM(replica_half.shape, F32)] * 2
        + [pltpu.SemaphoreType.DMA((2,)), pltpu.SemaphoreType.DMA((5, 2)), pltpu.SemaphoreType.DMA((2,))],
    )
    got = swap(send, "dp", 1)
    parts = from_shards(parts)
    parts[0], keep = call(fetch_kernel, [shard_rows_here, replica_half], parts[0], keep, name="fetch", flops=product // 4)
    shard = call(first_shards_kernel, shard_rows_here, *parts, name="shard_sum")
    keep, got = scatter_replicas(keep, send, got, (shard,))
    shard = call(first_shards_kernel, shard_rows_here, shard, swap(shard, "dp", 1), name="replica_sum")
    mine, shard = gather_replicas(keep, got, shard)
    other = swap(mine, "dp", 1)
    left_rows = from_shards([shard] * n_shards)
    left_up, gram_up, keep, send = call(
        functools.partial(right_up_kernel, n_shards), [shaped(rank, rows), shaped(rank, rank), replica_half, replica_half],
        *left_rows, gu, eu, after=(other,), name="right_up", flops=product,
        scratch_shapes=[pltpu.VMEM((3 * rank, rows), BF16), wide, stage],
    )
    left_down, *parts = call(
        right_down_kernel, [shaped(rank, ff)] + [shaped(rows_here, rows + rank * n_shards)] * n_shards, mine, other, gd, ed, after=(left_up,),
        name="right_down", flops=product, scratch_shapes=[pltpu.VMEM((3 * rank, ff), BF16), narrow, stage],
    )
    got = swap(send, "dp", 1)
    shard, gram_down = call(
        functools.partial(sum_shards_kernel, n_shards), [shard_rows_here, shaped(rank, rank)], *from_shards(parts), name="shard_sum"
    )
    pieces = mean_replicas(keep, got, shard)
    mine = call(stack_kernel, shaped(half, *pieces[0].shape), *pieces, name="stack_z")
    other = swap(mine, "dp", 1)
    inv_up, inv_down, lhs_up, lhs_down = call(
        basis_kernel,
        [shaped(rank, rank)] * 2 + [shaped(rows, 4 * rank, dtype=BF16), shaped(ff, 4 * rank, dtype=BF16)],
        left_up, left_down, gram_up, gram_down, gu, eu, gd, ed, mine, name="basis", in_specs=[VMEM] * 8 + [ANY],
    )
    rhs_up, shard = call(
        factor_up_kernel, [shaped(4 * rank, ff, dtype=BF16), shaped(rows_here, rows + 128)], mine, other, inv_up,
        name="factor_up", scratch_shapes=[wide, stage],
    )
    right_rows = from_shards([shard] * n_shards)
    error_up, rebuilt_up = call(
        error_up_kernel, [shaped(1, rows, ff, dtype=BF16), shaped(rows, ff)], gu, eu, lhs_up, rhs_up, name="error_up", flops=product // 2,
    )
    limit = CLIP_RMS * (2.0 * rows * ff * n_shards) ** 0.5
    outs = [shaped(1, rows, ff, dtype=BF16), shaped(1, ff, rows, dtype=BF16), shaped(rows, ff, dtype=BF16), shaped(ff, rows, dtype=BF16)]
    new_error_up, new_error_down, update_up, update_down = call(
        functools.partial(last_kernel, limit, n_shards), outs, error_up, *right_rows, inv_down, gd, ed, rebuilt_up, lhs_down, name="last",
        flops=product, limit=16, out_specs=[HBM] * 4,
        scratch_shapes=[narrow, pltpu.VMEM((4 * rank, rows), BF16)] + [pltpu.VMEM(shape, BF16) for shape in ((ff, rows), (rows, ff), (ff, rows))]
        + [pltpu.SemaphoreType.DMA((3 * STEPS + 1,))],
    )
    return new_error_up, update_up, new_error_down, update_down


def solution(mesh):
    placed = (
        P("dp", None, "tensor"),
        P("dp", None, "tensor"),
        P("dp", "tensor", None),
        P("dp", "tensor", None),
        P("tensor", None),
        P(),
    )
    return jax.shard_map(
        on_device,
        mesh=mesh,
        in_specs=placed,
        out_specs=(
            P("dp", None, "tensor"),
            P(None, "tensor"),
            P("dp", "tensor", None),
            P("tensor", None),
        ),
        check_vma=False,
    )
```

```python
import functools

import jax
import jax.numpy as jnp
from jax import lax
from jax.experimental import pallas as pl
from jax.experimental.pallas import tpu as pltpu
from jax.sharding import PartitionSpec as P

F32 = jnp.float32
BF16 = jnp.bfloat16
HIGHEST = lax.Precision.HIGHEST
CLIP_RMS = 0.1
STEPS = 4
MIB = 1024 * 1024
NT = ((1,), (1,))


def split3(x):
    first = x.astype(BF16)
    rest = x - first.astype(F32)
    second = rest.astype(BF16)
    return first, second, (rest - second.astype(F32)).astype(BF16)


def tree_sum(values):
    values = list(values)
    while len(values) > 1:
        values = [values[i] + values[i + 1] for i in range(0, len(values), 2)]
    return values[0]


def dot(a, b, dims=((1,), (0,)), precision=None):
    return lax.dot_general(a, b, (dims, ((), ())), precision=precision, preferred_element_type=F32)


def fold(x, rows):
    return jnp.concatenate([x[i : i + rows] for i in range(0, x.shape[0], rows)], axis=1)


def unfold(x, rows):
    count = rows // x.shape[0]
    width = x.shape[1] // count
    return jnp.concatenate([x[:, i * width : (i + 1) * width] for i in range(count)], axis=0)


def place(axis):
    index = lax.axis_index(axis)
    return lax.bitwise_and(index, 1), lax.shift_right_logical(index, 1)


def split_replicas(total, stage, keep, send):
    parity, _ = place("dp")
    half, per, _ = keep.shape
    for c in range(2 * half):
        stage[c] = total[c * per : (c + 1) * per, :]
    for c in range(half):
        keep[c] = stage[2 * c + parity]
        send[c] = stage[2 * c + 1 - parity]


def join_replicas(mine, other, stage, total):
    parity, _ = place("dp")
    half, per, _ = mine.shape
    width = total.shape[1]
    for c in range(half):
        stage[2 * c + parity] = mine[c, :, :width]
        stage[2 * c + 1 - parity] = other[c, :, :width]
    for c in range(2 * half):
        total[c * per : (c + 1) * per, :] = stage[c]


def split_shards(total, extra, outs):
    me = lax.axis_index("tensor")
    rows, width = outs[0].shape[0], total.shape[1]
    for j, out in enumerate(outs):
        owner = lax.bitwise_xor(me, j)
        out[:, :width] = total[pl.ds(pl.multiple_of(owner * rows, rows), rows), :]
        if extra is not None:
            out[:, width:] = fold(extra, rows)


def join_shards(pieces, total):
    me = lax.axis_index("tensor")
    rows, width = pieces[0].shape[0], total.shape[1]
    for j, piece in enumerate(pieces):
        owner = lax.bitwise_xor(me, j)
        total[pl.ds(pl.multiple_of(owner * rows, rows), rows), :] = piece[:, :width]


def left_kernel(n_shards, gu, eu, qu, gd, ed, qd, *refs):
    *outs, gu_in, eu_in, qu_in, pieces_up, total_up, gd_in, ed_in, qd_in, pieces_down, total_down, stage, kept, sent, q_sems, sems, out_sems = refs
    halves = [pltpu.make_async_copy(src, dst, out_sems.at[i]) for i, (src, dst) in enumerate(((sent, outs[-1]), (kept, outs[-2])))]
    up, down = (qu_in, pieces_up, total_up), (qd_in, pieces_down, total_down)
    firsts = [pltpu.make_async_copy(src, dst, q_sems.at[i]) for i, (src, dst) in enumerate(((qd, qd_in), (qu, qu_in)))]
    stages = []
    for g, e, g_in, e_in, part, count in ((gd, ed, gd_in, ed_in, down, 3), (gu, eu, gu_in, eu_in, up, 2)):
        block = g_in.shape[0] // count
        for i in range(count):
            rows = pl.ds(i * block, block)
            n = len(stages)
            copies = [pltpu.make_async_copy(src.at[0, rows, :], dst.at[rows, :], sems.at[n, k]) for k, (src, dst) in enumerate(((g, g_in), (e, e_in)))]
            stages.append((copies, g_in, e_in, slice(i * block, (i + 1) * block), part))

    def fetch(n):
        if n < len(stages):
            for copy in stages[n][0]:
                copy.start()

    firsts[0].start()
    fetch(0)
    firsts[1].start()
    for n, (first, (q, pieces, _)) in enumerate(zip(firsts, (down, up))):
        first.wait()
        fetch(n + 1)
        split_rows(q, pieces)
    for n, (copies, g, e, rows, (_, pieces, total)) in enumerate(stages):
        for copy in copies:
            copy.wait()
        fetch(n + 3)
        total[:, rows] = add_pieces(dot(pieces[...], g[rows, :], NT) + dot(pieces[...], e[rows, :], NT))
        if n == 2:
            split_replicas(total_down, stage, kept, sent)
            for half in halves:
                half.start()
    split_shards(total_up, None, outs[:n_shards])
    for half in halves:
        half.wait()


def fetch_kernel(*refs):
    half = len(refs) // 2
    for source, out in zip(refs[:half], refs[half:]):
        out[...] = source[...]


def sum_shards_kernel(n_shards, *refs):
    terms, (out, gram) = refs[:n_shards], refs[n_shards:]
    total = tree_sum(term[...] for term in terms)
    out[...] = total[:, : out.shape[1]]
    gram[...] = unfold(total[:, out.shape[1] :], gram.shape[0])


def first_shards_kernel(*refs):
    refs[-1][...] = tree_sum(term[...] for term in refs[:-1])


def own_and_other(j, bit):
    mine = lax.bitwise_and(lax.shift_right_logical(lax.axis_index("dp"), bit), 1)
    return 2 * j + mine, 2 * j + 1 - mine


def split_chunks(bit, chunks, keep, send):
    for j in range(keep.shape[0]):
        mine, other = own_and_other(j, bit)
        keep[j] = chunks[mine]
        send[j] = chunks[other]


def halve_kernel(bit, keep, got, keep_out, send_out, chunks):
    chunks[...] = keep[...] + got[...]
    split_chunks(bit, chunks, keep_out, send_out)


def sum_kernel(scale, mine, other, out):
    out[...] = (mine[...] + other[...]) * scale


def double_kernel(bit, mine, other, out):
    for j in range(mine.shape[0]):
        here, there = own_and_other(j, bit)
        out[here] = mine[j]
        out[there] = other[j]


def half_sum_kernel(keep, got, shard, out):
    count, per, ff = keep.shape
    block = shard.shape[1] // count
    for c in range(count):
        out[c, :, :ff] = keep[c] + got[c]
        out[c, :, ff:] = fold(shard[:, c * block : (c + 1) * block], per)


def join_shard(chunks, ff, rows):
    return jnp.concatenate([unfold(chunks[c, :, ff:], rows) for c in range(chunks.shape[0])], axis=1)


def double_apart_kernel(bit, mine, other, out, shard):
    ff = out.shape[2]
    for j in range(mine.shape[0]):
        here, there = own_and_other(j, bit)
        out[here] = mine[j, :, :ff]
        out[there] = other[j, :, :ff]
    shard[...] = join_shard(mine, ff, shard.shape[0]) + join_shard(other, ff, shard.shape[0])


def add_columns_kernel(chunks, shard, out):
    count, per, ff = chunks.shape
    block = shard.shape[1] // count
    for c in range(count):
        out[c, :, :ff] = chunks[c]
        out[c, :, ff:] = fold(shard[:, c * block : (c + 1) * block], per)


def split_z_kernel(keep, got, shard, *refs):
    *outs, stage = refs
    _, z = place("dp")
    half, per, ff = keep.shape
    block = shard.shape[1] // half
    for c in range(half):
        stage[c, :, :ff] = keep[c] + got[c]
        stage[c, :, ff:] = fold(shard[:, c * block : (c + 1) * block], per)
    for j, out in zip([0, *range(half - 1, 0, -1)], outs):
        out[...] = stage[lax.bitwise_xor(z, j)]


def mean_kernel(n_dp, *refs):
    refs[-1][...] = tree_sum(ref[...] for ref in refs[:-1]) / n_dp


def stack_kernel(*refs):
    _, z = place("dp")
    for j, ref in enumerate(refs[:-1]):
        refs[-1][lax.bitwise_xor(z, j)] = ref[...]


def shard_rows(mine, other, ff, rows):
    half = mine.shape[0]
    return jnp.concatenate([unfold(mine[c, :, ff:] + other[c, :, ff:], rows) for c in range(half)], axis=1)


def split_rows(left, pieces):
    rank = left.shape[0]
    for i, piece in enumerate(split3(left[...])):
        pieces[i * rank : (i + 1) * rank, :] = piece


def add_pieces(t):
    rank = t.shape[0] // 3
    return t[:rank] + (t[rank : 2 * rank] + t[2 * rank :])


def right_down_kernel(mine, other, g, e, left, *refs):
    *outs, pieces, total, stage = refs
    join_replicas(mine, other, stage, left)
    split_rows(left, pieces)
    total[...] = add_pieces(dot(pieces[...], g[0]) + dot(pieces[...], e[0]))
    split_shards(total, dot(left[...], left[...], NT, HIGHEST), outs)


def right_up_kernel(n_shards, *refs):
    shards, refs = refs[:n_shards], refs[n_shards:]
    g, e, left, gram, keep, send, pieces, total, stage = refs
    join_shards(shards, left)
    split_rows(left, pieces)
    block = total.shape[1] // STEPS
    for i in range(STEPS):
        part = slice(i * block, (i + 1) * block)
        total[:, part] = add_pieces(dot(pieces[...], g[0, :, part]) + dot(pieces[...], e[0, :, part]))
    split_replicas(total, stage, keep, send)
    gram[...] = dot(left[...], left[...], NT, HIGHEST)


def inverse_factors(grams):
    rank = grams[0].shape[0]
    count = rank // 8
    panel = 4
    lane = lax.broadcasted_iota(jnp.int32, (8, 2 * rank), 1)
    row = lax.broadcasted_iota(jnp.int32, (8, 2 * rank), 0)
    states, pivots = [], []
    for gram in grams:
        wide = jnp.concatenate([gram, jnp.zeros_like(gram)], axis=1)
        states.append([wide[i : i + 8] + (lane == row + (rank + i)).astype(F32) for i in range(0, rank, 8)])
        pivots.append([])
    for start in range(0, rank, panel):
        at = start // 8
        below = range(at, count)
        spread = [
            [{i: jnp.broadcast_to(blocks[i][:, start + j : start + j + 1], (8, 2 * rank)) for i in below} for j in range(panel)]
            for blocks in states
        ]
        for j in range(panel):
            inner = (start + j) % 8
            for blocks, columns, found in zip(states, spread, pivots):
                pivot = columns[j][at][inner : inner + 1, :]
                found.append(pivot)
                inverse = 1.0 / pivot
                factor = {i: jnp.where(row > inner, columns[j][i], 0.0) if i == at else columns[j][i] for i in below}
                for later in columns[j + 1 :]:
                    head = later[at][inner : inner + 1, :] * inverse
                    for i in below:
                        later[i] = later[i] - factor[i] * head
                scaled = blocks[at][inner : inner + 1, :] * inverse
                for i in below:
                    blocks[i] = blocks[i] - factor[i] * scaled
    results = []
    for blocks, found in zip(states, pivots):
        rows = [block / jnp.sqrt(jnp.concatenate(found[8 * i : 8 * i + 8], axis=0)) for i, block in enumerate(blocks)]
        results.append(jnp.concatenate(rows, axis=0)[:, rank:])
    return results


def basis_kernel(left_up, left_down, gram_up, gram_down, *refs):
    inv_up, inv_down, lhs_up, lhs_down = refs[-4:]
    inverses = inverse_factors([gram_up[...], gram_down[...]])
    rank = left_up.shape[0]
    for inverse, inv, left, lhs in zip(inverses, (inv_up, inv_down), (left_up, left_down), (lhs_up, lhs_down)):
        inv[...] = inverse
        first, second, _ = split3(dot(inverse, left[...], precision=HIGHEST).T)
        lhs[:, :rank] = first
        lhs[:, rank : 2 * rank] = first
        lhs[:, 2 * rank : 3 * rank] = second
        lhs[:, 3 * rank :] = second


def right_factor(inv, total, rhs):
    rank = inv.shape[0]
    right = dot(inv[...], total[...], precision=HIGHEST)
    first, second, _ = split3(right)
    rhs[:rank, :] = first
    rhs[rank : 2 * rank, :] = second
    rhs[2 * rank : 3 * rank, :] = first
    rhs[3 * rank :, :] = second
    return jnp.sum(right * right)


def factor_up_kernel(mine, other, inv, rhs, shard, total, stage):
    join_replicas(mine, other, stage, total)
    square = right_factor(inv, total, rhs)
    rows, ff = shard.shape[0], total.shape[1]
    width = shard.shape[1] - 128
    shard[:, :width] = shard_rows(mine, other, ff, rows)
    shard[:, width:] = jnp.full((rows, 128), square, F32)


def blocks_of(rows):
    block = rows // STEPS
    return [slice(i * block, (i + 1) * block) for i in range(STEPS)]


def error_up_kernel(g, e, lhs, rhs, out, kept, error, sems):
    copies = []
    for i, part in enumerate(blocks_of(error.shape[0])):
        rebuilt = dot(lhs[part, :], rhs[...])
        kept[part, :] = rebuilt
        error[part, :] = (g[0, part, :].astype(F32) + e[0, part, :].astype(F32) - rebuilt).astype(BF16)
        window = pl.ds(part.start, part.stop - part.start)
        copies.append(pltpu.make_async_copy(error.at[window, :], out.at[0, window, :], sems.at[i]))
        copies[i].start()
    for copy in copies:
        copy.wait()


def last_kernel(limit, n_shards, *refs):
    shards, refs = refs[:n_shards], refs[n_shards:]
    inv, g, e, rebuilt_up, lhs, out_error, out_up, out_down, total, rhs, error, up, down, sems = refs
    copies = []

    def write(src, dst):
        copies.append(pltpu.make_async_copy(src, dst, sems.at[len(copies)]))
        copies[-1].start()

    join_shards(shards, total)
    square = right_factor(inv, total, rhs)
    width = total.shape[1]
    norm_sq = square + tree_sum(shard[:8, width:] for shard in shards)
    factor = jnp.minimum(jnp.float32(1.0), limit / jnp.sqrt(norm_sq))[:1, :1]
    for part, part_up in zip(blocks_of(down.shape[0]), blocks_of(up.shape[0])):
        rebuilt = dot(lhs[part, :], rhs[...])
        down[part, :] = (factor * rebuilt).astype(BF16)
        error[part, :] = (g[0, part, :].astype(F32) + e[0, part, :].astype(F32) - rebuilt).astype(BF16)
        up[part_up, :] = (factor * rebuilt_up[part_up, :]).astype(BF16)
        window = pl.ds(part.start, part.stop - part.start)
        write(down.at[window, :], out_down.at[window, :])
        write(error.at[window, :], out_error.at[0, window, :])
        window = pl.ds(part_up.start, part_up.stop - part_up.start)
        write(up.at[window, :], out_up.at[window, :])
    for copy in copies:
        copy.wait()


def shaped(*dims, dtype=F32):
    return jax.ShapeDtypeStruct(dims, dtype)


def whole(shape):
    return pl.BlockSpec(shape, lambda *_: (0,) * len(shape))


def row_blocks(rows, columns):
    return pl.BlockSpec((rows // STEPS, columns), lambda i: (i, 0))


def replica_blocks(rows, columns):
    return pl.BlockSpec((1, rows // STEPS, columns), lambda i: (0, i, 0))


VMEM = pl.BlockSpec(memory_space=pltpu.VMEM)
ANY = pl.BlockSpec(memory_space=pl.ANY)
HBM = pl.BlockSpec(memory_space=pltpu.HBM)


def call(kernel, out_shape, *args, after=(), in_specs=None, flops=0, limit=12, name=None, **more):
    arrays = list(args) + jax.tree.leaves(out_shape)
    size = sum(a.size * a.dtype.itemsize for a in arrays)
    skip = len(after)
    return pl.pallas_call(
        lambda *refs: kernel(*refs[skip:]), out_shape=out_shape, in_specs=[ANY] * skip + (in_specs or [VMEM] * len(args)),
        compiler_params=pltpu.CompilerParams(vmem_limit_bytes=int(limit * MIB)),
        cost_estimate=pl.CostEstimate(flops=flops, bytes_accessed=size, transcendentals=0), name=name, **more,
    )(*after, *args)


def swap(x, axis, distance):
    pairs = [(i, i ^ distance) for i in range(lax.axis_size(axis))]
    return lax.ppermute(x, axis, pairs)


def from_shards(parts):
    return [parts[0]] + [swap(parts[j], "tensor", j) for j in range(1, len(parts))]


def scatter_replicas(keep, send, got, after):
    n_dp = lax.axis_size("dp")
    for bit in range(n_dp.bit_length() - 2):
        got = swap(send, "dp", 1 << bit) if bit else got
        if bit == n_dp.bit_length() - 3:
            return keep, got
        count, per, ff = keep.shape
        out = shaped(count // 2, per, ff)
        keep, send = call(
            functools.partial(halve_kernel, bit + 1), [out, out], keep, got, after=after if bit == 0 else (), name="halve",
            scratch_shapes=[pltpu.VMEM(keep.shape, F32)],
        )


def gather_replicas(keep, got, shard):
    n_dp = lax.axis_size("dp")
    last = n_dp.bit_length() - 2
    count, per, ff = keep.shape
    columns = ff + shard.shape[0] * shard.shape[1] // (count * per)
    both = shaped(count, per, columns)
    total = call(half_sum_kernel, both, keep, got, shard, name="half_sum")
    mine = call(functools.partial(sum_kernel, 1.0 / n_dp), both, total, swap(total, "dp", 1 << last), name="mean")
    for bit in range(last - 1, 0, -1):
        other = swap(mine, "dp", 1 << bit)
        count *= 2
        mine, shard = call(functools.partial(double_apart_kernel, bit), [shaped(count, per, ff), shaped(*shard.shape)], mine, other, name="double")
        if bit > 1:
            mine = call(add_columns_kernel, shaped(count, per, ff + (columns - ff) // (count // keep.shape[0])), mine, shard, name="add_columns")
    return mine, shard


def from_z(parts):
    got = {j: swap(parts[j], "dp", 2 * j) for j in range(len(parts) - 1, 0, -1)}
    return [parts[0]] + [got[j] for j in range(1, len(parts))]


def mean_replicas(keep, got, shard):
    n_dp = lax.axis_size("dp")
    half, per, ff = keep.shape
    piece = shaped(per, ff + shard.shape[0] * shard.shape[1] // (half * per))
    stage = pltpu.VMEM((half, *piece.shape), F32)
    parts = call(split_z_kernel, [piece] * half, keep, got, shard, name="split_z", scratch_shapes=[stage])
    parts = [parts[0], *parts[:0:-1]]
    mean = call(functools.partial(mean_kernel, n_dp), piece, *from_z(parts), name="replica_mean")
    return from_z([mean] * half)


def on_device(gu, eu, gd, ed, qu, qd):
    qu, qd = qu.T, qd.T
    n_dp, n_shards = lax.axis_size("dp"), lax.axis_size("tensor")
    _, rows, ff = gu.shape
    rank = qu.shape[0]
    half, per, rows_here = n_dp // 2, rank // n_dp, rank // n_shards
    shard_rows_here = shaped(rows_here, rows)
    replica_half = shaped(half, per, ff)
    stage = pltpu.VMEM((n_dp, per, ff), F32)
    wide = pltpu.VMEM((rank, ff), F32)
    narrow = pltpu.VMEM((rank, rows), F32)
    product = 4 * rows * ff * 4 * rank

    buffers = [
        [pltpu.VMEM(g.shape[1:], BF16)] * 2 + [pltpu.VMEM(q.shape, F32), pltpu.VMEM((3 * rank, q.shape[1]), BF16), total]
        for g, q, total in ((gu, qu, narrow), (gd, qd, wide))
    ]
    *parts, keep, send = call(
        functools.partial(left_kernel, n_shards), [shard_rows_here] * n_shards + [replica_half] * 2, gu, eu, qu, gd, ed, qd,
        name="left", flops=2 * product, limit=53.75, in_specs=[HBM] * 6, out_specs=[VMEM] * n_shards + [HBM] * 2,
        scratch_shapes=buffers[0] + buffers[1] + [stage] + [pltpu.VMEM(replica_half.shape, F32)] * 2
        + [pltpu.SemaphoreType.DMA((2,)), pltpu.SemaphoreType.DMA((5, 2)), pltpu.SemaphoreType.DMA((2,))],
    )
    got = swap(send, "dp", 1)
    parts = from_shards(parts)
    parts[0], keep = call(fetch_kernel, [shard_rows_here, replica_half], parts[0], keep, name="fetch", flops=product // 4)
    shard = call(first_shards_kernel, shard_rows_here, *parts, name="shard_sum")
    keep, got = scatter_replicas(keep, send, got, (shard,))
    shard = call(first_shards_kernel, shard_rows_here, shard, swap(shard, "dp", 1), name="replica_sum")
    mine, shard = gather_replicas(keep, got, shard)
    other = swap(mine, "dp", 1)
    left_rows = from_shards([shard] * n_shards)
    left_up, gram_up, keep, send = call(
        functools.partial(right_up_kernel, n_shards), [shaped(rank, rows), shaped(rank, rank), replica_half, replica_half],
        *left_rows, gu, eu, after=(other,), name="right_up", flops=product,
        scratch_shapes=[pltpu.VMEM((3 * rank, rows), BF16), wide, stage],
    )
    left_down, *parts = call(
        right_down_kernel, [shaped(rank, ff)] + [shaped(rows_here, rows + rank * n_shards)] * n_shards, mine, other, gd, ed, after=(left_up,),
        name="right_down", flops=product, scratch_shapes=[pltpu.VMEM((3 * rank, ff), BF16), narrow, stage],
    )
    got = swap(send, "dp", 1)
    shard, gram_down = call(
        functools.partial(sum_shards_kernel, n_shards), [shard_rows_here, shaped(rank, rank)], *from_shards(parts), name="shard_sum"
    )
    pieces = mean_replicas(keep, got, shard)
    mine = call(stack_kernel, shaped(half, *pieces[0].shape), *pieces, name="stack_z")
    other = swap(mine, "dp", 1)
    inv_up, inv_down, lhs_up, lhs_down = call(
        basis_kernel,
        [shaped(rank, rank)] * 2 + [shaped(rows, 4 * rank, dtype=BF16), shaped(ff, 4 * rank, dtype=BF16)],
        left_up, left_down, gram_up, gram_down, gu, eu, gd, ed, mine, name="basis", in_specs=[VMEM] * 8 + [ANY],
    )
    rhs_up, shard = call(
        factor_up_kernel, [shaped(4 * rank, ff, dtype=BF16), shaped(rows_here, rows + 128)], mine, other, inv_up,
        name="factor_up", scratch_shapes=[wide, stage],
    )
    right_rows = from_shards([shard] * n_shards)
    new_error_up, rebuilt_up = call(
        error_up_kernel, [shaped(1, rows, ff, dtype=BF16), shaped(rows, ff)], gu, eu, lhs_up, rhs_up, name="error_up", flops=product // 2,
        out_specs=[HBM, VMEM], scratch_shapes=[pltpu.VMEM((rows, ff), BF16), pltpu.SemaphoreType.DMA((STEPS,))],
    )
    limit = CLIP_RMS * (2.0 * rows * ff * n_shards) ** 0.5
    outs = [shaped(1, ff, rows, dtype=BF16), shaped(rows, ff, dtype=BF16), shaped(ff, rows, dtype=BF16)]
    new_error_down, update_up, update_down = call(
        functools.partial(last_kernel, limit, n_shards), outs, *right_rows, inv_down, gd, ed, rebuilt_up, lhs_down, name="last",
        flops=product, limit=16, out_specs=[HBM] * 3,
        scratch_shapes=[narrow, pltpu.VMEM((4 * rank, rows), BF16)] + [pltpu.VMEM(shape, BF16) for shape in ((ff, rows), (rows, ff), (ff, rows))]
        + [pltpu.SemaphoreType.DMA((3 * STEPS,))],
    )
    return new_error_up, update_up, new_error_down, update_down


def solution(mesh):
    placed = (
        P("dp", None, "tensor"),
        P("dp", None, "tensor"),
        P("dp", "tensor", None),
        P("dp", "tensor", None),
        P("tensor", None),
        P(),
    )
    return jax.shard_map(
        on_device,
        mesh=mesh,
        in_specs=placed,
        out_specs=(
            P("dp", None, "tensor"),
            P(None, "tensor"),
            P("dp", "tensor", None),
            P("tensor", None),
        ),
        check_vma=False,
    )
```

```python
import functools

import jax
import jax.numpy as jnp
from jax import lax
from jax.experimental import pallas as pl
from jax.experimental.pallas import tpu as pltpu
from jax.sharding import PartitionSpec as P

F32 = jnp.float32
BF16 = jnp.bfloat16
HIGHEST = lax.Precision.HIGHEST
CLIP_RMS = 0.1
STEPS = 4
MIB = 1024 * 1024
NT = ((1,), (1,))


def split3(x):
    first = x.astype(BF16)
    rest = x - first.astype(F32)
    second = rest.astype(BF16)
    return first, second, (rest - second.astype(F32)).astype(BF16)


def tree_sum(values):
    values = list(values)
    while len(values) > 1:
        values = [values[i] + values[i + 1] for i in range(0, len(values), 2)]
    return values[0]


def dot(a, b, dims=((1,), (0,)), precision=None):
    return lax.dot_general(a, b, (dims, ((), ())), precision=precision, preferred_element_type=F32)


def fold(x, rows):
    return jnp.concatenate([x[i : i + rows] for i in range(0, x.shape[0], rows)], axis=1)


def unfold(x, rows):
    count = rows // x.shape[0]
    width = x.shape[1] // count
    return jnp.concatenate([x[:, i * width : (i + 1) * width] for i in range(count)], axis=0)


def place(axis):
    index = lax.axis_index(axis)
    return lax.bitwise_and(index, 1), lax.shift_right_logical(index, 1)


def split_replicas(total, stage, keep, send):
    parity, _ = place("dp")
    half, per, _ = keep.shape
    for c in range(2 * half):
        stage[c] = total[c * per : (c + 1) * per, :]
    for c in range(half):
        keep[c] = stage[2 * c + parity]
        send[c] = stage[2 * c + 1 - parity]


def join_replicas(mine, other, stage, total):
    parity, _ = place("dp")
    half, per, _ = mine.shape
    width = total.shape[1]
    for c in range(half):
        stage[2 * c + parity] = mine[c, :, :width]
        stage[2 * c + 1 - parity] = other[c, :, :width]
    for c in range(2 * half):
        total[c * per : (c + 1) * per, :] = stage[c]


def split_shards(total, extra, outs):
    me = lax.axis_index("tensor")
    rows, width = outs[0].shape[0], total.shape[1]
    for j, out in enumerate(outs):
        owner = lax.bitwise_xor(me, j)
        out[:, :width] = total[pl.ds(pl.multiple_of(owner * rows, rows), rows), :]
        if extra is not None:
            out[:, width:] = fold(extra, rows)


def join_shards(pieces, total):
    me = lax.axis_index("tensor")
    rows, width = pieces[0].shape[0], total.shape[1]
    for j, piece in enumerate(pieces):
        owner = lax.bitwise_xor(me, j)
        total[pl.ds(pl.multiple_of(owner * rows, rows), rows), :] = piece[:, :width]


def left_kernel(n_shards, gu, eu, qu, gd, ed, qd, *refs):
    *outs, gu_in, eu_in, qu_in, pieces_up, total_up, gd_in, ed_in, qd_in, pieces_down, total_down, stage, kept, sent, q_sems, sems, out_sems = refs
    halves = [pltpu.make_async_copy(src, dst, out_sems.at[i]) for i, (src, dst) in enumerate(((sent, outs[-1]), (kept, outs[-2])))]
    up, down = (qu_in, pieces_up, total_up), (qd_in, pieces_down, total_down)
    firsts = [pltpu.make_async_copy(src, dst, q_sems.at[i]) for i, (src, dst) in enumerate(((qd, qd_in), (qu, qu_in)))]
    stages = []
    for g, e, g_in, e_in, part, count in ((gd, ed, gd_in, ed_in, down, 3), (gu, eu, gu_in, eu_in, up, 2)):
        block = g_in.shape[0] // count
        for i in range(count):
            rows = pl.ds(i * block, block)
            n = len(stages)
            copies = [pltpu.make_async_copy(src.at[0, rows, :], dst.at[rows, :], sems.at[n, k]) for k, (src, dst) in enumerate(((g, g_in), (e, e_in)))]
            stages.append((copies, g_in, e_in, slice(i * block, (i + 1) * block), part))

    def fetch(n):
        if n < len(stages):
            for copy in stages[n][0]:
                copy.start()

    firsts[0].start()
    fetch(0)
    firsts[1].start()
    for n, (first, (q, pieces, _)) in enumerate(zip(firsts, (down, up))):
        first.wait()
        fetch(n + 1)
        split_rows(q, pieces)
    for n, (copies, g, e, rows, (_, pieces, total)) in enumerate(stages):
        for copy in copies:
            copy.wait()
        fetch(n + 3)
        total[:, rows] = add_pieces(dot(pieces[...], g[rows, :], NT) + dot(pieces[...], e[rows, :], NT))
        if n == 2:
            split_replicas(total_down, stage, kept, sent)
            for half in halves:
                half.start()
    split_shards(total_up, None, outs[:n_shards])
    for half in halves:
        half.wait()


def fetch_kernel(*refs):
    half = len(refs) // 2
    for source, out in zip(refs[:half], refs[half:]):
        out[...] = source[...]


def sum_shards_kernel(n_shards, *refs):
    terms, (out, gram) = refs[:n_shards], refs[n_shards:]
    total = tree_sum(term[...] for term in terms)
    out[...] = total[:, : out.shape[1]]
    gram[...] = unfold(total[:, out.shape[1] :], gram.shape[0])


def first_shards_kernel(*refs):
    refs[-1][...] = tree_sum(term[...] for term in refs[:-1])


def own_and_other(j, bit):
    mine = lax.bitwise_and(lax.shift_right_logical(lax.axis_index("dp"), bit), 1)
    return 2 * j + mine, 2 * j + 1 - mine


def split_chunks(bit, chunks, keep, send):
    for j in range(keep.shape[0]):
        mine, other = own_and_other(j, bit)
        keep[j] = chunks[mine]
        send[j] = chunks[other]


def halve_kernel(bit, keep, got, keep_out, send_out, chunks):
    chunks[...] = keep[...] + got[...]
    split_chunks(bit, chunks, keep_out, send_out)


def sum_kernel(scale, mine, other, out):
    out[...] = (mine[...] + other[...]) * scale


def double_kernel(bit, mine, other, out):
    for j in range(mine.shape[0]):
        here, there = own_and_other(j, bit)
        out[here] = mine[j]
        out[there] = other[j]


def half_sum_kernel(keep, got, shard, out):
    count, per, ff = keep.shape
    block = shard.shape[1] // count
    for c in range(count):
        out[c, :, :ff] = keep[c] + got[c]
        out[c, :, ff:] = fold(shard[:, c * block : (c + 1) * block], per)


def join_shard(chunks, ff, rows):
    return jnp.concatenate([unfold(chunks[c, :, ff:], rows) for c in range(chunks.shape[0])], axis=1)


def double_apart_kernel(bit, mine, other, out, shard):
    ff = out.shape[2]
    for j in range(mine.shape[0]):
        here, there = own_and_other(j, bit)
        out[here] = mine[j, :, :ff]
        out[there] = other[j, :, :ff]
    shard[...] = join_shard(mine, ff, shard.shape[0]) + join_shard(other, ff, shard.shape[0])


def add_columns_kernel(chunks, shard, out):
    count, per, ff = chunks.shape
    block = shard.shape[1] // count
    for c in range(count):
        out[c, :, :ff] = chunks[c]
        out[c, :, ff:] = fold(shard[:, c * block : (c + 1) * block], per)


def split_z_kernel(keep, got, shard, *refs):
    *outs, stage = refs
    _, z = place("dp")
    half, per, ff = keep.shape
    block = shard.shape[1] // half
    for c in range(half):
        stage[c, :, :ff] = keep[c] + got[c]
        stage[c, :, ff:] = fold(shard[:, c * block : (c + 1) * block], per)
    for j, out in zip([0, *range(half - 1, 0, -1)], outs):
        out[...] = stage[lax.bitwise_xor(z, j)]


def mean_kernel(n_dp, *refs):
    refs[-1][...] = tree_sum(ref[...] for ref in refs[:-1]) / n_dp


def stack_kernel(*refs):
    _, z = place("dp")
    for j, ref in enumerate(refs[:-1]):
        refs[-1][lax.bitwise_xor(z, j)] = ref[...]


def shard_rows(mine, other, ff, rows):
    half = mine.shape[0]
    return jnp.concatenate([unfold(mine[c, :, ff:] + other[c, :, ff:], rows) for c in range(half)], axis=1)


def split_rows(left, pieces):
    rank = left.shape[0]
    for i, piece in enumerate(split3(left[...])):
        pieces[i * rank : (i + 1) * rank, :] = piece


def add_pieces(t):
    rank = t.shape[0] // 3
    return t[:rank] + (t[rank : 2 * rank] + t[2 * rank :])


def right_down_kernel(mine, other, g, e, left, *refs):
    *outs, pieces, total, stage = refs
    join_replicas(mine, other, stage, left)
    split_rows(left, pieces)
    total[...] = add_pieces(dot(pieces[...], g[0]) + dot(pieces[...], e[0]))
    split_shards(total, dot(left[...], left[...], NT, HIGHEST), outs)


def right_up_kernel(n_shards, *refs):
    shards, refs = refs[:n_shards], refs[n_shards:]
    g, e, left, gram, keep, send, pieces, total, stage = refs
    join_shards(shards, left)
    split_rows(left, pieces)
    block = total.shape[1] // STEPS
    for i in range(STEPS):
        part = slice(i * block, (i + 1) * block)
        total[:, part] = add_pieces(dot(pieces[...], g[0, :, part]) + dot(pieces[...], e[0, :, part]))
    split_replicas(total, stage, keep, send)
    gram[...] = dot(left[...], left[...], NT, HIGHEST)


def inverse_factors(grams):
    rank = grams[0].shape[0]
    count = rank // 8
    panel = 4
    lane = lax.broadcasted_iota(jnp.int32, (8, 2 * rank), 1)
    row = lax.broadcasted_iota(jnp.int32, (8, 2 * rank), 0)
    states, pivots = [], []
    for gram in grams:
        wide = jnp.concatenate([gram, jnp.zeros_like(gram)], axis=1)
        states.append([wide[i : i + 8] + (lane == row + (rank + i)).astype(F32) for i in range(0, rank, 8)])
        pivots.append([])
    for start in range(0, rank, panel):
        at = start // 8
        below = range(at, count)
        spread = [
            [{i: jnp.broadcast_to(blocks[i][:, start + j : start + j + 1], (8, 2 * rank)) for i in below} for j in range(panel)]
            for blocks in states
        ]
        for j in range(panel):
            inner = (start + j) % 8
            for blocks, columns, found in zip(states, spread, pivots):
                pivot = columns[j][at][inner : inner + 1, :]
                found.append(pivot)
                inverse = 1.0 / pivot
                factor = {i: jnp.where(row > inner, columns[j][i], 0.0) if i == at else columns[j][i] for i in below}
                for later in columns[j + 1 :]:
                    head = later[at][inner : inner + 1, :] * inverse
                    for i in below:
                        later[i] = later[i] - factor[i] * head
                scaled = blocks[at][inner : inner + 1, :] * inverse
                for i in below:
                    blocks[i] = blocks[i] - factor[i] * scaled
    results = []
    for blocks, found in zip(states, pivots):
        rows = [block / jnp.sqrt(jnp.concatenate(found[8 * i : 8 * i + 8], axis=0)) for i, block in enumerate(blocks)]
        results.append(jnp.concatenate(rows, axis=0)[:, rank:])
    return results


def basis_kernel(left_up, left_down, gram_up, gram_down, *refs):
    inv_up, inv_down, lhs_up, lhs_down = refs[-4:]
    inverses = inverse_factors([gram_up[...], gram_down[...]])
    rank = left_up.shape[0]
    for inverse, inv, left, lhs in zip(inverses, (inv_up, inv_down), (left_up, left_down), (lhs_up, lhs_down)):
        inv[...] = inverse
        first, second, _ = split3(dot(inverse, left[...], precision=HIGHEST).T)
        lhs[:, :rank] = first
        lhs[:, rank : 2 * rank] = first
        lhs[:, 2 * rank : 3 * rank] = second
        lhs[:, 3 * rank :] = second


def right_factor(inv, total, rhs):
    rank = inv.shape[0]
    right = dot(inv[...], total[...], precision=HIGHEST)
    first, second, _ = split3(right)
    rhs[:rank, :] = first
    rhs[rank : 2 * rank, :] = second
    rhs[2 * rank : 3 * rank, :] = first
    rhs[3 * rank :, :] = second
    return jnp.sum(right * right)


def factor_up_kernel(mine, other, inv, rhs, shard, total, stage):
    join_replicas(mine, other, stage, total)
    square = right_factor(inv, total, rhs)
    rows, ff = shard.shape[0], total.shape[1]
    width = shard.shape[1] - 128
    shard[:, :width] = shard_rows(mine, other, ff, rows)
    shard[:, width:] = jnp.full((rows, 128), square, F32)


def blocks_of(rows):
    block = rows // STEPS
    return [slice(i * block, (i + 1) * block) for i in range(STEPS)]


def error_up_kernel(g, e, lhs, rhs, g_down, e_down, out, kept, merged, error, sems):
    copies = []
    for i, part in enumerate(blocks_of(error.shape[0])):
        rebuilt = dot(lhs[part, :], rhs[...])
        kept[part, :] = rebuilt
        error[part, :] = (g[0, part, :].astype(F32) + e[0, part, :].astype(F32) - rebuilt).astype(BF16)
        window = pl.ds(part.start, part.stop - part.start)
        copies.append(pltpu.make_async_copy(error.at[window, :], out.at[0, window, :], sems.at[i]))
        copies[i].start()
    for part in blocks_of(merged.shape[0]):
        merged[part, :] = g_down[0, part, :].astype(F32) + e_down[0, part, :].astype(F32)
    for copy in copies:
        copy.wait()


def last_kernel(limit, n_shards, *refs):
    shards, refs = refs[:n_shards], refs[n_shards:]
    inv, merged, rebuilt_up, lhs, out_error, out_up, out_down, total, rhs, error, up, down, sems = refs
    copies = []

    def write(src, dst):
        copies.append(pltpu.make_async_copy(src, dst, sems.at[len(copies)]))
        copies[-1].start()

    join_shards(shards, total)
    square = right_factor(inv, total, rhs)
    width = total.shape[1]
    norm_sq = square + tree_sum(shard[:8, width:] for shard in shards)
    factor = jnp.minimum(jnp.float32(1.0), limit / jnp.sqrt(norm_sq))[:1, :1]
    for part in blocks_of(up.shape[0]):
        up[part, :] = (factor * rebuilt_up[part, :]).astype(BF16)
        window = pl.ds(part.start, part.stop - part.start)
        write(up.at[window, :], out_up.at[window, :])
    for part in blocks_of(down.shape[0]):
        rebuilt = dot(lhs[part, :], rhs[...])
        down[part, :] = (factor * rebuilt).astype(BF16)
        error[part, :] = (merged[part, :] - rebuilt).astype(BF16)
        window = pl.ds(part.start, part.stop - part.start)
        write(down.at[window, :], out_down.at[window, :])
        write(error.at[window, :], out_error.at[0, window, :])
    for copy in copies:
        copy.wait()


def shaped(*dims, dtype=F32):
    return jax.ShapeDtypeStruct(dims, dtype)


def whole(shape):
    return pl.BlockSpec(shape, lambda *_: (0,) * len(shape))


def row_blocks(rows, columns):
    return pl.BlockSpec((rows // STEPS, columns), lambda i: (i, 0))


def replica_blocks(rows, columns):
    return pl.BlockSpec((1, rows // STEPS, columns), lambda i: (0, i, 0))


VMEM = pl.BlockSpec(memory_space=pltpu.VMEM)
ANY = pl.BlockSpec(memory_space=pl.ANY)
HBM = pl.BlockSpec(memory_space=pltpu.HBM)


def call(kernel, out_shape, *args, after=(), in_specs=None, flops=0, limit=12, name=None, **more):
    arrays = list(args) + jax.tree.leaves(out_shape)
    size = sum(a.size * a.dtype.itemsize for a in arrays)
    skip = len(after)
    return pl.pallas_call(
        lambda *refs: kernel(*refs[skip:]), out_shape=out_shape, in_specs=[ANY] * skip + (in_specs or [VMEM] * len(args)),
        compiler_params=pltpu.CompilerParams(vmem_limit_bytes=int(limit * MIB)),
        cost_estimate=pl.CostEstimate(flops=flops, bytes_accessed=size, transcendentals=0), name=name, **more,
    )(*after, *args)


def swap(x, axis, distance):
    pairs = [(i, i ^ distance) for i in range(lax.axis_size(axis))]
    return lax.ppermute(x, axis, pairs)


def from_shards(parts):
    return [parts[0]] + [swap(parts[j], "tensor", j) for j in range(1, len(parts))]


def scatter_replicas(keep, send, got, after):
    n_dp = lax.axis_size("dp")
    for bit in range(n_dp.bit_length() - 2):
        got = swap(send, "dp", 1 << bit) if bit else got
        if bit == n_dp.bit_length() - 3:
            return keep, got
        count, per, ff = keep.shape
        out = shaped(count // 2, per, ff)
        keep, send = call(
            functools.partial(halve_kernel, bit + 1), [out, out], keep, got, after=after if bit == 0 else (), name="halve",
            scratch_shapes=[pltpu.VMEM(keep.shape, F32)],
        )


def gather_replicas(keep, got, shard):
    n_dp = lax.axis_size("dp")
    last = n_dp.bit_length() - 2
    count, per, ff = keep.shape
    columns = ff + shard.shape[0] * shard.shape[1] // (count * per)
    both = shaped(count, per, columns)
    total = call(half_sum_kernel, both, keep, got, shard, name="half_sum")
    mine = call(functools.partial(sum_kernel, 1.0 / n_dp), both, total, swap(total, "dp", 1 << last), name="mean")
    for bit in range(last - 1, 0, -1):
        other = swap(mine, "dp", 1 << bit)
        count *= 2
        mine, shard = call(functools.partial(double_apart_kernel, bit), [shaped(count, per, ff), shaped(*shard.shape)], mine, other, name="double")
        if bit > 1:
            mine = call(add_columns_kernel, shaped(count, per, ff + (columns - ff) // (count // keep.shape[0])), mine, shard, name="add_columns")
    return mine, shard


def from_z(parts):
    got = {j: swap(parts[j], "dp", 2 * j) for j in range(len(parts) - 1, 0, -1)}
    return [parts[0]] + [got[j] for j in range(1, len(parts))]


def mean_replicas(keep, got, shard):
    n_dp = lax.axis_size("dp")
    half, per, ff = keep.shape
    piece = shaped(per, ff + shard.shape[0] * shard.shape[1] // (half * per))
    stage = pltpu.VMEM((half, *piece.shape), F32)
    parts = call(split_z_kernel, [piece] * half, keep, got, shard, name="split_z", scratch_shapes=[stage])
    parts = [parts[0], *parts[:0:-1]]
    mean = call(functools.partial(mean_kernel, n_dp), piece, *from_z(parts), name="replica_mean")
    return from_z([mean] * half)


def on_device(gu, eu, gd, ed, qu, qd):
    qu, qd = qu.T, qd.T
    n_dp, n_shards = lax.axis_size("dp"), lax.axis_size("tensor")
    _, rows, ff = gu.shape
    rank = qu.shape[0]
    half, per, rows_here = n_dp // 2, rank // n_dp, rank // n_shards
    shard_rows_here = shaped(rows_here, rows)
    replica_half = shaped(half, per, ff)
    stage = pltpu.VMEM((n_dp, per, ff), F32)
    wide = pltpu.VMEM((rank, ff), F32)
    narrow = pltpu.VMEM((rank, rows), F32)
    product = 4 * rows * ff * 4 * rank

    buffers = [
        [pltpu.VMEM(g.shape[1:], BF16)] * 2 + [pltpu.VMEM(q.shape, F32), pltpu.VMEM((3 * rank, q.shape[1]), BF16), total]
        for g, q, total in ((gu, qu, narrow), (gd, qd, wide))
    ]
    *parts, keep, send = call(
        functools.partial(left_kernel, n_shards), [shard_rows_here] * n_shards + [replica_half] * 2, gu, eu, qu, gd, ed, qd,
        name="left", flops=2 * product, limit=53.75, in_specs=[HBM] * 6, out_specs=[VMEM] * n_shards + [HBM] * 2,
        scratch_shapes=buffers[0] + buffers[1] + [stage] + [pltpu.VMEM(replica_half.shape, F32)] * 2
        + [pltpu.SemaphoreType.DMA((2,)), pltpu.SemaphoreType.DMA((5, 2)), pltpu.SemaphoreType.DMA((2,))],
    )
    got = swap(send, "dp", 1)
    parts = from_shards(parts)
    parts[0], keep = call(fetch_kernel, [shard_rows_here, replica_half], parts[0], keep, name="fetch", flops=product // 4)
    shard = call(first_shards_kernel, shard_rows_here, *parts, name="shard_sum")
    keep, got = scatter_replicas(keep, send, got, (shard,))
    shard = call(first_shards_kernel, shard_rows_here, shard, swap(shard, "dp", 1), name="replica_sum")
    mine, shard = gather_replicas(keep, got, shard)
    other = swap(mine, "dp", 1)
    left_rows = from_shards([shard] * n_shards)
    left_up, gram_up, keep, send = call(
        functools.partial(right_up_kernel, n_shards), [shaped(rank, rows), shaped(rank, rank), replica_half, replica_half],
        *left_rows, gu, eu, after=(other,), name="right_up", flops=product,
        scratch_shapes=[pltpu.VMEM((3 * rank, rows), BF16), wide, stage],
    )
    left_down, *parts = call(
        right_down_kernel, [shaped(rank, ff)] + [shaped(rows_here, rows + rank * n_shards)] * n_shards, mine, other, gd, ed, after=(left_up,),
        name="right_down", flops=product, scratch_shapes=[pltpu.VMEM((3 * rank, ff), BF16), narrow, stage],
    )
    got = swap(send, "dp", 1)
    shard, gram_down = call(
        functools.partial(sum_shards_kernel, n_shards), [shard_rows_here, shaped(rank, rank)], *from_shards(parts), name="shard_sum"
    )
    pieces = mean_replicas(keep, got, shard)
    mine = call(stack_kernel, shaped(half, *pieces[0].shape), *pieces, name="stack_z")
    other = swap(mine, "dp", 1)
    inv_up, inv_down, lhs_up, lhs_down = call(
        basis_kernel,
        [shaped(rank, rank)] * 2 + [shaped(rows, 4 * rank, dtype=BF16), shaped(ff, 4 * rank, dtype=BF16)],
        left_up, left_down, gram_up, gram_down, gu, eu, gd, ed, mine, name="basis", in_specs=[VMEM] * 8 + [ANY],
    )
    rhs_up, shard = call(
        factor_up_kernel, [shaped(4 * rank, ff, dtype=BF16), shaped(rows_here, rows + 128)], mine, other, inv_up,
        name="factor_up", scratch_shapes=[wide, stage],
    )
    right_rows = from_shards([shard] * n_shards)
    new_error_up, rebuilt_up, merged_down = call(
        error_up_kernel, [shaped(1, rows, ff, dtype=BF16), shaped(rows, ff), shaped(ff, rows)], gu, eu, lhs_up, rhs_up, gd, ed, name="error_up", flops=product // 2,
        out_specs=[HBM, VMEM, VMEM], limit=16, scratch_shapes=[pltpu.VMEM((rows, ff), BF16), pltpu.SemaphoreType.DMA((STEPS,))],
    )
    limit = CLIP_RMS * (2.0 * rows * ff * n_shards) ** 0.5
    outs = [shaped(1, ff, rows, dtype=BF16), shaped(rows, ff, dtype=BF16), shaped(ff, rows, dtype=BF16)]
    new_error_down, update_up, update_down = call(
        functools.partial(last_kernel, limit, n_shards), outs, *right_rows, inv_down, merged_down, rebuilt_up, lhs_down, name="last",
        flops=product, limit=16, out_specs=[HBM] * 3,
        scratch_shapes=[narrow, pltpu.VMEM((4 * rank, rows), BF16)] + [pltpu.VMEM(shape, BF16) for shape in ((ff, rows), (rows, ff), (ff, rows))]
        + [pltpu.SemaphoreType.DMA((3 * STEPS,))],
    )
    return new_error_up, update_up, new_error_down, update_down


def solution(mesh):
    placed = (
        P("dp", None, "tensor"),
        P("dp", None, "tensor"),
        P("dp", "tensor", None),
        P("dp", "tensor", None),
        P("tensor", None),
        P(),
    )
    return jax.shard_map(
        on_device,
        mesh=mesh,
        in_specs=placed,
        out_specs=(
            P("dp", None, "tensor"),
            P(None, "tensor"),
            P("dp", "tensor", None),
            P("tensor", None),
        ),
        check_vma=False,
    )
```

```python
import functools

import jax
import jax.numpy as jnp
from jax import lax
from jax.experimental import pallas as pl
from jax.experimental.pallas import tpu as pltpu
from jax.sharding import PartitionSpec as P

F32 = jnp.float32
BF16 = jnp.bfloat16
HIGHEST = lax.Precision.HIGHEST
CLIP_RMS = 0.1
STEPS = 4
MIB = 1024 * 1024
NT = ((1,), (1,))


def split3(x):
    first = x.astype(BF16)
    rest = x - first.astype(F32)
    second = rest.astype(BF16)
    return first, second, (rest - second.astype(F32)).astype(BF16)


def tree_sum(values):
    values = list(values)
    while len(values) > 1:
        values = [values[i] + values[i + 1] for i in range(0, len(values), 2)]
    return values[0]


def dot(a, b, dims=((1,), (0,)), precision=None):
    return lax.dot_general(a, b, (dims, ((), ())), precision=precision, preferred_element_type=F32)


def fold(x, rows):
    return jnp.concatenate([x[i : i + rows] for i in range(0, x.shape[0], rows)], axis=1)


def unfold(x, rows):
    count = rows // x.shape[0]
    width = x.shape[1] // count
    return jnp.concatenate([x[:, i * width : (i + 1) * width] for i in range(count)], axis=0)


def place(axis):
    index = lax.axis_index(axis)
    return lax.bitwise_and(index, 1), lax.shift_right_logical(index, 1)


def split_replicas(total, stage, keep, send):
    parity, _ = place("dp")
    half, per, _ = keep.shape
    for c in range(2 * half):
        stage[c] = total[c * per : (c + 1) * per, :]
    for c in range(half):
        keep[c] = stage[2 * c + parity]
        send[c] = stage[2 * c + 1 - parity]


def join_replicas(mine, other, stage, total):
    parity, _ = place("dp")
    half, per, _ = mine.shape
    width = total.shape[1]
    for c in range(half):
        stage[2 * c + parity] = mine[c, :, :width]
        stage[2 * c + 1 - parity] = other[c, :, :width]
    for c in range(2 * half):
        total[c * per : (c + 1) * per, :] = stage[c]


def split_shards(total, extra, outs):
    me = lax.axis_index("tensor")
    rows, width = outs[0].shape[0], total.shape[1]
    for j, out in enumerate(outs):
        owner = lax.bitwise_xor(me, j)
        out[:, :width] = total[pl.ds(pl.multiple_of(owner * rows, rows), rows), :]
        if extra is not None:
            out[:, width:] = fold(extra, rows)


def join_shards(pieces, total):
    me = lax.axis_index("tensor")
    rows, width = pieces[0].shape[0], total.shape[1]
    for j, piece in enumerate(pieces):
        owner = lax.bitwise_xor(me, j)
        total[pl.ds(pl.multiple_of(owner * rows, rows), rows), :] = piece[:, :width]


def left_kernel(n_shards, gu, eu, qu, gd, ed, qd, *refs):
    *outs, gu_in, eu_in, qu_in, pieces_up, total_up, gd_in, ed_in, qd_in, pieces_down, total_down, stage, kept, sent, q_sems, sems, out_sems = refs
    halves = [pltpu.make_async_copy(src, dst, out_sems.at[i]) for i, (src, dst) in enumerate(((sent, outs[-1]), (kept, outs[-2])))]
    up, down = (qu_in, pieces_up, total_up), (qd_in, pieces_down, total_down)
    firsts = [pltpu.make_async_copy(src, dst, q_sems.at[i]) for i, (src, dst) in enumerate(((qd, qd_in), (qu, qu_in)))]
    stages = []
    for g, e, g_in, e_in, part, count in ((gd, ed, gd_in, ed_in, down, 3), (gu, eu, gu_in, eu_in, up, 2)):
        block = g_in.shape[0] // count
        for i in range(count):
            rows = pl.ds(i * block, block)
            n = len(stages)
            copies = [pltpu.make_async_copy(src.at[0, rows, :], dst.at[rows, :], sems.at[n, k]) for k, (src, dst) in enumerate(((g, g_in), (e, e_in)))]
            stages.append((copies, g_in, e_in, slice(i * block, (i + 1) * block), part))

    def fetch(n):
        if n < len(stages):
            for copy in stages[n][0]:
                copy.start()

    firsts[0].start()
    fetch(0)
    firsts[1].start()
    for n, (first, (q, pieces, _)) in enumerate(zip(firsts, (down, up))):
        first.wait()
        fetch(n + 1)
        split_rows(q, pieces)
    for n, (copies, g, e, rows, (_, pieces, total)) in enumerate(stages):
        for copy in copies:
            copy.wait()
        fetch(n + 3)
        total[:, rows] = add_pieces(dot(pieces[...], g[rows, :], NT) + dot(pieces[...], e[rows, :], NT))
        if n == 2:
            split_replicas(total_down, stage, kept, sent)
            for half in halves:
                half.start()
    split_shards(total_up, None, outs[:n_shards])
    for half in halves:
        half.wait()


def fetch_kernel(*refs):
    half = len(refs) // 2
    for source, out in zip(refs[:half], refs[half:]):
        out[...] = source[...]


def sum_shards_kernel(n_shards, *refs):
    terms, (out, gram) = refs[:n_shards], refs[n_shards:]
    total = tree_sum(term[...] for term in terms)
    out[...] = total[:, : out.shape[1]]
    gram[...] = unfold(total[:, out.shape[1] :], gram.shape[0])


def first_shards_kernel(*refs):
    refs[-1][...] = tree_sum(term[...] for term in refs[:-1])


def own_and_other(j, bit):
    mine = lax.bitwise_and(lax.shift_right_logical(lax.axis_index("dp"), bit), 1)
    return 2 * j + mine, 2 * j + 1 - mine


def split_chunks(bit, chunks, keep, send):
    for j in range(keep.shape[0]):
        mine, other = own_and_other(j, bit)
        keep[j] = chunks[mine]
        send[j] = chunks[other]


def halve_kernel(bit, keep, got, keep_out, send_out, chunks):
    chunks[...] = keep[...] + got[...]
    split_chunks(bit, chunks, keep_out, send_out)


def sum_kernel(scale, mine, other, out):
    out[...] = (mine[...] + other[...]) * scale


def double_kernel(bit, mine, other, out):
    for j in range(mine.shape[0]):
        here, there = own_and_other(j, bit)
        out[here] = mine[j]
        out[there] = other[j]


def half_sum_kernel(keep, got, shard, out):
    count, per, ff = keep.shape
    block = shard.shape[1] // count
    for c in range(count):
        out[c, :, :ff] = keep[c] + got[c]
        out[c, :, ff:] = fold(shard[:, c * block : (c + 1) * block], per)


def join_shard(chunks, ff, rows):
    return jnp.concatenate([unfold(chunks[c, :, ff:], rows) for c in range(chunks.shape[0])], axis=1)


def double_apart_kernel(bit, mine, other, out, shard):
    ff = out.shape[2]
    for j in range(mine.shape[0]):
        here, there = own_and_other(j, bit)
        out[here] = mine[j, :, :ff]
        out[there] = other[j, :, :ff]
    shard[...] = join_shard(mine, ff, shard.shape[0]) + join_shard(other, ff, shard.shape[0])


def add_columns_kernel(chunks, shard, out):
    count, per, ff = chunks.shape
    block = shard.shape[1] // count
    for c in range(count):
        out[c, :, :ff] = chunks[c]
        out[c, :, ff:] = fold(shard[:, c * block : (c + 1) * block], per)


def split_z_kernel(keep, got, shard, *refs):
    *outs, stage = refs
    _, z = place("dp")
    half, per, ff = keep.shape
    block = shard.shape[1] // half
    for c in range(half):
        stage[c, :, :ff] = keep[c] + got[c]
        stage[c, :, ff:] = fold(shard[:, c * block : (c + 1) * block], per)
    for j, out in zip([0, *range(half - 1, 0, -1)], outs):
        out[...] = stage[lax.bitwise_xor(z, j)]


def mean_kernel(n_dp, *refs):
    refs[-1][...] = tree_sum(ref[...] for ref in refs[:-1]) / n_dp


def stack_kernel(*refs):
    _, z = place("dp")
    for j, ref in enumerate(refs[:-1]):
        refs[-1][lax.bitwise_xor(z, j)] = ref[...]


def shard_rows(mine, other, ff, rows):
    half = mine.shape[0]
    return jnp.concatenate([unfold(mine[c, :, ff:] + other[c, :, ff:], rows) for c in range(half)], axis=1)


def split_rows(left, pieces):
    rank = left.shape[0]
    for i, piece in enumerate(split3(left[...])):
        pieces[i * rank : (i + 1) * rank, :] = piece


def add_pieces(t):
    rank = t.shape[0] // 3
    return t[:rank] + (t[rank : 2 * rank] + t[2 * rank :])


def right_down_kernel(mine, other, g, e, left, *refs):
    *outs, pieces, total, stage = refs
    join_replicas(mine, other, stage, left)
    split_rows(left, pieces)
    total[...] = add_pieces(dot(pieces[...], g[0]) + dot(pieces[...], e[0]))
    split_shards(total, dot(left[...], left[...], NT, HIGHEST), outs)


def right_up_kernel(n_shards, *refs):
    shards, refs = refs[:n_shards], refs[n_shards:]
    g, e, left, gram, keep, send, pieces, total, stage = refs
    join_shards(shards, left)
    split_rows(left, pieces)
    block = total.shape[1] // STEPS
    for i in range(STEPS):
        part = slice(i * block, (i + 1) * block)
        total[:, part] = add_pieces(dot(pieces[...], g[0, :, part]) + dot(pieces[...], e[0, :, part]))
    split_replicas(total, stage, keep, send)
    gram[...] = dot(left[...], left[...], NT, HIGHEST)


def inverse_factors(grams):
    rank = grams[0].shape[0]
    count = rank // 8
    panel = 4
    lane = lax.broadcasted_iota(jnp.int32, (8, 2 * rank), 1)
    row = lax.broadcasted_iota(jnp.int32, (8, 2 * rank), 0)
    states, pivots = [], []
    for gram in grams:
        wide = jnp.concatenate([gram, jnp.zeros_like(gram)], axis=1)
        states.append([wide[i : i + 8] + (lane == row + (rank + i)).astype(F32) for i in range(0, rank, 8)])
        pivots.append([])
    for start in range(0, rank, panel):
        at = start // 8
        below = range(at, count)
        spread = [
            [{i: jnp.broadcast_to(blocks[i][:, start + j : start + j + 1], (8, 2 * rank)) for i in below} for j in range(panel)]
            for blocks in states
        ]
        for j in range(panel):
            inner = (start + j) % 8
            for blocks, columns, found in zip(states, spread, pivots):
                pivot = columns[j][at][inner : inner + 1, :]
                found.append(pivot)
                inverse = 1.0 / pivot
                factor = {i: jnp.where(row > inner, columns[j][i], 0.0) if i == at else columns[j][i] for i in below}
                for later in columns[j + 1 :]:
                    head = later[at][inner : inner + 1, :] * inverse
                    for i in below:
                        later[i] = later[i] - factor[i] * head
                scaled = blocks[at][inner : inner + 1, :] * inverse
                for i in below:
                    blocks[i] = blocks[i] - factor[i] * scaled
    results = []
    for blocks, found in zip(states, pivots):
        rows = [block / jnp.sqrt(jnp.concatenate(found[8 * i : 8 * i + 8], axis=0)) for i, block in enumerate(blocks)]
        results.append(jnp.concatenate(rows, axis=0)[:, rank:])
    return results


def basis_kernel(left_up, left_down, gram_up, gram_down, *refs):
    inv_up, inv_down, lhs_up, lhs_down = refs[-4:]
    inverses = inverse_factors([gram_up[...], gram_down[...]])
    rank = left_up.shape[0]
    for inverse, inv, left, lhs in zip(inverses, (inv_up, inv_down), (left_up, left_down), (lhs_up, lhs_down)):
        inv[...] = inverse
        first, second, _ = split3(dot(inverse, left[...], precision=HIGHEST).T)
        lhs[:, :rank] = first
        lhs[:, rank : 2 * rank] = first
        lhs[:, 2 * rank : 3 * rank] = second
        lhs[:, 3 * rank :] = second


def right_factor(inv, total, rhs):
    rank = inv.shape[0]
    right = dot(inv[...], total[...], precision=HIGHEST)
    first, second, _ = split3(right)
    rhs[:rank, :] = first
    rhs[rank : 2 * rank, :] = second
    rhs[2 * rank : 3 * rank, :] = first
    rhs[3 * rank :, :] = second
    return jnp.sum(right * right)


def factor_up_kernel(mine, other, inv, rhs, shard, total, stage):
    join_replicas(mine, other, stage, total)
    square = right_factor(inv, total, rhs)
    rows, ff = shard.shape[0], total.shape[1]
    width = shard.shape[1] - 128
    shard[:, :width] = shard_rows(mine, other, ff, rows)
    shard[:, width:] = jnp.full((rows, 128), square, F32)


def blocks_of(rows):
    block = rows // STEPS
    return [slice(i * block, (i + 1) * block) for i in range(STEPS)]


def error_up_kernel(g, e, lhs, rhs, g_down, e_down, out, kept, merged, error, sems):
    copies = []
    for i, part in enumerate(blocks_of(error.shape[0])):
        rebuilt = dot(lhs[part, :], rhs[...])
        kept[part, :] = rebuilt
        error[part, :] = (g[0, part, :].astype(F32) + e[0, part, :].astype(F32) - rebuilt).astype(BF16)
        window = pl.ds(part.start, part.stop - part.start)
        copies.append(pltpu.make_async_copy(error.at[window, :], out.at[0, window, :], sems.at[i]))
        copies[i].start()
    for part in blocks_of(merged.shape[0]):
        merged[part, :] = g_down[0, part, :].astype(F32) + e_down[0, part, :].astype(F32)
    for copy in copies:
        copy.wait()


def last_kernel(limit, n_shards, *refs):
    shards, refs = refs[:n_shards], refs[n_shards:]
    inv, merged, rebuilt_up, lhs, out_error, out_up, out_down, total, rhs, error, up, down, sems = refs
    copies = []

    def write(src, dst):
        copies.append(pltpu.make_async_copy(src, dst, sems.at[len(copies)]))
        copies[-1].start()

    join_shards(shards, total)
    square = right_factor(inv, total, rhs)
    width = total.shape[1]
    norm_sq = square + tree_sum(shard[:8, width:] for shard in shards)
    factor = jnp.minimum(jnp.float32(1.0), limit / jnp.sqrt(norm_sq))[:1, :1]
    for part in blocks_of(up.shape[0]):
        up[part, :] = (factor * rebuilt_up[part, :]).astype(BF16)
        window = pl.ds(part.start, part.stop - part.start)
        write(up.at[window, :], out_up.at[window, :])
    for part in blocks_of(down.shape[0]):
        rebuilt = dot(lhs[part, :], rhs[...])
        down[part, :] = (factor * rebuilt).astype(BF16)
        error[part, :] = (merged[part, :] - rebuilt).astype(BF16)
        window = pl.ds(part.start, part.stop - part.start)
        write(down.at[window, :], out_down.at[window, :])
        write(error.at[window, :], out_error.at[0, window, :])
    for copy in copies:
        copy.wait()


def shaped(*dims, dtype=F32):
    return jax.ShapeDtypeStruct(dims, dtype)


def whole(shape):
    return pl.BlockSpec(shape, lambda *_: (0,) * len(shape))


def row_blocks(rows, columns):
    return pl.BlockSpec((rows // STEPS, columns), lambda i: (i, 0))


def replica_blocks(rows, columns):
    return pl.BlockSpec((1, rows // STEPS, columns), lambda i: (0, i, 0))


VMEM = pl.BlockSpec(memory_space=pltpu.VMEM)
ANY = pl.BlockSpec(memory_space=pl.ANY)
HBM = pl.BlockSpec(memory_space=pltpu.HBM)


def call(kernel, out_shape, *args, after=(), in_specs=None, flops=0, limit=12, name=None, **more):
    arrays = list(args) + jax.tree.leaves(out_shape)
    size = sum(a.size * a.dtype.itemsize for a in arrays)
    skip = len(after)
    return pl.pallas_call(
        lambda *refs: kernel(*refs[skip:]), out_shape=out_shape, in_specs=[ANY] * skip + (in_specs or [VMEM] * len(args)),
        compiler_params=pltpu.CompilerParams(vmem_limit_bytes=int(limit * MIB)),
        cost_estimate=pl.CostEstimate(flops=flops, bytes_accessed=size, transcendentals=0), name=name, **more,
    )(*after, *args)


def swap(x, axis, distance):
    pairs = [(i, i ^ distance) for i in range(lax.axis_size(axis))]
    return lax.ppermute(x, axis, pairs)


def from_shards(parts):
    return [parts[0]] + [swap(parts[j], "tensor", j) for j in range(1, len(parts))]


def scatter_replicas(keep, send, got, after):
    n_dp = lax.axis_size("dp")
    for bit in range(n_dp.bit_length() - 2):
        got = swap(send, "dp", 1 << bit) if bit else got
        if bit == n_dp.bit_length() - 3:
            return keep, got
        count, per, ff = keep.shape
        out = shaped(count // 2, per, ff)
        keep, send = call(
            functools.partial(halve_kernel, bit + 1), [out, out], keep, got, after=after if bit == 0 else (), name="halve",
            scratch_shapes=[pltpu.VMEM(keep.shape, F32)],
        )


def gather_replicas(keep, got, shard):
    n_dp = lax.axis_size("dp")
    last = n_dp.bit_length() - 2
    count, per, ff = keep.shape
    columns = ff + shard.shape[0] * shard.shape[1] // (count * per)
    both = shaped(count, per, columns)
    total = call(half_sum_kernel, both, keep, got, shard, name="half_sum")
    mine = call(functools.partial(sum_kernel, 1.0 / n_dp), both, total, swap(total, "dp", 1 << last), name="mean")
    for bit in range(last - 1, 0, -1):
        other = swap(mine, "dp", 1 << bit)
        count *= 2
        mine, shard = call(functools.partial(double_apart_kernel, bit), [shaped(count, per, ff), shaped(*shard.shape)], mine, other, name="double")
        if bit > 1:
            mine = call(add_columns_kernel, shaped(count, per, ff + (columns - ff) // (count // keep.shape[0])), mine, shard, name="add_columns")
    return mine, shard


def from_z(parts):
    got = {j: swap(parts[j], "dp", 2 * j) for j in range(len(parts) - 1, 0, -1)}
    return [parts[0]] + [got[j] for j in range(1, len(parts))]


def mean_replicas(keep, got, shard):
    n_dp = lax.axis_size("dp")
    half, per, ff = keep.shape
    piece = shaped(per, ff + shard.shape[0] * shard.shape[1] // (half * per))
    stage = pltpu.VMEM((half, *piece.shape), F32)
    parts = call(split_z_kernel, [piece] * half, keep, got, shard, name="split_z", scratch_shapes=[stage])
    parts = [parts[0], *parts[:0:-1]]
    parts = from_z(parts)
    mean = call(functools.partial(mean_kernel, n_dp), piece, parts[0], *parts[:0:-1], name="replica_mean")
    return from_z([mean] * half)


def on_device(gu, eu, gd, ed, qu, qd):
    qu, qd = qu.T, qd.T
    n_dp, n_shards = lax.axis_size("dp"), lax.axis_size("tensor")
    _, rows, ff = gu.shape
    rank = qu.shape[0]
    half, per, rows_here = n_dp // 2, rank // n_dp, rank // n_shards
    shard_rows_here = shaped(rows_here, rows)
    replica_half = shaped(half, per, ff)
    stage = pltpu.VMEM((n_dp, per, ff), F32)
    wide = pltpu.VMEM((rank, ff), F32)
    narrow = pltpu.VMEM((rank, rows), F32)
    product = 4 * rows * ff * 4 * rank

    buffers = [
        [pltpu.VMEM(g.shape[1:], BF16)] * 2 + [pltpu.VMEM(q.shape, F32), pltpu.VMEM((3 * rank, q.shape[1]), BF16), total]
        for g, q, total in ((gu, qu, narrow), (gd, qd, wide))
    ]
    *parts, keep, send = call(
        functools.partial(left_kernel, n_shards), [shard_rows_here] * n_shards + [replica_half] * 2, gu, eu, qu, gd, ed, qd,
        name="left", flops=2 * product, limit=53.75, in_specs=[HBM] * 6, out_specs=[VMEM] * n_shards + [HBM] * 2,
        scratch_shapes=buffers[0] + buffers[1] + [stage] + [pltpu.VMEM(replica_half.shape, F32)] * 2
        + [pltpu.SemaphoreType.DMA((2,)), pltpu.SemaphoreType.DMA((5, 2)), pltpu.SemaphoreType.DMA((2,))],
    )
    got = swap(send, "dp", 1)
    parts = from_shards(parts)
    parts[0], keep = call(fetch_kernel, [shard_rows_here, replica_half], parts[0], keep, name="fetch", flops=product // 4)
    shard = call(first_shards_kernel, shard_rows_here, *parts, name="shard_sum")
    keep, got = scatter_replicas(keep, send, got, (shard,))
    shard = call(first_shards_kernel, shard_rows_here, shard, swap(shard, "dp", 1), name="replica_sum")
    mine, shard = gather_replicas(keep, got, shard)
    other = swap(mine, "dp", 1)
    left_rows = from_shards([shard] * n_shards)
    left_up, gram_up, keep, send = call(
        functools.partial(right_up_kernel, n_shards), [shaped(rank, rows), shaped(rank, rank), replica_half, replica_half],
        *left_rows, gu, eu, after=(other,), name="right_up", flops=product,
        scratch_shapes=[pltpu.VMEM((3 * rank, rows), BF16), wide, stage],
    )
    left_down, *parts = call(
        right_down_kernel, [shaped(rank, ff)] + [shaped(rows_here, rows + rank * n_shards)] * n_shards, mine, other, gd, ed, after=(left_up,),
        name="right_down", flops=product, scratch_shapes=[pltpu.VMEM((3 * rank, ff), BF16), narrow, stage],
    )
    got = swap(send, "dp", 1)
    shard, gram_down = call(
        functools.partial(sum_shards_kernel, n_shards), [shard_rows_here, shaped(rank, rank)], *from_shards(parts), name="shard_sum"
    )
    pieces = mean_replicas(keep, got, shard)
    mine = call(stack_kernel, shaped(half, *pieces[0].shape), *pieces, name="stack_z")
    other = swap(mine, "dp", 1)
    inv_up, inv_down, lhs_up, lhs_down = call(
        basis_kernel,
        [shaped(rank, rank)] * 2 + [shaped(rows, 4 * rank, dtype=BF16), shaped(ff, 4 * rank, dtype=BF16)],
        left_up, left_down, gram_up, gram_down, gu, eu, gd, ed, mine, name="basis", in_specs=[VMEM] * 8 + [ANY],
    )
    rhs_up, shard = call(
        factor_up_kernel, [shaped(4 * rank, ff, dtype=BF16), shaped(rows_here, rows + 128)], mine, other, inv_up,
        name="factor_up", scratch_shapes=[wide, stage],
    )
    right_rows = from_shards([shard] * n_shards)
    new_error_up, rebuilt_up, merged_down = call(
        error_up_kernel, [shaped(1, rows, ff, dtype=BF16), shaped(rows, ff), shaped(ff, rows)], gu, eu, lhs_up, rhs_up, gd, ed, name="error_up", flops=product // 2,
        out_specs=[HBM, VMEM, VMEM], limit=16, scratch_shapes=[pltpu.VMEM((rows, ff), BF16), pltpu.SemaphoreType.DMA((STEPS,))],
    )
    limit = CLIP_RMS * (2.0 * rows * ff * n_shards) ** 0.5
    outs = [shaped(1, ff, rows, dtype=BF16), shaped(rows, ff, dtype=BF16), shaped(ff, rows, dtype=BF16)]
    new_error_down, update_up, update_down = call(
        functools.partial(last_kernel, limit, n_shards), outs, *right_rows, inv_down, merged_down, rebuilt_up, lhs_down, name="last",
        flops=product, limit=16, out_specs=[HBM] * 3,
        scratch_shapes=[narrow, pltpu.VMEM((4 * rank, rows), BF16)] + [pltpu.VMEM(shape, BF16) for shape in ((ff, rows), (rows, ff), (ff, rows))]
        + [pltpu.SemaphoreType.DMA((3 * STEPS,))],
    )
    return new_error_up, update_up, new_error_down, update_down


def solution(mesh):
    placed = (
        P("dp", None, "tensor"),
        P("dp", None, "tensor"),
        P("dp", "tensor", None),
        P("dp", "tensor", None),
        P("tensor", None),
        P(),
    )
    return jax.shard_map(
        on_device,
        mesh=mesh,
        in_specs=placed,
        out_specs=(
            P("dp", None, "tensor"),
            P(None, "tensor"),
            P("dp", "tensor", None),
            P("tensor", None),
        ),
        check_vma=False,
    )
```
